32 devices in a mesh: seq: 8 (over z, x), head: 4 (over y, core).
Axes of the slice: x: 2, y: 2, z: 4, core: 2. Of those that a mesh axis runs over, the one named last changes fastest.
Arguments:
- query_rows: bfloat16 [2048, 4096], P('seq', 'head'), may hold values from -6 to 6
- key_rows: bfloat16 [2048, 4096], P('seq', 'head'), may hold values from -6 to 6
- value_rows: bfloat16 [2048, 4096], P('seq', 'head'), may hold values from -150 to 150
- log_decay: float32 [32, 2048], P('head', 'seq'), may hold values from -3 to 0
- out_grad: bfloat16 [2048, 4096], P('seq', 'head'), may hold values from -6 to 6
- norm_gain: float32 [4096], P('head'), may hold values from 0.1 to 1.9
- state_in: float32 [32, 128, 128], P('head'), may hold values from -96 to 96
- state_out_grad: float32 [32, 128, 128], P('head'), may hold values from -0.4375 to 0.4375
Outputs:
- query_grad: bfloat16 [2048, 4096], P('seq', 'head')
- key_grad: bfloat16 [2048, 4096], P('seq', 'head')
- value_grad: bfloat16 [2048, 4096], P('seq', 'head')
- state_in_grad: float32 [32, 128, 128], P('head')
The draws below stay inside these ranges and needn't reach their ends.
All inputs are finite; a program needn't handle non-finite values.
Results may differ from the reference program's by a relative error of at most 0.0059.
Values sent between devices are 32-bit elements; how exact they have to be, the bound alone decides.
No kernel may reach another device: no remote copies, remote signals or barrier semaphores. Data moves between devices by JAX's collectives and lax.ppermute only.
A program may use at most 128 MiB of HBM per device.

```python
import jax
import jax.numpy as jnp
from jax import lax

HEAD_COUNT = 32
DH = 128
TOK_DEV = 256
SLAB_TOKENS = 2048


def draw_value_rows(key, part):
    random_keys = jax.random.split(key, 3)
    head_position = (jnp.arange(HEAD_COUNT) + jax.random.uniform(random_keys[0], (HEAD_COUNT,))) / HEAD_COUNT
    head_scale = jnp.repeat(jnp.power(10.0, head_position), DH)
    token_scale = jnp.exp(jax.random.uniform(random_keys[1], (SLAB_TOKENS, 1), minval=0.0, maxval=jnp.log(10.0)))
    base_rows = jnp.clip(jax.random.normal(random_keys[2], (SLAB_TOKENS, HEAD_COUNT * DH)), -6.0, 6.0)
    return (0.25 * base_rows * head_scale[None, :] * token_scale).astype(jnp.bfloat16)


def draw_log_decay(key, part):
    random_keys = jax.random.split(key, 7)
    slow_share = 0.5
    is_slow = jax.random.uniform(random_keys[0], (HEAD_COUNT,)) < slow_share
    slow_rate = jnp.exp(jax.random.uniform(random_keys[1], (HEAD_COUNT,), minval=jnp.log(0.05), maxval=jnp.log(0.3))) / SLAB_TOKENS
    fast_low = jnp.maximum(1.0 / 50.0, 4.0 / TOK_DEV)
    fast_high = jnp.maximum(1.0 / 30.0, 6.0 / TOK_DEV)
    fast_rate = jnp.exp(jax.random.uniform(random_keys[2], (HEAD_COUNT,), minval=jnp.log(fast_low), maxval=jnp.log(fast_high)))
    baseline_rate = jnp.where(is_slow, slow_rate, fast_rate)
    segment_count = SLAB_TOKENS // TOK_DEV
    segment_scale = jnp.exp(jax.random.uniform(random_keys[3], (HEAD_COUNT, segment_count), minval=-jnp.log(2.0), maxval=jnp.log(2.0)))
    whole_segment = jnp.repeat(segment_scale, TOK_DEV, axis=1)
    token_noise = jnp.exp(jax.random.uniform(random_keys[4], (HEAD_COUNT, SLAB_TOKENS), minval=jnp.log(0.7), maxval=jnp.log(1.4)))
    spike_positions = jax.random.randint(random_keys[5], (HEAD_COUNT, 2), 0, SLAB_TOKENS)
    spike_loss = jax.random.uniform(random_keys[6], (HEAD_COUNT, 2), minval=jnp.log(0.5), maxval=jnp.log(0.8))
    token_places = jnp.arange(SLAB_TOKENS)
    spike_events = jnp.sum(jnp.where(token_places[None, :, None] == spike_positions[:, None, :], spike_loss[:, None, :], 0.0), axis=2)
    return (-baseline_rate[:, None] * whole_segment * token_noise + spike_events).astype(jnp.float32)


def shard_levels(stream_key, shape, cuts, least, high):
    def one(position, blocks):
        steps = jax.random.uniform(jax.random.fold_in(jax.random.fold_in(stream_key, 6), position), (blocks,), jnp.float32, least / len(cuts), high / len(cuts))
        return jnp.repeat(jnp.exp(steps), shape[position] // blocks).reshape((-1,) + (1,) * (len(shape) - position - 1))

    factor_of = one(*cuts[0])
    for cut in cuts[1:]:
        factor_of = factor_of * one(*cut)
    return factor_of


def noise(rng, shape, scale, most, cuts=(), dtype=jnp.bfloat16):
    gain = shard_levels(rng, shape, cuts, -0.22, 0.18) if cuts else 1.0
    result = jax.random.normal(rng, shape, jnp.float32) * scale * gain
    return jnp.minimum(jnp.maximum(result, -most), most).astype(dtype)


def setup_inputs(seed: int = 0) -> dict:
    seeds = jax.random.split(jax.random.key(seed), 9)
    query_rows = noise(seeds[0], (SLAB_TOKENS, HEAD_COUNT * DH), 1.0, 6.0, ((0, 8), (1, 4)))
    key_rows = noise(seeds[1], (SLAB_TOKENS, HEAD_COUNT * DH), 1.0, 6.0, ((0, 8), (1, 4)))
    value_rows = draw_value_rows(jax.random.fold_in(seeds[8], 71), 0)
    log_decay = draw_log_decay(jax.random.fold_in(seeds[8], 71), 0)
    out_grad = noise(seeds[4], (SLAB_TOKENS, HEAD_COUNT * DH), 1.0, 6.0, ((0, 8), (1, 4)))
    norm_gain = jnp.clip(1.0 + 0.18 * jax.random.normal(seeds[5], (HEAD_COUNT * DH,), jnp.float32), 0.1, 1.9)
    state_in = noise(seeds[6], (HEAD_COUNT, DH, DH), 16.0, 96.0, ((0, 4),), jnp.float32)
    state_out_grad = noise(seeds[7], (HEAD_COUNT, DH, DH), 0.03, 0.4375, ((0, 4),), jnp.float32)
    return dict(query_rows=query_rows, key_rows=key_rows, value_rows=value_rows, log_decay=log_decay, out_grad=out_grad, norm_gain=norm_gain, state_in=state_in, state_out_grad=state_out_grad)


EPSILON = 1e-06

def round_bf(values):
    return lax.optimization_barrier(values.astype(jnp.bfloat16)).astype(jnp.float32)

def decay_tables(decay_rows):
    cum_log = jnp.cumsum(decay_rows, axis=1)
    block_log = cum_log[:, -1]
    length = decay_rows.shape[1]
    causal = jnp.arange(length)[:, None] >= jnp.arange(length)[None, :]
    spread = cum_log[:, :, None] - cum_log[:, None, :]
    decay_mat = jnp.where(causal[None], jnp.exp(jnp.minimum(spread, 0.0)), 0.0)
    return (cum_log, block_log, decay_mat)

def reference(query_rows, key_rows, value_rows, log_decay, out_grad, norm_gain, state_in, state_out_grad):
    block_count = SLAB_TOKENS // TOK_DEV
    feature_count = HEAD_COUNT * DH
    block_shape = (block_count, TOK_DEV, HEAD_COUNT, DH)
    query_blocks = query_rows.reshape(block_shape)
    key_blocks = key_rows.reshape(block_shape)
    value_blocks = value_rows.reshape(block_shape)
    grad_blocks = out_grad.reshape(block_count, TOK_DEV, feature_count)
    decay_blocks = log_decay.reshape(HEAD_COUNT, block_count, TOK_DEV).transpose(1, 0, 2)

    def forward_step(states_prev, inputs):
        query_heads, key_heads, value_heads, grad_rows, decay_rows = inputs
        cum_log, block_log, decay_mat = decay_tables(decay_rows)
        query_f = query_heads.astype(jnp.float32)
        key_f = key_heads.astype(jnp.float32)
        value_f = value_heads.astype(jnp.float32)
        growth = jnp.exp(cum_log).T[:, :, None]
        shrink = jnp.exp(block_log[:, None] - cum_log).T[:, :, None]
        states_bf = round_bf(states_prev)
        weights = round_bf(jnp.einsum('thd,shd->hts', query_f, key_f) * decay_mat)
        attended = jnp.einsum('hts,shd->thd', weights, value_f) + growth * jnp.einsum('thd,hde->the', query_f, states_bf)
        flat_rows = attended.reshape(TOK_DEV, feature_count)
        inv_rms = lax.rsqrt(lax.optimization_barrier(jnp.mean(flat_rows * flat_rows, axis=1)) + EPSILON)
        gained = norm_gain[None, :] * grad_rows.astype(jnp.float32)
        inner = lax.optimization_barrier(jnp.sum(gained * flat_rows, axis=1))
        attn_grad = round_bf(gained * inv_rms[:, None] - flat_rows * (inner * inv_rms ** 3 / feature_count)[:, None])
        grad_heads = attn_grad.reshape(TOK_DEV, HEAD_COUNT, DH)
        score_grad = round_bf(jnp.einsum('the,she->hts', grad_heads, value_f) * decay_mat)
        query_grad = jnp.einsum('hts,shd->thd', score_grad, key_f) + growth * jnp.einsum('the,hde->thd', grad_heads, states_bf)
        key_part = jnp.einsum('hts,thd->shd', score_grad, query_f)
        value_part = jnp.einsum('hts,the->she', weights, grad_heads)
        key_decayed = round_bf(key_f * shrink)
        summary = jnp.einsum('shd,she->hde', key_decayed, value_f)
        query_decayed = round_bf(query_f * growth)
        grad_summary = jnp.einsum('thd,the->hde', query_decayed, grad_heads)
        states_next = jnp.exp(block_log)[:, None, None] * states_prev + summary
        return (states_next, (query_grad.astype(jnp.bfloat16), key_part, value_part, grad_summary, block_log))
    unused_state, per_block = lax.scan(forward_step, state_in, (query_blocks, key_blocks, value_blocks, grad_blocks, decay_blocks))
    query_grads, key_parts, value_parts, grad_summaries, block_logs = per_block

    def reverse_step(grads_here, inputs):
        summary_here, log_here = inputs
        return (summary_here + jnp.exp(log_here)[:, None, None] * grads_here, grads_here)
    final_carry, grads_all = lax.scan(reverse_step, state_out_grad, (grad_summaries, block_logs), reverse=True)

    def finish_step(inputs):
        key_heads, value_heads, decay_rows, key_part, value_part, grads_here = inputs
        cum_log = jnp.cumsum(decay_rows, axis=1)
        block_log = cum_log[:, -1]
        shrink = jnp.exp(block_log[:, None] - cum_log).T[:, :, None]
        grads_bf = round_bf(grads_here)
        key_f = key_heads.astype(jnp.float32)
        value_f = value_heads.astype(jnp.float32)
        key_grad = key_part + shrink * jnp.einsum('hde,she->shd', grads_bf, value_f)
        value_grad = value_part + shrink * jnp.einsum('hde,shd->she', grads_bf, key_f)
        return (key_grad.astype(jnp.bfloat16), value_grad.astype(jnp.bfloat16))
    key_grads, value_grads = lax.map(finish_step, (key_blocks, value_blocks, decay_blocks, key_parts, value_parts, grads_all))
    return (query_grads.reshape(SLAB_TOKENS, feature_count), key_grads.reshape(SLAB_TOKENS, feature_count), value_grads.reshape(SLAB_TOKENS, feature_count), final_carry)
```

```python
import functools

import jax
import jax.numpy as jnp
from jax import lax
from jax.experimental import pallas as pl
from jax.experimental.pallas import tpu as pltpu
from jax.sharding import PartitionSpec as P

EPSILON = 1e-06
F32 = jnp.float32
BF16 = jnp.bfloat16
LOG_ROWS = 8
MASKED = -1e30

CONTRACT_ROWS = (((0,), (0,)), ((), ()))
CONTRACT_COLS = (((1,), (1,)), ((), ()))
VMEM = pl.BlockSpec(memory_space=pltpu.VMEM)


def call(body, outs, operands, scratch=(), flops=0):
    size = sum(x.size * x.dtype.itemsize for x in (*operands, *outs))
    return pl.pallas_call(
        body,
        out_shape=outs,
        in_specs=[VMEM] * len(operands),
        out_specs=[VMEM] * len(outs),
        scratch_shapes=list(scratch),
        compiler_params=pltpu.CompilerParams(vmem_limit_bytes=40 * 1024 * 1024),
        cost_estimate=pl.CostEstimate(flops=flops, bytes_accessed=size, transcendentals=0),
    )(*operands)


def shaped(shape, dtype=F32):
    return jax.ShapeDtypeStruct(shape, dtype)


def dot(a, b, dims=(((1,), (0,)), ((), ()))):
    return lax.dot_general(a, b, dims, preferred_element_type=F32)


def exact_dot(a, b, dims=(((1,), (0,)), ((), ()))):
    return lax.dot_general(
        a, b, dims, precision=lax.Precision.HIGHEST, preferred_element_type=F32
    )


def lanes(h, size):
    return slice(h * size, (h + 1) * size)


def share_rows(rows, count):
    share = 8
    while share * count < rows:
        share *= 2
    return share


def causal_mask(length):
    row = lax.broadcasted_iota(jnp.int32, (length, length), 0)
    col = lax.broadcasted_iota(jnp.int32, (length, length), 1)
    return row >= col


def summary_body(heads, size, share, key_ref, value_ref, decay_ref, send_ref, cum_ref, cum_col_ref):
    length = key_ref.shape[0]
    decay = decay_ref[...]
    causal = jnp.where(causal_mask(length), 1.0, 0.0)
    cum_col = exact_dot(causal, decay, CONTRACT_COLS)
    cum_ref[...] = exact_dot(decay, causal, CONTRACT_COLS)
    cum_col_ref[...] = cum_col
    block_log = cum_col[length - 1 : length, :]
    shrink = jnp.exp(block_log - cum_col)
    per_head = size // share
    for h in range(heads):
        key_decayed = (key_ref[:, lanes(h, size)].astype(F32) * shrink[:, h : h + 1]).astype(BF16)
        summary = dot(key_decayed, value_ref[:, lanes(h, size)], CONTRACT_ROWS)
        log_rows = jnp.broadcast_to(block_log[:, h : h + 1], (LOG_ROWS, size))
        for part in range(per_head):
            send_ref[h * per_head + part, :share] = summary[part * share : (part + 1) * share]
            send_ref[h * per_head + part, share:] = log_rows
    for spare in range(heads * per_head, send_ref.shape[0]):
        send_ref[spare] = jnp.zeros(send_ref.shape[1:], F32)


def own_rows(ref, share):
    start = lax.axis_index("seq") * share
    start = jnp.where(start < ref.shape[0], start, 0)
    return ref[pl.ds(pl.multiple_of(start, share), share), :]


def forward_scan_body(share, parts_ref, state_ref, states_ref, logs_ref):
    state = own_rows(state_ref, share)
    for b in range(parts_ref.shape[0]):
        states_ref[b] = state
        logs = parts_ref[b, share:]
        logs_ref[b] = logs
        state = jnp.exp(logs[:1]) * state + parts_ref[b, :share]


def reverse_scan_body(share, parts_ref, logs_ref, state_ref, grads_ref, total_ref):
    grad = own_rows(state_ref, share)
    for b in reversed(range(parts_ref.shape[0])):
        grads_ref[b] = grad
        grad = jnp.exp(logs_ref[b][:1]) * grad + parts_ref[b]
    total_ref[...] = grad


def decay_matrix(cum_ref, cum_col, causal, h):
    spread = cum_col[:, h : h + 1] - cum_ref[h : h + 1, :]
    return jnp.exp(jnp.where(causal, jnp.minimum(spread, 0.0), MASKED))


def intra_body(heads, size, query_ref, key_ref, value_ref, cum_ref, cum_col_ref, weight_ref, intra_ref):
    causal = causal_mask(query_ref.shape[0])
    cum_col = cum_col_ref[...]
    for h in range(heads):
        cut = lanes(h, size)
        scores = dot(query_ref[:, cut], key_ref[:, cut], CONTRACT_COLS)
        weights = (scores * decay_matrix(cum_ref, cum_col, causal, h)).astype(BF16)
        weight_ref[h] = weights
        intra_ref[:, cut] = dot(weights, value_ref[:, cut])


def attended_body(
    heads, size, intra_ref, query_ref, states_ref, cum_col_ref, upstream_ref, gain_ref, attended_ref, sums_ref
):
    length = query_ref.shape[0]
    growth = jnp.exp(cum_col_ref[...])
    square = jnp.zeros((length, size), F32)
    inner = jnp.zeros((length, size), F32)
    for h in range(heads):
        cut = lanes(h, size)
        carried = dot(query_ref[:, cut], states_ref[h].astype(BF16))
        attended = intra_ref[:, cut] + growth[:, h : h + 1] * carried
        attended_ref[:, cut] = attended
        square += attended * attended
        inner += gain_ref[:, cut] * upstream_ref[:, cut].astype(F32) * attended
    ones = jnp.ones((1, size), F32)
    sums_ref[...] = jnp.concatenate(
        [exact_dot(ones, square, CONTRACT_COLS), exact_dot(ones, inner, CONTRACT_COLS)]
        + [jnp.zeros((6, length), F32)],
        axis=0,
    )


def attn_grad_body(
    heads,
    size,
    share,
    feature_count,
    attended_ref,
    sums_ref,
    query_ref,
    cum_col_ref,
    upstream_ref,
    gain_ref,
    attn_grad_ref,
    send_ref,
):
    sums = jnp.sum(sums_ref[...], axis=0)
    inv_row = lax.rsqrt(sums[:1] / feature_count + EPSILON)
    coefficient_row = sums[1:2] * inv_row * inv_row * inv_row / feature_count
    columns = jnp.transpose(
        jnp.concatenate([inv_row, coefficient_row, jnp.zeros_like(sums[2:])], axis=0)
    )
    inv_rms, coefficient = columns[:, :1], columns[:, 1:2]
    growth = jnp.exp(cum_col_ref[...])
    per_head = size // share
    for h in range(heads):
        cut = lanes(h, size)
        gained = gain_ref[:, cut] * upstream_ref[:, cut].astype(F32)
        attn_grad = (gained * inv_rms - attended_ref[:, cut] * coefficient).astype(BF16)
        attn_grad_ref[:, cut] = attn_grad
        query_decayed = (query_ref[:, cut].astype(F32) * growth[:, h : h + 1]).astype(BF16)
        summary = dot(query_decayed, attn_grad, CONTRACT_ROWS)
        for part in range(per_head):
            send_ref[h * per_head + part] = summary[part * share : (part + 1) * share]
    for spare in range(heads * per_head, send_ref.shape[0]):
        send_ref[spare] = jnp.zeros(send_ref.shape[1:], F32)


def score_grad_body(
    heads,
    size,
    attn_grad_ref,
    query_ref,
    key_ref,
    value_ref,
    states_ref,
    weight_ref,
    cum_ref,
    cum_col_ref,
    query_grad_ref,
    key_part_ref,
    value_part_ref,
):
    causal = causal_mask(query_ref.shape[0])
    cum_col = cum_col_ref[...]
    growth = jnp.exp(cum_col)
    for h in range(heads):
        cut = lanes(h, size)
        attn_grad = attn_grad_ref[:, cut]
        scores = dot(attn_grad, value_ref[:, cut], CONTRACT_COLS)
        score_grad = (scores * decay_matrix(cum_ref, cum_col, causal, h)).astype(BF16)
        carried = dot(attn_grad, states_ref[h].astype(BF16), CONTRACT_COLS)
        query_grad = dot(score_grad, key_ref[:, cut]) + growth[:, h : h + 1] * carried
        query_grad_ref[:, cut] = query_grad.astype(BF16)
        key_part_ref[:, cut] = dot(score_grad, query_ref[:, cut], CONTRACT_ROWS)
        value_part_ref[:, cut] = dot(weight_ref[h], attn_grad, CONTRACT_ROWS)


def finish_body(
    heads, size, key_part_ref, value_part_ref, key_ref, value_ref, grads_ref, cum_col_ref, key_grad_ref, value_grad_ref
):
    length = key_ref.shape[0]
    cum_col = cum_col_ref[...]
    shrink = jnp.exp(cum_col[length - 1 : length, :] - cum_col)
    for h in range(heads):
        cut = lanes(h, size)
        grads = grads_ref[h].astype(BF16)
        column = shrink[:, h : h + 1]
        key_state = dot(value_ref[:, cut], grads, CONTRACT_COLS)
        key_grad_ref[:, cut] = (key_part_ref[:, cut] + column * key_state).astype(BF16)
        value_state = dot(key_ref[:, cut], grads)
        value_grad_ref[:, cut] = (value_part_ref[:, cut] + column * value_state).astype(BF16)


def swap(parts):
    return lax.all_to_all(parts, "seq", 0, 0)


def on_device(
    query_rows, key_rows, value_rows, log_decay, out_grad, norm_gain, state_in, state_out_grad
):
    heads, length = log_decay.shape
    size = state_in.shape[1]
    width = heads * size
    blocks = lax.axis_size("seq")
    share = share_rows(width, blocks)
    feature_count = width * lax.axis_size("head")
    gain = norm_gain.reshape(1, width)

    send, cum_log, cum_col = call(
        functools.partial(summary_body, heads, size, share),
        [
            shaped((blocks, share + LOG_ROWS, size)),
            shaped((heads, length)),
            shaped((length, heads)),
        ],
        [key_rows, value_rows, log_decay],
    )
    parts = swap(send)
    weights, intra = call(
        functools.partial(intra_body, heads, size),
        [shaped((heads, length, length), BF16), shaped((length, width))],
        [query_rows, key_rows, value_rows, cum_log, cum_col],
        flops=4 * heads * length * length * size,
    )
    states, logs = call(
        functools.partial(forward_scan_body, share),
        [shaped((blocks, share, size)), shaped((blocks, LOG_ROWS, size))],
        [parts, state_in.reshape(width, size)],
    )
    states = swap(states).reshape(-1, size)[:width].reshape(heads, size, size)
    attended, sums = call(
        functools.partial(attended_body, heads, size),
        [shaped((length, width)), shaped((8, length))],
        [intra, query_rows, states, cum_col, out_grad, gain],
    )
    all_sums = lax.psum(sums, "head")[None]
    attn_grad, send = call(
        functools.partial(attn_grad_body, heads, size, share, feature_count),
        [shaped((length, width), BF16), shaped((blocks, share, size))],
        [attended, all_sums, query_rows, cum_col, out_grad, gain],
    )
    parts = swap(send)
    query_grad, key_part, value_part = call(
        functools.partial(score_grad_body, heads, size),
        [shaped((length, width), BF16), shaped((length, width)), shaped((length, width))],
        [attn_grad, query_rows, key_rows, value_rows, states, weights, cum_log, cum_col],
        flops=10 * heads * length * length * size,
    )
    grads, total = call(
        functools.partial(reverse_scan_body, share),
        [shaped((blocks, share, size)), shaped((share, size))],
        [parts, logs, state_out_grad.reshape(width, size)],
    )
    grads = swap(grads).reshape(-1, size)[:width].reshape(heads, size, size)
    state_in_grad = lax.all_gather(total, "seq").reshape(-1, size)[:width]
    key_grad, value_grad = call(
        functools.partial(finish_body, heads, size),
        [shaped((length, width), BF16), shaped((length, width), BF16)],
        [key_part, value_part, key_rows, value_rows, grads, cum_col],
    )
    return (query_grad, key_grad, value_grad, state_in_grad.reshape(heads, size, size))


def solution(mesh):
    return jax.shard_map(
        on_device,
        mesh=mesh,
        in_specs=(
            P("seq", "head"),
            P("seq", "head"),
            P("seq", "head"),
            P("head", "seq"),
            P("seq", "head"),
            P("head"),
            P("head", None, None),
            P("head", None, None),
        ),
        out_specs=(P("seq", "head"), P("seq", "head"), P("seq", "head"), P("head", None, None)),
        check_vma=False,
    )
```

```python
import functools

import jax
import jax.numpy as jnp
from jax import lax
from jax.experimental import pallas as pl
from jax.experimental.pallas import tpu as pltpu
from jax.sharding import PartitionSpec as P

EPSILON = 1e-06
F32 = jnp.float32
BF16 = jnp.bfloat16
LOG_ROWS = 8
MASKED = -1e30

CONTRACT_ROWS = (((0,), (0,)), ((), ()))
CONTRACT_COLS = (((1,), (1,)), ((), ()))
VMEM = pl.BlockSpec(memory_space=pltpu.VMEM)


def call(body, outs, operands, scratch=(), flops=0):
    size = sum(x.size * x.dtype.itemsize for x in (*operands, *outs))
    return pl.pallas_call(
        body,
        out_shape=outs,
        in_specs=[VMEM] * len(operands),
        out_specs=[VMEM] * len(outs),
        scratch_shapes=list(scratch),
        compiler_params=pltpu.CompilerParams(vmem_limit_bytes=24 * 1024 * 1024),
        cost_estimate=pl.CostEstimate(flops=flops, bytes_accessed=size, transcendentals=0),
    )(*operands)


def shaped(shape, dtype=F32):
    return jax.ShapeDtypeStruct(shape, dtype)


def dot(a, b, dims=(((1,), (0,)), ((), ()))):
    return lax.dot_general(a, b, dims, preferred_element_type=F32)


def exact_dot(a, b, dims=(((1,), (0,)), ((), ()))):
    return lax.dot_general(
        a, b, dims, precision=lax.Precision.HIGHEST, preferred_element_type=F32
    )


def lanes(h, size):
    return slice(h * size, (h + 1) * size)


def causal_mask(length):
    row = lax.broadcasted_iota(jnp.int32, (length, length), 0)
    col = lax.broadcasted_iota(jnp.int32, (length, length), 1)
    return row >= col


class Plan:
    def __init__(self, heads, size, blocks):
        self.heads, self.size, self.blocks = heads, size, blocks
        self.members = next(m for m in (4, 2, 1) if heads % m == 0 and blocks % m == 0)
        self.groups = blocks // self.members
        self.own = heads // self.members
        self.rows = self.own * size

    def member(self):
        return lax.rem(lax.axis_index("seq"), self.members)

    def group(self):
        return lax.div(lax.axis_index("seq"), self.members)

    def peer(self, k):
        return lax.bitwise_xor(self.member(), k)

    def rows_of(self, member):
        return pl.ds(pl.multiple_of(member * self.rows, self.rows), self.rows)

    def swap_in_group(self, pieces):
        span = self.members
        return [pieces[0]] + [
            lax.ppermute(
                pieces[k], "seq", [(i, i // span * span + (i % span ^ k)) for i in range(self.blocks)]
            )
            for k in range(1, span)
        ]

    def from_groups(self, piece, earlier_only):
        received = []
        for step in range(1, self.groups):
            pairs = [(i, i + step * self.members) for i in range(self.blocks)]
            if earlier_only:
                pairs = [(i, j) for i, j in pairs if j < self.blocks]
            else:
                pairs = [(i, j % self.blocks) for i, j in pairs]
            received.append(lax.ppermute(piece, "seq", pairs))
        return received


def own_decays(plan, log_tile_ref, base):
    first = base + plan.member() * plan.own
    rows = [log_tile_ref[pl.ds(first + j, 1), :] for j in range(plan.own)]
    return jnp.concatenate([jnp.broadcast_to(jnp.exp(row), (plan.size, plan.size)) for row in rows])


def summary_body(plan, key_ref, value_ref, decay_ref, *refs):
    send_refs, (cum_ref, cum_col_ref, held_ref) = refs[: plan.members], refs[plan.members :]
    length, heads, size = key_ref.shape[0], plan.heads, plan.size
    decay = decay_ref[...]
    causal = jnp.where(causal_mask(length), 1.0, 0.0)
    cum_col = exact_dot(causal, decay, CONTRACT_COLS)
    cum_row = exact_dot(decay, causal, CONTRACT_COLS)
    cum_ref[...] = cum_row
    cum_col_ref[...] = cum_col
    block_log = cum_col[length - 1 : length, :]
    shrink = jnp.exp(block_log - cum_col)
    for h in range(heads):
        key_decayed = (key_ref[:, lanes(h, size)].astype(F32) * shrink[:, h : h + 1]).astype(BF16)
        held_ref[h * size : (h + 1) * size] = dot(
            key_decayed, value_ref[:, lanes(h, size)], CONTRACT_ROWS
        )
    log_tile = jnp.broadcast_to(cum_row[:, length - 1 : length], (heads, size))
    if heads < LOG_ROWS:
        log_tile = jnp.concatenate([log_tile, jnp.zeros((LOG_ROWS - heads, size), F32)])
    for k, send_ref in enumerate(send_refs):
        send_ref[: plan.rows] = held_ref[plan.rows_of(plan.peer(k))]
        send_ref[plan.rows :] = log_tile


def group_total_body(plan, *refs):
    part_refs, (total_ref, logs_ref, held_ref) = refs[: plan.members], refs[plan.members :]
    for k, part_ref in enumerate(part_refs):
        held_ref[plan.peer(k)] = part_ref[...]
    total = jnp.zeros((plan.rows, plan.size), F32)
    log_total = jnp.zeros((LOG_ROWS, plan.size), F32)
    for b in range(plan.members):
        total = own_decays(plan, held_ref.at[b], plan.rows) * total + held_ref[b, : plan.rows]
        logs_ref[b] = held_ref[b, plan.rows :]
        log_total += held_ref[b, plan.rows :]
    total_ref[: plan.rows] = total
    total_ref[plan.rows :] = log_total


def stage_groups(plan, total_refs, held_ref):
    for step, total_ref in enumerate(total_refs):
        held_ref[lax.rem(plan.group() - step + plan.groups, plan.groups)] = total_ref[...]


def forward_scan_body(plan, *refs):
    part_refs, refs = refs[: plan.members], refs[plan.members :]
    total_refs, refs = refs[: plan.groups], refs[plan.groups :]
    state_ref, refs = refs[0], refs[1:]
    send_refs, (groups_ref, held_ref) = refs[: plan.members], refs[plan.members :]
    stage_groups(plan, total_refs, groups_ref)
    state = state_ref[plan.rows_of(plan.member())]
    for group in range(plan.groups - 1):
        after = own_decays(plan, groups_ref.at[group], plan.rows) * state + groups_ref[group, : plan.rows]
        state = jnp.where(group < plan.group(), after, state)
    for k, part_ref in enumerate(part_refs):
        held_ref[plan.peer(k)] = part_ref[...]
    for b in range(plan.members):
        summary = held_ref[b, : plan.rows]
        decays = own_decays(plan, held_ref.at[b], plan.rows)
        held_ref[b, : plan.rows] = state
        state = decays * state + summary
    for k, send_ref in enumerate(send_refs):
        send_ref[...] = held_ref[plan.peer(k), : plan.rows]


def group_grad_body(plan, *refs):
    part_refs, (logs_ref, total_ref, held_ref) = refs[: plan.members], refs[plan.members :]
    for k, part_ref in enumerate(part_refs):
        held_ref[plan.peer(k)] = part_ref[...]
    total = jnp.zeros((plan.rows, plan.size), F32)
    log_total = jnp.zeros((LOG_ROWS, plan.size), F32)
    for b in reversed(range(plan.members)):
        total = own_decays(plan, logs_ref.at[b], 0) * total + held_ref[b]
        log_total += logs_ref[b]
    total_ref[: plan.rows] = total
    total_ref[plan.rows :] = log_total


def reverse_scan_body(plan, *refs):
    part_refs, refs = refs[: plan.members], refs[plan.members :]
    total_refs, refs = refs[: plan.groups], refs[plan.groups :]
    (logs_ref, grad_ref), refs = refs[:2], refs[2:]
    send_refs, (all_ref, groups_ref, held_ref) = refs[: plan.members], refs[plan.members :]
    stage_groups(plan, total_refs, groups_ref)
    grad = grad_ref[plan.rows_of(plan.member())]
    leaving = grad
    for group in reversed(range(plan.groups)):
        leaving = jnp.where(group == plan.group(), grad, leaving)
        grad = own_decays(plan, groups_ref.at[group], plan.rows) * grad + groups_ref[group, : plan.rows]
    all_ref[...] = grad
    for k, part_ref in enumerate(part_refs):
        held_ref[plan.peer(k)] = part_ref[...]
    grad = leaving
    for b in reversed(range(plan.members)):
        summary = held_ref[b]
        held_ref[b] = grad
        grad = own_decays(plan, logs_ref.at[b], 0) * grad + summary
    for k, send_ref in enumerate(send_refs):
        send_ref[...] = held_ref[plan.peer(k)]


def decay_matrix(cum_ref, cum_col, causal, h):
    spread = cum_col[:, h : h + 1] - cum_ref[h : h + 1, :]
    return jnp.exp(jnp.where(causal, jnp.minimum(spread, 0.0), MASKED))


def intra_body(plan, query_ref, key_ref, value_ref, cum_ref, cum_col_ref, weight_ref, intra_ref):
    causal = causal_mask(query_ref.shape[0])
    cum_col = cum_col_ref[...]
    for h in range(plan.heads):
        cut = lanes(h, plan.size)
        scores = dot(query_ref[:, cut], key_ref[:, cut], CONTRACT_COLS)
        weights = (scores * decay_matrix(cum_ref, cum_col, causal, h)).astype(BF16)
        weight_ref[h] = weights
        intra_ref[:, cut] = dot(weights, value_ref[:, cut])


def gather_rounded(plan, piece_refs, whole_ref):
    for k, piece_ref in enumerate(piece_refs):
        whole_ref[plan.rows_of(plan.peer(k))] = piece_ref[...].astype(BF16)


def attended_body(plan, *refs):
    state_refs, refs = refs[: plan.members], refs[plan.members :]
    intra_ref, query_ref, cum_col_ref, upstream_ref, gain_ref = refs[:5]
    attended_ref, sums_ref, states_ref = refs[5:]
    size, length = plan.size, query_ref.shape[0]
    gather_rounded(plan, state_refs, states_ref)
    growth = jnp.exp(cum_col_ref[...])
    square = jnp.zeros((length, size), F32)
    inner = jnp.zeros((length, size), F32)
    for h in range(plan.heads):
        cut = lanes(h, size)
        carried = dot(query_ref[:, cut], states_ref[cut])
        attended = intra_ref[:, cut] + growth[:, h : h + 1] * carried
        attended_ref[:, cut] = attended
        square += attended * attended
        inner += gain_ref[:, cut] * upstream_ref[:, cut].astype(F32) * attended
    ones = jnp.ones((1, size), F32)
    sums_ref[...] = jnp.concatenate(
        [exact_dot(ones, square, CONTRACT_COLS), exact_dot(ones, inner, CONTRACT_COLS)]
        + [jnp.zeros((6, length), F32)],
        axis=0,
    )


def attn_grad_body(plan, parties, *refs):
    sums_refs, refs = refs[:parties], refs[parties:]
    attended_ref, query_ref, cum_col_ref, upstream_ref, gain_ref = refs[:5]
    attn_grad_ref, refs = refs[5], refs[6:]
    send_refs, (held_ref,) = refs[: plan.members], refs[plan.members :]
    size = plan.size
    feature_count = plan.heads * size * parties
    sums = sum(ref[...] for ref in sums_refs)
    inv_row = lax.rsqrt(sums[:1] / feature_count + EPSILON)
    coefficient_row = sums[1:2] * inv_row * inv_row * inv_row / feature_count
    columns = jnp.transpose(
        jnp.concatenate([inv_row, coefficient_row, jnp.zeros_like(sums[2:])], axis=0)
    )
    inv_rms, coefficient = columns[:, :1], columns[:, 1:2]
    growth = jnp.exp(cum_col_ref[...])
    for h in range(plan.heads):
        cut = lanes(h, size)
        gained = gain_ref[:, cut] * upstream_ref[:, cut].astype(F32)
        attn_grad = (gained * inv_rms - attended_ref[:, cut] * coefficient).astype(BF16)
        attn_grad_ref[:, cut] = attn_grad
        query_decayed = (query_ref[:, cut].astype(F32) * growth[:, h : h + 1]).astype(BF16)
        held_ref[cut] = dot(query_decayed, attn_grad, CONTRACT_ROWS)
    for k, send_ref in enumerate(send_refs):
        send_ref[...] = held_ref[plan.rows_of(plan.peer(k))]


def score_grad_body(
    plan,
    attn_grad_ref,
    query_ref,
    key_ref,
    value_ref,
    states_ref,
    weight_ref,
    cum_ref,
    cum_col_ref,
    query_grad_ref,
    key_part_ref,
    value_part_ref,
):
    causal = causal_mask(query_ref.shape[0])
    cum_col = cum_col_ref[...]
    growth = jnp.exp(cum_col)
    for h in range(plan.heads):
        cut = lanes(h, plan.size)
        attn_grad = attn_grad_ref[:, cut]
        scores = dot(attn_grad, value_ref[:, cut], CONTRACT_COLS)
        score_grad = (scores * decay_matrix(cum_ref, cum_col, causal, h)).astype(BF16)
        carried = dot(attn_grad, states_ref[cut], CONTRACT_COLS)
        query_grad = dot(score_grad, key_ref[:, cut]) + growth[:, h : h + 1] * carried
        query_grad_ref[:, cut] = query_grad.astype(BF16)
        key_part_ref[:, cut] = dot(score_grad, query_ref[:, cut], CONTRACT_ROWS)
        value_part_ref[:, cut] = dot(weight_ref[h], attn_grad, CONTRACT_ROWS)


def finish_body(plan, *refs):
    grad_refs, refs = refs[: plan.members], refs[plan.members :]
    key_part_ref, value_part_ref, key_ref, value_ref, cum_col_ref = refs[:5]
    key_grad_ref, value_grad_ref, grads_ref = refs[5:]
    length = key_ref.shape[0]
    gather_rounded(plan, grad_refs, grads_ref)
    cum_col = cum_col_ref[...]
    shrink = jnp.exp(cum_col[length - 1 : length, :] - cum_col)
    for h in range(plan.heads):
        cut = lanes(h, plan.size)
        grads = grads_ref[cut]
        column = shrink[:, h : h + 1]
        key_state = dot(value_ref[:, cut], grads, CONTRACT_COLS)
        key_grad_ref[:, cut] = (key_part_ref[:, cut] + column * key_state).astype(BF16)
        value_state = dot(key_ref[:, cut], grads)
        value_grad_ref[:, cut] = (value_part_ref[:, cut] + column * value_state).astype(BF16)


def join_body(plan, *refs):
    for k, piece_ref in enumerate(refs[:-1]):
        refs[-1][plan.rows_of(plan.peer(k))] = piece_ref[...]


def on_device(
    query_rows, key_rows, value_rows, log_decay, out_grad, norm_gain, state_in, state_out_grad
):
    heads, length = log_decay.shape
    size = state_in.shape[1]
    width = heads * size
    parties = lax.axis_size("head")
    plan = Plan(heads, size, lax.axis_size("seq"))
    bind = lambda body, *extra: functools.partial(body, plan, *extra)
    gain = norm_gain.reshape(1, width)
    piece = shaped((plan.rows, size))
    logged = shaped((plan.rows + LOG_ROWS, size))
    pieces = [piece] * plan.members
    table = shaped((length, width))
    rounded = shaped((length, width), BF16)
    hold = pltpu.VMEM((plan.members, plan.rows, size), F32)
    hold_logged = pltpu.VMEM((plan.members, plan.rows + LOG_ROWS, size), F32)
    hold_groups = pltpu.VMEM((plan.groups, plan.rows + LOG_ROWS, size), F32)
    hold_whole = pltpu.VMEM((width, size), F32)

    *sends, cum_log, cum_col = call(
        bind(summary_body),
        [logged] * plan.members + [shaped((heads, length)), shaped((length, heads))],
        [key_rows, value_rows, log_decay],
        [hold_whole],
    )
    parts = plan.swap_in_group(sends)
    weights, intra = call(
        bind(intra_body),
        [shaped((heads, length, length), BF16), table],
        [query_rows, key_rows, value_rows, cum_log, cum_col],
        flops=4 * heads * length * length * size,
    )
    total, logs = call(
        bind(group_total_body),
        [logged, shaped((plan.members, LOG_ROWS, size))],
        parts,
        [hold_logged],
    )
    totals = [total] + plan.from_groups(total, True)
    sends = call(
        bind(forward_scan_body),
        pieces,
        [*parts, *totals, state_in.reshape(width, size)],
        [hold_groups, hold_logged],
    )
    states = plan.swap_in_group(sends)
    attended, sums, states = call(
        bind(attended_body),
        [table, shaped((8, length)), shaped((width, size), BF16)],
        [*states, intra, query_rows, cum_col, out_grad, gain],
    )
    all_sums = [sums] + [
        lax.ppermute(sums, "head", [(i, (i + step) % parties) for i in range(parties)])
        for step in range(1, parties)
    ]
    attn_grad, *sends = call(
        bind(attn_grad_body, parties),
        [rounded] + pieces,
        [*all_sums, attended, query_rows, cum_col, out_grad, gain],
        [hold_whole],
    )
    parts = plan.swap_in_group(sends)
    query_grad, key_part, value_part = call(
        bind(score_grad_body),
        [rounded, table, table],
        [attn_grad, query_rows, key_rows, value_rows, states, weights, cum_log, cum_col],
        flops=10 * heads * length * length * size,
    )
    (total,) = call(bind(group_grad_body), [logged], [*parts, logs], [hold])
    totals = [total] + plan.from_groups(total, False)
    *sends, whole_total = call(
        bind(reverse_scan_body),
        pieces + [piece],
        [*parts, *totals, logs, state_out_grad.reshape(width, size)],
        [hold_groups, hold],
    )
    grads = plan.swap_in_group(sends)
    totals = plan.swap_in_group([whole_total] * plan.members)
    key_grad, value_grad = call(
        bind(finish_body),
        [rounded, rounded],
        [*grads, key_part, value_part, key_rows, value_rows, cum_col],
        [pltpu.VMEM((width, size), BF16)],
    )
    (state_in_grad,) = call(bind(join_body), [shaped((width, size))], totals)
    return (query_grad, key_grad, value_grad, state_in_grad.reshape(heads, size, size))


def solution(mesh):
    return jax.shard_map(
        on_device,
        mesh=mesh,
        in_specs=(
            P("seq", "head"),
            P("seq", "head"),
            P("seq", "head"),
            P("head", "seq"),
            P("seq", "head"),
            P("head"),
            P("head", None, None),
            P("head", None, None),
        ),
        out_specs=(P("seq", "head"), P("seq", "head"), P("seq", "head"), P("head", None, None)),
        check_vma=False,
    )
```

```python
import functools

import jax
import jax.numpy as jnp
from jax import lax
from jax.experimental import pallas as pl
from jax.experimental.pallas import tpu as pltpu
from jax.sharding import PartitionSpec as P

EPSILON = 1e-06
F32 = jnp.float32
BF16 = jnp.bfloat16
LOG_ROWS = 8
MASKED = -1e30

CONTRACT_ROWS = (((0,), (0,)), ((), ()))
CONTRACT_COLS = (((1,), (1,)), ((), ()))
VMEM = pl.BlockSpec(memory_space=pltpu.VMEM)
HBM = pl.BlockSpec(memory_space=pltpu.HBM)
ANY = pl.BlockSpec(memory_space=pl.ANY)


def call(body, outs, operands, scratch=(), flops=0, specs=None):
    size = sum(x.size * x.dtype.itemsize for x in (*operands, *outs))
    return pl.pallas_call(
        body,
        out_shape=outs,
        in_specs=specs or [VMEM] * len(operands),
        out_specs=[VMEM] * len(outs),
        scratch_shapes=list(scratch),
        compiler_params=pltpu.CompilerParams(vmem_limit_bytes=24 * 1024 * 1024),
        cost_estimate=pl.CostEstimate(flops=flops, bytes_accessed=size, transcendentals=0),
    )(*operands)


def shaped(shape, dtype=F32):
    return jax.ShapeDtypeStruct(shape, dtype)


def dot(a, b, dims=(((1,), (0,)), ((), ()))):
    return lax.dot_general(a, b, dims, preferred_element_type=F32)


def exact_dot(a, b, dims=(((1,), (0,)), ((), ()))):
    return lax.dot_general(
        a, b, dims, precision=lax.Precision.HIGHEST, preferred_element_type=F32
    )


def lanes(h, size):
    return slice(h * size, (h + 1) * size)


def causal_mask(length):
    row = lax.broadcasted_iota(jnp.int32, (length, length), 0)
    col = lax.broadcasted_iota(jnp.int32, (length, length), 1)
    return row >= col


class Plan:
    def __init__(self, heads, size, blocks):
        self.heads, self.size, self.blocks = heads, size, blocks
        self.members = next(m for m in (4, 2, 1) if heads % m == 0 and blocks % m == 0)
        self.groups = blocks // self.members
        self.own = heads // self.members
        self.rows = self.own * size
        self.ways = sorted(range(self.members), key=lambda way: (way > 0, -way.bit_count()))

    def member(self):
        return lax.rem(lax.axis_index("seq"), self.members)

    def group(self):
        return lax.div(lax.axis_index("seq"), self.members)

    def peer(self, k):
        return lax.bitwise_xor(self.member(), self.ways[k])

    def rows_of(self, member):
        return pl.ds(pl.multiple_of(member * self.rows, self.rows), self.rows)

    def swap_in_group(self, pieces):
        span = self.members
        swapped = [pieces[0]]
        for way, piece in zip(self.ways[1:], pieces[1:]):
            pairs = [(i, i // span * span + (i % span ^ way)) for i in range(self.blocks)]
            swapped.append(lax.ppermute(piece, "seq", pairs))
        return swapped

    def from_groups(self, piece):
        return [
            lax.ppermute(
                piece,
                "seq",
                [(i, (i + step * self.members) % self.blocks) for i in range(self.blocks)],
            )
            for step in range(1, self.groups)
        ]


def own_decays(plan, log_tile_ref, base):
    first = base + plan.member() * plan.own
    rows = [log_tile_ref[pl.ds(first + j, 1), :] for j in range(plan.own)]
    return jnp.concatenate([jnp.broadcast_to(jnp.exp(row), (plan.size, plan.size)) for row in rows])


def summary_body(plan, key_hbm, value_hbm, decay_hbm, *refs):
    send_refs, refs = refs[: plan.members], refs[plan.members :]
    cum_ref, cum_col_ref, held_ref, key_ref, value_ref, decay_ref, sems, decay_sem = refs
    length, heads, size = key_ref.shape[0], plan.heads, plan.size
    decay_copy = pltpu.make_async_copy(decay_hbm, decay_ref, decay_sem)
    decay_copy.start()
    copies = []
    for part in range(plan.members):
        cut = lanes(part, plan.rows)
        copies.append(
            [
                pltpu.make_async_copy(source.at[:, cut], target.at[:, cut], sems.at[part, i])
                for i, (source, target) in enumerate([(key_hbm, key_ref), (value_hbm, value_ref)])
            ]
        )
        for copy in copies[-1]:
            copy.start()
    decay_copy.wait()
    decay = decay_ref[...]
    causal = jnp.where(causal_mask(length), 1.0, 0.0)
    cum_col = exact_dot(causal, decay, CONTRACT_COLS)
    cum_row = exact_dot(decay, causal, CONTRACT_COLS)
    cum_ref[...] = cum_row
    cum_col_ref[...] = cum_col
    block_log = cum_col[length - 1 : length, :]
    shrink = jnp.exp(block_log - cum_col)
    for h in range(heads):
        if h % plan.own == 0:
            for copy in copies[h // plan.own]:
                copy.wait()
        key_decayed = (key_ref[:, lanes(h, size)].astype(F32) * shrink[:, h : h + 1]).astype(BF16)
        held_ref[h * size : (h + 1) * size] = dot(
            key_decayed, value_ref[:, lanes(h, size)], CONTRACT_ROWS
        )
    log_tile = jnp.broadcast_to(cum_row[:, length - 1 : length], (heads, size))
    if heads < LOG_ROWS:
        log_tile = jnp.concatenate([log_tile, jnp.zeros((LOG_ROWS - heads, size), F32)])
    for k, send_ref in enumerate(send_refs):
        send_ref[: plan.rows] = held_ref[plan.rows_of(plan.peer(k))]
        send_ref[plan.rows :] = log_tile


def group_total_body(plan, *refs):
    part_refs, (total_ref, logs_ref, held_ref) = refs[: plan.members], refs[plan.members :]
    for k, part_ref in enumerate(part_refs):
        held_ref[plan.peer(k)] = part_ref[...]
    total = jnp.zeros((plan.rows, plan.size), F32)
    log_total = jnp.zeros((LOG_ROWS, plan.size), F32)
    for b in range(plan.members):
        total = own_decays(plan, held_ref.at[b], plan.rows) * total + held_ref[b, : plan.rows]
        logs_ref[b] = held_ref[b, plan.rows :]
        log_total += held_ref[b, plan.rows :]
    total_ref[: plan.rows] = total
    total_ref[plan.rows :] = log_total


def stage_groups(plan, total_refs, held_ref):
    for step, total_ref in enumerate(total_refs):
        held_ref[lax.rem(plan.group() - step + plan.groups, plan.groups)] = total_ref[...]


def forward_scan_body(plan, *refs):
    part_refs, refs = refs[: plan.members], refs[plan.members :]
    total_refs, refs = refs[: plan.groups], refs[plan.groups :]
    state_ref, refs = refs[0], refs[1:]
    send_refs, (groups_ref, held_ref) = refs[: plan.members], refs[plan.members :]
    stage_groups(plan, total_refs, groups_ref)
    state = state_ref[plan.rows_of(plan.member())]
    for group in range(plan.groups - 1):
        after = own_decays(plan, groups_ref.at[group], plan.rows) * state + groups_ref[group, : plan.rows]
        state = jnp.where(group < plan.group(), after, state)
    for k, part_ref in enumerate(part_refs):
        held_ref[plan.peer(k)] = part_ref[...]
    for b in range(plan.members):
        summary = held_ref[b, : plan.rows]
        decays = own_decays(plan, held_ref.at[b], plan.rows)
        held_ref[b, : plan.rows] = state
        state = decays * state + summary
    for k, send_ref in enumerate(send_refs):
        send_ref[...] = held_ref[plan.peer(k), : plan.rows]


def group_grad_body(plan, *refs):
    part_refs, (logs_ref, total_ref, held_ref) = refs[: plan.members], refs[plan.members :]
    for k, part_ref in enumerate(part_refs):
        held_ref[plan.peer(k)] = part_ref[...]
    total = jnp.zeros((plan.rows, plan.size), F32)
    log_total = jnp.zeros((LOG_ROWS, plan.size), F32)
    for b in reversed(range(plan.members)):
        total = own_decays(plan, logs_ref.at[b], 0) * total + held_ref[b]
        log_total += logs_ref[b]
    total_ref[: plan.rows] = total
    total_ref[plan.rows :] = log_total


def reverse_scan_body(plan, *refs):
    part_refs, refs = refs[: plan.members], refs[plan.members :]
    total_refs, refs = refs[: plan.groups], refs[plan.groups :]
    (logs_ref, grad_ref, _), refs = refs[:3], refs[3:]
    send_refs, (all_ref, groups_ref, held_ref) = refs[: plan.members], refs[plan.members :]
    stage_groups(plan, total_refs, groups_ref)
    grad = grad_ref[plan.rows_of(plan.member())]
    leaving = grad
    for group in reversed(range(plan.groups)):
        leaving = jnp.where(group == plan.group(), grad, leaving)
        grad = own_decays(plan, groups_ref.at[group], plan.rows) * grad + groups_ref[group, : plan.rows]
    all_ref[...] = grad
    for k, part_ref in enumerate(part_refs):
        held_ref[plan.peer(k)] = part_ref[...]
    grad = leaving
    for b in reversed(range(plan.members)):
        summary = held_ref[b]
        held_ref[b] = grad
        grad = own_decays(plan, logs_ref.at[b], 0) * grad + summary
    for k, send_ref in enumerate(send_refs):
        send_ref[...] = held_ref[plan.peer(k)]


def decay_matrix(cum_ref, cum_col, causal, h):
    spread = cum_col[:, h : h + 1] - cum_ref[h : h + 1, :]
    return jnp.exp(jnp.where(causal, jnp.minimum(spread, 0.0), MASKED))


def intra_body(plan, query_ref, key_ref, value_ref, cum_ref, cum_col_ref, weight_ref, intra_ref):
    causal = causal_mask(query_ref.shape[0])
    cum_col = cum_col_ref[...]
    for h in range(plan.heads):
        cut = lanes(h, plan.size)
        scores = dot(query_ref[:, cut], key_ref[:, cut], CONTRACT_COLS)
        weights = (scores * decay_matrix(cum_ref, cum_col, causal, h)).astype(BF16)
        weight_ref[h] = weights
        intra_ref[:, cut] = dot(weights, value_ref[:, cut])


def gather_rounded(plan, piece_refs, whole_ref):
    for k, piece_ref in enumerate(piece_refs):
        whole_ref[plan.rows_of(plan.peer(k))] = piece_ref[...].astype(BF16)


def attended_body(plan, *refs):
    state_refs, refs = refs[: plan.members], refs[plan.members :]
    intra_ref, query_ref, cum_col_ref, upstream_ref, gain_ref = refs[:5]
    attended_ref, sums_ref, states_ref = refs[5:]
    size, length = plan.size, query_ref.shape[0]
    gather_rounded(plan, state_refs, states_ref)
    growth = jnp.exp(cum_col_ref[...])
    square = jnp.zeros((length, size), F32)
    inner = jnp.zeros((length, size), F32)
    for h in range(plan.heads):
        cut = lanes(h, size)
        carried = dot(query_ref[:, cut], states_ref[cut])
        attended = intra_ref[:, cut] + growth[:, h : h + 1] * carried
        attended_ref[:, cut] = attended
        square += attended * attended
        inner += gain_ref[:, cut] * upstream_ref[:, cut].astype(F32) * attended
    ones = jnp.ones((1, size), F32)
    sums_ref[...] = jnp.concatenate(
        [exact_dot(ones, square, CONTRACT_COLS), exact_dot(ones, inner, CONTRACT_COLS)]
        + [jnp.zeros((6, length), F32)],
        axis=0,
    )


def attn_grad_body(plan, parties, *refs):
    sums_refs, refs = refs[:parties], refs[parties:]
    attended_ref, query_ref, cum_col_ref, upstream_ref, gain_ref = refs[:5]
    attn_grad_ref, refs = refs[5], refs[6:]
    send_refs, (held_ref,) = refs[: plan.members], refs[plan.members :]
    size = plan.size
    feature_count = plan.heads * size * parties
    sums = sum(ref[...] for ref in sums_refs)
    inv_row = lax.rsqrt(sums[:1] / feature_count + EPSILON)
    coefficient_row = sums[1:2] * inv_row * inv_row * inv_row / feature_count
    columns = jnp.transpose(
        jnp.concatenate([inv_row, coefficient_row, jnp.zeros_like(sums[2:])], axis=0)
    )
    inv_rms, coefficient = columns[:, :1], columns[:, 1:2]
    growth = jnp.exp(cum_col_ref[...])
    for h in range(plan.heads):
        cut = lanes(h, size)
        gained = gain_ref[:, cut] * upstream_ref[:, cut].astype(F32)
        attn_grad = (gained * inv_rms - attended_ref[:, cut] * coefficient).astype(BF16)
        attn_grad_ref[:, cut] = attn_grad
        query_decayed = (query_ref[:, cut].astype(F32) * growth[:, h : h + 1]).astype(BF16)
        held_ref[cut] = dot(query_decayed, attn_grad, CONTRACT_ROWS)
    for k, send_ref in enumerate(send_refs):
        send_ref[...] = held_ref[plan.rows_of(plan.peer(k))]


def score_grad_body(
    plan,
    attn_grad_ref,
    query_ref,
    key_ref,
    value_ref,
    states_ref,
    weight_ref,
    cum_ref,
    cum_col_ref,
    query_grad_ref,
    key_part_ref,
    value_part_ref,
):
    causal = causal_mask(query_ref.shape[0])
    cum_col = cum_col_ref[...]
    growth = jnp.exp(cum_col)
    for h in range(plan.heads):
        cut = lanes(h, plan.size)
        attn_grad = attn_grad_ref[:, cut]
        scores = dot(attn_grad, value_ref[:, cut], CONTRACT_COLS)
        score_grad = (scores * decay_matrix(cum_ref, cum_col, causal, h)).astype(BF16)
        carried = dot(attn_grad, states_ref[cut], CONTRACT_COLS)
        query_grad = dot(score_grad, key_ref[:, cut]) + growth[:, h : h + 1] * carried
        query_grad_ref[:, cut] = query_grad.astype(BF16)
        key_part_ref[:, cut] = dot(score_grad, query_ref[:, cut], CONTRACT_ROWS)
        value_part_ref[:, cut] = dot(weight_ref[h], attn_grad, CONTRACT_ROWS)


def finish_body(plan, *refs):
    grad_refs, refs = refs[: plan.members], refs[plan.members :]
    key_part_ref, value_part_ref, key_ref, value_ref, cum_col_ref = refs[:5]
    key_grad_ref, value_grad_ref, done_ref, grads_ref = refs[5:]
    done_ref[...] = jnp.zeros_like(done_ref)
    length = key_ref.shape[0]
    gather_rounded(plan, grad_refs, grads_ref)
    cum_col = cum_col_ref[...]
    shrink = jnp.exp(cum_col[length - 1 : length, :] - cum_col)
    for h in range(plan.heads):
        cut = lanes(h, plan.size)
        grads = grads_ref[cut]
        column = shrink[:, h : h + 1]
        key_state = dot(value_ref[:, cut], grads, CONTRACT_COLS)
        key_grad_ref[:, cut] = (key_part_ref[:, cut] + column * key_state).astype(BF16)
        value_state = dot(key_ref[:, cut], grads)
        value_grad_ref[:, cut] = (value_part_ref[:, cut] + column * value_state).astype(BF16)


def join_body(plan, *refs):
    for k, piece_ref in enumerate(refs[:-2]):
        refs[-1][plan.rows_of(plan.peer(k))] = piece_ref[...]


def on_device(
    query_rows, key_rows, value_rows, log_decay, out_grad, norm_gain, state_in, state_out_grad
):
    heads, length = log_decay.shape
    size = state_in.shape[1]
    width = heads * size
    parties = lax.axis_size("head")
    plan = Plan(heads, size, lax.axis_size("seq"))
    bind = lambda body, *extra: functools.partial(body, plan, *extra)
    gain = norm_gain.reshape(1, width)
    piece = shaped((plan.rows, size))
    logged = shaped((plan.rows + LOG_ROWS, size))
    pieces = [piece] * plan.members
    table = shaped((length, width))
    rounded = shaped((length, width), BF16)
    hold = pltpu.VMEM((plan.members, plan.rows, size), F32)
    hold_logged = pltpu.VMEM((plan.members, plan.rows + LOG_ROWS, size), F32)
    hold_groups = pltpu.VMEM((plan.groups, plan.rows + LOG_ROWS, size), F32)
    hold_whole = pltpu.VMEM((width, size), F32)

    *sends, cum_log, cum_col = call(
        bind(summary_body),
        [logged] * plan.members + [shaped((heads, length)), shaped((length, heads))],
        [pltpu.with_memory_space_constraint(x, pltpu.HBM) for x in (key_rows, value_rows, log_decay)],
        [
            hold_whole,
            pltpu.VMEM((length, width), BF16),
            pltpu.VMEM((length, width), BF16),
            pltpu.VMEM((heads, length), F32),
            pltpu.SemaphoreType.DMA((plan.members, 2)),
            pltpu.SemaphoreType.DMA,
        ],
        specs=[HBM] * 3,
    )
    parts = plan.swap_in_group(sends)
    weights, intra = call(
        bind(intra_body),
        [shaped((heads, length, length), BF16), table],
        [query_rows, key_rows, value_rows, cum_log, cum_col],
        flops=4 * heads * length * length * size,
    )
    total, logs = call(
        bind(group_total_body),
        [logged, shaped((plan.members, LOG_ROWS, size))],
        parts,
        [hold_logged],
    )
    totals = [total] + plan.from_groups(total)
    sends = call(
        bind(forward_scan_body),
        pieces,
        [*parts, *totals, state_in.reshape(width, size)],
        [hold_groups, hold_logged],
    )
    states = plan.swap_in_group(sends)
    attended, sums, states = call(
        bind(attended_body),
        [table, shaped((8, length)), shaped((width, size), BF16)],
        [*states, intra, query_rows, cum_col, out_grad, gain],
    )
    all_sums = [sums] + [
        lax.ppermute(sums, "head", [(i, (i + step) % parties) for i in range(parties)])
        for step in range(1, parties)
    ]
    attn_grad, *sends = call(
        bind(attn_grad_body, parties),
        [rounded] + pieces,
        [*all_sums, attended, query_rows, cum_col, out_grad, gain],
        [hold_whole],
    )
    parts = plan.swap_in_group(sends)
    query_grad, key_part, value_part = call(
        bind(score_grad_body),
        [rounded, table, table],
        [attn_grad, query_rows, key_rows, value_rows, states, weights, cum_log, cum_col],
        flops=10 * heads * length * length * size,
    )
    (total,) = call(bind(group_grad_body), [logged], [*parts, logs], [hold])
    totals = [total] + plan.from_groups(total)
    *sends, whole_total = call(
        bind(reverse_scan_body),
        pieces + [piece],
        [*parts, *totals, logs, state_out_grad.reshape(width, size), key_part],
        [hold_groups, hold],
        specs=[VMEM] * (plan.members + plan.groups + 2) + [ANY],
    )
    grads = plan.swap_in_group(sends)
    totals = plan.swap_in_group([whole_total] * plan.members)
    key_grad, value_grad, done = call(
        bind(finish_body),
        [rounded, rounded, shaped((8, size))],
        [*grads, key_part, value_part, key_rows, value_rows, cum_col],
        [pltpu.VMEM((width, size), BF16)],
    )
    (state_in_grad,) = call(
        bind(join_body),
        [shaped((width, size))],
        [*totals, done],
    )
    return (query_grad, key_grad, value_grad, state_in_grad.reshape(heads, size, size))


def solution(mesh):
    return jax.shard_map(
        on_device,
        mesh=mesh,
        in_specs=(
            P("seq", "head"),
            P("seq", "head"),
            P("seq", "head"),
            P("head", "seq"),
            P("seq", "head"),
            P("head"),
            P("head", None, None),
            P("head", None, None),
        ),
        out_specs=(P("seq", "head"), P("seq", "head"), P("seq", "head"), P("head", None, None)),
        check_vma=False,
    )
```

```python
import functools

import jax
import jax.numpy as jnp
from jax import lax
from jax.experimental import pallas as pl
from jax.experimental.pallas import tpu as pltpu
from jax.sharding import PartitionSpec as P

EPSILON = 1e-06
F32 = jnp.float32
BF16 = jnp.bfloat16
LOG_ROWS = 8
MASKED = -1e30

CONTRACT_ROWS = (((0,), (0,)), ((), ()))
CONTRACT_COLS = (((1,), (1,)), ((), ()))
VMEM = pl.BlockSpec(memory_space=pltpu.VMEM)
HBM = pl.BlockSpec(memory_space=pltpu.HBM)
ANY = pl.BlockSpec(memory_space=pl.ANY)


def call(body, outs, operands, scratch=(), flops=0, specs=None):
    size = sum(x.size * x.dtype.itemsize for x in (*operands, *outs))
    return pl.pallas_call(
        body,
        out_shape=outs,
        in_specs=specs or [VMEM] * len(operands),
        out_specs=[VMEM] * len(outs),
        scratch_shapes=list(scratch),
        compiler_params=pltpu.CompilerParams(vmem_limit_bytes=24 * 1024 * 1024),
        cost_estimate=pl.CostEstimate(flops=flops, bytes_accessed=size, transcendentals=0),
    )(*operands)


def shaped(shape, dtype=F32):
    return jax.ShapeDtypeStruct(shape, dtype)


def dot(a, b, dims=(((1,), (0,)), ((), ()))):
    return lax.dot_general(a, b, dims, preferred_element_type=F32)


def exact_dot(a, b, dims=(((1,), (0,)), ((), ()))):
    return lax.dot_general(
        a, b, dims, precision=lax.Precision.HIGHEST, preferred_element_type=F32
    )


def lanes(h, size):
    return slice(h * size, (h + 1) * size)


def causal_mask(length):
    row = lax.broadcasted_iota(jnp.int32, (length, length), 0)
    col = lax.broadcasted_iota(jnp.int32, (length, length), 1)
    return row >= col


class Plan:
    def __init__(self, heads, size, blocks):
        self.heads, self.size, self.blocks = heads, size, blocks
        self.members = next(m for m in (4, 2, 1) if heads % m == 0 and blocks % m == 0)
        self.groups = blocks // self.members
        self.own = heads // self.members
        self.rows = self.own * size
        self.ways = sorted(range(self.members), key=lambda way: (way > 0, -way.bit_count()))

    def member(self):
        return lax.rem(lax.axis_index("seq"), self.members)

    def group(self):
        return lax.div(lax.axis_index("seq"), self.members)

    def peer(self, k):
        return lax.bitwise_xor(self.member(), self.ways[k])

    def rows_of(self, member):
        return pl.ds(pl.multiple_of(member * self.rows, self.rows), self.rows)

    def swap_in_group(self, pieces):
        span = self.members
        swapped = [pieces[0]]
        for way, piece in zip(self.ways[1:], pieces[1:]):
            pairs = [(i, i // span * span + (i % span ^ way)) for i in range(self.blocks)]
            swapped.append(lax.ppermute(piece, "seq", pairs))
        return swapped

    def from_groups(self, piece):
        return [
            lax.ppermute(
                piece,
                "seq",
                [(i, (i + step * self.members) % self.blocks) for i in range(self.blocks)],
            )
            for step in range(1, self.groups)
        ]


def own_decays(plan, log_tile_ref, base):
    first = base + plan.member() * plan.own
    rows = [log_tile_ref[pl.ds(first + j, 1), :] for j in range(plan.own)]
    return jnp.concatenate([jnp.broadcast_to(jnp.exp(row), (plan.size, plan.size)) for row in rows])


def summary_body(plan, key_hbm, value_hbm, decay_hbm, *refs):
    send_refs, refs = refs[: plan.members], refs[plan.members :]
    cum_ref, cum_col_ref, held_ref, key_ref, value_ref, decay_ref, sems, decay_sem = refs
    length, heads, size = key_ref.shape[0], plan.heads, plan.size
    decay_copy = pltpu.make_async_copy(decay_hbm, decay_ref, decay_sem)
    decay_copy.start()
    copies = []
    for part in range(plan.members):
        cut = lanes(part, plan.rows)
        copies.append(
            [
                pltpu.make_async_copy(source.at[:, cut], target.at[:, cut], sems.at[part, i])
                for i, (source, target) in enumerate([(key_hbm, key_ref), (value_hbm, value_ref)])
            ]
        )
        for copy in copies[-1]:
            copy.start()
    decay_copy.wait()
    decay = decay_ref[...]
    causal = jnp.where(causal_mask(length), 1.0, 0.0)
    cum_col = exact_dot(causal, decay, CONTRACT_COLS)
    cum_row = exact_dot(decay, causal, CONTRACT_COLS)
    cum_ref[...] = cum_row
    cum_col_ref[...] = cum_col
    block_log = cum_col[length - 1 : length, :]
    shrink = jnp.exp(block_log - cum_col)
    for h in range(heads):
        if h % plan.own == 0:
            for copy in copies[h // plan.own]:
                copy.wait()
        key_decayed = (key_ref[:, lanes(h, size)].astype(F32) * shrink[:, h : h + 1]).astype(BF16)
        held_ref[h * size : (h + 1) * size] = dot(
            key_decayed, value_ref[:, lanes(h, size)], CONTRACT_ROWS
        )
    log_tile = jnp.broadcast_to(cum_row[:, length - 1 : length], (heads, size))
    if heads < LOG_ROWS:
        log_tile = jnp.concatenate([log_tile, jnp.zeros((LOG_ROWS - heads, size), F32)])
    for k, send_ref in enumerate(send_refs):
        send_ref[: plan.rows] = held_ref[plan.rows_of(plan.peer(k))]
        send_ref[plan.rows :] = log_tile


def group_total_body(plan, *refs):
    part_refs, (total_ref, logs_ref, held_ref) = refs[: plan.members], refs[plan.members :]
    for k, part_ref in enumerate(part_refs):
        held_ref[plan.peer(k)] = part_ref[...]
    total = jnp.zeros((plan.rows, plan.size), F32)
    log_total = jnp.zeros((LOG_ROWS, plan.size), F32)
    for b in range(plan.members):
        total = own_decays(plan, held_ref.at[b], plan.rows) * total + held_ref[b, : plan.rows]
        logs_ref[b] = held_ref[b, plan.rows :]
        log_total += held_ref[b, plan.rows :]
    total_ref[: plan.rows] = total
    total_ref[plan.rows :] = log_total


def stage_groups(plan, total_refs, held_ref):
    for step, total_ref in enumerate(total_refs):
        held_ref[lax.rem(plan.group() - step + plan.groups, plan.groups)] = total_ref[...]


def forward_scan_body(plan, *refs):
    part_refs, refs = refs[: plan.members], refs[plan.members :]
    total_refs, refs = refs[: plan.groups], refs[plan.groups :]
    state_ref, refs = refs[0], refs[1:]
    send_refs, (before_ref, groups_ref, held_ref) = refs[: plan.members], refs[plan.members :]
    stage_groups(plan, total_refs, groups_ref)
    before = jnp.zeros((LOG_ROWS, plan.size), F32)
    state = state_ref[plan.rows_of(plan.member())]
    for group in range(plan.groups - 1):
        after = own_decays(plan, groups_ref.at[group], plan.rows) * state + groups_ref[group, : plan.rows]
        state = jnp.where(group < plan.group(), after, state)
        before += jnp.where(group < plan.group(), groups_ref[group, plan.rows :], 0.0)
    for k, part_ref in enumerate(part_refs):
        held_ref[plan.peer(k)] = part_ref[...]
    for b in range(plan.members):
        summary = held_ref[b, : plan.rows]
        decays = own_decays(plan, held_ref.at[b], plan.rows)
        held_ref[b, : plan.rows] = state
        state = decays * state + summary
        before += jnp.where(b < plan.member(), held_ref[b, plan.rows :], 0.0)
    before_ref[...] = before
    for k, send_ref in enumerate(send_refs):
        send_ref[...] = held_ref[plan.peer(k), : plan.rows]


def suffixes(plan, held_ref, logs_ref, grad):
    found = []
    for b in reversed(range(plan.members)):
        found.append(grad)
        grad = own_decays(plan, logs_ref.at[b], 0) * grad + held_ref[b]
    return found[::-1], grad


def prefixes(plan, held_ref, logs_ref, total, scale):
    found = []
    for b in range(plan.members):
        found.append(total)
        total = total + scale * held_ref[b]
        scale = scale * own_decays(plan, logs_ref.at[b], 0)
    return found


def group_grad_body(plan, *refs):
    part_refs, refs = refs[: plan.members], refs[plan.members :]
    (logs_ref, grad_ref, _, total_ref), refs = refs[:4], refs[4:]
    send_refs, (held_ref,) = refs[:-1], refs[-1:]
    for k, part_ref in enumerate(part_refs):
        held_ref[plan.peer(k)] = part_ref[...]
    zero = jnp.zeros((plan.rows, plan.size), F32)
    total_ref[: plan.rows] = suffixes(plan, held_ref, logs_ref, zero)[1]
    total_ref[plan.rows :] = sum(logs_ref[b] for b in range(plan.members))
    if send_refs:
        first = plan.group() == 0
        before = prefixes(plan, held_ref, logs_ref, zero, zero + 1.0)
        after = suffixes(plan, held_ref, logs_ref, grad_ref[plan.rows_of(plan.member())])[0]
        for b in range(plan.members):
            held_ref[b] = jnp.where(first, before[b], after[b])
        for k, send_ref in enumerate(send_refs):
            send_ref[...] = held_ref[plan.peer(k)]


def reverse_scan_body(plan, *refs):
    part_refs, refs = refs[: plan.members], refs[plan.members :]
    total_refs, refs = refs[: plan.groups], refs[plan.groups :]
    (logs_ref, grad_ref), refs = refs[:2], refs[2:]
    send_refs, (groups_ref, held_ref) = refs[:-2], refs[-2:]
    stage_groups(plan, total_refs, groups_ref)
    for k, part_ref in enumerate(part_refs):
        held_ref[plan.peer(k)] = part_ref[...]
    grad = grad_ref[plan.rows_of(plan.member())]
    leaving = grad
    for group in reversed(range(plan.groups)):
        leaving = jnp.where(group == plan.group(), grad, leaving)
        grad = own_decays(plan, groups_ref.at[group], plan.rows) * grad + groups_ref[group, : plan.rows]
    total = jnp.zeros((plan.rows, plan.size), F32)
    scale = total + 1.0
    for group in range(plan.groups - 1):
        earlier = group < plan.group()
        total = jnp.where(earlier, total + scale * groups_ref[group, : plan.rows], total)
        decays = own_decays(plan, groups_ref.at[group], plan.rows)
        scale = jnp.where(earlier, scale * decays, scale)
    after = suffixes(plan, held_ref, logs_ref, leaving)[0]
    before = prefixes(plan, held_ref, logs_ref, total, scale)
    if plan.groups == 2:
        first = plan.group() == 0
        found = [[jnp.where(first, after[b], before[b]) for b in range(plan.members)]]
    else:
        found = [before, after]
    for i, values in enumerate(found):
        for b in range(plan.members):
            held_ref[b] = values[b]
        for k in range(plan.members):
            send_refs[i * plan.members + k][...] = held_ref[plan.peer(k)]


def decay_matrix(cum_ref, cum_col, causal, h):
    spread = cum_col[:, h : h + 1] - cum_ref[h : h + 1, :]
    return jnp.exp(jnp.where(causal, jnp.minimum(spread, 0.0), MASKED))


def intra_body(plan, query_ref, key_ref, value_ref, cum_ref, cum_col_ref, weight_ref, intra_ref):
    causal = causal_mask(query_ref.shape[0])
    cum_col = cum_col_ref[...]
    for h in range(plan.heads):
        cut = lanes(h, plan.size)
        scores = dot(query_ref[:, cut], key_ref[:, cut], CONTRACT_COLS)
        weights = (scores * decay_matrix(cum_ref, cum_col, causal, h)).astype(BF16)
        weight_ref[h] = weights
        intra_ref[:, cut] = dot(weights, value_ref[:, cut])


def gather_rounded(plan, piece_refs, whole_ref):
    for k, piece_ref in enumerate(piece_refs):
        whole_ref[plan.rows_of(plan.peer(k))] = piece_ref[...].astype(BF16)


def attended_body(plan, *refs):
    state_refs, refs = refs[: plan.members], refs[plan.members :]
    intra_ref, query_ref, cum_col_ref, upstream_ref, gain_ref = refs[:5]
    attended_ref, sums_ref, states_ref = refs[5:]
    size, length = plan.size, query_ref.shape[0]
    gather_rounded(plan, state_refs, states_ref)
    growth = jnp.exp(cum_col_ref[...])
    square = jnp.zeros((length, size), F32)
    inner = jnp.zeros((length, size), F32)
    for h in range(plan.heads):
        cut = lanes(h, size)
        carried = dot(query_ref[:, cut], states_ref[cut])
        attended = intra_ref[:, cut] + growth[:, h : h + 1] * carried
        attended_ref[:, cut] = attended
        square += attended * attended
        inner += gain_ref[:, cut] * upstream_ref[:, cut].astype(F32) * attended
    ones = jnp.ones((1, size), F32)
    sums_ref[...] = jnp.concatenate(
        [exact_dot(ones, square, CONTRACT_COLS), exact_dot(ones, inner, CONTRACT_COLS)]
        + [jnp.zeros((6, length), F32)],
        axis=0,
    )


def attn_grad_body(plan, parties, *refs):
    sums_refs, refs = refs[:parties], refs[parties:]
    attended_ref, query_ref, cum_col_ref, upstream_ref, gain_ref = refs[:5]
    (attn_grad_ref, held_ref), send_refs = refs[5:7], refs[7:]
    size = plan.size
    feature_count = plan.heads * size * parties
    sums = sum(ref[...] for ref in sums_refs)
    inv_row = lax.rsqrt(sums[:1] / feature_count + EPSILON)
    coefficient_row = sums[1:2] * inv_row * inv_row * inv_row / feature_count
    columns = jnp.transpose(
        jnp.concatenate([inv_row, coefficient_row, jnp.zeros_like(sums[2:])], axis=0)
    )
    inv_rms, coefficient = columns[:, :1], columns[:, 1:2]
    growth = jnp.exp(cum_col_ref[...])
    for h in range(plan.heads):
        cut = lanes(h, size)
        gained = gain_ref[:, cut] * upstream_ref[:, cut].astype(F32)
        attn_grad = (gained * inv_rms - attended_ref[:, cut] * coefficient).astype(BF16)
        attn_grad_ref[:, cut] = attn_grad
        query_decayed = (query_ref[:, cut].astype(F32) * growth[:, h : h + 1]).astype(BF16)
        held_ref[cut] = dot(query_decayed, attn_grad, CONTRACT_ROWS)
    for k, send_ref in enumerate(send_refs):
        send_ref[...] = held_ref[plan.rows_of(plan.peer(k))]


def score_grad_body(
    plan,
    attn_grad_ref,
    query_ref,
    key_ref,
    value_ref,
    states_ref,
    weight_ref,
    cum_ref,
    cum_col_ref,
    query_grad_ref,
    key_part_ref,
    value_part_ref,
):
    causal = causal_mask(query_ref.shape[0])
    cum_col = cum_col_ref[...]
    growth = jnp.exp(cum_col)
    for h in range(plan.heads):
        cut = lanes(h, plan.size)
        attn_grad = attn_grad_ref[:, cut]
        scores = dot(attn_grad, value_ref[:, cut], CONTRACT_COLS)
        score_grad = (scores * decay_matrix(cum_ref, cum_col, causal, h)).astype(BF16)
        carried = dot(attn_grad, states_ref[cut], CONTRACT_COLS)
        query_grad = dot(score_grad, key_ref[:, cut]) + growth[:, h : h + 1] * carried
        query_grad_ref[:, cut] = query_grad.astype(BF16)
        key_part_ref[:, cut] = dot(score_grad, query_ref[:, cut], CONTRACT_ROWS)
        value_part_ref[:, cut] = dot(weight_ref[h], attn_grad, CONTRACT_ROWS)


def finish_body(plan, *refs):
    first_refs, refs = refs[: plan.members], refs[plan.members :]
    second_refs, refs = refs[: plan.members], refs[plan.members :]
    key_part_ref, value_part_ref, key_ref, value_ref, cum_col_ref, summary_ref, before_ref = refs[:7]
    key_grad_ref, value_grad_ref, total_ref, held_ref = refs[7:]
    length, size = key_ref.shape[0], plan.size
    swapped = jnp.where(plan.group() == 0, 0, 1) if plan.groups == 2 else 0
    for k in range(plan.members):
        held_ref[swapped, plan.rows_of(plan.peer(k))] = first_refs[k][...]
        held_ref[1 - swapped, plan.rows_of(plan.peer(k))] = second_refs[k][...]
    cum_col = cum_col_ref[...]
    block_log = cum_col[length - 1 : length, :]
    shrink = jnp.exp(block_log - cum_col)
    for h in range(plan.heads):
        cut = lanes(h, size)
        grads = held_ref[1, cut]
        scale = jnp.exp(before_ref[h : h + 1])
        scale_next = jnp.exp(before_ref[h : h + 1] + block_log[:, h : h + 1])
        total_ref[cut] = held_ref[0, cut] + scale * summary_ref[cut] + scale_next * grads
        grads = grads.astype(BF16)
        column = shrink[:, h : h + 1]
        key_state = dot(value_ref[:, cut], grads, CONTRACT_COLS)
        key_grad_ref[:, cut] = (key_part_ref[:, cut] + column * key_state).astype(BF16)
        value_state = dot(key_ref[:, cut], grads)
        value_grad_ref[:, cut] = (value_part_ref[:, cut] + column * value_state).astype(BF16)


def on_device(
    query_rows, key_rows, value_rows, log_decay, out_grad, norm_gain, state_in, state_out_grad
):
    heads, length = log_decay.shape
    size = state_in.shape[1]
    width = heads * size
    parties = lax.axis_size("head")
    plan = Plan(heads, size, lax.axis_size("seq"))
    bind = lambda body, *extra: functools.partial(body, plan, *extra)
    gain = norm_gain.reshape(1, width)
    piece = shaped((plan.rows, size))
    logged = shaped((plan.rows + LOG_ROWS, size))
    pieces = [piece] * plan.members
    table = shaped((length, width))
    rounded = shaped((length, width), BF16)
    hold = pltpu.VMEM((plan.members, plan.rows, size), F32)
    hold_logged = pltpu.VMEM((plan.members, plan.rows + LOG_ROWS, size), F32)
    hold_groups = pltpu.VMEM((plan.groups, plan.rows + LOG_ROWS, size), F32)
    hold_whole = pltpu.VMEM((width, size), F32)

    *sends, cum_log, cum_col = call(
        bind(summary_body),
        [logged] * plan.members + [shaped((heads, length)), shaped((length, heads))],
        [pltpu.with_memory_space_constraint(x, pltpu.HBM) for x in (key_rows, value_rows, log_decay)],
        [
            hold_whole,
            pltpu.VMEM((length, width), BF16),
            pltpu.VMEM((length, width), BF16),
            pltpu.VMEM((heads, length), F32),
            pltpu.SemaphoreType.DMA((plan.members, 2)),
            pltpu.SemaphoreType.DMA,
        ],
        specs=[HBM] * 3,
    )
    parts = plan.swap_in_group(sends)
    weights, intra = call(
        bind(intra_body),
        [shaped((heads, length, length), BF16), table],
        [query_rows, key_rows, value_rows, cum_log, cum_col],
        flops=4 * heads * length * length * size,
    )
    total, logs = call(
        bind(group_total_body),
        [logged, shaped((plan.members, LOG_ROWS, size))],
        parts,
        [hold_logged],
    )
    totals = [total] + plan.from_groups(total)
    *sends, before = call(
        bind(forward_scan_body),
        pieces + [shaped((LOG_ROWS, size))],
        [*parts, *totals, state_in.reshape(width, size)],
        [hold_groups, hold_logged],
    )
    states = plan.swap_in_group(sends)
    attended, sums, states = call(
        bind(attended_body),
        [table, shaped((8, length)), shaped((width, size), BF16)],
        [*states, intra, query_rows, cum_col, out_grad, gain],
    )
    all_sums = [sums] + [
        lax.ppermute(sums, "head", [(i, (i + step) % parties) for i in range(parties)])
        for step in range(1, parties)
    ]
    attn_grad, summary, *sends = call(
        bind(attn_grad_body, parties),
        [rounded, shaped((width, size))] + pieces,
        [*all_sums, attended, query_rows, cum_col, out_grad, gain],
    )
    parts = plan.swap_in_group(sends)
    query_grad, key_part, value_part = call(
        bind(score_grad_body),
        [rounded, table, table],
        [attn_grad, query_rows, key_rows, value_rows, states, weights, cum_log, cum_col],
        flops=10 * heads * length * length * size,
    )
    grad_rows = state_out_grad.reshape(width, size)
    two_sided = plan.groups == 2
    total, *sends = call(
        bind(group_grad_body),
        [logged] + pieces * two_sided,
        [*parts, logs, grad_rows, key_part],
        [hold],
        specs=[VMEM] * (plan.members + 2) + [ANY],
    )
    totals = [total] + plan.from_groups(total)
    swapped = [plan.swap_in_group(sends)] if two_sided else []
    sends = call(
        bind(reverse_scan_body),
        pieces * (1 if two_sided else 2),
        [*parts, *totals, logs, grad_rows],
        [hold_groups, hold],
    )
    for first in range(0, len(sends), plan.members):
        swapped.append(plan.swap_in_group(sends[first : first + plan.members]))
    key_grad, value_grad, state_in_grad = call(
        bind(finish_body),
        [rounded, rounded, shaped((width, size))],
        [*swapped[0], *swapped[1], key_part, value_part, key_rows, value_rows, cum_col, summary, before],
        [pltpu.VMEM((2, width, size), F32)],
    )
    return (query_grad, key_grad, value_grad, state_in_grad.reshape(heads, size, size))


def solution(mesh):
    return jax.shard_map(
        on_device,
        mesh=mesh,
        in_specs=(
            P("seq", "head"),
            P("seq", "head"),
            P("seq", "head"),
            P("head", "seq"),
            P("seq", "head"),
            P("head"),
            P("head", None, None),
            P("head", None, None),
        ),
        out_specs=(P("seq", "head"), P("seq", "head"), P("seq", "head"), P("head", None, None)),
        check_vma=False,
    )
```

```python
import functools

import jax
import jax.numpy as jnp
from jax import lax
from jax.experimental import pallas as pl
from jax.experimental.pallas import tpu as pltpu
from jax.sharding import PartitionSpec as P

EPSILON = 1e-06
F32 = jnp.float32
BF16 = jnp.bfloat16
LOG_ROWS = 8
MASKED = -1e30

CONTRACT_ROWS = (((0,), (0,)), ((), ()))
CONTRACT_COLS = (((1,), (1,)), ((), ()))
VMEM = pl.BlockSpec(memory_space=pltpu.VMEM)
HBM = pl.BlockSpec(memory_space=pltpu.HBM)
ANY = pl.BlockSpec(memory_space=pl.ANY)


def call(body, outs, operands, scratch=(), flops=0, specs=None):
    return pl.pallas_call(
        body,
        out_shape=outs,
        in_specs=specs or [VMEM] * len(operands),
        out_specs=[VMEM] * len(outs),
        scratch_shapes=list(scratch),
        compiler_params=pltpu.CompilerParams(vmem_limit_bytes=24 * 1024 * 1024),
        cost_estimate=pl.CostEstimate(flops=flops, bytes_accessed=0, transcendentals=0),
    )(*operands)


def shaped(shape, dtype=F32):
    return jax.ShapeDtypeStruct(shape, dtype)


def dot(a, b, dims=(((1,), (0,)), ((), ()))):
    return lax.dot_general(a, b, dims, preferred_element_type=F32)


def exact_dot(a, b, dims=(((1,), (0,)), ((), ()))):
    return lax.dot_general(
        a, b, dims, precision=lax.Precision.HIGHEST, preferred_element_type=F32
    )


def lanes(h, size):
    return slice(h * size, (h + 1) * size)


def causal_mask(length):
    row = lax.broadcasted_iota(jnp.int32, (length, length), 0)
    col = lax.broadcasted_iota(jnp.int32, (length, length), 1)
    return row >= col


class Plan:
    def __init__(self, heads, size, blocks):
        self.heads, self.size, self.blocks = heads, size, blocks
        self.members = next(m for m in (4, 2, 1) if heads % m == 0 and blocks % m == 0)
        self.groups = blocks // self.members
        self.own = heads // self.members
        self.rows = self.own * size
        self.chunks = self.own
        self.chunk_rows = self.rows // self.chunks

    def member(self):
        return lax.rem(lax.axis_index("seq"), self.members)

    def group(self):
        return lax.div(lax.axis_index("seq"), self.members)

    def rows_of(self, member):
        return pl.ds(pl.multiple_of(member * self.rows, self.rows), self.rows)

    def chunk_of(self, member, chunk):
        start = member * self.rows + chunk * self.chunk_rows
        return pl.ds(pl.multiple_of(start, self.chunk_rows), self.chunk_rows)

    def swap_in_group(self, pieces):
        span = self.members
        sets = [list(range(i, i + span)) for i in range(0, self.blocks, span)]
        return lax.all_to_all(pieces, "seq", 0, 0, axis_index_groups=sets)

    def from_groups(self, piece):
        return [
            lax.ppermute(
                piece,
                "seq",
                [(i, (i + step * self.members) % self.blocks) for i in range(self.blocks)],
            )
            for step in range(1, self.groups)
        ]


def own_decays(plan, log_tile_ref, chunk=None):
    count = plan.own if chunk is None else plan.own // plan.chunks
    first = plan.member() * plan.own + (0 if chunk is None else chunk * count)
    rows = [log_tile_ref[pl.ds(first + j, 1), :] for j in range(count)]
    return jnp.concatenate([jnp.broadcast_to(jnp.exp(row), (plan.size, plan.size)) for row in rows])


def summary_body(plan, key_hbm, value_hbm, decay_hbm, *refs):
    send_refs, refs = refs[: plan.chunks], refs[plan.chunks :]
    cum_ref, cum_col_ref, held_ref, key_ref, value_ref, decay_ref, sems, decay_sem = refs
    length, heads, size = key_ref.shape[0], plan.heads, plan.size
    decay_copy = pltpu.make_async_copy(decay_hbm, decay_ref, decay_sem)
    decay_copy.start()
    copies = []
    for part in range(plan.members):
        cut = lanes(part, plan.rows)
        copies.append(
            [
                pltpu.make_async_copy(source.at[:, cut], target.at[:, cut], sems.at[part, i])
                for i, (source, target) in enumerate([(key_hbm, key_ref), (value_hbm, value_ref)])
            ]
        )
        for copy in copies[-1]:
            copy.start()
    decay_copy.wait()
    decay = decay_ref[...]
    causal = jnp.where(causal_mask(length), 1.0, 0.0)
    cum_col = exact_dot(causal, decay, CONTRACT_COLS)
    cum_row = exact_dot(decay, causal, CONTRACT_COLS)
    cum_ref[...] = cum_row
    cum_col_ref[...] = cum_col
    block_log = cum_col[length - 1 : length, :]
    shrink = jnp.exp(block_log - cum_col)
    for h in range(heads):
        if h % plan.own == 0:
            for copy in copies[h // plan.own]:
                copy.wait()
        key_decayed = (key_ref[:, lanes(h, size)].astype(F32) * shrink[:, h : h + 1]).astype(BF16)
        held_ref[h * size : (h + 1) * size] = dot(
            key_decayed, value_ref[:, lanes(h, size)], CONTRACT_ROWS
        )
    log_tile = jnp.broadcast_to(cum_row[:, length - 1 : length], (heads, size))
    if heads < LOG_ROWS:
        log_tile = jnp.concatenate([log_tile, jnp.zeros((LOG_ROWS - heads, size), F32)])
    for chunk, send_ref in enumerate(send_refs):
        for member in range(plan.members):
            send_ref[member, : plan.chunk_rows] = held_ref[plan.chunk_of(member, chunk)]
            if chunk == 0:
                send_ref[member, plan.chunk_rows :] = log_tile


def group_total_body(plan, chunk, parts_ref, *refs):
    rows = plan.chunk_rows
    if chunk == 0:
        total_ref, logs_ref = refs
        for b in range(plan.members):
            logs_ref[b] = parts_ref[b, rows:]
        total_ref[rows:] = sum(logs_ref[b] for b in range(plan.members))
    else:
        logs_ref, total_ref = refs
    total = jnp.zeros((rows, plan.size), F32)
    for b in range(plan.members):
        total = own_decays(plan, logs_ref.at[b], chunk) * total + parts_ref[b, :rows]
    total_ref[:rows] = total


def stage_groups(plan, total_refs, held_ref):
    rows = held_ref.shape[1]
    for step, total_ref in enumerate(total_refs):
        held_ref[lax.rem(plan.group() - step + plan.groups, plan.groups)] = total_ref[:rows]


def forward_scan_body(plan, chunk, parts_ref, *refs):
    total_refs, refs = refs[: plan.groups], refs[plan.groups :]
    rows = plan.chunk_rows
    if chunk == 0:
        (state_ref, logs_ref), refs = refs[:2], refs[2:]
        send_ref, before_ref, group_logs_ref, groups_ref = refs
        for step, total_ref in enumerate(total_refs):
            group = lax.rem(plan.group() - step + plan.groups, plan.groups)
            group_logs_ref[group] = total_ref[rows:]
        before = jnp.zeros((LOG_ROWS, plan.size), F32)
        for group in range(plan.groups - 1):
            before += jnp.where(group < plan.group(), group_logs_ref[group], 0.0)
        for b in range(plan.members - 1):
            before += jnp.where(b < plan.member(), logs_ref[b], 0.0)
        before_ref[...] = before
    else:
        state_ref, logs_ref, group_logs_ref, send_ref, groups_ref = refs
    stage_groups(plan, total_refs, groups_ref)
    state = state_ref[plan.chunk_of(plan.member(), chunk)]
    for group in range(plan.groups - 1):
        after = own_decays(plan, group_logs_ref.at[group], chunk) * state + groups_ref[group]
        state = jnp.where(group < plan.group(), after, state)
    for b in range(plan.members):
        send_ref[b] = state
        state = own_decays(plan, logs_ref.at[b], chunk) * state + parts_ref[b, :rows]


def suffixes(plan, parts_ref, logs_ref, grad):
    found = []
    for b in reversed(range(plan.members)):
        found.append(grad)
        grad = own_decays(plan, logs_ref.at[b]) * grad + parts_ref[b]
    return found[::-1], grad


def prefixes(plan, parts_ref, logs_ref, total, scale):
    found = []
    for b in range(plan.members):
        found.append(total)
        total = total + scale * parts_ref[b]
        scale = scale * own_decays(plan, logs_ref.at[b])
    return found


def group_grad_body(plan, parts_ref, logs_ref, grad_ref, _, total_ref, *send_refs):
    zero = jnp.zeros((plan.rows, plan.size), F32)
    total_ref[...] = suffixes(plan, parts_ref, logs_ref, zero)[1]
    for send_ref in send_refs:
        first = plan.group() == 0
        before = prefixes(plan, parts_ref, logs_ref, zero, zero + 1.0)
        after = suffixes(plan, parts_ref, logs_ref, grad_ref[plan.rows_of(plan.member())])[0]
        for b in range(plan.members):
            send_ref[b] = jnp.where(first, before[b], after[b])


def reverse_scan_body(plan, parts_ref, *refs):
    total_refs, refs = refs[: plan.groups], refs[plan.groups :]
    (logs_ref, group_logs_ref, grad_ref), refs = refs[:3], refs[3:]
    send_refs, groups_ref = refs[:-1], refs[-1]
    stage_groups(plan, total_refs, groups_ref)
    grad = grad_ref[plan.rows_of(plan.member())]
    leaving = grad
    for group in reversed(range(plan.groups)):
        leaving = jnp.where(group == plan.group(), grad, leaving)
        grad = own_decays(plan, group_logs_ref.at[group]) * grad + groups_ref[group]
    total = jnp.zeros((plan.rows, plan.size), F32)
    scale = total + 1.0
    for group in range(plan.groups - 1):
        earlier = group < plan.group()
        total = jnp.where(earlier, total + scale * groups_ref[group], total)
        decays = own_decays(plan, group_logs_ref.at[group])
        scale = jnp.where(earlier, scale * decays, scale)
    after = suffixes(plan, parts_ref, logs_ref, leaving)[0]
    before = prefixes(plan, parts_ref, logs_ref, total, scale)
    first = plan.group() == 0
    for b in range(plan.members):
        if plan.groups == 2:
            send_refs[0][b] = jnp.where(first, after[b], before[b])
        else:
            send_refs[0][b] = before[b]
            send_refs[1][b] = after[b]


def decay_matrix(cum_ref, cum_col, causal, h):
    spread = cum_col[:, h : h + 1] - cum_ref[h : h + 1, :]
    return jnp.exp(jnp.where(causal, jnp.minimum(spread, 0.0), MASKED))


def intra_body(plan, query_ref, key_ref, value_ref, cum_ref, cum_col_ref, weight_ref, intra_ref):
    causal = causal_mask(query_ref.shape[0])
    cum_col = cum_col_ref[...]
    for h in range(plan.heads):
        cut = lanes(h, plan.size)
        scores = dot(query_ref[:, cut], key_ref[:, cut], CONTRACT_COLS)
        weights = (scores * decay_matrix(cum_ref, cum_col, causal, h)).astype(BF16)
        weight_ref[h] = weights
        intra_ref[:, cut] = dot(weights, value_ref[:, cut])


def attended_body(plan, *refs):
    state_refs, refs = refs[: plan.chunks], refs[plan.chunks :]
    intra_ref, query_ref, cum_col_ref, upstream_ref, gain_ref = refs[:5]
    attended_ref, sums_ref, states_ref = refs[5:]
    size, length = plan.size, query_ref.shape[0]
    for chunk, state_ref in enumerate(state_refs):
        for member in range(plan.members):
            states_ref[plan.chunk_of(member, chunk)] = state_ref[member].astype(BF16)
    growth = jnp.exp(cum_col_ref[...])
    square = jnp.zeros((length, size), F32)
    inner = jnp.zeros((length, size), F32)
    for h in range(plan.heads):
        cut = lanes(h, size)
        carried = dot(query_ref[:, cut], states_ref[cut])
        attended = intra_ref[:, cut] + growth[:, h : h + 1] * carried
        attended_ref[:, cut] = attended
        square += attended * attended
        inner += gain_ref[:, cut] * upstream_ref[:, cut].astype(F32) * attended
    ones = jnp.ones((1, size), F32)
    sums_ref[...] = jnp.concatenate(
        [exact_dot(ones, square, CONTRACT_COLS), exact_dot(ones, inner, CONTRACT_COLS)]
        + [jnp.zeros((6, length), F32)],
        axis=0,
    )


def attn_grad_body(plan, parties, *refs):
    sums_refs, refs = refs[:parties], refs[parties:]
    attended_ref, query_ref, cum_col_ref, upstream_ref, gain_ref = refs[:5]
    attn_grad_ref, send_ref = refs[5:]
    size = plan.size
    feature_count = plan.heads * size * parties
    sums = sum(ref[...] for ref in sums_refs)
    inv_row = lax.rsqrt(sums[:1] / feature_count + EPSILON)
    coefficient_row = sums[1:2] * inv_row * inv_row * inv_row / feature_count
    columns = jnp.transpose(
        jnp.concatenate([inv_row, coefficient_row, jnp.zeros_like(sums[2:])], axis=0)
    )
    inv_rms, coefficient = columns[:, :1], columns[:, 1:2]
    growth = jnp.exp(cum_col_ref[...])
    for h in range(plan.heads):
        cut = lanes(h, size)
        gained = gain_ref[:, cut] * upstream_ref[:, cut].astype(F32)
        attn_grad = (gained * inv_rms - attended_ref[:, cut] * coefficient).astype(BF16)
        attn_grad_ref[:, cut] = attn_grad
        query_decayed = (query_ref[:, cut].astype(F32) * growth[:, h : h + 1]).astype(BF16)
        member, place = divmod(h, plan.own)
        send_ref[member, lanes(place, size)] = dot(query_decayed, attn_grad, CONTRACT_ROWS)


def score_grad_body(
    plan,
    attn_grad_ref,
    query_ref,
    key_ref,
    value_ref,
    states_ref,
    weight_ref,
    cum_ref,
    cum_col_ref,
    query_grad_ref,
    key_part_ref,
    value_part_ref,
):
    causal = causal_mask(query_ref.shape[0])
    cum_col = cum_col_ref[...]
    growth = jnp.exp(cum_col)
    for h in range(plan.heads):
        cut = lanes(h, plan.size)
        attn_grad = attn_grad_ref[:, cut]
        scores = dot(attn_grad, value_ref[:, cut], CONTRACT_COLS)
        score_grad = (scores * decay_matrix(cum_ref, cum_col, causal, h)).astype(BF16)
        carried = dot(attn_grad, states_ref[cut], CONTRACT_COLS)
        query_grad = dot(score_grad, key_ref[:, cut]) + growth[:, h : h + 1] * carried
        query_grad_ref[:, cut] = query_grad.astype(BF16)
        key_part_ref[:, cut] = dot(score_grad, query_ref[:, cut], CONTRACT_ROWS)
        value_part_ref[:, cut] = dot(weight_ref[h], attn_grad, CONTRACT_ROWS)


def finish_body(plan, *refs):
    first_ref, second_ref, key_part_ref, value_part_ref, key_ref, value_ref, cum_col_ref = refs[:7]
    summary_ref, before_ref, key_grad_ref, value_grad_ref, total_ref, held_ref = refs[7:]
    length, size = key_ref.shape[0], plan.size
    swapped = jnp.where(plan.group() == 0, 0, 1) if plan.groups == 2 else 0
    held_ref[swapped] = first_ref[...]
    held_ref[1 - swapped] = second_ref[...]
    cum_col = cum_col_ref[...]
    block_log = cum_col[length - 1 : length, :]
    shrink = jnp.exp(block_log - cum_col)
    for h in range(plan.heads):
        cut = lanes(h, size)
        grads = held_ref[1, cut]
        scale = jnp.exp(before_ref[h : h + 1])
        scale_next = jnp.exp(before_ref[h : h + 1] + block_log[:, h : h + 1])
        total_ref[cut] = held_ref[0, cut] + scale * summary_ref[cut] + scale_next * grads
        grads = grads.astype(BF16)
        column = shrink[:, h : h + 1]
        key_state = dot(value_ref[:, cut], grads, CONTRACT_COLS)
        key_grad_ref[:, cut] = (key_part_ref[:, cut] + column * key_state).astype(BF16)
        value_state = dot(key_ref[:, cut], grads)
        value_grad_ref[:, cut] = (value_part_ref[:, cut] + column * value_state).astype(BF16)


def on_device(
    query_rows, key_rows, value_rows, log_decay, out_grad, norm_gain, state_in, state_out_grad
):
    heads, length = log_decay.shape
    size = state_in.shape[1]
    width = heads * size
    parties = lax.axis_size("head")
    plan = Plan(heads, size, lax.axis_size("seq"))
    bind = lambda body, *extra: functools.partial(body, plan, *extra)
    gain = norm_gain.reshape(1, width)
    chunk_piece = shaped((plan.chunk_rows, size))
    pieces = shaped((plan.members, plan.rows, size))
    chunk_pieces = shaped((plan.members, plan.chunk_rows, size))
    logged = shaped((plan.chunk_rows + LOG_ROWS, size))
    block_logs = shaped((plan.members, LOG_ROWS, size))
    group_logs = shaped((plan.groups, LOG_ROWS, size))
    table = shaped((length, width))
    rounded = shaped((length, width), BF16)
    hold_groups = pltpu.VMEM((plan.groups, plan.rows, size), F32)
    hold_chunk_groups = pltpu.VMEM((plan.groups, plan.chunk_rows, size), F32)
    chunks = range(plan.chunks)
    state_rows = state_in.reshape(width, size)

    *sends, cum_log, cum_col = call(
        bind(summary_body),
        [shaped((plan.members, plan.chunk_rows + LOG_ROWS, size))]
        + [chunk_pieces] * (plan.chunks - 1)
        + [shaped((heads, length)), shaped((length, heads))],
        [pltpu.with_memory_space_constraint(x, pltpu.HBM) for x in (key_rows, value_rows, log_decay)],
        [
            pltpu.VMEM((width, size), F32),
            pltpu.VMEM((length, width), BF16),
            pltpu.VMEM((length, width), BF16),
            pltpu.VMEM((heads, length), F32),
            pltpu.SemaphoreType.DMA((plan.members, 2)),
            pltpu.SemaphoreType.DMA,
        ],
        specs=[HBM] * 3,
    )
    parts = [plan.swap_in_group(send) for send in sends]
    weights, intra = call(
        bind(intra_body),
        [shaped((heads, length, length), BF16), table],
        [query_rows, key_rows, value_rows, cum_log, cum_col],
        flops=4 * heads * length * length * size,
    )
    totals = []
    for c in chunks:
        if c == 0:
            total, logs = call(bind(group_total_body, c), [logged, block_logs], [parts[c]])
        else:
            (total,) = call(bind(group_total_body, c), [chunk_piece], [parts[c], logs])
        totals.append([total] + plan.from_groups(total))
    states = []
    for c in chunks:
        operands = [parts[c], *totals[c], state_rows, logs]
        scratch = [hold_chunk_groups]
        if c == 0:
            send, before, all_logs = call(
                bind(forward_scan_body, c),
                [chunk_pieces, shaped((LOG_ROWS, size)), group_logs],
                operands,
                scratch,
            )
        else:
            (send,) = call(bind(forward_scan_body, c), [chunk_pieces], [*operands, all_logs], scratch)
        states.append(plan.swap_in_group(send))
    attended, sums, states = call(
        bind(attended_body),
        [table, shaped((8, length)), shaped((width, size), BF16)],
        [*states, intra, query_rows, cum_col, out_grad, gain],
    )
    all_sums = [sums] + [
        lax.ppermute(sums, "head", [(i, (i + step) % parties) for i in range(parties)])
        for step in range(1, parties)
    ]
    attn_grad, summary = call(
        bind(attn_grad_body, parties),
        [rounded, pieces],
        [*all_sums, attended, query_rows, cum_col, out_grad, gain],
    )
    parts = plan.swap_in_group(summary)
    query_grad, key_part, value_part = call(
        bind(score_grad_body),
        [rounded, table, table],
        [attn_grad, query_rows, key_rows, value_rows, states, weights, cum_log, cum_col],
        flops=10 * heads * length * length * size,
    )
    grad_rows = state_out_grad.reshape(width, size)
    two_sided = plan.groups == 2
    total, *sends = call(
        bind(group_grad_body),
        [shaped((plan.rows, size))] + [pieces] * two_sided,
        [parts, logs, grad_rows, key_part],
        specs=[VMEM] * 3 + [ANY],
    )
    totals = [total] + plan.from_groups(total)
    swapped = [plan.swap_in_group(send) for send in sends]
    sends = call(
        bind(reverse_scan_body),
        [pieces] * (1 if two_sided else 2),
        [parts, *totals, logs, all_logs, grad_rows],
        [hold_groups],
    )
    swapped += [plan.swap_in_group(send) for send in sends]
    key_grad, value_grad, state_in_grad = call(
        bind(finish_body),
        [rounded, rounded, shaped((width, size))],
        [
            *[x.reshape(width, size) for x in swapped],
            key_part,
            value_part,
            key_rows,
            value_rows,
            cum_col,
            summary.reshape(width, size),
            before,
        ],
        [pltpu.VMEM((2, width, size), F32)],
    )
    return (query_grad, key_grad, value_grad, state_in_grad.reshape(heads, size, size))


def solution(mesh):
    return jax.shard_map(
        on_device,
        mesh=mesh,
        in_specs=(
            P("seq", "head"),
            P("seq", "head"),
            P("seq", "head"),
            P("head", "seq"),
            P("seq", "head"),
            P("head"),
            P("head", None, None),
            P("head", None, None),
        ),
        out_specs=(P("seq", "head"), P("seq", "head"), P("seq", "head"), P("head", None, None)),
        check_vma=False,
    )
```

```python
import functools

import jax
import jax.numpy as jnp
from jax import lax
from jax.experimental import pallas as pl
from jax.experimental.pallas import tpu as pltpu
from jax.sharding import PartitionSpec as P

EPSILON = 1e-06
F32 = jnp.float32
BF16 = jnp.bfloat16
LOG_ROWS = 8
LONG = 10**10
MASKED = -1e30

CONTRACT_ROWS = (((0,), (0,)), ((), ()))
CONTRACT_COLS = (((1,), (1,)), ((), ()))
VMEM = pl.BlockSpec(memory_space=pltpu.VMEM)
HBM = pl.BlockSpec(memory_space=pltpu.HBM)
ANY = pl.BlockSpec(memory_space=pl.ANY)


def call(body, outs, operands, scratch=(), flops=0, specs=None):
    return pl.pallas_call(
        body,
        out_shape=outs,
        in_specs=specs or [VMEM] * len(operands),
        out_specs=[VMEM] * len(outs),
        scratch_shapes=list(scratch),
        compiler_params=pltpu.CompilerParams(vmem_limit_bytes=24 * 1024 * 1024),
        cost_estimate=pl.CostEstimate(flops=flops, bytes_accessed=0, transcendentals=0),
    )(*operands)


def shaped(shape, dtype=F32):
    return jax.ShapeDtypeStruct(shape, dtype)


def dot(a, b, dims=(((1,), (0,)), ((), ()))):
    return lax.dot_general(a, b, dims, preferred_element_type=F32)


def exact_dot(a, b, dims=(((1,), (0,)), ((), ()))):
    return lax.dot_general(
        a, b, dims, precision=lax.Precision.HIGHEST, preferred_element_type=F32
    )


def lanes(h, size):
    return slice(h * size, (h + 1) * size)


def causal_mask(length):
    row = lax.broadcasted_iota(jnp.int32, (length, length), 0)
    col = lax.broadcasted_iota(jnp.int32, (length, length), 1)
    return row >= col


class Plan:
    def __init__(self, heads, size, blocks):
        self.heads, self.size, self.blocks = heads, size, blocks
        self.members = next(m for m in (4, 2, 1) if heads % m == 0 and blocks % m == 0)
        self.groups = blocks // self.members
        self.own = heads // self.members
        self.rows = self.own * size
        self.chunks = self.own
        self.chunk_rows = self.rows // self.chunks
        self.ways = sorted(range(self.members), key=lambda way: (way > 0, -way.bit_count()))

    def member(self):
        return lax.rem(lax.axis_index("seq"), self.members)

    def group(self):
        return lax.div(lax.axis_index("seq"), self.members)

    def peer(self, k):
        return lax.bitwise_xor(self.member(), self.ways[k])

    def rows_of(self, member):
        return pl.ds(pl.multiple_of(member * self.rows, self.rows), self.rows)

    def chunk_of(self, member, chunk):
        start = member * self.rows + chunk * self.chunk_rows
        return pl.ds(pl.multiple_of(start, self.chunk_rows), self.chunk_rows)

    def swap_in_group(self, pieces):
        span = self.members
        swapped = [pieces[0]]
        for way, piece in zip(self.ways[1:], pieces[1:]):
            pairs = [(i, i // span * span + (i % span ^ way)) for i in range(self.blocks)]
            swapped.append(lax.ppermute(piece, "seq", pairs))
        return swapped

    def from_groups(self, piece):
        return [
            lax.ppermute(
                piece,
                "seq",
                [(i, (i + step * self.members) % self.blocks) for i in range(self.blocks)],
            )
            for step in range(1, self.groups)
        ]


def own_decays(plan, log_tile_ref, chunk=None):
    count = plan.own if chunk is None else plan.own // plan.chunks
    first = plan.member() * plan.own + (0 if chunk is None else chunk * count)
    rows = [log_tile_ref[pl.ds(first + j, 1), :] for j in range(count)]
    return jnp.concatenate([jnp.broadcast_to(jnp.exp(row), (plan.size, plan.size)) for row in rows])


def summary_body(plan, key_hbm, value_hbm, decay_hbm, *refs):
    send_refs, refs = refs[: plan.members * plan.chunks], refs[plan.members * plan.chunks :]
    cum_ref, cum_col_ref, held_ref, key_ref, value_ref, decay_ref, sems, decay_sem = refs
    length, heads, size = key_ref.shape[0], plan.heads, plan.size
    decay_copy = pltpu.make_async_copy(decay_hbm, decay_ref, decay_sem)
    decay_copy.start()
    copies = []
    for part in range(plan.members):
        cut = lanes(part, plan.rows)
        copies.append(
            [
                pltpu.make_async_copy(source.at[:, cut], target.at[:, cut], sems.at[part, i])
                for i, (source, target) in enumerate([(key_hbm, key_ref), (value_hbm, value_ref)])
            ]
        )
        for copy in copies[-1]:
            copy.start()
    decay_copy.wait()
    decay = decay_ref[...]
    causal = jnp.where(causal_mask(length), 1.0, 0.0)
    cum_col = exact_dot(causal, decay, CONTRACT_COLS)
    cum_row = exact_dot(decay, causal, CONTRACT_COLS)
    cum_ref[...] = cum_row
    cum_col_ref[...] = cum_col
    block_log = cum_col[length - 1 : length, :]
    shrink = jnp.exp(block_log - cum_col)
    for h in range(heads):
        if h % plan.own == 0:
            for copy in copies[h // plan.own]:
                copy.wait()
        key_decayed = (key_ref[:, lanes(h, size)].astype(F32) * shrink[:, h : h + 1]).astype(BF16)
        held_ref[h * size : (h + 1) * size] = dot(
            key_decayed, value_ref[:, lanes(h, size)], CONTRACT_ROWS
        )
    log_tile = jnp.broadcast_to(cum_row[:, length - 1 : length], (heads, size))
    if heads < LOG_ROWS:
        log_tile = jnp.concatenate([log_tile, jnp.zeros((LOG_ROWS - heads, size), F32)])
    for i, send_ref in enumerate(send_refs):
        chunk, k = divmod(i, plan.members)
        send_ref[: plan.chunk_rows] = held_ref[plan.chunk_of(plan.peer(k), chunk)]
        if chunk == 0:
            send_ref[plan.chunk_rows :] = log_tile


def group_total_body(plan, chunk, *refs):
    part_refs, refs = refs[: plan.members], refs[plan.members :]
    rows = plan.chunk_rows
    if chunk == 0:
        total_ref, logs_ref = refs[:2]
        for k, part_ref in enumerate(part_refs):
            logs_ref[plan.peer(k)] = part_ref[rows:]
        total_ref[rows:] = sum(logs_ref[b] for b in range(plan.members))
    else:
        logs_ref, total_ref = refs[:2]
    held_ref = refs[2]
    for k, part_ref in enumerate(part_refs):
        held_ref[plan.peer(k)] = part_ref[:rows]
    total = jnp.zeros((rows, plan.size), F32)
    for b in range(plan.members):
        total = own_decays(plan, logs_ref.at[b], chunk) * total + held_ref[b]
    total_ref[:rows] = total


def stage_groups(plan, total_refs, held_ref):
    rows = held_ref.shape[1]
    for step, total_ref in enumerate(total_refs):
        held_ref[lax.rem(plan.group() - step + plan.groups, plan.groups)] = total_ref[:rows]


def forward_scan_body(plan, chunk, *refs):
    part_refs, refs = refs[: plan.members], refs[plan.members :]
    total_refs, refs = refs[: plan.groups], refs[plan.groups :]
    rows = plan.chunk_rows
    if chunk == 0:
        (state_ref, logs_ref), refs = refs[:2], refs[2:]
        send_refs, (before_ref, group_logs_ref, groups_ref, held_ref) = refs[:-4], refs[-4:]
        for step, total_ref in enumerate(total_refs):
            group = lax.rem(plan.group() - step + plan.groups, plan.groups)
            group_logs_ref[group] = total_ref[rows:]
        before = jnp.zeros((LOG_ROWS, plan.size), F32)
        for group in range(plan.groups - 1):
            before += jnp.where(group < plan.group(), group_logs_ref[group], 0.0)
        for b in range(plan.members - 1):
            before += jnp.where(b < plan.member(), logs_ref[b], 0.0)
        before_ref[...] = before
    else:
        (state_ref, logs_ref, group_logs_ref), refs = refs[:3], refs[3:]
        send_refs, (groups_ref, held_ref) = refs[:-2], refs[-2:]
    stage_groups(plan, total_refs, groups_ref)
    state = state_ref[plan.chunk_of(plan.member(), chunk)]
    for group in range(plan.groups - 1):
        after = own_decays(plan, group_logs_ref.at[group], chunk) * state + groups_ref[group]
        state = jnp.where(group < plan.group(), after, state)
    for k, part_ref in enumerate(part_refs):
        held_ref[plan.peer(k)] = part_ref[:rows]
    for b in range(plan.members):
        summary = held_ref[b]
        held_ref[b] = state
        state = own_decays(plan, logs_ref.at[b], chunk) * state + summary
    for k, send_ref in enumerate(send_refs):
        send_ref[...] = held_ref[plan.peer(k)]


def suffixes(plan, held_ref, logs_ref, grad):
    found = []
    for b in reversed(range(plan.members)):
        found.append(grad)
        grad = own_decays(plan, logs_ref.at[b]) * grad + held_ref[b]
    return found[::-1], grad


def prefixes(plan, held_ref, logs_ref, total, scale):
    found = []
    for b in range(plan.members):
        found.append(total)
        total = total + scale * held_ref[b]
        scale = scale * own_decays(plan, logs_ref.at[b])
    return found


def group_grad_body(plan, *refs):
    part_refs, refs = refs[: plan.members], refs[plan.members :]
    (logs_ref, grad_ref, _, total_ref), refs = refs[:4], refs[4:]
    send_refs, (held_ref,) = refs[:-1], refs[-1:]
    for k, part_ref in enumerate(part_refs):
        held_ref[plan.peer(k)] = part_ref[...]
    zero = jnp.zeros((plan.rows, plan.size), F32)
    total_ref[...] = suffixes(plan, held_ref, logs_ref, zero)[1]
    if send_refs:
        first = plan.group() == 0
        before = prefixes(plan, held_ref, logs_ref, zero, zero + 1.0)
        after = suffixes(plan, held_ref, logs_ref, grad_ref[plan.rows_of(plan.member())])[0]
        for b in range(plan.members):
            held_ref[b] = jnp.where(first, before[b], after[b])
        for k, send_ref in enumerate(send_refs):
            send_ref[...] = held_ref[plan.peer(k)]


def reverse_scan_body(plan, *refs):
    part_refs, refs = refs[: plan.members], refs[plan.members :]
    total_refs, refs = refs[: plan.groups], refs[plan.groups :]
    (logs_ref, group_logs_ref, grad_ref), refs = refs[:3], refs[3:]
    send_refs, (groups_ref, held_ref) = refs[:-2], refs[-2:]
    stage_groups(plan, total_refs, groups_ref)
    for k, part_ref in enumerate(part_refs):
        held_ref[plan.peer(k)] = part_ref[...]
    grad = grad_ref[plan.rows_of(plan.member())]
    leaving = grad
    for group in reversed(range(plan.groups)):
        leaving = jnp.where(group == plan.group(), grad, leaving)
        grad = own_decays(plan, group_logs_ref.at[group]) * grad + groups_ref[group]
    total = jnp.zeros((plan.rows, plan.size), F32)
    scale = total + 1.0
    for group in range(plan.groups - 1):
        earlier = group < plan.group()
        total = jnp.where(earlier, total + scale * groups_ref[group], total)
        decays = own_decays(plan, group_logs_ref.at[group])
        scale = jnp.where(earlier, scale * decays, scale)
    after = suffixes(plan, held_ref, logs_ref, leaving)[0]
    before = prefixes(plan, held_ref, logs_ref, total, scale)
    if plan.groups == 2:
        first = plan.group() == 0
        found = [[jnp.where(first, after[b], before[b]) for b in range(plan.members)]]
    else:
        found = [before, after]
    for i, values in enumerate(found):
        for b in range(plan.members):
            held_ref[b] = values[b]
        for k in range(plan.members):
            send_refs[i * plan.members + k][...] = held_ref[plan.peer(k)]


def decay_matrix(cum_ref, cum_col, causal, h):
    spread = cum_col[:, h : h + 1] - cum_ref[h : h + 1, :]
    return jnp.exp(jnp.where(causal, jnp.minimum(spread, 0.0), MASKED))


def intra_body(plan, query_ref, key_ref, value_ref, cum_ref, cum_col_ref, weight_ref, intra_ref):
    causal = causal_mask(query_ref.shape[0])
    cum_col = cum_col_ref[...]
    for h in range(plan.heads):
        cut = lanes(h, plan.size)
        scores = dot(query_ref[:, cut], key_ref[:, cut], CONTRACT_COLS)
        weights = (scores * decay_matrix(cum_ref, cum_col, causal, h)).astype(BF16)
        weight_ref[h] = weights
        intra_ref[:, cut] = dot(weights, value_ref[:, cut])


def attended_body(plan, *refs):
    state_refs, refs = refs[: plan.members * plan.chunks], refs[plan.members * plan.chunks :]
    intra_ref, query_ref, cum_col_ref, upstream_ref, gain_ref = refs[:5]
    attended_ref, sums_ref, states_ref = refs[5:]
    size, length = plan.size, query_ref.shape[0]
    for i, state_ref in enumerate(state_refs):
        chunk, k = divmod(i, plan.members)
        states_ref[plan.chunk_of(plan.peer(k), chunk)] = state_ref[...].astype(BF16)
    growth = jnp.exp(cum_col_ref[...])
    square = jnp.zeros((length, size), F32)
    inner = jnp.zeros((length, size), F32)
    for h in range(plan.heads):
        cut = lanes(h, size)
        carried = dot(query_ref[:, cut], states_ref[cut])
        attended = intra_ref[:, cut] + growth[:, h : h + 1] * carried
        attended_ref[:, cut] = attended
        square += attended * attended
        inner += gain_ref[:, cut] * upstream_ref[:, cut].astype(F32) * attended
    ones = jnp.ones((1, size), F32)
    sums_ref[...] = jnp.concatenate(
        [exact_dot(ones, square, CONTRACT_COLS), exact_dot(ones, inner, CONTRACT_COLS)]
        + [jnp.zeros((6, length), F32)],
        axis=0,
    )


def attn_grad_body(plan, parties, *refs):
    sums_refs, refs = refs[:parties], refs[parties:]
    attended_ref, query_ref, cum_col_ref, upstream_ref, gain_ref = refs[:5]
    (attn_grad_ref, held_ref), send_refs = refs[5:7], refs[7:]
    size = plan.size
    feature_count = plan.heads * size * parties
    sums = sum(ref[...] for ref in sums_refs)
    inv_row = lax.rsqrt(sums[:1] / feature_count + EPSILON)
    coefficient_row = sums[1:2] * inv_row * inv_row * inv_row / feature_count
    columns = jnp.transpose(
        jnp.concatenate([inv_row, coefficient_row, jnp.zeros_like(sums[2:])], axis=0)
    )
    inv_rms, coefficient = columns[:, :1], columns[:, 1:2]
    growth = jnp.exp(cum_col_ref[...])
    for h in range(plan.heads):
        cut = lanes(h, size)
        gained = gain_ref[:, cut] * upstream_ref[:, cut].astype(F32)
        attn_grad = (gained * inv_rms - attended_ref[:, cut] * coefficient).astype(BF16)
        attn_grad_ref[:, cut] = attn_grad
        query_decayed = (query_ref[:, cut].astype(F32) * growth[:, h : h + 1]).astype(BF16)
        held_ref[cut] = dot(query_decayed, attn_grad, CONTRACT_ROWS)
    for k, send_ref in enumerate(send_refs):
        send_ref[...] = held_ref[plan.rows_of(plan.peer(k))]


def score_grad_body(
    plan,
    attn_grad_ref,
    query_ref,
    key_ref,
    value_ref,
    states_ref,
    weight_ref,
    cum_ref,
    cum_col_ref,
    query_grad_ref,
    key_part_ref,
    value_part_ref,
):
    causal = causal_mask(query_ref.shape[0])
    cum_col = cum_col_ref[...]
    growth = jnp.exp(cum_col)
    for h in range(plan.heads):
        cut = lanes(h, plan.size)
        attn_grad = attn_grad_ref[:, cut]
        scores = dot(attn_grad, value_ref[:, cut], CONTRACT_COLS)
        score_grad = (scores * decay_matrix(cum_ref, cum_col, causal, h)).astype(BF16)
        carried = dot(attn_grad, states_ref[cut], CONTRACT_COLS)
        query_grad = dot(score_grad, key_ref[:, cut]) + growth[:, h : h + 1] * carried
        query_grad_ref[:, cut] = query_grad.astype(BF16)
        key_part_ref[:, cut] = dot(score_grad, query_ref[:, cut], CONTRACT_ROWS)
        value_part_ref[:, cut] = dot(weight_ref[h], attn_grad, CONTRACT_ROWS)


def finish_body(plan, *refs):
    first_refs, refs = refs[: plan.members], refs[plan.members :]
    second_refs, refs = refs[: plan.members], refs[plan.members :]
    key_part_ref, value_part_ref, key_ref, value_ref, cum_col_ref, summary_ref, before_ref = refs[:7]
    key_grad_ref, value_grad_ref, total_ref, held_ref = refs[7:]
    length, size = key_ref.shape[0], plan.size
    swapped = jnp.where(plan.group() == 0, 0, 1) if plan.groups == 2 else 0
    for k in range(plan.members):
        held_ref[swapped, plan.rows_of(plan.peer(k))] = first_refs[k][...]
        held_ref[1 - swapped, plan.rows_of(plan.peer(k))] = second_refs[k][...]
    cum_col = cum_col_ref[...]
    block_log = cum_col[length - 1 : length, :]
    shrink = jnp.exp(block_log - cum_col)
    for h in range(plan.heads):
        cut = lanes(h, size)
        grads = held_ref[1, cut]
        scale = jnp.exp(before_ref[h : h + 1])
        scale_next = jnp.exp(before_ref[h : h + 1] + block_log[:, h : h + 1])
        total_ref[cut] = held_ref[0, cut] + scale * summary_ref[cut] + scale_next * grads
        grads = grads.astype(BF16)
        column = shrink[:, h : h + 1]
        key_state = dot(value_ref[:, cut], grads, CONTRACT_COLS)
        key_grad_ref[:, cut] = (key_part_ref[:, cut] + column * key_state).astype(BF16)
        value_state = dot(key_ref[:, cut], grads)
        value_grad_ref[:, cut] = (value_part_ref[:, cut] + column * value_state).astype(BF16)


def on_device(
    query_rows, key_rows, value_rows, log_decay, out_grad, norm_gain, state_in, state_out_grad
):
    heads, length = log_decay.shape
    size = state_in.shape[1]
    width = heads * size
    parties = lax.axis_size("head")
    plan = Plan(heads, size, lax.axis_size("seq"))
    bind = lambda body, *extra: functools.partial(body, plan, *extra)
    gain = norm_gain.reshape(1, width)
    piece = shaped((plan.rows, size))
    pieces = [piece] * plan.members
    chunk_piece = shaped((plan.chunk_rows, size))
    chunk_pieces = [chunk_piece] * plan.members
    logged = shaped((plan.chunk_rows + LOG_ROWS, size))
    block_logs = shaped((plan.members, LOG_ROWS, size))
    group_logs = shaped((plan.groups, LOG_ROWS, size))
    table = shaped((length, width))
    rounded = shaped((length, width), BF16)
    hold = pltpu.VMEM((plan.members, plan.rows, size), F32)
    hold_groups = pltpu.VMEM((plan.groups, plan.rows, size), F32)
    hold_chunk = pltpu.VMEM((plan.members, plan.chunk_rows, size), F32)
    hold_chunk_groups = pltpu.VMEM((plan.groups, plan.chunk_rows, size), F32)
    chunks = range(plan.chunks)
    state_rows = state_in.reshape(width, size)

    *sends, cum_log, cum_col = call(
        bind(summary_body),
        [logged] * plan.members
        + chunk_pieces * (plan.chunks - 1)
        + [shaped((heads, length)), shaped((length, heads))],
        [pltpu.with_memory_space_constraint(x, pltpu.HBM) for x in (key_rows, value_rows, log_decay)],
        [
            pltpu.VMEM((width, size), F32),
            pltpu.VMEM((length, width), BF16),
            pltpu.VMEM((length, width), BF16),
            pltpu.VMEM((heads, length), F32),
            pltpu.SemaphoreType.DMA((plan.members, 2)),
            pltpu.SemaphoreType.DMA,
        ],
        specs=[HBM] * 3,
    )
    parts = [
        plan.swap_in_group(sends[c * plan.members : (c + 1) * plan.members]) for c in chunks
    ]
    weights, intra = call(
        bind(intra_body),
        [shaped((heads, length, length), BF16), table],
        [query_rows, key_rows, value_rows, cum_log, cum_col],
        flops=4 * heads * length * length * size,
    )
    totals = []
    for c in chunks:
        if c == 0:
            total, logs = call(
                bind(group_total_body, c), [logged, block_logs], parts[c], [hold_chunk]
            )
        else:
            (total,) = call(
                bind(group_total_body, c),
                [chunk_piece],
                [*parts[c], logs],
                [hold_chunk],
                flops=LONG,
            )
        totals.append([total] + plan.from_groups(total))
    states = []
    for c in chunks:
        operands = [*parts[c], *totals[c], state_rows, logs]
        scratch = [hold_chunk_groups, hold_chunk]
        if c == 0:
            *sends, before, all_logs = call(
                bind(forward_scan_body, c),
                chunk_pieces + [shaped((LOG_ROWS, size)), group_logs],
                operands,
                scratch,
            )
        else:
            sends = call(bind(forward_scan_body, c), chunk_pieces, [*operands, all_logs], scratch)
        states += plan.swap_in_group(sends)
    attended, sums, states = call(
        bind(attended_body),
        [table, shaped((8, length)), shaped((width, size), BF16)],
        [*states, intra, query_rows, cum_col, out_grad, gain],
    )
    all_sums = [sums] + [
        lax.ppermute(sums, "head", [(i, (i + step) % parties) for i in range(parties)])
        for step in range(1, parties)
    ]
    attn_grad, summary, *sends = call(
        bind(attn_grad_body, parties),
        [rounded, shaped((width, size))] + pieces,
        [*all_sums, attended, query_rows, cum_col, out_grad, gain],
    )
    parts = plan.swap_in_group(sends)
    query_grad, key_part, value_part = call(
        bind(score_grad_body),
        [rounded, table, table],
        [attn_grad, query_rows, key_rows, value_rows, states, weights, cum_log, cum_col],
        flops=10 * heads * length * length * size,
    )
    grad_rows = state_out_grad.reshape(width, size)
    two_sided = plan.groups == 2
    total, *sends = call(
        bind(group_grad_body),
        [piece] + pieces * two_sided,
        [*parts, logs, grad_rows, key_part],
        [hold],
        specs=[VMEM] * (plan.members + 2) + [ANY],
    )
    totals = [total] + plan.from_groups(total)
    swapped = [plan.swap_in_group(sends)] if two_sided else []
    sends = call(
        bind(reverse_scan_body),
        pieces * (1 if two_sided else 2),
        [*parts, *totals, logs, all_logs, grad_rows],
        [hold_groups, hold],
    )
    for first in range(0, len(sends), plan.members):
        swapped.append(plan.swap_in_group(sends[first : first + plan.members]))
    key_grad, value_grad, state_in_grad = call(
        bind(finish_body),
        [rounded, rounded, shaped((width, size))],
        [*swapped[0], *swapped[1], key_part, value_part, key_rows, value_rows, cum_col, summary, before],
        [pltpu.VMEM((2, width, size), F32)],
    )
    return (query_grad, key_grad, value_grad, state_in_grad.reshape(heads, size, size))


def solution(mesh):
    return jax.shard_map(
        on_device,
        mesh=mesh,
        in_specs=(
            P("seq", "head"),
            P("seq", "head"),
            P("seq", "head"),
            P("head", "seq"),
            P("seq", "head"),
            P("head"),
            P("head", None, None),
            P("head", None, None),
        ),
        out_specs=(P("seq", "head"), P("seq", "head"), P("seq", "head"), P("head", None, None)),
        check_vma=False,
    )
```

```python
import functools

import jax
import jax.numpy as jnp
from jax import lax
from jax.experimental import pallas as pl
from jax.experimental.pallas import tpu as pltpu
from jax.sharding import PartitionSpec as P

EPSILON = 1e-06
F32 = jnp.float32
BF16 = jnp.bfloat16
LOG_ROWS = 8
LONG = 10**10
MASKED = -1e30

CONTRACT_ROWS = (((0,), (0,)), ((), ()))
CONTRACT_COLS = (((1,), (1,)), ((), ()))
VMEM = pl.BlockSpec(memory_space=pltpu.VMEM)
HBM = pl.BlockSpec(memory_space=pltpu.HBM)
ANY = pl.BlockSpec(memory_space=pl.ANY)


def call(body, outs, operands, scratch=(), flops=0, specs=None, out_specs=None):
    return pl.pallas_call(
        body,
        out_shape=outs,
        in_specs=specs or [VMEM] * len(operands),
        out_specs=out_specs or [VMEM] * len(outs),
        scratch_shapes=list(scratch),
        compiler_params=pltpu.CompilerParams(vmem_limit_bytes=24 * 1024 * 1024),
        cost_estimate=pl.CostEstimate(flops=flops, bytes_accessed=0, transcendentals=0),
    )(*operands)


def shaped(shape, dtype=F32):
    return jax.ShapeDtypeStruct(shape, dtype)


def dot(a, b, dims=(((1,), (0,)), ((), ()))):
    return lax.dot_general(a, b, dims, preferred_element_type=F32)


def split(x):
    high = x.astype(BF16)
    rest = x - high.astype(F32)
    middle = rest.astype(BF16)
    low = (rest - middle.astype(F32)).astype(BF16)
    return jnp.concatenate([high, middle, low], axis=1)


def thrice(x):
    return jnp.concatenate([x, x, x], axis=1)


def lanes(h, size):
    return slice(h * size, (h + 1) * size)


def causal_mask(length):
    row = lax.broadcasted_iota(jnp.int32, (length, length), 0)
    col = lax.broadcasted_iota(jnp.int32, (length, length), 1)
    return row >= col


class Plan:
    def __init__(self, heads, size, blocks):
        self.heads, self.size, self.blocks = heads, size, blocks
        self.members = next(m for m in (4, 2, 1) if heads % m == 0 and blocks % m == 0)
        self.groups = blocks // self.members
        self.own = heads // self.members
        self.rows = self.own * size
        self.chunks = self.own
        self.chunk_rows = self.rows // self.chunks
        self.near = [way for way in range(self.members) if way.bit_count() == 1]
        self.far = [way for way in range(self.members) if way.bit_count() > 1]
        self.ways = [0] + self.far + self.near

    def member(self):
        return lax.rem(lax.axis_index("seq"), self.members)

    def group(self):
        return lax.div(lax.axis_index("seq"), self.members)

    def peer(self, k):
        return self.toward(self.ways[k])

    def toward(self, way):
        return lax.bitwise_xor(self.member(), way)

    def rows_of(self, member):
        return pl.ds(pl.multiple_of(member * self.rows, self.rows), self.rows)

    def chunk_of(self, member, chunk):
        start = member * self.rows + chunk * self.chunk_rows
        return pl.ds(pl.multiple_of(start, self.chunk_rows), self.chunk_rows)

    def swap(self, piece, way):
        span = self.members
        pairs = [(i, i // span * span + (i % span ^ way)) for i in range(self.blocks)]
        return lax.ppermute(piece, "seq", pairs) if way else piece

    def swap_in_group(self, pieces):
        return [self.swap(piece, way) for way, piece in zip(self.ways, pieces)]

    def first_messages(self):
        cuts = [(way, c) for c in range(self.chunks) for way in [0] + self.near]
        return cuts + [(way, None) for way in self.far]

    def part_of(self, ref, way, chunk):
        start = chunk * self.chunk_rows if way in self.far else 0
        return ref[start : start + self.chunk_rows]

    def from_groups(self, piece):
        return [
            lax.ppermute(
                piece,
                "seq",
                [(i, (i + step * self.members) % self.blocks) for i in range(self.blocks)],
            )
            for step in range(1, self.groups)
        ]


def own_decays(plan, log_tile_ref, chunk=None):
    count = plan.own if chunk is None else plan.own // plan.chunks
    first = plan.member() * plan.own + (0 if chunk is None else chunk * count)
    rows = [log_tile_ref[pl.ds(first + j, 1), :] for j in range(count)]
    return jnp.concatenate([jnp.broadcast_to(jnp.exp(row), (plan.size, plan.size)) for row in rows])


def summary_body(plan, key_hbm, value_hbm, decay_hbm, *refs):
    count = len(plan.first_messages())
    send_refs, refs = refs[:count], refs[count:]
    cum_ref, cum_col_ref, held_ref, key_ref, value_ref, decay_ref, sems = refs
    length, heads, size = key_ref.shape[0], plan.heads, plan.size
    copies = [
        pltpu.make_async_copy(source, target, sems.at[i])
        for i, (source, target) in enumerate(
            [(decay_hbm, decay_ref), (key_hbm, key_ref), (value_hbm, value_ref)]
        )
    ]
    for copy in copies:
        copy.start()
    causal = thrice(jnp.where(causal_mask(length), 1.0, 0.0).astype(BF16))
    copies[0].wait()
    decay = split(decay_ref[...])
    cum_col = dot(causal, decay, CONTRACT_COLS)
    cum_row = dot(decay, causal, CONTRACT_COLS)
    cum_ref[...] = cum_row
    cum_col_ref[...] = cum_col
    shrink = jnp.exp(cum_col[length - 1 : length, :] - cum_col)
    copies[1].wait()
    copies[2].wait()
    for h in range(heads):
        key_decayed = (key_ref[:, lanes(h, size)].astype(F32) * shrink[:, h : h + 1]).astype(BF16)
        held_ref[h * size : (h + 1) * size] = dot(
            key_decayed, value_ref[:, lanes(h, size)], CONTRACT_ROWS
        )
    log_tile = jnp.broadcast_to(cum_row[:, length - 1 : length], (heads, size))
    if heads < LOG_ROWS:
        log_tile = jnp.concatenate([log_tile, jnp.zeros((LOG_ROWS - heads, size), F32)])
    for (way, chunk), send_ref in zip(plan.first_messages(), send_refs):
        member = plan.toward(way)
        whole = chunk is None
        part = plan.rows_of(member) if whole else plan.chunk_of(member, chunk)
        rows = plan.rows if whole else plan.chunk_rows
        send_ref[:rows] = held_ref[part]
        if not chunk:
            send_ref[rows:] = log_tile


def group_total_body(plan, chunk, *refs):
    part_refs, refs = refs[: plan.members], refs[plan.members :]
    rows = plan.chunk_rows
    if chunk == 0:
        total_ref, logs_ref = refs[:2]
        for k, part_ref in enumerate(part_refs):
            logs_ref[plan.peer(k)] = part_ref[part_ref.shape[0] - LOG_ROWS :]
        total_ref[rows:] = sum(logs_ref[b] for b in range(plan.members))
    else:
        logs_ref, total_ref = refs[:2]
    held_ref = refs[2]
    for way, part_ref in zip(plan.ways, part_refs):
        held_ref[plan.toward(way)] = plan.part_of(part_ref, way, chunk)
    total = jnp.zeros((rows, plan.size), F32)
    for b in range(plan.members):
        total = own_decays(plan, logs_ref.at[b], chunk) * total + held_ref[b]
    total_ref[:rows] = total


def stage_groups(plan, total_refs, held_ref):
    rows = held_ref.shape[1]
    for step, total_ref in enumerate(total_refs):
        held_ref[lax.rem(plan.group() - step + plan.groups, plan.groups)] = total_ref[:rows]


def forward_scan_body(plan, chunk, *refs):
    last = chunk == plan.chunks - 1
    part_refs, refs = refs[: plan.members], refs[plan.members :]
    total_refs, refs = refs[: plan.groups], refs[plan.groups :]
    (state_ref, logs_ref), refs = refs[:2], refs[2:]
    rows = plan.chunk_rows
    if chunk > 0:
        group_logs_ref, refs = refs[0], refs[1:]
    far_parts = chunk * len(plan.far) if last else 0
    far_refs, refs = refs[:far_parts], refs[far_parts:]
    send_refs, refs = refs[: plan.members], refs[plan.members :]
    if chunk == 0:
        before_ref, group_logs_ref = refs[:2]
        for step, total_ref in enumerate(total_refs):
            group = lax.rem(plan.group() - step + plan.groups, plan.groups)
            group_logs_ref[group] = total_ref[rows:]
        before = jnp.zeros((LOG_ROWS, plan.size), F32)
        for group in range(plan.groups - 1):
            before += jnp.where(group < plan.group(), group_logs_ref[group], 0.0)
        for b in range(plan.members - 1):
            before += jnp.where(b < plan.member(), logs_ref[b], 0.0)
        before_ref[...] = before
    groups_ref, held_ref = refs[-2:]
    stage_groups(plan, total_refs, groups_ref)
    state = state_ref[plan.chunk_of(plan.member(), chunk)]
    for group in range(plan.groups - 1):
        after = own_decays(plan, group_logs_ref.at[group], chunk) * state + groups_ref[group]
        state = jnp.where(group < plan.group(), after, state)
    for way, part_ref in zip(plan.ways, part_refs):
        held_ref[plan.toward(way)] = plan.part_of(part_ref, way, chunk)
    for b in range(plan.members):
        summary = held_ref[b]
        held_ref[b] = state
        state = own_decays(plan, logs_ref.at[b], chunk) * state + summary
    for i, (way, send_ref) in enumerate(zip(plan.ways, send_refs)):
        if way in plan.far and last:
            for c in range(chunk):
                send_ref[c * rows : (c + 1) * rows] = far_refs[c * len(plan.far) + i - 1][...]
            send_ref[chunk * rows :] = held_ref[plan.toward(way)]
        else:
            send_ref[...] = held_ref[plan.toward(way)]


def suffixes(plan, held_ref, logs_ref, grad):
    found = []
    for b in reversed(range(plan.members)):
        found.append(grad)
        grad = own_decays(plan, logs_ref.at[b]) * grad + held_ref[b]
    return found[::-1], grad


def prefixes(plan, held_ref, logs_ref, total, scale):
    found = []
    for b in range(plan.members):
        found.append(total)
        total = total + scale * held_ref[b]
        scale = scale * own_decays(plan, logs_ref.at[b])
    return found


def group_grad_body(plan, *refs):
    part_refs, refs = refs[: plan.members], refs[plan.members :]
    (logs_ref, grad_ref, _, total_ref), refs = refs[:4], refs[4:]
    send_refs, (held_ref,) = refs[:-1], refs[-1:]
    for k, part_ref in enumerate(part_refs):
        held_ref[plan.peer(k)] = part_ref[...]
    zero = jnp.zeros((plan.rows, plan.size), F32)
    total_ref[...] = suffixes(plan, held_ref, logs_ref, zero)[1]
    if send_refs:
        first = plan.group() == 0
        before = prefixes(plan, held_ref, logs_ref, zero, zero + 1.0)
        after = suffixes(plan, held_ref, logs_ref, grad_ref[plan.rows_of(plan.member())])[0]
        for b in range(plan.members):
            held_ref[b] = jnp.where(first, before[b], after[b])
        for k, send_ref in enumerate(send_refs):
            send_ref[...] = held_ref[plan.peer(k)]


def reverse_scan_body(plan, *refs):
    part_refs, refs = refs[: plan.members], refs[plan.members :]
    total_refs, refs = refs[: plan.groups], refs[plan.groups :]
    (logs_ref, group_logs_ref, grad_ref), refs = refs[:3], refs[3:]
    send_refs, (groups_ref, held_ref) = refs[:-2], refs[-2:]
    stage_groups(plan, total_refs, groups_ref)
    for k, part_ref in enumerate(part_refs):
        held_ref[plan.peer(k)] = part_ref[...]
    grad = grad_ref[plan.rows_of(plan.member())]
    leaving = grad
    for group in reversed(range(plan.groups)):
        leaving = jnp.where(group == plan.group(), grad, leaving)
        grad = own_decays(plan, group_logs_ref.at[group]) * grad + groups_ref[group]
    total = jnp.zeros((plan.rows, plan.size), F32)
    scale = total + 1.0
    for group in range(plan.groups - 1):
        earlier = group < plan.group()
        total = jnp.where(earlier, total + scale * groups_ref[group], total)
        decays = own_decays(plan, group_logs_ref.at[group])
        scale = jnp.where(earlier, scale * decays, scale)
    after = suffixes(plan, held_ref, logs_ref, leaving)[0]
    before = prefixes(plan, held_ref, logs_ref, total, scale)
    if plan.groups == 2:
        first = plan.group() == 0
        found = [[jnp.where(first, after[b], before[b]) for b in range(plan.members)]]
    else:
        found = [before, after]
    for i, values in enumerate(found):
        for b in range(plan.members):
            held_ref[b] = values[b]
        for k in range(plan.members):
            send_refs[i * plan.members + k][...] = held_ref[plan.peer(k)]


def decay_matrix(cum_ref, cum_col, causal, h):
    spread = cum_col[:, h : h + 1] - cum_ref[h : h + 1, :]
    return jnp.exp(jnp.where(causal, jnp.minimum(spread, 0.0), MASKED))


def intra_body(
    plan,
    query_ref,
    key_ref,
    value_ref,
    cum_ref,
    cum_col_ref,
    upstream_ref,
    gain_ref,
    *refs,
):
    weight_ref, intra_ref, gained_ref, query_decayed_ref = refs[-4:]
    causal = causal_mask(query_ref.shape[0])
    cum_col = cum_col_ref[...]
    growth = jnp.exp(cum_col)
    for h in range(plan.heads):
        cut = lanes(h, plan.size)
        query = query_ref[:, cut]
        scores = dot(query, key_ref[:, cut], CONTRACT_COLS)
        weights = (scores * decay_matrix(cum_ref, cum_col, causal, h)).astype(BF16)
        weight_ref[h] = weights
        intra_ref[:, cut] = dot(weights, value_ref[:, cut])
        gained_ref[:, cut] = gain_ref[:, cut] * upstream_ref[:, cut].astype(F32)
        query_decayed = query.astype(F32) * growth[:, h : h + 1]
        query_decayed_ref[h] = jnp.transpose(query_decayed).astype(BF16)


def attended_body(plan, *refs):
    count = len(plan.first_messages())
    state_refs, refs = refs[:count], refs[count:]
    intra_ref, query_ref, cum_col_ref, gained_ref = refs[:4]
    attended_ref, sums_ref, states_ref = refs[4:]
    size, length = plan.size, query_ref.shape[0]
    for (way, chunk), state_ref in zip(plan.first_messages(), state_refs):
        member = plan.toward(way)
        part = plan.rows_of(member) if chunk is None else plan.chunk_of(member, chunk)
        states_ref[part] = state_ref[...].astype(BF16)
    growth = jnp.exp(cum_col_ref[...])
    square = jnp.zeros((length, size), F32)
    inner = jnp.zeros((length, size), F32)
    for h in range(plan.heads):
        cut = lanes(h, size)
        carried = dot(query_ref[:, cut], states_ref[cut])
        attended = intra_ref[:, cut] + growth[:, h : h + 1] * carried
        attended_ref[:, cut] = attended
        square += attended * attended
        inner += gained_ref[:, cut] * attended
    ones = jnp.ones((8, 3 * size), BF16)
    is_square = lax.broadcasted_iota(jnp.int32, (8, length), 0) == 0
    sums_ref[...] = jnp.where(
        is_square,
        dot(ones, split(square), CONTRACT_COLS),
        dot(ones, split(inner), CONTRACT_COLS),
    )


def attn_grad_body(plan, parties, *refs):
    sums_refs, refs = refs[:parties], refs[parties:]
    attended_ref, query_decayed_ref, gained_ref, attn_grad_ref, held_ref = refs[:5]
    send_refs = refs[5:]
    size, length = plan.size, attended_ref.shape[0]
    feature_count = plan.heads * size * parties
    sums = sum(ref[...] for ref in sums_refs)
    inv_row = lax.rsqrt(sums[:1] / feature_count + EPSILON)
    coefficient_row = sums[1:2] * inv_row * inv_row * inv_row / feature_count
    is_inverse = lax.broadcasted_iota(jnp.int32, (8, length), 0) == 0
    columns = jnp.transpose(jnp.where(is_inverse, inv_row, coefficient_row))
    inv_rms = jnp.broadcast_to(columns[:, :1], (length, size))
    coefficient = jnp.broadcast_to(columns[:, 1:2], (length, size))
    for h in range(plan.heads):
        cut = lanes(h, size)
        attn_grad = gained_ref[:, cut] * inv_rms - attended_ref[:, cut] * coefficient
        attn_grad = attn_grad.astype(BF16)
        attn_grad_ref[:, cut] = attn_grad
        held_ref[cut] = dot(query_decayed_ref[h], attn_grad)
    for k, send_ref in enumerate(send_refs):
        send_ref[...] = held_ref[plan.rows_of(plan.peer(k))]


def score_grad_body(
    plan,
    attn_grad_ref,
    query_ref,
    key_ref,
    value_ref,
    states_ref,
    weight_ref,
    cum_ref,
    cum_col_ref,
    query_grad_ref,
    key_part_ref,
    value_part_ref,
):
    causal = causal_mask(query_ref.shape[0])
    cum_col = cum_col_ref[...]
    growth = jnp.exp(cum_col)
    for h in range(plan.heads):
        cut = lanes(h, plan.size)
        attn_grad = attn_grad_ref[:, cut]
        scores = dot(attn_grad, value_ref[:, cut], CONTRACT_COLS)
        score_grad = (scores * decay_matrix(cum_ref, cum_col, causal, h)).astype(BF16)
        carried = dot(attn_grad, states_ref[cut], CONTRACT_COLS)
        query_grad = dot(score_grad, key_ref[:, cut]) + growth[:, h : h + 1] * carried
        query_grad_ref[:, cut] = query_grad.astype(BF16)
        key_part_ref[:, cut] = dot(score_grad, query_ref[:, cut], CONTRACT_ROWS)
        value_part_ref[:, cut] = dot(weight_ref[h], attn_grad, CONTRACT_ROWS)


def finish_body(plan, *refs):
    first_refs, refs = refs[: plan.members], refs[plan.members :]
    second_refs, refs = refs[: plan.members], refs[plan.members :]
    key_part_ref, value_part_ref, key_ref, value_ref, cum_col_ref, summary_ref, before_ref = refs[:7]
    key_out, value_out, total_out, held_ref, key_grad_ref, value_grad_ref, total_ref, sems = refs[7:]
    length, size = key_ref.shape[0], plan.size
    swapped = jnp.where(plan.group() == 0, 0, 1) if plan.groups == 2 else 0
    for k in range(plan.members):
        held_ref[swapped, plan.rows_of(plan.peer(k))] = first_refs[k][...]
        held_ref[1 - swapped, plan.rows_of(plan.peer(k))] = second_refs[k][...]
    cum_col = cum_col_ref[...]
    block_log = cum_col[length - 1 : length, :]
    shrink = jnp.exp(block_log - cum_col)
    copies = []
    half = max(plan.heads // 2, 1)
    for h in range(plan.heads):
        cut = lanes(h, size)
        grads = held_ref[1, cut]
        scale = jnp.exp(before_ref[h : h + 1])
        scale_next = jnp.exp(before_ref[h : h + 1] + block_log[:, h : h + 1])
        total_ref[cut] = held_ref[0, cut] + scale * summary_ref[cut] + scale_next * grads
        grads = grads.astype(BF16)
        column = shrink[:, h : h + 1]
        key_state = dot(value_ref[:, cut], grads, CONTRACT_COLS)
        key_grad_ref[:, cut] = (key_part_ref[:, cut] + column * key_state).astype(BF16)
        value_state = dot(key_ref[:, cut], grads)
        value_grad_ref[:, cut] = (value_part_ref[:, cut] + column * value_state).astype(BF16)
        if (h + 1) % half == 0:
            done = slice((h + 1 - half) * size, (h + 1) * size)
            for source, target, index in [
                (total_ref, total_out, (done,)),
                (key_grad_ref, key_out, (slice(None), done)),
                (value_grad_ref, value_out, (slice(None), done)),
            ]:
                copies.append(
                    pltpu.make_async_copy(source.at[index], target.at[index], sems.at[len(copies)])
                )
                copies[-1].start()
    for copy in copies:
        copy.wait()


def on_device(
    query_rows, key_rows, value_rows, log_decay, out_grad, norm_gain, state_in, state_out_grad
):
    heads, length = log_decay.shape
    size = state_in.shape[1]
    width = heads * size
    parties = lax.axis_size("head")
    plan = Plan(heads, size, lax.axis_size("seq"))
    bind = lambda body, *extra: functools.partial(body, plan, *extra)
    gain = norm_gain.reshape(1, width)
    piece = shaped((plan.rows, size))
    pieces = [piece] * plan.members
    chunk_piece = shaped((plan.chunk_rows, size))
    chunk_pieces = [chunk_piece] * plan.members
    logged = shaped((plan.chunk_rows + LOG_ROWS, size))
    block_logs = shaped((plan.members, LOG_ROWS, size))
    group_logs = shaped((plan.groups, LOG_ROWS, size))
    table = shaped((length, width))
    rounded = shaped((length, width), BF16)
    hold = pltpu.VMEM((plan.members, plan.rows, size), F32)
    hold_groups = pltpu.VMEM((plan.groups, plan.rows, size), F32)
    hold_chunk = pltpu.VMEM((plan.members, plan.chunk_rows, size), F32)
    hold_chunk_groups = pltpu.VMEM((plan.groups, plan.chunk_rows, size), F32)
    chunks = range(plan.chunks)
    state_rows = state_in.reshape(width, size)

    messages = plan.first_messages()
    *sends, cum_log, cum_col = call(
        bind(summary_body),
        [
            shaped(
                (
                    (plan.rows if chunk is None else plan.chunk_rows) + (0 if chunk else LOG_ROWS),
                    size,
                )
            )
            for _, chunk in messages
        ]
        + [shaped((heads, length)), shaped((length, heads))],
        [pltpu.with_memory_space_constraint(x, pltpu.HBM) for x in (key_rows, value_rows, log_decay)],
        [
            pltpu.VMEM((width, size), F32),
            pltpu.VMEM((length, width), BF16),
            pltpu.VMEM((length, width), BF16),
            pltpu.VMEM((heads, length), F32),
            pltpu.SemaphoreType.DMA((3,)),
        ],
        specs=[HBM] * 3,
    )
    received = {key: plan.swap(send, key[0]) for key, send in zip(messages, sends)}
    parts = [[received[way, None if way in plan.far else c] for way in plan.ways] for c in chunks]
    totals = []
    for c in chunks:
        if c == 0:
            total, logs = call(
                bind(group_total_body, c), [logged, block_logs], parts[c], [hold_chunk]
            )
        else:
            (total,) = call(
                bind(group_total_body, c),
                [chunk_piece],
                [*parts[c], logs],
                [hold_chunk],
                flops=LONG,
            )
        totals.append([total] + plan.from_groups(total))
    states = {}
    far_parts = []
    for c in chunks:
        last = c == plan.chunks - 1
        operands = [*parts[c], *totals[c], state_rows, logs]
        outs = [piece if way in plan.far and last else chunk_piece for way in plan.ways]
        if c == 0:
            outs += [shaped((LOG_ROWS, size)), group_logs]
        else:
            operands += [all_logs]
        sends = call(
            bind(forward_scan_body, c),
            outs,
            operands + (far_parts if last else []),
            [hold_chunk_groups, hold_chunk],
        )
        if c == 0:
            before, all_logs = sends[plan.members :]
        for way, send in zip(plan.ways, sends):
            if way not in plan.far:
                states[way, c] = plan.swap(send, way)
            elif last:
                states[way, None] = plan.swap(send, way)
            else:
                far_parts.append(send)
    early = [states[way, 0] for way in plan.near] if plan.chunks > 1 else []
    weights, intra, gained, query_decayed = call(
        bind(intra_body),
        [
            shaped((heads, length, length), BF16),
            table,
            table,
            shaped((heads, size, length), BF16),
        ],
        [query_rows, key_rows, value_rows, cum_log, cum_col, out_grad, gain, *early],
        specs=[VMEM] * 7 + [ANY] * len(early),
        flops=LONG // 10,
    )
    attended, sums, states = call(
        bind(attended_body),
        [table, shaped((8, length)), shaped((width, size), BF16)],
        [*[states[key] for key in messages], intra, query_rows, cum_col, gained],
    )
    all_sums = [sums] + [
        lax.ppermute(sums, "head", [(i, (i + step) % parties) for i in range(parties)])
        for step in range(1, parties)
    ]
    attn_grad, summary, *sends = call(
        bind(attn_grad_body, parties),
        [rounded, shaped((width, size))] + pieces,
        [*all_sums, attended, query_decayed, gained],
    )
    parts = plan.swap_in_group(sends)
    query_grad, key_part, value_part = call(
        bind(score_grad_body),
        [rounded, table, table],
        [attn_grad, query_rows, key_rows, value_rows, states, weights, cum_log, cum_col],
        flops=10 * heads * length * length * size,
    )
    grad_rows = state_out_grad.reshape(width, size)
    two_sided = plan.groups == 2
    total, *sends = call(
        bind(group_grad_body),
        [piece] + pieces * two_sided,
        [*parts, logs, grad_rows, key_part],
        [hold],
        specs=[VMEM] * (plan.members + 2) + [ANY],
    )
    totals = [total] + plan.from_groups(total)
    swapped = [plan.swap_in_group(sends)] if two_sided else []
    sends = call(
        bind(reverse_scan_body),
        pieces * (1 if two_sided else 2),
        [*parts, *totals, logs, all_logs, grad_rows],
        [hold_groups, hold],
    )
    for first in range(0, len(sends), plan.members):
        swapped.append(plan.swap_in_group(sends[first : first + plan.members]))
    key_grad, value_grad, state_in_grad = call(
        bind(finish_body),
        [rounded, rounded, shaped((width, size))],
        [*swapped[0], *swapped[1], key_part, value_part, key_rows, value_rows, cum_col, summary, before],
        [
            pltpu.VMEM((2, width, size), F32),
            pltpu.VMEM((length, width), BF16),
            pltpu.VMEM((length, width), BF16),
            pltpu.VMEM((width, size), F32),
            pltpu.SemaphoreType.DMA((6,)),
        ],
        out_specs=[HBM] * 3,
    )
    return (query_grad, key_grad, value_grad, state_in_grad.reshape(heads, size, size))


def solution(mesh):
    return jax.shard_map(
        on_device,
        mesh=mesh,
        in_specs=(
            P("seq", "head"),
            P("seq", "head"),
            P("seq", "head"),
            P("head", "seq"),
            P("seq", "head"),
            P("head"),
            P("head", None, None),
            P("head", None, None),
        ),
        out_specs=(P("seq", "head"), P("seq", "head"), P("seq", "head"), P("head", None, None)),
        check_vma=False,
    )
```

```python
import functools

import jax
import jax.numpy as jnp
from jax import lax
from jax.experimental import pallas as pl
from jax.experimental.pallas import tpu as pltpu
from jax.sharding import PartitionSpec as P

EPSILON = 1e-06
F32 = jnp.float32
BF16 = jnp.bfloat16
LOG_ROWS = 8
LONG = 10**10
MASKED = -1e30

CONTRACT_ROWS = (((0,), (0,)), ((), ()))
CONTRACT_COLS = (((1,), (1,)), ((), ()))
VMEM = pl.BlockSpec(memory_space=pltpu.VMEM)
HBM = pl.BlockSpec(memory_space=pltpu.HBM)
ANY = pl.BlockSpec(memory_space=pl.ANY)


def call(body, outs, operands, scratch=(), flops=0, specs=None, out_specs=None):
    return pl.pallas_call(
        body,
        out_shape=outs,
        in_specs=specs or [VMEM] * len(operands),
        out_specs=out_specs or [VMEM] * len(outs),
        scratch_shapes=list(scratch),
        compiler_params=pltpu.CompilerParams(vmem_limit_bytes=24 * 1024 * 1024),
        cost_estimate=pl.CostEstimate(flops=flops, bytes_accessed=0, transcendentals=0),
    )(*operands)


def shaped(shape, dtype=F32):
    return jax.ShapeDtypeStruct(shape, dtype)


def dot(a, b, dims=(((1,), (0,)), ((), ()))):
    return lax.dot_general(a, b, dims, preferred_element_type=F32)


def split(x):
    high = x.astype(BF16)
    rest = x - high.astype(F32)
    middle = rest.astype(BF16)
    low = (rest - middle.astype(F32)).astype(BF16)
    return jnp.concatenate([high, middle, low], axis=1)


def thrice(x):
    return jnp.concatenate([x, x, x], axis=1)


def lanes(h, size):
    return slice(h * size, (h + 1) * size)


def causal_mask(length):
    row = lax.broadcasted_iota(jnp.int32, (length, length), 0)
    col = lax.broadcasted_iota(jnp.int32, (length, length), 1)
    return row >= col


class Plan:
    def __init__(self, heads, size, blocks):
        self.heads, self.size, self.blocks = heads, size, blocks
        self.members = next(m for m in (4, 2, 1) if heads % m == 0 and blocks % m == 0)
        self.groups = blocks // self.members
        self.own = heads // self.members
        self.rows = self.own * size
        self.chunks = self.own
        self.chunk_rows = self.rows // self.chunks
        self.near = [way for way in range(self.members) if way.bit_count() == 1]
        self.far = [way for way in range(self.members) if way.bit_count() > 1]
        self.ways = [0] + self.far + self.near

    def member(self):
        return lax.rem(lax.axis_index("seq"), self.members)

    def group(self):
        return lax.div(lax.axis_index("seq"), self.members)

    def peer(self, k):
        return self.toward(self.ways[k])

    def toward(self, way):
        return lax.bitwise_xor(self.member(), way)

    def rows_of(self, member):
        return pl.ds(pl.multiple_of(member * self.rows, self.rows), self.rows)

    def chunk_of(self, member, chunk):
        start = member * self.rows + chunk * self.chunk_rows
        return pl.ds(pl.multiple_of(start, self.chunk_rows), self.chunk_rows)

    def swap(self, piece, way):
        span = self.members
        pairs = [(i, i // span * span + (i % span ^ way)) for i in range(self.blocks)]
        return lax.ppermute(piece, "seq", pairs) if way else piece

    def swap_in_group(self, pieces):
        return [self.swap(piece, way) for way, piece in zip(self.ways, pieces)]

    def first_messages(self):
        return [(way, c) for c in range(self.chunks) for way in self.ways]

    def last_messages(self):
        cuts = [(way, c) for c in range(self.chunks) for way in [0] + self.near]
        return cuts + [(way, None) for way in self.far]

    def from_groups(self, piece):
        return [
            lax.ppermute(
                piece,
                "seq",
                [(i, (i + step * self.members) % self.blocks) for i in range(self.blocks)],
            )
            for step in range(1, self.groups)
        ]


def own_decays(plan, log_tile_ref, chunk=None):
    count = plan.own if chunk is None else plan.own // plan.chunks
    first = plan.member() * plan.own + (0 if chunk is None else chunk * count)
    rows = [log_tile_ref[pl.ds(first + j, 1), :] for j in range(count)]
    return jnp.concatenate([jnp.broadcast_to(jnp.exp(row), (plan.size, plan.size)) for row in rows])


def summary_body(plan, key_hbm, value_hbm, decay_hbm, *refs):
    count = len(plan.first_messages())
    send_refs, refs = refs[:count], refs[count:]
    cum_ref, cum_col_ref, held_ref, key_ref, value_ref, decay_ref, sems = refs
    length, heads, size = key_ref.shape[0], plan.heads, plan.size
    copies = [
        pltpu.make_async_copy(source, target, sems.at[i])
        for i, (source, target) in enumerate(
            [(decay_hbm, decay_ref), (key_hbm, key_ref), (value_hbm, value_ref)]
        )
    ]
    for copy in copies:
        copy.start()
    causal = thrice(jnp.where(causal_mask(length), 1.0, 0.0).astype(BF16))
    copies[0].wait()
    decay = split(decay_ref[...])
    cum_col = dot(causal, decay, CONTRACT_COLS)
    cum_row = dot(decay, causal, CONTRACT_COLS)
    cum_ref[...] = cum_row
    cum_col_ref[...] = cum_col
    shrink = jnp.exp(cum_col[length - 1 : length, :] - cum_col)
    copies[1].wait()
    copies[2].wait()
    for h in range(heads):
        key_decayed = (key_ref[:, lanes(h, size)].astype(F32) * shrink[:, h : h + 1]).astype(BF16)
        held_ref[h * size : (h + 1) * size] = dot(
            key_decayed, value_ref[:, lanes(h, size)], CONTRACT_ROWS
        )
    log_tile = jnp.broadcast_to(cum_row[:, length - 1 : length], (heads, size))
    if heads < LOG_ROWS:
        log_tile = jnp.concatenate([log_tile, jnp.zeros((LOG_ROWS - heads, size), F32)])
    for (way, chunk), send_ref in zip(plan.first_messages(), send_refs):
        send_ref[: plan.chunk_rows] = held_ref[plan.chunk_of(plan.toward(way), chunk)]
        if chunk == 0:
            send_ref[plan.chunk_rows :] = log_tile


def group_total_body(plan, chunk, *refs):
    part_refs, refs = refs[: plan.members], refs[plan.members :]
    rows = plan.chunk_rows
    if chunk == 0:
        total_ref, logs_ref = refs[:2]
        for k, part_ref in enumerate(part_refs):
            logs_ref[plan.peer(k)] = part_ref[rows:]
        total_ref[rows:] = sum(logs_ref[b] for b in range(plan.members))
    else:
        logs_ref, total_ref = refs[:2]
    held_ref = refs[2]
    for way, part_ref in zip(plan.ways, part_refs):
        held_ref[plan.toward(way)] = part_ref[:rows]
    total = jnp.zeros((rows, plan.size), F32)
    for b in range(plan.members):
        total = own_decays(plan, logs_ref.at[b], chunk) * total + held_ref[b]
    total_ref[:rows] = total


def stage_groups(plan, total_refs, held_ref):
    rows = held_ref.shape[1]
    for step, total_ref in enumerate(total_refs):
        held_ref[lax.rem(plan.group() - step + plan.groups, plan.groups)] = total_ref[:rows]


def forward_scan_body(plan, chunk, *refs):
    last = chunk == plan.chunks - 1
    part_refs, refs = refs[: plan.members], refs[plan.members :]
    total_refs, refs = refs[: plan.groups], refs[plan.groups :]
    (state_ref, logs_ref), refs = refs[:2], refs[2:]
    rows = plan.chunk_rows
    if chunk > 0:
        group_logs_ref, refs = refs[0], refs[1:]
    far_parts = chunk * len(plan.far) if last else 0
    far_refs, refs = refs[:far_parts], refs[far_parts:]
    send_refs, refs = refs[: plan.members], refs[plan.members :]
    if chunk == 0:
        before_ref, group_logs_ref = refs[:2]
        for step, total_ref in enumerate(total_refs):
            group = lax.rem(plan.group() - step + plan.groups, plan.groups)
            group_logs_ref[group] = total_ref[rows:]
        before = jnp.zeros((LOG_ROWS, plan.size), F32)
        for group in range(plan.groups - 1):
            before += jnp.where(group < plan.group(), group_logs_ref[group], 0.0)
        for b in range(plan.members - 1):
            before += jnp.where(b < plan.member(), logs_ref[b], 0.0)
        before_ref[...] = before
    groups_ref, held_ref = refs[-2:]
    stage_groups(plan, total_refs, groups_ref)
    state = state_ref[plan.chunk_of(plan.member(), chunk)]
    for group in range(plan.groups - 1):
        after = own_decays(plan, group_logs_ref.at[group], chunk) * state + groups_ref[group]
        state = jnp.where(group < plan.group(), after, state)
    for way, part_ref in zip(plan.ways, part_refs):
        held_ref[plan.toward(way)] = part_ref[:rows]
    for b in range(plan.members):
        summary = held_ref[b]
        held_ref[b] = state
        state = own_decays(plan, logs_ref.at[b], chunk) * state + summary
    for i, (way, send_ref) in enumerate(zip(plan.ways, send_refs)):
        if way in plan.far and last:
            for c in range(chunk):
                send_ref[c * rows : (c + 1) * rows] = far_refs[c * len(plan.far) + i - 1][...]
            send_ref[chunk * rows :] = held_ref[plan.toward(way)]
        else:
            send_ref[...] = held_ref[plan.toward(way)]


def suffixes(plan, held_ref, logs_ref, grad):
    found = []
    for b in reversed(range(plan.members)):
        found.append(grad)
        grad = own_decays(plan, logs_ref.at[b]) * grad + held_ref[b]
    return found[::-1], grad


def prefixes(plan, held_ref, logs_ref, total, scale):
    found = []
    for b in range(plan.members):
        found.append(total)
        total = total + scale * held_ref[b]
        scale = scale * own_decays(plan, logs_ref.at[b])
    return found


def group_grad_body(plan, *refs):
    part_refs, refs = refs[: plan.members], refs[plan.members :]
    (logs_ref, grad_ref, _, total_ref), refs = refs[:4], refs[4:]
    send_refs, (held_ref,) = refs[:-1], refs[-1:]
    for k, part_ref in enumerate(part_refs):
        held_ref[plan.peer(k)] = part_ref[...]
    zero = jnp.zeros((plan.rows, plan.size), F32)
    total_ref[...] = suffixes(plan, held_ref, logs_ref, zero)[1]
    if send_refs:
        first = plan.group() == 0
        before = prefixes(plan, held_ref, logs_ref, zero, zero + 1.0)
        after = suffixes(plan, held_ref, logs_ref, grad_ref[plan.rows_of(plan.member())])[0]
        for b in range(plan.members):
            held_ref[b] = jnp.where(first, before[b], after[b])
        for k, send_ref in enumerate(send_refs):
            send_ref[...] = held_ref[plan.peer(k)]


def reverse_scan_body(plan, *refs):
    part_refs, refs = refs[: plan.members], refs[plan.members :]
    total_refs, refs = refs[: plan.groups], refs[plan.groups :]
    (logs_ref, group_logs_ref, grad_ref), refs = refs[:3], refs[3:]
    send_refs, (groups_ref, held_ref) = refs[:-2], refs[-2:]
    stage_groups(plan, total_refs, groups_ref)
    for k, part_ref in enumerate(part_refs):
        held_ref[plan.peer(k)] = part_ref[...]
    grad = grad_ref[plan.rows_of(plan.member())]
    leaving = grad
    for group in reversed(range(plan.groups)):
        leaving = jnp.where(group == plan.group(), grad, leaving)
        grad = own_decays(plan, group_logs_ref.at[group]) * grad + groups_ref[group]
    total = jnp.zeros((plan.rows, plan.size), F32)
    scale = total + 1.0
    for group in range(plan.groups - 1):
        earlier = group < plan.group()
        total = jnp.where(earlier, total + scale * groups_ref[group], total)
        decays = own_decays(plan, group_logs_ref.at[group])
        scale = jnp.where(earlier, scale * decays, scale)
    after = suffixes(plan, held_ref, logs_ref, leaving)[0]
    before = prefixes(plan, held_ref, logs_ref, total, scale)
    if plan.groups == 2:
        first = plan.group() == 0
        found = [[jnp.where(first, after[b], before[b]) for b in range(plan.members)]]
    else:
        found = [before, after]
    for i, values in enumerate(found):
        for b in range(plan.members):
            held_ref[b] = values[b]
        for k in range(plan.members):
            send_refs[i * plan.members + k][...] = held_ref[plan.peer(k)]


def decay_matrix(cum_ref, cum_col, causal, h):
    spread = cum_col[:, h : h + 1] - cum_ref[h : h + 1, :]
    return jnp.exp(jnp.where(causal, jnp.minimum(spread, 0.0), MASKED))


def intra_body(
    plan,
    query_ref,
    key_ref,
    value_ref,
    cum_ref,
    cum_col_ref,
    upstream_ref,
    gain_ref,
    *refs,
):
    weight_ref, intra_ref, gained_ref, query_decayed_ref = refs[-4:]
    causal = causal_mask(query_ref.shape[0])
    cum_col = cum_col_ref[...]
    growth = jnp.exp(cum_col)
    for h in range(plan.heads):
        cut = lanes(h, plan.size)
        query = query_ref[:, cut]
        scores = dot(query, key_ref[:, cut], CONTRACT_COLS)
        weights = (scores * decay_matrix(cum_ref, cum_col, causal, h)).astype(BF16)
        weight_ref[h] = weights
        intra_ref[:, cut] = dot(weights, value_ref[:, cut])
        gained_ref[:, cut] = gain_ref[:, cut] * upstream_ref[:, cut].astype(F32)
        query_decayed = query.astype(F32) * growth[:, h : h + 1]
        query_decayed_ref[h] = jnp.transpose(query_decayed).astype(BF16)


def attended_body(plan, *refs):
    count = len(plan.last_messages())
    state_refs, refs = refs[:count], refs[count:]
    intra_ref, query_ref, cum_col_ref, gained_ref = refs[:4]
    attended_ref, sums_ref, states_ref = refs[4:]
    size, length = plan.size, query_ref.shape[0]
    for (way, chunk), state_ref in zip(plan.last_messages(), state_refs):
        member = plan.toward(way)
        part = plan.rows_of(member) if chunk is None else plan.chunk_of(member, chunk)
        states_ref[part] = state_ref[...].astype(BF16)
    growth = jnp.exp(cum_col_ref[...])
    square = jnp.zeros((length, size), F32)
    inner = jnp.zeros((length, size), F32)
    for h in range(plan.heads):
        cut = lanes(h, size)
        carried = dot(query_ref[:, cut], states_ref[cut])
        attended = intra_ref[:, cut] + growth[:, h : h + 1] * carried
        attended_ref[:, cut] = attended
        square += attended * attended
        inner += gained_ref[:, cut] * attended
    ones = jnp.ones((8, 3 * size), BF16)
    is_square = lax.broadcasted_iota(jnp.int32, (8, length), 0) == 0
    sums_ref[...] = jnp.where(
        is_square,
        dot(ones, split(square), CONTRACT_COLS),
        dot(ones, split(inner), CONTRACT_COLS),
    )


def attn_grad_body(plan, parties, *refs):
    sums_refs, refs = refs[:parties], refs[parties:]
    attended_ref, query_decayed_ref, gained_ref, attn_grad_ref, held_ref = refs[:5]
    send_refs = refs[5:]
    size, length = plan.size, attended_ref.shape[0]
    feature_count = plan.heads * size * parties
    sums = sum(ref[...] for ref in sums_refs)
    inv_row = lax.rsqrt(sums[:1] / feature_count + EPSILON)
    coefficient_row = sums[1:2] * inv_row * inv_row * inv_row / feature_count
    is_inverse = lax.broadcasted_iota(jnp.int32, (8, length), 0) == 0
    columns = jnp.transpose(jnp.where(is_inverse, inv_row, coefficient_row))
    inv_rms = jnp.broadcast_to(columns[:, :1], (length, size))
    coefficient = jnp.broadcast_to(columns[:, 1:2], (length, size))
    for h in range(plan.heads):
        cut = lanes(h, size)
        attn_grad = gained_ref[:, cut] * inv_rms - attended_ref[:, cut] * coefficient
        attn_grad = attn_grad.astype(BF16)
        attn_grad_ref[:, cut] = attn_grad
        held_ref[cut] = dot(query_decayed_ref[h], attn_grad)
    for k, send_ref in enumerate(send_refs):
        send_ref[...] = held_ref[plan.rows_of(plan.peer(k))]


def score_grad_body(
    plan,
    attn_grad_ref,
    query_ref,
    key_ref,
    value_ref,
    states_ref,
    weight_ref,
    cum_ref,
    cum_col_ref,
    query_grad_ref,
    key_part_ref,
    value_part_ref,
):
    causal = causal_mask(query_ref.shape[0])
    cum_col = cum_col_ref[...]
    growth = jnp.exp(cum_col)
    for h in range(plan.heads):
        cut = lanes(h, plan.size)
        attn_grad = attn_grad_ref[:, cut]
        scores = dot(attn_grad, value_ref[:, cut], CONTRACT_COLS)
        score_grad = (scores * decay_matrix(cum_ref, cum_col, causal, h)).astype(BF16)
        carried = dot(attn_grad, states_ref[cut], CONTRACT_COLS)
        query_grad = dot(score_grad, key_ref[:, cut]) + growth[:, h : h + 1] * carried
        query_grad_ref[:, cut] = query_grad.astype(BF16)
        key_part_ref[:, cut] = dot(score_grad, query_ref[:, cut], CONTRACT_ROWS)
        value_part_ref[:, cut] = dot(weight_ref[h], attn_grad, CONTRACT_ROWS)


def finish_body(plan, *refs):
    first_refs, refs = refs[: plan.members], refs[plan.members :]
    second_refs, refs = refs[: plan.members], refs[plan.members :]
    key_part_ref, value_part_ref, key_ref, value_ref, cum_col_ref, summary_ref, before_ref = refs[:7]
    key_out, value_out, total_out, held_ref, key_grad_ref, value_grad_ref, total_ref, sems = refs[7:]
    length, size = key_ref.shape[0], plan.size
    swapped = jnp.where(plan.group() == 0, 0, 1) if plan.groups == 2 else 0
    for k in range(plan.members):
        held_ref[swapped, plan.rows_of(plan.peer(k))] = first_refs[k][...]
        held_ref[1 - swapped, plan.rows_of(plan.peer(k))] = second_refs[k][...]
    cum_col = cum_col_ref[...]
    block_log = cum_col[length - 1 : length, :]
    shrink = jnp.exp(block_log - cum_col)
    copies = []
    half = max(plan.heads // 2, 1)
    for h in range(plan.heads):
        cut = lanes(h, size)
        grads = held_ref[1, cut]
        scale = jnp.exp(before_ref[h : h + 1])
        scale_next = jnp.exp(before_ref[h : h + 1] + block_log[:, h : h + 1])
        total_ref[cut] = held_ref[0, cut] + scale * summary_ref[cut] + scale_next * grads
        grads = grads.astype(BF16)
        column = shrink[:, h : h + 1]
        key_state = dot(value_ref[:, cut], grads, CONTRACT_COLS)
        key_grad_ref[:, cut] = (key_part_ref[:, cut] + column * key_state).astype(BF16)
        value_state = dot(key_ref[:, cut], grads)
        value_grad_ref[:, cut] = (value_part_ref[:, cut] + column * value_state).astype(BF16)
        if (h + 1) % half == 0:
            done = slice((h + 1 - half) * size, (h + 1) * size)
            for source, target, index in [
                (total_ref, total_out, (done,)),
                (key_grad_ref, key_out, (slice(None), done)),
                (value_grad_ref, value_out, (slice(None), done)),
            ]:
                copies.append(
                    pltpu.make_async_copy(source.at[index], target.at[index], sems.at[len(copies)])
                )
                copies[-1].start()
    for copy in copies:
        copy.wait()


def on_device(
    query_rows, key_rows, value_rows, log_decay, out_grad, norm_gain, state_in, state_out_grad
):
    heads, length = log_decay.shape
    size = state_in.shape[1]
    width = heads * size
    parties = lax.axis_size("head")
    plan = Plan(heads, size, lax.axis_size("seq"))
    bind = lambda body, *extra: functools.partial(body, plan, *extra)
    gain = norm_gain.reshape(1, width)
    piece = shaped((plan.rows, size))
    pieces = [piece] * plan.members
    chunk_piece = shaped((plan.chunk_rows, size))
    chunk_pieces = [chunk_piece] * plan.members
    logged = shaped((plan.chunk_rows + LOG_ROWS, size))
    block_logs = shaped((plan.members, LOG_ROWS, size))
    group_logs = shaped((plan.groups, LOG_ROWS, size))
    table = shaped((length, width))
    rounded = shaped((length, width), BF16)
    hold = pltpu.VMEM((plan.members, plan.rows, size), F32)
    hold_groups = pltpu.VMEM((plan.groups, plan.rows, size), F32)
    hold_chunk = pltpu.VMEM((plan.members, plan.chunk_rows, size), F32)
    hold_chunk_groups = pltpu.VMEM((plan.groups, plan.chunk_rows, size), F32)
    chunks = range(plan.chunks)
    state_rows = state_in.reshape(width, size)

    messages = plan.first_messages()
    *sends, cum_log, cum_col = call(
        bind(summary_body),
        [chunk_piece if chunk else logged for _, chunk in messages]
        + [shaped((heads, length)), shaped((length, heads))],
        [pltpu.with_memory_space_constraint(x, pltpu.HBM) for x in (key_rows, value_rows, log_decay)],
        [
            pltpu.VMEM((width, size), F32),
            pltpu.VMEM((length, width), BF16),
            pltpu.VMEM((length, width), BF16),
            pltpu.VMEM((heads, length), F32),
            pltpu.SemaphoreType.DMA((3,)),
        ],
        specs=[HBM] * 3,
    )
    received = {key: plan.swap(send, key[0]) for key, send in zip(messages, sends)}
    parts = [[received[way, c] for way in plan.ways] for c in chunks]
    totals = []
    for c in chunks:
        if c == 0:
            total, logs = call(
                bind(group_total_body, c), [logged, block_logs], parts[c], [hold_chunk]
            )
        else:
            (total,) = call(
                bind(group_total_body, c),
                [chunk_piece],
                [*parts[c], logs],
                [hold_chunk],
                flops=LONG,
            )
        totals.append([total] + plan.from_groups(total))
    states = {}
    far_parts = []
    for c in chunks:
        last = c == plan.chunks - 1
        operands = [*parts[c], *totals[c], state_rows, logs]
        outs = [piece if way in plan.far and last else chunk_piece for way in plan.ways]
        if c == 0:
            outs += [shaped((LOG_ROWS, size)), group_logs]
        else:
            operands += [all_logs]
        sends = call(
            bind(forward_scan_body, c),
            outs,
            operands + (far_parts if last else []),
            [hold_chunk_groups, hold_chunk],
        )
        if c == 0:
            before, all_logs = sends[plan.members :]
        for way, send in zip(plan.ways, sends):
            if way not in plan.far:
                states[way, c] = plan.swap(send, way)
            elif last:
                states[way, None] = plan.swap(send, way)
            else:
                far_parts.append(send)
    early = [states[way, 0] for way in plan.near] if plan.chunks > 1 else []
    weights, intra, gained, query_decayed = call(
        bind(intra_body),
        [
            shaped((heads, length, length), BF16),
            table,
            table,
            shaped((heads, size, length), BF16),
        ],
        [query_rows, key_rows, value_rows, cum_log, cum_col, out_grad, gain, *early],
        specs=[VMEM] * 7 + [ANY] * len(early),
        flops=LONG // 10,
    )
    attended, sums, states = call(
        bind(attended_body),
        [table, shaped((8, length)), shaped((width, size), BF16)],
        [*[states[key] for key in plan.last_messages()], intra, query_rows, cum_col, gained],
    )
    all_sums = [sums] + [
        lax.ppermute(sums, "head", [(i, i ^ way) for i in range(parties)])
        for way in range(1, parties)
    ]
    attn_grad, summary, *sends = call(
        bind(attn_grad_body, parties),
        [rounded, shaped((width, size))] + pieces,
        [*all_sums, attended, query_decayed, gained],
    )
    parts = plan.swap_in_group(sends)
    query_grad, key_part, value_part = call(
        bind(score_grad_body),
        [rounded, table, table],
        [attn_grad, query_rows, key_rows, value_rows, states, weights, cum_log, cum_col],
        flops=10 * heads * length * length * size,
    )
    grad_rows = state_out_grad.reshape(width, size)
    two_sided = plan.groups == 2
    total, *sends = call(
        bind(group_grad_body),
        [piece] + pieces * two_sided,
        [*parts, logs, grad_rows, key_part],
        [hold],
        specs=[VMEM] * (plan.members + 2) + [ANY],
    )
    totals = [total] + plan.from_groups(total)
    swapped = [plan.swap_in_group(sends)] if two_sided else []
    sends = call(
        bind(reverse_scan_body),
        pieces * (1 if two_sided else 2),
        [*parts, *totals, logs, all_logs, grad_rows],
        [hold_groups, hold],
    )
    for first in range(0, len(sends), plan.members):
        swapped.append(plan.swap_in_group(sends[first : first + plan.members]))
    key_grad, value_grad, state_in_grad = call(
        bind(finish_body),
        [rounded, rounded, shaped((width, size))],
        [*swapped[0], *swapped[1], key_part, value_part, key_rows, value_rows, cum_col, summary, before],
        [
            pltpu.VMEM((2, width, size), F32),
            pltpu.VMEM((length, width), BF16),
            pltpu.VMEM((length, width), BF16),
            pltpu.VMEM((width, size), F32),
            pltpu.SemaphoreType.DMA((6,)),
        ],
        out_specs=[HBM] * 3,
    )
    return (query_grad, key_grad, value_grad, state_in_grad.reshape(heads, size, size))


def solution(mesh):
    return jax.shard_map(
        on_device,
        mesh=mesh,
        in_specs=(
            P("seq", "head"),
            P("seq", "head"),
            P("seq", "head"),
            P("head", "seq"),
            P("seq", "head"),
            P("head"),
            P("head", None, None),
            P("head", None, None),
        ),
        out_specs=(P("seq", "head"), P("seq", "head"), P("seq", "head"), P("head", None, None)),
        check_vma=False,
    )
```

```python
import functools

import jax
import jax.numpy as jnp
from jax import lax
from jax.experimental import pallas as pl
from jax.experimental.pallas import tpu as pltpu
from jax.sharding import PartitionSpec as P

EPSILON = 1e-06
F32 = jnp.float32
BF16 = jnp.bfloat16
LOG_ROWS = 8
LONG = 10**10
MASKED = -1e30

CONTRACT_ROWS = (((0,), (0,)), ((), ()))
CONTRACT_COLS = (((1,), (1,)), ((), ()))
VMEM = pl.BlockSpec(memory_space=pltpu.VMEM)
HBM = pl.BlockSpec(memory_space=pltpu.HBM)
ANY = pl.BlockSpec(memory_space=pl.ANY)


def call(body, outs, operands, scratch=(), flops=0, specs=None, out_specs=None):
    return pl.pallas_call(
        body,
        out_shape=outs,
        in_specs=specs or [VMEM] * len(operands),
        out_specs=out_specs or [VMEM] * len(outs),
        scratch_shapes=list(scratch),
        compiler_params=pltpu.CompilerParams(vmem_limit_bytes=24 * 1024 * 1024),
        cost_estimate=pl.CostEstimate(flops=flops, bytes_accessed=0, transcendentals=0),
    )(*operands)


def shaped(shape, dtype=F32):
    return jax.ShapeDtypeStruct(shape, dtype)


def dot(a, b, dims=(((1,), (0,)), ((), ()))):
    return lax.dot_general(a, b, dims, preferred_element_type=F32)


def split(x):
    high = x.astype(BF16)
    rest = x - high.astype(F32)
    middle = rest.astype(BF16)
    low = (rest - middle.astype(F32)).astype(BF16)
    return jnp.concatenate([high, middle, low], axis=1)


def thrice(x):
    return jnp.concatenate([x, x, x], axis=1)


def lanes(h, size):
    return slice(h * size, (h + 1) * size)


def causal_mask(length):
    row = lax.broadcasted_iota(jnp.int32, (length, length), 0)
    col = lax.broadcasted_iota(jnp.int32, (length, length), 1)
    return row >= col


class Plan:
    def __init__(self, heads, size, blocks):
        self.heads, self.size, self.blocks = heads, size, blocks
        self.members = next(m for m in (4, 2, 1) if heads % m == 0 and blocks % m == 0)
        self.groups = blocks // self.members
        self.own = heads // self.members
        self.rows = self.own * size
        self.chunks = self.own
        self.chunk_rows = self.rows // self.chunks
        self.near = [way for way in range(self.members) if way.bit_count() == 1]
        self.far = [way for way in range(self.members) if way.bit_count() > 1]
        self.ways = [0] + self.far + self.near

    def member(self):
        return lax.rem(lax.axis_index("seq"), self.members)

    def group(self):
        return lax.div(lax.axis_index("seq"), self.members)

    def peer(self, k):
        return self.toward(self.ways[k])

    def toward(self, way):
        return lax.bitwise_xor(self.member(), way)

    def rows_of(self, member):
        return pl.ds(pl.multiple_of(member * self.rows, self.rows), self.rows)

    def chunk_of(self, member, chunk):
        start = member * self.rows + chunk * self.chunk_rows
        return pl.ds(pl.multiple_of(start, self.chunk_rows), self.chunk_rows)

    def swap(self, piece, way):
        span = self.members
        pairs = [(i, i // span * span + (i % span ^ way)) for i in range(self.blocks)]
        return lax.ppermute(piece, "seq", pairs) if way else piece

    def swap_in_group(self, pieces, order=None):
        return [self.swap(piece, way) for way, piece in zip(order or self.ways, pieces)]

    def first_messages(self):
        return [(way, c) for c in range(self.chunks) for way in self.ways]

    def last_messages(self):
        cuts = [(way, c) for c in range(self.chunks) for way in [0] + self.near]
        return cuts + [(way, None) for way in self.far]

    def from_groups(self, piece):
        return [
            lax.ppermute(
                piece,
                "seq",
                [(i, (i + step * self.members) % self.blocks) for i in range(self.blocks)],
            )
            for step in range(1, self.groups)
        ]


def own_decays(plan, log_tile_ref, chunk=None):
    count = plan.own if chunk is None else plan.own // plan.chunks
    first = plan.member() * plan.own + (0 if chunk is None else chunk * count)
    rows = [log_tile_ref[pl.ds(first + j, 1), :] for j in range(count)]
    return jnp.concatenate([jnp.broadcast_to(jnp.exp(row), (plan.size, plan.size)) for row in rows])


def summary_body(plan, key_hbm, value_hbm, decay_hbm, *refs):
    count = len(plan.first_messages())
    send_refs, refs = refs[:count], refs[count:]
    cum_ref, cum_col_ref, held_ref, key_ref, value_ref, decay_ref, sems = refs
    length, heads, size = key_ref.shape[0], plan.heads, plan.size
    copies = [
        pltpu.make_async_copy(source, target, sems.at[i])
        for i, (source, target) in enumerate(
            [(decay_hbm, decay_ref), (key_hbm, key_ref), (value_hbm, value_ref)]
        )
    ]
    for copy in copies:
        copy.start()
    causal = thrice(jnp.where(causal_mask(length), 1.0, 0.0).astype(BF16))
    copies[0].wait()
    decay = split(decay_ref[...])
    cum_col = dot(causal, decay, CONTRACT_COLS)
    cum_row = dot(decay, causal, CONTRACT_COLS)
    cum_ref[...] = cum_row
    cum_col_ref[...] = cum_col
    shrink = jnp.exp(cum_col[length - 1 : length, :] - cum_col)
    copies[1].wait()
    copies[2].wait()
    for h in range(heads):
        key_decayed = (key_ref[:, lanes(h, size)].astype(F32) * shrink[:, h : h + 1]).astype(BF16)
        held_ref[h * size : (h + 1) * size] = dot(
            key_decayed, value_ref[:, lanes(h, size)], CONTRACT_ROWS
        )
    log_tile = jnp.broadcast_to(cum_row[:, length - 1 : length], (heads, size))
    if heads < LOG_ROWS:
        log_tile = jnp.concatenate([log_tile, jnp.zeros((LOG_ROWS - heads, size), F32)])
    for (way, chunk), send_ref in zip(plan.first_messages(), send_refs):
        send_ref[: plan.chunk_rows] = held_ref[plan.chunk_of(plan.toward(way), chunk)]
        if chunk == 0:
            send_ref[plan.chunk_rows :] = log_tile


def group_total_body(plan, chunk, *refs):
    part_refs, refs = refs[: plan.members], refs[plan.members :]
    rows = plan.chunk_rows
    if chunk == 0:
        total_ref, logs_ref = refs[:2]
        for k, part_ref in enumerate(part_refs):
            logs_ref[plan.peer(k)] = part_ref[rows:]
        total_ref[rows:] = sum(logs_ref[b] for b in range(plan.members))
    else:
        logs_ref, total_ref = refs[:2]
    held_ref = refs[2]
    for way, part_ref in zip(plan.ways, part_refs):
        held_ref[plan.toward(way)] = part_ref[:rows]
    total = jnp.zeros((rows, plan.size), F32)
    for b in range(plan.members):
        total = own_decays(plan, logs_ref.at[b], chunk) * total + held_ref[b]
    total_ref[:rows] = total


def stage_groups(plan, total_refs, held_ref):
    rows = held_ref.shape[1]
    for step, total_ref in enumerate(total_refs):
        held_ref[lax.rem(plan.group() - step + plan.groups, plan.groups)] = total_ref[:rows]


def forward_scan_body(plan, chunk, *refs):
    last = chunk == plan.chunks - 1
    part_refs, refs = refs[: plan.members], refs[plan.members :]
    total_refs, refs = refs[: plan.groups], refs[plan.groups :]
    (state_ref, logs_ref), refs = refs[:2], refs[2:]
    rows = plan.chunk_rows
    if chunk > 0:
        group_logs_ref, refs = refs[0], refs[1:]
    far_parts = chunk * len(plan.far) if last else 0
    far_refs, refs = refs[:far_parts], refs[far_parts:]
    send_refs, refs = refs[: plan.members], refs[plan.members :]
    if chunk == 0:
        before_ref, group_logs_ref = refs[:2]
        for step, total_ref in enumerate(total_refs):
            group = lax.rem(plan.group() - step + plan.groups, plan.groups)
            group_logs_ref[group] = total_ref[rows:]
        before = jnp.zeros((LOG_ROWS, plan.size), F32)
        for group in range(plan.groups - 1):
            before += jnp.where(group < plan.group(), group_logs_ref[group], 0.0)
        for b in range(plan.members - 1):
            before += jnp.where(b < plan.member(), logs_ref[b], 0.0)
        before_ref[...] = before
    groups_ref, held_ref = refs[-2:]
    stage_groups(plan, total_refs, groups_ref)
    state = state_ref[plan.chunk_of(plan.member(), chunk)]
    for group in range(plan.groups - 1):
        after = own_decays(plan, group_logs_ref.at[group], chunk) * state + groups_ref[group]
        state = jnp.where(group < plan.group(), after, state)
    for way, part_ref in zip(plan.ways, part_refs):
        held_ref[plan.toward(way)] = part_ref[:rows]
    for b in range(plan.members):
        summary = held_ref[b]
        held_ref[b] = state
        state = own_decays(plan, logs_ref.at[b], chunk) * state + summary
    for i, (way, send_ref) in enumerate(zip(plan.ways, send_refs)):
        if way in plan.far and last:
            for c in range(chunk):
                send_ref[c * rows : (c + 1) * rows] = far_refs[c * len(plan.far) + i - 1][...]
            send_ref[chunk * rows :] = held_ref[plan.toward(way)]
        else:
            send_ref[...] = held_ref[plan.toward(way)]


def suffixes(plan, held_ref, logs_ref, grad):
    found = []
    for b in reversed(range(plan.members)):
        found.append(grad)
        grad = own_decays(plan, logs_ref.at[b]) * grad + held_ref[b]
    return found[::-1], grad


def prefixes(plan, held_ref, logs_ref, total, scale):
    found = []
    for b in range(plan.members):
        found.append(total)
        total = total + scale * held_ref[b]
        scale = scale * own_decays(plan, logs_ref.at[b])
    return found


def group_grad_body(plan, *refs):
    part_refs, refs = refs[: plan.members], refs[plan.members :]
    (logs_ref, grad_ref, _, total_ref), refs = refs[:4], refs[4:]
    send_refs, (held_ref,) = refs[:-1], refs[-1:]
    for k, part_ref in enumerate(part_refs):
        held_ref[plan.peer(k)] = part_ref[...]
    zero = jnp.zeros((plan.rows, plan.size), F32)
    total_ref[...] = suffixes(plan, held_ref, logs_ref, zero)[1]
    if send_refs:
        first = plan.group() == 0
        before = prefixes(plan, held_ref, logs_ref, zero, zero + 1.0)
        after = suffixes(plan, held_ref, logs_ref, grad_ref[plan.rows_of(plan.member())])[0]
        for b in range(plan.members):
            held_ref[b] = jnp.where(first, before[b], after[b])
        for way, send_ref in enumerate(send_refs):
            send_ref[...] = held_ref[plan.toward(way)]


def reverse_scan_body(plan, *refs):
    part_refs, refs = refs[: plan.members], refs[plan.members :]
    total_refs, refs = refs[: plan.groups], refs[plan.groups :]
    (logs_ref, group_logs_ref, grad_ref), refs = refs[:3], refs[3:]
    send_refs, (groups_ref, held_ref) = refs[:-2], refs[-2:]
    stage_groups(plan, total_refs, groups_ref)
    for k, part_ref in enumerate(part_refs):
        held_ref[plan.peer(k)] = part_ref[...]
    grad = grad_ref[plan.rows_of(plan.member())]
    leaving = grad
    for group in reversed(range(plan.groups)):
        leaving = jnp.where(group == plan.group(), grad, leaving)
        grad = own_decays(plan, group_logs_ref.at[group]) * grad + groups_ref[group]
    total = jnp.zeros((plan.rows, plan.size), F32)
    scale = total + 1.0
    for group in range(plan.groups - 1):
        earlier = group < plan.group()
        total = jnp.where(earlier, total + scale * groups_ref[group], total)
        decays = own_decays(plan, group_logs_ref.at[group])
        scale = jnp.where(earlier, scale * decays, scale)
    after = suffixes(plan, held_ref, logs_ref, leaving)[0]
    before = prefixes(plan, held_ref, logs_ref, total, scale)
    if plan.groups == 2:
        first = plan.group() == 0
        found = [[jnp.where(first, after[b], before[b]) for b in range(plan.members)]]
    else:
        found = [before, after]
    for i, values in enumerate(found):
        for b in range(plan.members):
            held_ref[b] = values[b]
        for k in range(plan.members):
            send_refs[i * plan.members + k][...] = held_ref[plan.peer(k)]


def decay_matrix(cum_ref, cum_col, causal, h):
    spread = cum_col[:, h : h + 1] - cum_ref[h : h + 1, :]
    return jnp.exp(jnp.where(causal, jnp.minimum(spread, 0.0), MASKED))


def intra_body(
    plan,
    query_ref,
    key_ref,
    value_ref,
    cum_ref,
    cum_col_ref,
    upstream_ref,
    gain_ref,
    *refs,
):
    weight_ref, intra_ref, gained_ref, query_decayed_ref = refs[-4:]
    causal = causal_mask(query_ref.shape[0])
    cum_col = cum_col_ref[...]
    growth = jnp.exp(cum_col)
    for h in range(plan.heads):
        cut = lanes(h, plan.size)
        query = query_ref[:, cut]
        scores = dot(query, key_ref[:, cut], CONTRACT_COLS)
        weights = (scores * decay_matrix(cum_ref, cum_col, causal, h)).astype(BF16)
        weight_ref[h] = weights
        intra_ref[:, cut] = dot(weights, value_ref[:, cut])
        gained_ref[:, cut] = gain_ref[:, cut] * upstream_ref[:, cut].astype(F32)
        query_decayed = query.astype(F32) * growth[:, h : h + 1]
        query_decayed_ref[h] = jnp.transpose(query_decayed).astype(BF16)


def attended_body(plan, *refs):
    count = len(plan.last_messages())
    state_refs, refs = refs[:count], refs[count:]
    intra_ref, query_ref, cum_col_ref, gained_ref = refs[:4]
    attended_ref, sums_ref, states_ref = refs[4:]
    size, length = plan.size, query_ref.shape[0]
    for (way, chunk), state_ref in zip(plan.last_messages(), state_refs):
        member = plan.toward(way)
        part = plan.rows_of(member) if chunk is None else plan.chunk_of(member, chunk)
        states_ref[part] = state_ref[...].astype(BF16)
    growth = jnp.exp(cum_col_ref[...])
    square = jnp.zeros((length, size), F32)
    inner = jnp.zeros((length, size), F32)
    for h in range(plan.heads):
        cut = lanes(h, size)
        carried = dot(query_ref[:, cut], states_ref[cut])
        attended = intra_ref[:, cut] + growth[:, h : h + 1] * carried
        attended_ref[:, cut] = attended
        square += attended * attended
        inner += gained_ref[:, cut] * attended
    ones = jnp.ones((8, 3 * size), BF16)
    is_square = lax.broadcasted_iota(jnp.int32, (8, length), 0) == 0
    sums_ref[...] = jnp.where(
        is_square,
        dot(ones, split(square), CONTRACT_COLS),
        dot(ones, split(inner), CONTRACT_COLS),
    )


def attn_grad_body(plan, parties, *refs):
    sums_refs, refs = refs[:parties], refs[parties:]
    attended_ref, query_decayed_ref, gained_ref, attn_grad_ref, held_ref = refs[:5]
    send_refs = refs[5:]
    size, length = plan.size, attended_ref.shape[0]
    feature_count = plan.heads * size * parties
    sums = sum(ref[...] for ref in sums_refs)
    inv_row = lax.rsqrt(sums[:1] / feature_count + EPSILON)
    coefficient_row = sums[1:2] * inv_row * inv_row * inv_row / feature_count
    is_inverse = lax.broadcasted_iota(jnp.int32, (8, length), 0) == 0
    columns = jnp.transpose(jnp.where(is_inverse, inv_row, coefficient_row))
    inv_rms = jnp.broadcast_to(columns[:, :1], (length, size))
    coefficient = jnp.broadcast_to(columns[:, 1:2], (length, size))
    for h in range(plan.heads):
        cut = lanes(h, size)
        attn_grad = gained_ref[:, cut] * inv_rms - attended_ref[:, cut] * coefficient
        attn_grad = attn_grad.astype(BF16)
        attn_grad_ref[:, cut] = attn_grad
        held_ref[cut] = dot(query_decayed_ref[h], attn_grad)
    for k, send_ref in enumerate(send_refs):
        send_ref[...] = held_ref[plan.rows_of(plan.peer(k))]


def score_grad_body(
    plan,
    attn_grad_ref,
    query_ref,
    key_ref,
    value_ref,
    states_ref,
    weight_ref,
    cum_ref,
    cum_col_ref,
    query_grad_ref,
    key_part_ref,
    value_part_ref,
):
    causal = causal_mask(query_ref.shape[0])
    cum_col = cum_col_ref[...]
    growth = jnp.exp(cum_col)
    for h in range(plan.heads):
        cut = lanes(h, plan.size)
        attn_grad = attn_grad_ref[:, cut]
        scores = dot(attn_grad, value_ref[:, cut], CONTRACT_COLS)
        score_grad = (scores * decay_matrix(cum_ref, cum_col, causal, h)).astype(BF16)
        carried = dot(attn_grad, states_ref[cut], CONTRACT_COLS)
        query_grad = dot(score_grad, key_ref[:, cut]) + growth[:, h : h + 1] * carried
        query_grad_ref[:, cut] = query_grad.astype(BF16)
        key_part_ref[:, cut] = dot(score_grad, query_ref[:, cut], CONTRACT_ROWS)
        value_part_ref[:, cut] = dot(weight_ref[h], attn_grad, CONTRACT_ROWS)


def finish_body(plan, *refs):
    first_refs, refs = refs[: plan.members], refs[plan.members :]
    second_refs, refs = refs[: plan.members], refs[plan.members :]
    key_part_ref, value_part_ref, key_ref, value_ref, cum_col_ref, summary_ref, before_ref = refs[:7]
    key_out, value_out, total_out, held_ref, key_grad_ref, value_grad_ref, total_ref, sems = refs[7:]
    length, size = key_ref.shape[0], plan.size
    swapped = jnp.where(plan.group() == 0, 0, 1) if plan.groups == 2 else 0
    for k, way in enumerate(range(plan.members) if plan.groups == 2 else plan.ways):
        held_ref[swapped, plan.rows_of(plan.toward(way))] = first_refs[k][...]
        held_ref[1 - swapped, plan.rows_of(plan.peer(k))] = second_refs[k][...]
    cum_col = cum_col_ref[...]
    block_log = cum_col[length - 1 : length, :]
    shrink = jnp.exp(block_log - cum_col)
    copies = []
    half = max(plan.heads // 2, 1)
    for h in range(plan.heads):
        cut = lanes(h, size)
        grads = held_ref[1, cut]
        scale = jnp.exp(before_ref[h : h + 1])
        scale_next = jnp.exp(before_ref[h : h + 1] + block_log[:, h : h + 1])
        total_ref[cut] = held_ref[0, cut] + scale * summary_ref[cut] + scale_next * grads
        grads = grads.astype(BF16)
        column = shrink[:, h : h + 1]
        key_state = dot(value_ref[:, cut], grads, CONTRACT_COLS)
        key_grad_ref[:, cut] = (key_part_ref[:, cut] + column * key_state).astype(BF16)
        value_state = dot(key_ref[:, cut], grads)
        value_grad_ref[:, cut] = (value_part_ref[:, cut] + column * value_state).astype(BF16)
        if (h + 1) % half == 0:
            done = slice((h + 1 - half) * size, (h + 1) * size)
            for source, target, index in [
                (total_ref, total_out, (done,)),
                (key_grad_ref, key_out, (slice(None), done)),
                (value_grad_ref, value_out, (slice(None), done)),
            ]:
                copies.append(
                    pltpu.make_async_copy(source.at[index], target.at[index], sems.at[len(copies)])
                )
                copies[-1].start()
    for copy in copies:
        copy.wait()


def on_device(
    query_rows, key_rows, value_rows, log_decay, out_grad, norm_gain, state_in, state_out_grad
):
    heads, length = log_decay.shape
    size = state_in.shape[1]
    width = heads * size
    parties = lax.axis_size("head")
    plan = Plan(heads, size, lax.axis_size("seq"))
    bind = lambda body, *extra: functools.partial(body, plan, *extra)
    gain = norm_gain.reshape(1, width)
    piece = shaped((plan.rows, size))
    pieces = [piece] * plan.members
    chunk_piece = shaped((plan.chunk_rows, size))
    chunk_pieces = [chunk_piece] * plan.members
    logged = shaped((plan.chunk_rows + LOG_ROWS, size))
    block_logs = shaped((plan.members, LOG_ROWS, size))
    group_logs = shaped((plan.groups, LOG_ROWS, size))
    table = shaped((length, width))
    rounded = shaped((length, width), BF16)
    hold = pltpu.VMEM((plan.members, plan.rows, size), F32)
    hold_groups = pltpu.VMEM((plan.groups, plan.rows, size), F32)
    hold_chunk = pltpu.VMEM((plan.members, plan.chunk_rows, size), F32)
    hold_chunk_groups = pltpu.VMEM((plan.groups, plan.chunk_rows, size), F32)
    chunks = range(plan.chunks)
    state_rows = state_in.reshape(width, size)

    messages = plan.first_messages()
    *sends, cum_log, cum_col = call(
        bind(summary_body),
        [chunk_piece if chunk else logged for _, chunk in messages]
        + [shaped((heads, length)), shaped((length, heads))],
        [pltpu.with_memory_space_constraint(x, pltpu.HBM) for x in (key_rows, value_rows, log_decay)],
        [
            pltpu.VMEM((width, size), F32),
            pltpu.VMEM((length, width), BF16),
            pltpu.VMEM((length, width), BF16),
            pltpu.VMEM((heads, length), F32),
            pltpu.SemaphoreType.DMA((3,)),
        ],
        specs=[HBM] * 3,
    )
    received = {key: plan.swap(send, key[0]) for key, send in zip(messages, sends)}
    parts = [[received[way, c] for way in plan.ways] for c in chunks]
    totals = []
    for c in chunks:
        if c == 0:
            total, logs = call(
                bind(group_total_body, c), [logged, block_logs], parts[c], [hold_chunk]
            )
        else:
            (total,) = call(
                bind(group_total_body, c),
                [chunk_piece],
                [*parts[c], logs],
                [hold_chunk],
                flops=LONG,
            )
        totals.append([total] + plan.from_groups(total))
    states = {}
    far_parts = []
    for c in chunks:
        last = c == plan.chunks - 1
        operands = [*parts[c], *totals[c], state_rows, logs]
        outs = [piece if way in plan.far and last else chunk_piece for way in plan.ways]
        if c == 0:
            outs += [shaped((LOG_ROWS, size)), group_logs]
        else:
            operands += [all_logs]
        sends = call(
            bind(forward_scan_body, c),
            outs,
            operands + (far_parts if last else []),
            [hold_chunk_groups, hold_chunk],
        )
        if c == 0:
            before, all_logs = sends[plan.members :]
        for way, send in zip(plan.ways, sends):
            if way not in plan.far:
                states[way, c] = plan.swap(send, way)
            elif last:
                states[way, None] = plan.swap(send, way)
            else:
                far_parts.append(send)
    early = [states[way, 0] for way in plan.near] if plan.chunks > 1 else []
    weights, intra, gained, query_decayed = call(
        bind(intra_body),
        [
            shaped((heads, length, length), BF16),
            table,
            table,
            shaped((heads, size, length), BF16),
        ],
        [query_rows, key_rows, value_rows, cum_log, cum_col, out_grad, gain, *early],
        specs=[VMEM] * 7 + [ANY] * len(early),
        flops=LONG // 10,
    )
    attended, sums, states = call(
        bind(attended_body),
        [table, shaped((8, length)), shaped((width, size), BF16)],
        [*[states[key] for key in plan.last_messages()], intra, query_rows, cum_col, gained],
    )
    all_sums = [sums] + [
        lax.ppermute(sums, "head", [(i, (i + step) % parties) for i in range(parties)])
        for step in range(1, parties)
    ]
    attn_grad, summary, *sends = call(
        bind(attn_grad_body, parties),
        [rounded, shaped((width, size))] + pieces,
        [*all_sums, attended, query_decayed, gained],
    )
    parts = plan.swap_in_group(sends)
    query_grad, key_part, value_part = call(
        bind(score_grad_body),
        [rounded, table, table],
        [attn_grad, query_rows, key_rows, value_rows, states, weights, cum_log, cum_col],
        flops=10 * heads * length * length * size,
    )
    grad_rows = state_out_grad.reshape(width, size)
    two_sided = plan.groups == 2
    total, *sends = call(
        bind(group_grad_body),
        [piece] + pieces * two_sided,
        [*parts, logs, grad_rows, key_part],
        [hold],
        specs=[VMEM] * (plan.members + 2) + [ANY],
    )
    totals = [total] + plan.from_groups(total)
    swapped = [plan.swap_in_group(sends, range(plan.members))] if two_sided else []
    sends = call(
        bind(reverse_scan_body),
        pieces * (1 if two_sided else 2),
        [*parts, *totals, logs, all_logs, grad_rows],
        [hold_groups, hold],
    )
    for first in range(0, len(sends), plan.members):
        swapped.append(plan.swap_in_group(sends[first : first + plan.members]))
    key_grad, value_grad, state_in_grad = call(
        bind(finish_body),
        [rounded, rounded, shaped((width, size))],
        [*swapped[0], *swapped[1], key_part, value_part, key_rows, value_rows, cum_col, summary, before],
        [
            pltpu.VMEM((2, width, size), F32),
            pltpu.VMEM((length, width), BF16),
            pltpu.VMEM((length, width), BF16),
            pltpu.VMEM((width, size), F32),
            pltpu.SemaphoreType.DMA((6,)),
        ],
        out_specs=[HBM] * 3,
    )
    return (query_grad, key_grad, value_grad, state_in_grad.reshape(heads, size, size))


def solution(mesh):
    return jax.shard_map(
        on_device,
        mesh=mesh,
        in_specs=(
            P("seq", "head"),
            P("seq", "head"),
            P("seq", "head"),
            P("head", "seq"),
            P("seq", "head"),
            P("head"),
            P("head", None, None),
            P("head", None, None),
        ),
        out_specs=(P("seq", "head"), P("seq", "head"), P("seq", "head"), P("head", None, None)),
        check_vma=False,
    )
```

```python
import functools

import jax
import jax.numpy as jnp
from jax import lax
from jax.experimental import pallas as pl
from jax.experimental.pallas import tpu as pltpu
from jax.sharding import PartitionSpec as P

EPSILON = 1e-06
F32 = jnp.float32
BF16 = jnp.bfloat16
LOG_ROWS = 8
LONG = 10**10
MASKED = -1e30

CONTRACT_ROWS = (((0,), (0,)), ((), ()))
CONTRACT_COLS = (((1,), (1,)), ((), ()))
VMEM = pl.BlockSpec(memory_space=pltpu.VMEM)
HBM = pl.BlockSpec(memory_space=pltpu.HBM)
ANY = pl.BlockSpec(memory_space=pl.ANY)


def call(body, outs, operands, scratch=(), flops=0, specs=None, out_specs=None):
    return pl.pallas_call(
        body,
        out_shape=outs,
        in_specs=specs or [VMEM] * len(operands),
        out_specs=out_specs or [VMEM] * len(outs),
        scratch_shapes=list(scratch),
        compiler_params=pltpu.CompilerParams(vmem_limit_bytes=24 * 1024 * 1024),
        cost_estimate=pl.CostEstimate(flops=flops, bytes_accessed=0, transcendentals=0),
    )(*operands)


def shaped(shape, dtype=F32):
    return jax.ShapeDtypeStruct(shape, dtype)


def dot(a, b, dims=(((1,), (0,)), ((), ()))):
    return lax.dot_general(a, b, dims, preferred_element_type=F32)


def split(x):
    high = x.astype(BF16)
    rest = x - high.astype(F32)
    middle = rest.astype(BF16)
    low = (rest - middle.astype(F32)).astype(BF16)
    return jnp.concatenate([high, middle, low], axis=1)


def thrice(x):
    return jnp.concatenate([x, x, x], axis=1)


def lanes(h, size):
    return slice(h * size, (h + 1) * size)


def causal_mask(length):
    row = lax.broadcasted_iota(jnp.int32, (length, length), 0)
    col = lax.broadcasted_iota(jnp.int32, (length, length), 1)
    return row >= col


class Plan:
    def __init__(self, heads, size, blocks):
        self.heads, self.size, self.blocks = heads, size, blocks
        self.members = next(m for m in (4, 2, 1) if heads % m == 0 and blocks % m == 0)
        self.groups = blocks // self.members
        self.own = heads // self.members
        self.rows = self.own * size
        self.chunks = self.own
        self.chunk_rows = self.rows // self.chunks
        self.near = [way for way in range(self.members) if way.bit_count() == 1]
        self.far = [way for way in range(self.members) if way.bit_count() > 1]
        self.ways = [0] + self.far + self.near
        self.early_ways = [0] + self.near[::-1] + self.far

    def member(self):
        return lax.rem(lax.axis_index("seq"), self.members)

    def group(self):
        return lax.div(lax.axis_index("seq"), self.members)

    def peer(self, k):
        return self.toward(self.ways[k])

    def toward(self, way):
        return lax.bitwise_xor(self.member(), way)

    def rows_of(self, member):
        return pl.ds(pl.multiple_of(member * self.rows, self.rows), self.rows)

    def chunk_of(self, member, chunk):
        start = member * self.rows + chunk * self.chunk_rows
        return pl.ds(pl.multiple_of(start, self.chunk_rows), self.chunk_rows)

    def swap(self, piece, way):
        span = self.members
        pairs = [(i, i // span * span + (i % span ^ way)) for i in range(self.blocks)]
        return lax.ppermute(piece, "seq", pairs) if way else piece

    def swap_in_group(self, pieces, order=None):
        return [self.swap(piece, way) for way, piece in zip(order or self.ways, pieces)]

    def first_messages(self):
        return [(way, c) for c in range(self.chunks) for way in self.ways]

    def last_messages(self):
        cuts = [(way, c) for c in range(self.chunks) for way in [0] + self.near]
        return cuts + [(way, None) for way in self.far]

    def from_groups(self, piece):
        return [
            lax.ppermute(
                piece,
                "seq",
                [(i, (i + step * self.members) % self.blocks) for i in range(self.blocks)],
            )
            for step in range(1, self.groups)
        ]


def own_decays(plan, log_tile_ref, chunk=None):
    count = plan.own if chunk is None else plan.own // plan.chunks
    first = plan.member() * plan.own + (0 if chunk is None else chunk * count)
    rows = [log_tile_ref[pl.ds(first + j, 1), :] for j in range(count)]
    return jnp.concatenate([jnp.broadcast_to(jnp.exp(row), (plan.size, plan.size)) for row in rows])


def summary_body(plan, key_hbm, value_hbm, decay_hbm, *refs):
    count = len(plan.first_messages())
    send_refs, refs = refs[:count], refs[count:]
    cum_ref, cum_col_ref, held_ref, key_ref, value_ref, decay_ref, sems = refs
    length, heads, size = key_ref.shape[0], plan.heads, plan.size
    copies = [
        pltpu.make_async_copy(source, target, sems.at[i])
        for i, (source, target) in enumerate(
            [(decay_hbm, decay_ref), (key_hbm, key_ref), (value_hbm, value_ref)]
        )
    ]
    for copy in copies:
        copy.start()
    causal = thrice(jnp.where(causal_mask(length), 1.0, 0.0).astype(BF16))
    copies[0].wait()
    decay = split(decay_ref[...])
    cum_col = dot(causal, decay, CONTRACT_COLS)
    cum_row = dot(decay, causal, CONTRACT_COLS)
    cum_ref[...] = cum_row
    cum_col_ref[...] = cum_col
    shrink = jnp.exp(cum_col[length - 1 : length, :] - cum_col)
    copies[1].wait()
    copies[2].wait()
    for h in range(heads):
        key_decayed = (key_ref[:, lanes(h, size)].astype(F32) * shrink[:, h : h + 1]).astype(BF16)
        held_ref[h * size : (h + 1) * size] = dot(
            key_decayed, value_ref[:, lanes(h, size)], CONTRACT_ROWS
        )
    log_tile = jnp.broadcast_to(cum_row[:, length - 1 : length], (heads, size))
    if heads < LOG_ROWS:
        log_tile = jnp.concatenate([log_tile, jnp.zeros((LOG_ROWS - heads, size), F32)])
    for (way, chunk), send_ref in zip(plan.first_messages(), send_refs):
        send_ref[: plan.chunk_rows] = held_ref[plan.chunk_of(plan.toward(way), chunk)]
        if chunk == 0:
            send_ref[plan.chunk_rows :] = log_tile


def group_total_body(plan, chunk, *refs):
    part_refs, refs = refs[: plan.members], refs[plan.members :]
    rows = plan.chunk_rows
    if chunk == 0:
        total_ref, logs_ref = refs[:2]
        for k, part_ref in enumerate(part_refs):
            logs_ref[plan.peer(k)] = part_ref[rows:]
        total_ref[rows:] = sum(logs_ref[b] for b in range(plan.members))
    else:
        logs_ref, total_ref = refs[:2]
    held_ref = refs[2]
    for way, part_ref in zip(plan.ways, part_refs):
        held_ref[plan.toward(way)] = part_ref[:rows]
    total = jnp.zeros((rows, plan.size), F32)
    for b in range(plan.members):
        total = own_decays(plan, logs_ref.at[b], chunk) * total + held_ref[b]
    total_ref[:rows] = total


def stage_groups(plan, total_refs, held_ref):
    rows = held_ref.shape[1]
    for step, total_ref in enumerate(total_refs):
        held_ref[lax.rem(plan.group() - step + plan.groups, plan.groups)] = total_ref[:rows]


def forward_scan_body(plan, chunk, *refs):
    last = chunk == plan.chunks - 1
    part_refs, refs = refs[: plan.members], refs[plan.members :]
    total_refs, refs = refs[: plan.groups], refs[plan.groups :]
    (state_ref, logs_ref), refs = refs[:2], refs[2:]
    rows = plan.chunk_rows
    if chunk > 0:
        group_logs_ref, refs = refs[0], refs[1:]
    far_parts = chunk * len(plan.far) if last else 0
    far_refs, refs = refs[:far_parts], refs[far_parts:]
    send_refs, refs = refs[: plan.members], refs[plan.members :]
    if chunk == 0:
        before_ref, group_logs_ref = refs[:2]
        for step, total_ref in enumerate(total_refs):
            group = lax.rem(plan.group() - step + plan.groups, plan.groups)
            group_logs_ref[group] = total_ref[rows:]
        before = jnp.zeros((LOG_ROWS, plan.size), F32)
        for group in range(plan.groups - 1):
            before += jnp.where(group < plan.group(), group_logs_ref[group], 0.0)
        for b in range(plan.members - 1):
            before += jnp.where(b < plan.member(), logs_ref[b], 0.0)
        before_ref[...] = before
    groups_ref, held_ref = refs[-2:]
    stage_groups(plan, total_refs, groups_ref)
    state = state_ref[plan.chunk_of(plan.member(), chunk)]
    for group in range(plan.groups - 1):
        after = own_decays(plan, group_logs_ref.at[group], chunk) * state + groups_ref[group]
        state = jnp.where(group < plan.group(), after, state)
    for way, part_ref in zip(plan.ways, part_refs):
        held_ref[plan.toward(way)] = part_ref[:rows]
    for b in range(plan.members):
        summary = held_ref[b]
        held_ref[b] = state
        state = own_decays(plan, logs_ref.at[b], chunk) * state + summary
    for i, (way, send_ref) in enumerate(zip(plan.ways, send_refs)):
        if way in plan.far and last:
            for c in range(chunk):
                send_ref[c * rows : (c + 1) * rows] = far_refs[c * len(plan.far) + i - 1][...]
            send_ref[chunk * rows :] = held_ref[plan.toward(way)]
        else:
            send_ref[...] = held_ref[plan.toward(way)]


def suffixes(plan, held_ref, logs_ref, grad):
    found = []
    for b in reversed(range(plan.members)):
        found.append(grad)
        grad = own_decays(plan, logs_ref.at[b]) * grad + held_ref[b]
    return found[::-1], grad


def prefixes(plan, held_ref, logs_ref, total, scale):
    found = []
    for b in range(plan.members):
        found.append(total)
        total = total + scale * held_ref[b]
        scale = scale * own_decays(plan, logs_ref.at[b])
    return found


def early_body(plan, *refs):
    part_refs, refs = refs[: plan.members], refs[plan.members :]
    (logs_ref, grad_ref), send_refs, held_ref = refs[:2], refs[3:-1], refs[-1]
    for k, part_ref in enumerate(part_refs):
        held_ref[plan.peer(k)] = part_ref[...]
    first = plan.group() == 0
    zero = jnp.zeros((plan.rows, plan.size), F32)
    before = prefixes(plan, held_ref, logs_ref, zero, zero + 1.0)
    after = suffixes(plan, held_ref, logs_ref, grad_ref[plan.rows_of(plan.member())])[0]
    for b in range(plan.members):
        held_ref[b] = jnp.where(first, before[b], after[b])
    for way, send_ref in zip(plan.early_ways, send_refs):
        send_ref[: plan.rows] = held_ref[plan.toward(way)]
        if send_ref.shape[0] > plan.rows:
            send_ref[plan.rows :] = logs_ref[0]


def group_grad_body(plan, *refs):
    part_refs, (logs_ref, _, total_ref, held_ref) = refs[: plan.members], refs[plan.members :]
    for k, part_ref in enumerate(part_refs):
        held_ref[plan.peer(k)] = part_ref[...]
    zero = jnp.zeros((plan.rows, plan.size), F32)
    total_ref[...] = suffixes(plan, held_ref, logs_ref, zero)[1]


def reverse_scan_body(plan, *refs):
    part_refs, refs = refs[: plan.members], refs[plan.members :]
    total_refs, refs = refs[: plan.groups], refs[plan.groups :]
    (logs_ref, group_logs_ref, grad_ref, _), refs = refs[:4], refs[4:]
    send_refs, (groups_ref, held_ref) = refs[:-2], refs[-2:]
    stage_groups(plan, total_refs, groups_ref)
    for k, part_ref in enumerate(part_refs):
        held_ref[plan.peer(k)] = part_ref[...]
    grad = grad_ref[plan.rows_of(plan.member())]
    leaving = grad
    for group in reversed(range(plan.groups)):
        leaving = jnp.where(group == plan.group(), grad, leaving)
        grad = own_decays(plan, group_logs_ref.at[group]) * grad + groups_ref[group]
    total = jnp.zeros((plan.rows, plan.size), F32)
    scale = total + 1.0
    for group in range(plan.groups - 1):
        earlier = group < plan.group()
        total = jnp.where(earlier, total + scale * groups_ref[group], total)
        decays = own_decays(plan, group_logs_ref.at[group])
        scale = jnp.where(earlier, scale * decays, scale)
    after = suffixes(plan, held_ref, logs_ref, leaving)[0]
    before = prefixes(plan, held_ref, logs_ref, total, scale)
    if plan.groups == 2:
        first = plan.group() == 0
        found = [[jnp.where(first, after[b], before[b]) for b in range(plan.members)]]
    else:
        found = [before, after]
    for i, values in enumerate(found):
        for b in range(plan.members):
            held_ref[b] = values[b]
        for k in range(plan.members):
            send_refs[i * plan.members + k][...] = held_ref[plan.peer(k)]


def decay_matrix(cum_ref, cum_col, causal, h):
    spread = cum_col[:, h : h + 1] - cum_ref[h : h + 1, :]
    return jnp.exp(jnp.where(causal, jnp.minimum(spread, 0.0), MASKED))


def intra_body(
    plan,
    query_ref,
    key_ref,
    value_ref,
    cum_ref,
    cum_col_ref,
    upstream_ref,
    gain_ref,
    *refs,
):
    weight_ref, intra_ref, gained_ref, query_decayed_ref = refs[-4:]
    causal = causal_mask(query_ref.shape[0])
    cum_col = cum_col_ref[...]
    growth = jnp.exp(cum_col)
    for h in range(plan.heads):
        cut = lanes(h, plan.size)
        query = query_ref[:, cut]
        scores = dot(query, key_ref[:, cut], CONTRACT_COLS)
        weights = (scores * decay_matrix(cum_ref, cum_col, causal, h)).astype(BF16)
        weight_ref[h] = weights
        intra_ref[:, cut] = dot(weights, value_ref[:, cut])
        gained_ref[:, cut] = gain_ref[:, cut] * upstream_ref[:, cut].astype(F32)
        query_decayed = query.astype(F32) * growth[:, h : h + 1]
        query_decayed_ref[h] = jnp.transpose(query_decayed).astype(BF16)


def attended_body(plan, *refs):
    count = len(plan.last_messages())
    state_refs, refs = refs[:count], refs[count:]
    intra_ref, query_ref, cum_col_ref, gained_ref = refs[:4]
    attended_ref, sums_ref, states_ref = refs[4:]
    size, length = plan.size, query_ref.shape[0]
    for (way, chunk), state_ref in zip(plan.last_messages(), state_refs):
        member = plan.toward(way)
        part = plan.rows_of(member) if chunk is None else plan.chunk_of(member, chunk)
        states_ref[part] = state_ref[...].astype(BF16)
    growth = jnp.exp(cum_col_ref[...])
    square = jnp.zeros((length, size), F32)
    inner = jnp.zeros((length, size), F32)
    for h in range(plan.heads):
        cut = lanes(h, size)
        carried = dot(query_ref[:, cut], states_ref[cut])
        attended = intra_ref[:, cut] + growth[:, h : h + 1] * carried
        attended_ref[:, cut] = attended
        square += attended * attended
        inner += gained_ref[:, cut] * attended
    ones = jnp.ones((8, 3 * size), BF16)
    is_square = lax.broadcasted_iota(jnp.int32, (8, length), 0) == 0
    sums_ref[...] = jnp.where(
        is_square,
        dot(ones, split(square), CONTRACT_COLS),
        dot(ones, split(inner), CONTRACT_COLS),
    )


def attn_grad_body(plan, parties, *refs):
    sums_refs, refs = refs[:parties], refs[parties:]
    attended_ref, query_decayed_ref, gained_ref, attn_grad_ref, held_ref = refs[:5]
    send_refs = refs[5:]
    size, length = plan.size, attended_ref.shape[0]
    feature_count = plan.heads * size * parties
    sums = sum(ref[...] for ref in sums_refs)
    inv_row = lax.rsqrt(sums[:1] / feature_count + EPSILON)
    coefficient_row = sums[1:2] * inv_row * inv_row * inv_row / feature_count
    is_inverse = lax.broadcasted_iota(jnp.int32, (8, length), 0) == 0
    columns = jnp.transpose(jnp.where(is_inverse, inv_row, coefficient_row))
    inv_rms = jnp.broadcast_to(columns[:, :1], (length, size))
    coefficient = jnp.broadcast_to(columns[:, 1:2], (length, size))
    for h in range(plan.heads):
        cut = lanes(h, size)
        attn_grad = gained_ref[:, cut] * inv_rms - attended_ref[:, cut] * coefficient
        attn_grad = attn_grad.astype(BF16)
        attn_grad_ref[:, cut] = attn_grad
        held_ref[cut] = dot(query_decayed_ref[h], attn_grad)
    for k, send_ref in enumerate(send_refs):
        send_ref[...] = held_ref[plan.rows_of(plan.peer(k))]


def score_grad_body(
    plan,
    attn_grad_ref,
    query_ref,
    key_ref,
    value_ref,
    states_ref,
    weight_ref,
    cum_ref,
    cum_col_ref,
    query_grad_ref,
    key_part_ref,
    value_part_ref,
):
    causal = causal_mask(query_ref.shape[0])
    cum_col = cum_col_ref[...]
    growth = jnp.exp(cum_col)
    for h in range(plan.heads):
        cut = lanes(h, plan.size)
        attn_grad = attn_grad_ref[:, cut]
        scores = dot(attn_grad, value_ref[:, cut], CONTRACT_COLS)
        score_grad = (scores * decay_matrix(cum_ref, cum_col, causal, h)).astype(BF16)
        carried = dot(attn_grad, states_ref[cut], CONTRACT_COLS)
        query_grad = dot(score_grad, key_ref[:, cut]) + growth[:, h : h + 1] * carried
        query_grad_ref[:, cut] = query_grad.astype(BF16)
        key_part_ref[:, cut] = dot(score_grad, query_ref[:, cut], CONTRACT_ROWS)
        value_part_ref[:, cut] = dot(weight_ref[h], attn_grad, CONTRACT_ROWS)


def finish_body(plan, *refs):
    first_refs, refs = refs[: plan.members], refs[plan.members :]
    second_refs, refs = refs[: plan.members], refs[plan.members :]
    key_part_ref, value_part_ref, key_ref, value_ref, cum_col_ref, summary_ref, before_ref = refs[:7]
    key_out, value_out, total_out, held_ref, key_grad_ref, value_grad_ref, total_ref, sems = refs[7:]
    length, size = key_ref.shape[0], plan.size
    swapped = jnp.where(plan.group() == 0, 0, 1) if plan.groups == 2 else 0
    for k, way in enumerate(plan.early_ways if plan.groups == 2 else plan.ways):
        held_ref[swapped, plan.rows_of(plan.toward(way))] = first_refs[k][: plan.rows]
        held_ref[1 - swapped, plan.rows_of(plan.peer(k))] = second_refs[k][...]
    cum_col = cum_col_ref[...]
    block_log = cum_col[length - 1 : length, :]
    shrink = jnp.exp(block_log - cum_col)
    copies = []
    batch = max(plan.heads // 4, 1)
    for h in range(plan.heads):
        cut = lanes(h, size)
        grads = held_ref[1, cut]
        scale = jnp.exp(before_ref[h : h + 1])
        scale_next = jnp.exp(before_ref[h : h + 1] + block_log[:, h : h + 1])
        total_ref[cut] = held_ref[0, cut] + scale * summary_ref[cut] + scale_next * grads
        grads = grads.astype(BF16)
        column = shrink[:, h : h + 1]
        key_state = dot(value_ref[:, cut], grads, CONTRACT_COLS)
        key_grad_ref[:, cut] = (key_part_ref[:, cut] + column * key_state).astype(BF16)
        value_state = dot(key_ref[:, cut], grads)
        value_grad_ref[:, cut] = (value_part_ref[:, cut] + column * value_state).astype(BF16)
        if (h + 1) % batch == 0:
            done = slice((h + 1 - batch) * size, (h + 1) * size)
            for source, target, index in [
                (total_ref, total_out, (done,)),
                (key_grad_ref, key_out, (slice(None), done)),
                (value_grad_ref, value_out, (slice(None), done)),
            ]:
                copies.append(
                    pltpu.make_async_copy(source.at[index], target.at[index], sems.at[len(copies)])
                )
                copies[-1].start()
    for copy in copies:
        copy.wait()


def on_device(
    query_rows, key_rows, value_rows, log_decay, out_grad, norm_gain, state_in, state_out_grad
):
    heads, length = log_decay.shape
    size = state_in.shape[1]
    width = heads * size
    parties = lax.axis_size("head")
    plan = Plan(heads, size, lax.axis_size("seq"))
    bind = lambda body, *extra: functools.partial(body, plan, *extra)
    gain = norm_gain.reshape(1, width)
    piece = shaped((plan.rows, size))
    pieces = [piece] * plan.members
    chunk_piece = shaped((plan.chunk_rows, size))
    chunk_pieces = [chunk_piece] * plan.members
    logged = shaped((plan.chunk_rows + LOG_ROWS, size))
    block_logs = shaped((plan.members, LOG_ROWS, size))
    group_logs = shaped((plan.groups, LOG_ROWS, size))
    table = shaped((length, width))
    rounded = shaped((length, width), BF16)
    hold = pltpu.VMEM((plan.members, plan.rows, size), F32)
    hold_groups = pltpu.VMEM((plan.groups, plan.rows, size), F32)
    hold_chunk = pltpu.VMEM((plan.members, plan.chunk_rows, size), F32)
    hold_chunk_groups = pltpu.VMEM((plan.groups, plan.chunk_rows, size), F32)
    chunks = range(plan.chunks)
    state_rows = state_in.reshape(width, size)

    messages = plan.first_messages()
    *sends, cum_log, cum_col = call(
        bind(summary_body),
        [chunk_piece if chunk else logged for _, chunk in messages]
        + [shaped((heads, length)), shaped((length, heads))],
        [pltpu.with_memory_space_constraint(x, pltpu.HBM) for x in (key_rows, value_rows, log_decay)],
        [
            pltpu.VMEM((width, size), F32),
            pltpu.VMEM((length, width), BF16),
            pltpu.VMEM((length, width), BF16),
            pltpu.VMEM((heads, length), F32),
            pltpu.SemaphoreType.DMA((3,)),
        ],
        specs=[HBM] * 3,
    )
    received = {key: plan.swap(send, key[0]) for key, send in zip(messages, sends)}
    parts = [[received[way, c] for way in plan.ways] for c in chunks]
    totals = []
    for c in chunks:
        if c == 0:
            total, logs = call(
                bind(group_total_body, c), [logged, block_logs], parts[c], [hold_chunk]
            )
        else:
            (total,) = call(
                bind(group_total_body, c),
                [chunk_piece],
                [*parts[c], logs],
                [hold_chunk],
                flops=LONG,
            )
        totals.append([total] + plan.from_groups(total))
    states = {}
    far_parts = []
    for c in chunks:
        last = c == plan.chunks - 1
        operands = [*parts[c], *totals[c], state_rows, logs]
        outs = [piece if way in plan.far and last else chunk_piece for way in plan.ways]
        if c == 0:
            outs += [shaped((LOG_ROWS, size)), group_logs]
        else:
            operands += [all_logs]
        sends = call(
            bind(forward_scan_body, c),
            outs,
            operands + (far_parts if last else []),
            [hold_chunk_groups, hold_chunk],
        )
        if c == 0:
            before, all_logs = sends[plan.members :]
        for way, send in zip(plan.ways, sends):
            if way not in plan.far:
                states[way, c] = plan.swap(send, way)
            elif last:
                states[way, None] = plan.swap(send, way)
            else:
                far_parts.append(send)
    early = [states[way, 0] for way in plan.near] if plan.chunks > 1 else []
    weights, intra, gained, query_decayed = call(
        bind(intra_body),
        [
            shaped((heads, length, length), BF16),
            table,
            table,
            shaped((heads, size, length), BF16),
        ],
        [query_rows, key_rows, value_rows, cum_log, cum_col, out_grad, gain, *early],
        specs=[VMEM] * 7 + [ANY] * len(early),
        flops=LONG // 10,
    )
    attended, sums, states = call(
        bind(attended_body),
        [table, shaped((8, length)), shaped((width, size), BF16)],
        [*[states[key] for key in plan.last_messages()], intra, query_rows, cum_col, gained],
    )
    all_sums = [sums] + [
        lax.ppermute(sums, "head", [(i, (i + step) % parties) for i in range(parties)])
        for step in range(1, parties)
    ]
    attn_grad, summary, *sends = call(
        bind(attn_grad_body, parties),
        [rounded, shaped((width, size))] + pieces,
        [*all_sums, attended, query_decayed, gained],
    )
    parts = plan.swap_in_group(sends)
    query_grad, key_part, value_part = call(
        bind(score_grad_body),
        [rounded, table, table],
        [attn_grad, query_rows, key_rows, value_rows, states, weights, cum_log, cum_col],
        flops=10 * heads * length * length * size,
    )
    grad_rows = state_out_grad.reshape(width, size)
    two_sided = plan.groups == 2
    tie, swapped = key_part, []
    if two_sided:
        sends = call(
            bind(early_body),
            [piece, shaped((plan.rows + LOG_ROWS, size))] + pieces[2:],
            [*parts, logs, grad_rows, key_part],
            [hold],
            specs=[VMEM] * (plan.members + 2) + [ANY],
        )
        tie = sends[0]
        swapped = [plan.swap_in_group(sends, plan.early_ways)]
    (total,) = call(
        bind(group_grad_body),
        [piece],
        [*parts, logs, tie],
        [hold],
        specs=[VMEM] * (plan.members + 1) + [ANY],
    )
    totals = [total] + plan.from_groups(total)
    sends = call(
        bind(reverse_scan_body),
        pieces * (1 if two_sided else 2),
        [*parts, *totals, logs, all_logs, grad_rows, swapped[0][1] if two_sided else tie],
        [hold_groups, hold],
        specs=[VMEM] * (plan.members + plan.groups + 3) + [ANY],
    )
    for first in range(0, len(sends), plan.members):
        swapped.append(plan.swap_in_group(sends[first : first + plan.members]))
    key_grad, value_grad, state_in_grad = call(
        bind(finish_body),
        [rounded, rounded, shaped((width, size))],
        [*swapped[0], *swapped[1], key_part, value_part, key_rows, value_rows, cum_col, summary, before],
        [
            pltpu.VMEM((2, width, size), F32),
            pltpu.VMEM((length, width), BF16),
            pltpu.VMEM((length, width), BF16),
            pltpu.VMEM((width, size), F32),
            pltpu.SemaphoreType.DMA((12,)),
        ],
        out_specs=[HBM] * 3,
    )
    return (query_grad, key_grad, value_grad, state_in_grad.reshape(heads, size, size))


def solution(mesh):
    return jax.shard_map(
        on_device,
        mesh=mesh,
        in_specs=(
            P("seq", "head"),
            P("seq", "head"),
            P("seq", "head"),
            P("head", "seq"),
            P("seq", "head"),
            P("head"),
            P("head", None, None),
            P("head", None, None),
        ),
        out_specs=(P("seq", "head"), P("seq", "head"), P("seq", "head"), P("head", None, None)),
        check_vma=False,
    )
```

```python
import functools

import jax
import jax.numpy as jnp
from jax import lax
from jax.experimental import pallas as pl
from jax.experimental.pallas import tpu as pltpu
from jax.sharding import PartitionSpec as P

EPSILON = 1e-06
F32 = jnp.float32
BF16 = jnp.bfloat16
LOG_ROWS = 8
LONG = 10**10
MASKED = -1e30

CONTRACT_ROWS = (((0,), (0,)), ((), ()))
CONTRACT_COLS = (((1,), (1,)), ((), ()))
VMEM = pl.BlockSpec(memory_space=pltpu.VMEM)
HBM = pl.BlockSpec(memory_space=pltpu.HBM)
ANY = pl.BlockSpec(memory_space=pl.ANY)


def call(body, outs, operands, scratch=(), flops=0, specs=None, out_specs=None, aliases=None):
    return pl.pallas_call(
        body,
        out_shape=outs,
        in_specs=specs or [VMEM] * len(operands),
        out_specs=out_specs or [VMEM] * len(outs),
        scratch_shapes=list(scratch),
        input_output_aliases=aliases or {},
        compiler_params=pltpu.CompilerParams(vmem_limit_bytes=24 * 1024 * 1024),
        cost_estimate=pl.CostEstimate(flops=flops, bytes_accessed=0, transcendentals=0),
    )(*operands)


def shaped(shape, dtype=F32):
    return jax.ShapeDtypeStruct(shape, dtype)


def dot(a, b, dims=(((1,), (0,)), ((), ()))):
    return lax.dot_general(a, b, dims, preferred_element_type=F32)


def split(x):
    high = x.astype(BF16)
    rest = x - high.astype(F32)
    middle = rest.astype(BF16)
    low = (rest - middle.astype(F32)).astype(BF16)
    return jnp.concatenate([high, middle, low], axis=1)


def thrice(x):
    return jnp.concatenate([x, x, x], axis=1)


def lanes(h, size):
    return slice(h * size, (h + 1) * size)


def causal_mask(length):
    row = lax.broadcasted_iota(jnp.int32, (length, length), 0)
    col = lax.broadcasted_iota(jnp.int32, (length, length), 1)
    return row >= col


class Plan:
    def __init__(self, heads, size, blocks):
        self.heads, self.size, self.blocks = heads, size, blocks
        self.members = next(m for m in (4, 2, 1) if heads % m == 0 and blocks % m == 0)
        self.groups = blocks // self.members
        self.own = heads // self.members
        self.rows = self.own * size
        self.chunks = self.own
        self.chunk_rows = self.rows // self.chunks
        self.near = [way for way in range(self.members) if way.bit_count() == 1]
        self.far = [way for way in range(self.members) if way.bit_count() > 1]
        self.ways = [0] + self.far + self.near
        self.early_ways = [0] + self.near[::-1] + self.far

    def member(self):
        return lax.rem(lax.axis_index("seq"), self.members)

    def group(self):
        return lax.div(lax.axis_index("seq"), self.members)

    def peer(self, k):
        return self.toward(self.ways[k])

    def toward(self, way):
        return lax.bitwise_xor(self.member(), way)

    def rows_of(self, member):
        return pl.ds(pl.multiple_of(member * self.rows, self.rows), self.rows)

    def chunk_of(self, member, chunk):
        start = member * self.rows + chunk * self.chunk_rows
        return pl.ds(pl.multiple_of(start, self.chunk_rows), self.chunk_rows)

    def swap(self, piece, way):
        span = self.members
        pairs = [(i, i // span * span + (i % span ^ way)) for i in range(self.blocks)]
        return lax.ppermute(piece, "seq", pairs) if way else piece

    def swap_in_group(self, pieces, order=None):
        return [self.swap(piece, way) for way, piece in zip(order or self.ways, pieces)]

    def first_messages(self):
        return [(way, c) for c in range(self.chunks) for way in self.ways]

    def last_messages(self):
        cuts = [(way, c) for c in range(self.chunks) for way in [0] + self.near]
        return cuts + [(way, None) for way in self.far]

    def from_groups(self, piece):
        return [
            lax.ppermute(
                piece,
                "seq",
                [(i, (i + step * self.members) % self.blocks) for i in range(self.blocks)],
            )
            for step in range(1, self.groups)
        ]


def own_decays(plan, log_tile_ref, chunk=None):
    count = plan.own if chunk is None else plan.own // plan.chunks
    first = plan.member() * plan.own + (0 if chunk is None else chunk * count)
    rows = [log_tile_ref[pl.ds(first + j, 1), :] for j in range(count)]
    return jnp.concatenate([jnp.broadcast_to(jnp.exp(row), (plan.size, plan.size)) for row in rows])


def summary_body(plan, key_hbm, value_hbm, decay_hbm, *refs):
    count = len(plan.first_messages())
    send_refs, refs = refs[:count], refs[count:]
    cum_ref, cum_col_ref, held_ref, key_ref, value_ref, decay_ref, sems = refs
    length, heads, size = key_ref.shape[0], plan.heads, plan.size
    copies = [
        pltpu.make_async_copy(source, target, sems.at[i])
        for i, (source, target) in enumerate(
            [(decay_hbm, decay_ref), (key_hbm, key_ref), (value_hbm, value_ref)]
        )
    ]
    for copy in copies:
        copy.start()
    causal = thrice(jnp.where(causal_mask(length), 1.0, 0.0).astype(BF16))
    copies[0].wait()
    decay = split(decay_ref[...])
    cum_col = dot(causal, decay, CONTRACT_COLS)
    cum_row = dot(decay, causal, CONTRACT_COLS)
    cum_ref[...] = cum_row
    cum_col_ref[...] = cum_col
    shrink = jnp.exp(cum_col[length - 1 : length, :] - cum_col)
    copies[1].wait()
    copies[2].wait()
    for h in range(heads):
        key_decayed = (key_ref[:, lanes(h, size)].astype(F32) * shrink[:, h : h + 1]).astype(BF16)
        held_ref[h * size : (h + 1) * size] = dot(
            key_decayed, value_ref[:, lanes(h, size)], CONTRACT_ROWS
        )
    log_tile = jnp.broadcast_to(cum_row[:, length - 1 : length], (heads, size))
    if heads < LOG_ROWS:
        log_tile = jnp.concatenate([log_tile, jnp.zeros((LOG_ROWS - heads, size), F32)])
    for (way, chunk), send_ref in zip(plan.first_messages(), send_refs):
        send_ref[: plan.chunk_rows] = held_ref[plan.chunk_of(plan.toward(way), chunk)]
        if chunk == 0:
            send_ref[plan.chunk_rows :] = log_tile


def group_total_body(plan, chunk, *refs):
    part_refs, refs = refs[: plan.members], refs[plan.members :]
    rows = plan.chunk_rows
    if chunk == 0:
        total_ref, logs_ref = refs[:2]
        for k, part_ref in enumerate(part_refs):
            logs_ref[plan.peer(k)] = part_ref[rows:]
        total_ref[rows:] = sum(logs_ref[b] for b in range(plan.members))
    else:
        logs_ref, total_ref = refs[:2]
    held_ref = refs[2]
    for way, part_ref in zip(plan.ways, part_refs):
        held_ref[plan.toward(way)] = part_ref[:rows]
    total = jnp.zeros((rows, plan.size), F32)
    for b in range(plan.members):
        total = own_decays(plan, logs_ref.at[b], chunk) * total + held_ref[b]
    total_ref[:rows] = total


def stage_groups(plan, total_refs, held_ref):
    rows = held_ref.shape[1]
    for step, total_ref in enumerate(total_refs):
        held_ref[lax.rem(plan.group() - step + plan.groups, plan.groups)] = total_ref[:rows]


def forward_scan_body(plan, chunk, *refs):
    last = chunk == plan.chunks - 1
    part_refs, refs = refs[: plan.members], refs[plan.members :]
    total_refs, refs = refs[: plan.groups], refs[plan.groups :]
    (state_ref, logs_ref), refs = refs[:2], refs[2:]
    rows = plan.chunk_rows
    if chunk > 0:
        group_logs_ref, refs = refs[0], refs[1:]
    far_parts = chunk * len(plan.far) if last else 0
    far_refs, refs = refs[:far_parts], refs[far_parts:]
    send_refs, refs = refs[: plan.members], refs[plan.members :]
    if chunk == 0:
        before_ref, group_logs_ref = refs[:2]
        for step, total_ref in enumerate(total_refs):
            group = lax.rem(plan.group() - step + plan.groups, plan.groups)
            group_logs_ref[group] = total_ref[rows:]
        before = jnp.zeros((LOG_ROWS, plan.size), F32)
        for group in range(plan.groups - 1):
            before += jnp.where(group < plan.group(), group_logs_ref[group], 0.0)
        for b in range(plan.members - 1):
            before += jnp.where(b < plan.member(), logs_ref[b], 0.0)
        before_ref[...] = before
    groups_ref, held_ref = refs[-2:]
    stage_groups(plan, total_refs, groups_ref)
    state = state_ref[plan.chunk_of(plan.member(), chunk)]
    for group in range(plan.groups - 1):
        after = own_decays(plan, group_logs_ref.at[group], chunk) * state + groups_ref[group]
        state = jnp.where(group < plan.group(), after, state)
    for way, part_ref in zip(plan.ways, part_refs):
        held_ref[plan.toward(way)] = part_ref[:rows]
    for b in range(plan.members):
        summary = held_ref[b]
        held_ref[b] = state
        state = own_decays(plan, logs_ref.at[b], chunk) * state + summary
    for i, (way, send_ref) in enumerate(zip(plan.ways, send_refs)):
        if way in plan.far and last:
            for c in range(chunk):
                send_ref[c * rows : (c + 1) * rows] = far_refs[c * len(plan.far) + i - 1][...]
            send_ref[chunk * rows :] = held_ref[plan.toward(way)]
        else:
            send_ref[...] = held_ref[plan.toward(way)]


def suffixes(plan, held_ref, logs_ref, grad):
    found = []
    for b in reversed(range(plan.members)):
        found.append(grad)
        grad = own_decays(plan, logs_ref.at[b]) * grad + held_ref[b]
    return found[::-1], grad


def prefixes(plan, held_ref, logs_ref, total, scale):
    found = []
    for b in range(plan.members):
        found.append(total)
        total = total + scale * held_ref[b]
        scale = scale * own_decays(plan, logs_ref.at[b])
    return found


def early_body(plan, *refs):
    part_refs, refs = refs[: plan.members], refs[plan.members :]
    (logs_ref, grad_ref), send_refs, held_ref = refs[:2], refs[3:-1], refs[-1]
    for k, part_ref in enumerate(part_refs):
        held_ref[plan.peer(k)] = part_ref[...]
    first = plan.group() == 0
    zero = jnp.zeros((plan.rows, plan.size), F32)
    before = prefixes(plan, held_ref, logs_ref, zero, zero + 1.0)
    after = suffixes(plan, held_ref, logs_ref, grad_ref[plan.rows_of(plan.member())])[0]
    for b in range(plan.members):
        held_ref[b] = jnp.where(first, before[b], after[b])
    for way, send_ref in zip(plan.early_ways, send_refs):
        send_ref[: plan.rows] = held_ref[plan.toward(way)]
        if send_ref.shape[0] > plan.rows:
            send_ref[plan.rows :] = logs_ref[0]


def group_grad_body(plan, *refs):
    part_refs, (logs_ref, _, total_ref, held_ref) = refs[: plan.members], refs[plan.members :]
    for k, part_ref in enumerate(part_refs):
        held_ref[plan.peer(k)] = part_ref[...]
    zero = jnp.zeros((plan.rows, plan.size), F32)
    total_ref[...] = suffixes(plan, held_ref, logs_ref, zero)[1]


def reverse_scan_body(plan, *refs):
    part_refs, refs = refs[: plan.members], refs[plan.members :]
    total_refs, refs = refs[: plan.groups], refs[plan.groups :]
    (logs_ref, group_logs_ref, grad_ref, _), refs = refs[:4], refs[4:]
    send_refs, (groups_ref, held_ref) = refs[:-2], refs[-2:]
    stage_groups(plan, total_refs, groups_ref)
    for k, part_ref in enumerate(part_refs):
        held_ref[plan.peer(k)] = part_ref[...]
    grad = grad_ref[plan.rows_of(plan.member())]
    leaving = grad
    for group in reversed(range(plan.groups)):
        leaving = jnp.where(group == plan.group(), grad, leaving)
        grad = own_decays(plan, group_logs_ref.at[group]) * grad + groups_ref[group]
    total = jnp.zeros((plan.rows, plan.size), F32)
    scale = total + 1.0
    for group in range(plan.groups - 1):
        earlier = group < plan.group()
        total = jnp.where(earlier, total + scale * groups_ref[group], total)
        decays = own_decays(plan, group_logs_ref.at[group])
        scale = jnp.where(earlier, scale * decays, scale)
    after = suffixes(plan, held_ref, logs_ref, leaving)[0]
    before = prefixes(plan, held_ref, logs_ref, total, scale)
    if plan.groups == 2:
        first = plan.group() == 0
        found = [[jnp.where(first, after[b], before[b]) for b in range(plan.members)]]
    else:
        found = [before, after]
    for i, values in enumerate(found):
        for b in range(plan.members):
            held_ref[b] = values[b]
        for k in range(plan.members):
            send_refs[i * plan.members + k][...] = held_ref[plan.peer(k)]


def decay_matrix(cum_ref, cum_col, causal, h):
    spread = cum_col[:, h : h + 1] - cum_ref[h : h + 1, :]
    return jnp.exp(jnp.where(causal, jnp.minimum(spread, 0.0), MASKED))


def intra_body(
    plan,
    query_ref,
    key_ref,
    value_ref,
    cum_ref,
    cum_col_ref,
    upstream_ref,
    gain_ref,
    *refs,
):
    weight_ref, intra_ref, gained_ref, query_decayed_ref = refs[-4:]
    causal = causal_mask(query_ref.shape[0])
    cum_col = cum_col_ref[...]
    growth = jnp.exp(cum_col)
    for h in range(plan.heads):
        cut = lanes(h, plan.size)
        query = query_ref[:, cut]
        scores = dot(query, key_ref[:, cut], CONTRACT_COLS)
        weights = (scores * decay_matrix(cum_ref, cum_col, causal, h)).astype(BF16)
        weight_ref[h] = weights
        intra_ref[:, cut] = dot(weights, value_ref[:, cut])
        gained_ref[:, cut] = gain_ref[:, cut] * upstream_ref[:, cut].astype(F32)
        query_decayed = query.astype(F32) * growth[:, h : h + 1]
        query_decayed_ref[h] = jnp.transpose(query_decayed).astype(BF16)


def attended_body(plan, *refs):
    count = len(plan.last_messages())
    state_refs, refs = refs[:count], refs[count:]
    intra_ref, query_ref, cum_col_ref, gained_ref = refs[:4]
    attended_ref, sums_ref, states_ref = refs[4:]
    size, length = plan.size, query_ref.shape[0]
    for (way, chunk), state_ref in zip(plan.last_messages(), state_refs):
        member = plan.toward(way)
        part = plan.rows_of(member) if chunk is None else plan.chunk_of(member, chunk)
        states_ref[part] = state_ref[...].astype(BF16)
    growth = jnp.exp(cum_col_ref[...])
    square = jnp.zeros((length, size), F32)
    inner = jnp.zeros((length, size), F32)
    for h in range(plan.heads):
        cut = lanes(h, size)
        carried = dot(query_ref[:, cut], states_ref[cut])
        attended = intra_ref[:, cut] + growth[:, h : h + 1] * carried
        attended_ref[:, cut] = attended
        square += attended * attended
        inner += gained_ref[:, cut] * attended
    ones = jnp.ones((8, 3 * size), BF16)
    is_square = lax.broadcasted_iota(jnp.int32, (8, length), 0) == 0
    sums_ref[...] = jnp.where(
        is_square,
        dot(ones, split(square), CONTRACT_COLS),
        dot(ones, split(inner), CONTRACT_COLS),
    )


def attn_grad_body(plan, parties, *refs):
    sums_refs, refs = refs[:parties], refs[parties:]
    attended_ref, query_decayed_ref, gained_ref, attn_grad_ref, held_ref = refs[:5]
    send_refs = refs[5:]
    size, length = plan.size, attended_ref.shape[0]
    feature_count = plan.heads * size * parties
    sums = sum(ref[...] for ref in sums_refs)
    inv_row = lax.rsqrt(sums[:1] / feature_count + EPSILON)
    coefficient_row = sums[1:2] * inv_row * inv_row * inv_row / feature_count
    is_inverse = lax.broadcasted_iota(jnp.int32, (8, length), 0) == 0
    columns = jnp.transpose(jnp.where(is_inverse, inv_row, coefficient_row))
    inv_rms = jnp.broadcast_to(columns[:, :1], (length, size))
    coefficient = jnp.broadcast_to(columns[:, 1:2], (length, size))
    for h in range(plan.heads):
        cut = lanes(h, size)
        attn_grad = gained_ref[:, cut] * inv_rms - attended_ref[:, cut] * coefficient
        attn_grad = attn_grad.astype(BF16)
        attn_grad_ref[:, cut] = attn_grad
        held_ref[cut] = dot(query_decayed_ref[h], attn_grad)
    for k, send_ref in enumerate(send_refs):
        send_ref[...] = held_ref[plan.rows_of(plan.peer(k))]


def score_grad_body(
    plan,
    attn_grad_ref,
    query_ref,
    key_ref,
    value_ref,
    states_ref,
    weight_ref,
    cum_ref,
    cum_col_ref,
    query_grad_ref,
    key_part_ref,
    value_part_ref,
    key_decayed_ref,
    value_decayed_ref,
):
    length = query_ref.shape[0]
    causal = causal_mask(length)
    cum_col = cum_col_ref[...]
    growth = jnp.exp(cum_col)
    shrink = jnp.exp(cum_col[length - 1 : length, :] - cum_col)
    for h in range(plan.heads):
        cut = lanes(h, plan.size)
        attn_grad = attn_grad_ref[:, cut]
        scores = dot(attn_grad, value_ref[:, cut], CONTRACT_COLS)
        score_grad = (scores * decay_matrix(cum_ref, cum_col, causal, h)).astype(BF16)
        carried = dot(attn_grad, states_ref[cut], CONTRACT_COLS)
        query_grad = dot(score_grad, key_ref[:, cut]) + growth[:, h : h + 1] * carried
        query_grad_ref[:, cut] = query_grad.astype(BF16)
        key_part_ref[:, cut] = dot(score_grad, query_ref[:, cut], CONTRACT_ROWS)
        value_part_ref[:, cut] = dot(weight_ref[h], attn_grad, CONTRACT_ROWS)
        column = shrink[:, h : h + 1]
        key_decayed_ref[:, cut] = (key_ref[:, cut].astype(F32) * column).astype(BF16)
        value_decayed_ref[:, cut] = (value_ref[:, cut].astype(F32) * column).astype(BF16)


def finish_body(plan, ways, *refs):
    early_refs, refs = refs[: len(ways)], refs[len(ways) :]
    late_refs, refs = refs[: len(ways)], refs[len(ways) :]
    key_part_ref, value_part_ref, key_ref, value_ref, summary_ref, before_ref, logs_ref = refs[:7]
    key_out, value_out, total_out, key_grad_ref, value_grad_ref, total_ref, sems = refs[-7:]
    size, rows = plan.size, plan.rows
    first = plan.group() == 0
    copies = []
    for i, way in enumerate(ways):
        owner = plan.toward(way)
        before, after = early_refs[i][:rows], late_refs[i][:rows]
        if plan.groups == 2:
            before, after = jnp.where(first, before, after), jnp.where(first, after, before)
        for j in range(plan.own):
            head = owner * plan.own + j
            part = pl.ds(pl.multiple_of(head * size, size), size)
            cut = slice(i * rows + j * size, i * rows + (j + 1) * size)
            grads = after[lanes(j, size)]
            log_before = before_ref[pl.ds(head, 1)]
            scale = jnp.exp(log_before)
            scale_next = jnp.exp(log_before + logs_ref[plan.member(), pl.ds(head, 1)])
            total_ref[cut] = (
                before[lanes(j, size)] + scale * summary_ref[part] + scale_next * grads
            )
            grads = grads.astype(BF16)
            key_state = dot(value_ref[:, part], grads, CONTRACT_COLS)
            key_grad_ref[:, cut] = (key_part_ref[:, part] + key_state).astype(BF16)
            value_state = dot(key_ref[:, part], grads)
            value_grad_ref[:, cut] = (value_part_ref[:, part] + value_state).astype(BF16)
        done, place = lanes(i, rows), plan.rows_of(owner)
        for source, target in [
            (total_ref.at[done], total_out.at[place]),
            (key_grad_ref.at[:, done], key_out.at[:, place]),
            (value_grad_ref.at[:, done], value_out.at[:, place]),
        ]:
            copies.append(pltpu.make_async_copy(source, target, sems.at[len(copies)]))
            copies[-1].start()
    for copy in copies:
        copy.wait()


def on_device(
    query_rows, key_rows, value_rows, log_decay, out_grad, norm_gain, state_in, state_out_grad
):
    heads, length = log_decay.shape
    size = state_in.shape[1]
    width = heads * size
    parties = lax.axis_size("head")
    plan = Plan(heads, size, lax.axis_size("seq"))
    bind = lambda body, *extra: functools.partial(body, plan, *extra)
    gain = norm_gain.reshape(1, width)
    piece = shaped((plan.rows, size))
    pieces = [piece] * plan.members
    chunk_piece = shaped((plan.chunk_rows, size))
    chunk_pieces = [chunk_piece] * plan.members
    logged = shaped((plan.chunk_rows + LOG_ROWS, size))
    block_logs = shaped((plan.members, LOG_ROWS, size))
    group_logs = shaped((plan.groups, LOG_ROWS, size))
    table = shaped((length, width))
    rounded = shaped((length, width), BF16)
    hold = pltpu.VMEM((plan.members, plan.rows, size), F32)
    hold_groups = pltpu.VMEM((plan.groups, plan.rows, size), F32)
    hold_chunk = pltpu.VMEM((plan.members, plan.chunk_rows, size), F32)
    hold_chunk_groups = pltpu.VMEM((plan.groups, plan.chunk_rows, size), F32)
    chunks = range(plan.chunks)
    state_rows = state_in.reshape(width, size)

    messages = plan.first_messages()
    *sends, cum_log, cum_col = call(
        bind(summary_body),
        [chunk_piece if chunk else logged for _, chunk in messages]
        + [shaped((heads, length)), shaped((length, heads))],
        [pltpu.with_memory_space_constraint(x, pltpu.HBM) for x in (key_rows, value_rows, log_decay)],
        [
            pltpu.VMEM((width, size), F32),
            pltpu.VMEM((length, width), BF16),
            pltpu.VMEM((length, width), BF16),
            pltpu.VMEM((heads, length), F32),
            pltpu.SemaphoreType.DMA((3,)),
        ],
        specs=[HBM] * 3,
    )
    received = {key: plan.swap(send, key[0]) for key, send in zip(messages, sends)}
    parts = [[received[way, c] for way in plan.ways] for c in chunks]
    totals = []
    for c in chunks:
        if c == 0:
            total, logs = call(
                bind(group_total_body, c), [logged, block_logs], parts[c], [hold_chunk]
            )
        else:
            (total,) = call(
                bind(group_total_body, c),
                [chunk_piece],
                [*parts[c], logs],
                [hold_chunk],
                flops=LONG,
            )
        totals.append([total] + plan.from_groups(total))
    states = {}
    far_parts = []
    for c in chunks:
        last = c == plan.chunks - 1
        operands = [*parts[c], *totals[c], state_rows, logs]
        outs = [piece if way in plan.far and last else chunk_piece for way in plan.ways]
        if c == 0:
            outs += [shaped((LOG_ROWS, size)), group_logs]
        else:
            operands += [all_logs]
        sends = call(
            bind(forward_scan_body, c),
            outs,
            operands + (far_parts if last else []),
            [hold_chunk_groups, hold_chunk],
        )
        if c == 0:
            before, all_logs = sends[plan.members :]
        for way, send in zip(plan.ways, sends):
            if way not in plan.far:
                states[way, c] = plan.swap(send, way)
            elif last:
                states[way, None] = plan.swap(send, way)
            else:
                far_parts.append(send)
    early = [states[way, 0] for way in plan.near] if plan.chunks > 1 else []
    weights, intra, gained, query_decayed = call(
        bind(intra_body),
        [
            shaped((heads, length, length), BF16),
            table,
            table,
            shaped((heads, size, length), BF16),
        ],
        [query_rows, key_rows, value_rows, cum_log, cum_col, out_grad, gain, *early],
        specs=[VMEM] * 7 + [ANY] * len(early),
        flops=LONG // 10,
    )
    attended, sums, states = call(
        bind(attended_body),
        [table, shaped((8, length)), shaped((width, size), BF16)],
        [*[states[key] for key in plan.last_messages()], intra, query_rows, cum_col, gained],
    )
    all_sums = [sums] + [
        lax.ppermute(sums, "head", [(i, (i + step) % parties) for i in range(parties)])
        for step in range(1, parties)
    ]
    attn_grad, summary, *sends = call(
        bind(attn_grad_body, parties),
        [rounded, shaped((width, size))] + pieces,
        [*all_sums, attended, query_decayed, gained],
    )
    parts = plan.swap_in_group(sends)
    query_grad, key_part, value_part, key_decayed, value_decayed = call(
        bind(score_grad_body),
        [rounded, table, table, rounded, rounded],
        [attn_grad, query_rows, key_rows, value_rows, states, weights, cum_log, cum_col],
        flops=10 * heads * length * length * size,
    )
    grad_rows = state_out_grad.reshape(width, size)
    two_sided = plan.groups == 2
    tie, swapped = key_part, []
    if two_sided:
        sends = call(
            bind(early_body),
            [piece, shaped((plan.rows + LOG_ROWS, size))] + pieces[2:],
            [*parts, logs, grad_rows, key_part],
            [hold],
            specs=[VMEM] * (plan.members + 2) + [ANY],
        )
        tie = sends[0]
        swapped = [dict(zip(plan.early_ways, plan.swap_in_group(sends, plan.early_ways)))]
    (total,) = call(
        bind(group_grad_body),
        [piece],
        [*parts, logs, tie],
        [hold],
        specs=[VMEM] * (plan.members + 1) + [ANY],
    )
    totals = [total] + plan.from_groups(total)
    sends = call(
        bind(reverse_scan_body),
        pieces * (1 if two_sided else 2),
        [*parts, *totals, logs, all_logs, grad_rows, swapped[0][plan.early_ways[1]] if two_sided else tie],
        [hold_groups, hold],
        specs=[VMEM] * (plan.members + plan.groups + 3) + [ANY],
    )
    for first in range(0, len(sends), plan.members):
        pieces_back = plan.swap_in_group(sends[first : first + plan.members])
        swapped.append(dict(zip(plan.ways, pieces_back)))
    outs = []
    for ways in ([0] + plan.far, plan.near):
        if not ways:
            continue
        operands = [
            *[pieces_back[way] for pieces_back in swapped for way in ways],
            key_part,
            value_part,
            key_decayed,
            value_decayed,
            summary,
            before,
            logs,
        ]
        if two_sided and not outs:
            outs = [swapped[0][way] for way in plan.near]
        count = len(operands)
        outs = call(
            bind(finish_body, ways),
            [rounded, rounded, shaped((width, size))],
            [*operands, *outs],
            [
                pltpu.VMEM((length, len(ways) * plan.rows), BF16),
                pltpu.VMEM((length, len(ways) * plan.rows), BF16),
                pltpu.VMEM((len(ways) * plan.rows, size), F32),
                pltpu.SemaphoreType.DMA((3 * len(ways),)),
            ],
            specs=[VMEM] * count + [ANY] * len(outs),
            out_specs=[HBM] * 3,
            aliases={count + i: i for i in range(3)} if len(outs) == 3 else None,
        )
    key_grad, value_grad, state_in_grad = outs
    return (query_grad, key_grad, value_grad, state_in_grad.reshape(heads, size, size))


def solution(mesh):
    return jax.shard_map(
        on_device,
        mesh=mesh,
        in_specs=(
            P("seq", "head"),
            P("seq", "head"),
            P("seq", "head"),
            P("head", "seq"),
            P("seq", "head"),
            P("head"),
            P("head", None, None),
            P("head", None, None),
        ),
        out_specs=(P("seq", "head"), P("seq", "head"), P("seq", "head"), P("head", None, None)),
        check_vma=False,
    )
```

```python
import functools

import jax
import jax.numpy as jnp
from jax import lax
from jax.experimental import pallas as pl
from jax.experimental.pallas import tpu as pltpu
from jax.sharding import PartitionSpec as P

EPSILON = 1e-06
F32 = jnp.float32
BF16 = jnp.bfloat16
LOG_ROWS = 8
LONG = 10**10
MASKED = -1e30

CONTRACT_ROWS = (((0,), (0,)), ((), ()))
CONTRACT_COLS = (((1,), (1,)), ((), ()))
VMEM = pl.BlockSpec(memory_space=pltpu.VMEM)
HBM = pl.BlockSpec(memory_space=pltpu.HBM)
ANY = pl.BlockSpec(memory_space=pl.ANY)


def call(body, outs, operands, scratch=(), flops=0, specs=None, out_specs=None, aliases=None):
    return pl.pallas_call(
        body,
        out_shape=outs,
        in_specs=specs or [VMEM] * len(operands),
        out_specs=out_specs or [VMEM] * len(outs),
        scratch_shapes=list(scratch),
        input_output_aliases=aliases or {},
        compiler_params=pltpu.CompilerParams(vmem_limit_bytes=24 * 1024 * 1024),
        cost_estimate=pl.CostEstimate(flops=flops, bytes_accessed=0, transcendentals=0),
    )(*operands)


def shaped(shape, dtype=F32):
    return jax.ShapeDtypeStruct(shape, dtype)


def dot(a, b, dims=(((1,), (0,)), ((), ()))):
    return lax.dot_general(a, b, dims, preferred_element_type=F32)


def split(x):
    high = x.astype(BF16)
    rest = x - high.astype(F32)
    middle = rest.astype(BF16)
    low = (rest - middle.astype(F32)).astype(BF16)
    return jnp.concatenate([high, middle, low], axis=1)


def thrice(x):
    return jnp.concatenate([x, x, x], axis=1)


def lanes(h, size):
    return slice(h * size, (h + 1) * size)


def causal_mask(length):
    row = lax.broadcasted_iota(jnp.int32, (length, length), 0)
    col = lax.broadcasted_iota(jnp.int32, (length, length), 1)
    return row >= col


class Plan:
    def __init__(self, heads, size, blocks):
        self.heads, self.size, self.blocks = heads, size, blocks
        self.members = next(m for m in (4, 2, 1) if heads % m == 0 and blocks % m == 0)
        self.groups = blocks // self.members
        self.own = heads // self.members
        self.rows = self.own * size
        self.chunks = self.own
        self.chunk_rows = self.rows // self.chunks
        self.near = [way for way in range(self.members) if way.bit_count() == 1]
        self.far = [way for way in range(self.members) if way.bit_count() > 1]
        self.ways = [0] + self.far + self.near
        self.early_ways = [0] + self.far + self.near[::-1]

    def member(self):
        return lax.rem(lax.axis_index("seq"), self.members)

    def group(self):
        return lax.div(lax.axis_index("seq"), self.members)

    def peer(self, k):
        return self.toward(self.ways[k])

    def toward(self, way):
        return lax.bitwise_xor(self.member(), way)

    def rows_of(self, member):
        return pl.ds(pl.multiple_of(member * self.rows, self.rows), self.rows)

    def chunk_of(self, member, chunk):
        start = member * self.rows + chunk * self.chunk_rows
        return pl.ds(pl.multiple_of(start, self.chunk_rows), self.chunk_rows)

    def swap(self, piece, way):
        span = self.members
        pairs = [(i, i // span * span + (i % span ^ way)) for i in range(self.blocks)]
        return lax.ppermute(piece, "seq", pairs) if way else piece

    def swap_in_group(self, pieces, order=None):
        return [self.swap(piece, way) for way, piece in zip(order or self.ways, pieces)]

    def first_messages(self):
        return [(way, c) for c in range(self.chunks) for way in self.ways]

    def last_messages(self):
        cuts = [(way, c) for c in range(self.chunks) for way in [0] + self.near]
        return cuts + [(way, None) for way in self.far]

    def from_groups(self, piece):
        return [
            lax.ppermute(
                piece,
                "seq",
                [(i, (i + step * self.members) % self.blocks) for i in range(self.blocks)],
            )
            for step in range(1, self.groups)
        ]


def own_decays(plan, log_tile_ref, chunk=None):
    count = plan.own if chunk is None else plan.own // plan.chunks
    first = plan.member() * plan.own + (0 if chunk is None else chunk * count)
    rows = [log_tile_ref[pl.ds(first + j, 1), :] for j in range(count)]
    return jnp.concatenate([jnp.broadcast_to(jnp.exp(row), (plan.size, plan.size)) for row in rows])


def summary_body(plan, key_hbm, value_hbm, decay_hbm, *refs):
    count = len(plan.first_messages())
    send_refs, refs = refs[:count], refs[count:]
    cum_ref, cum_col_ref, held_ref, key_ref, value_ref, decay_ref, sems = refs
    length, heads, size = key_ref.shape[0], plan.heads, plan.size
    copies = [
        pltpu.make_async_copy(source, target, sems.at[i])
        for i, (source, target) in enumerate(
            [(decay_hbm, decay_ref), (key_hbm, key_ref), (value_hbm, value_ref)]
        )
    ]
    for copy in copies:
        copy.start()
    causal = thrice(jnp.where(causal_mask(length), 1.0, 0.0).astype(BF16))
    copies[0].wait()
    decay = split(decay_ref[...])
    cum_col = dot(causal, decay, CONTRACT_COLS)
    cum_row = dot(decay, causal, CONTRACT_COLS)
    cum_ref[...] = cum_row
    cum_col_ref[...] = cum_col
    shrink = jnp.exp(cum_col[length - 1 : length, :] - cum_col)
    copies[1].wait()
    copies[2].wait()
    for h in range(heads):
        key_decayed = (key_ref[:, lanes(h, size)].astype(F32) * shrink[:, h : h + 1]).astype(BF16)
        held_ref[h * size : (h + 1) * size] = dot(
            key_decayed, value_ref[:, lanes(h, size)], CONTRACT_ROWS
        )
    log_tile = jnp.broadcast_to(cum_row[:, length - 1 : length], (heads, size))
    if heads < LOG_ROWS:
        log_tile = jnp.concatenate([log_tile, jnp.zeros((LOG_ROWS - heads, size), F32)])
    for (way, chunk), send_ref in zip(plan.first_messages(), send_refs):
        send_ref[: plan.chunk_rows] = held_ref[plan.chunk_of(plan.toward(way), chunk)]
        if chunk == 0:
            send_ref[plan.chunk_rows :] = log_tile


def group_total_body(plan, chunk, *refs):
    part_refs, refs = refs[: plan.members], refs[plan.members :]
    rows = plan.chunk_rows
    if chunk == 0:
        total_ref, logs_ref = refs[:2]
        for k, part_ref in enumerate(part_refs):
            logs_ref[plan.peer(k)] = part_ref[rows:]
        total_ref[rows:] = sum(logs_ref[b] for b in range(plan.members))
    else:
        logs_ref, total_ref = refs[:2]
    held_ref = refs[2]
    for way, part_ref in zip(plan.ways, part_refs):
        held_ref[plan.toward(way)] = part_ref[:rows]
    total = jnp.zeros((rows, plan.size), F32)
    for b in range(plan.members):
        total = own_decays(plan, logs_ref.at[b], chunk) * total + held_ref[b]
    total_ref[:rows] = total


def stage_groups(plan, total_refs, held_ref):
    rows = held_ref.shape[1]
    for step, total_ref in enumerate(total_refs):
        held_ref[lax.rem(plan.group() - step + plan.groups, plan.groups)] = total_ref[:rows]


def forward_scan_body(plan, chunk, *refs):
    last = chunk == plan.chunks - 1
    part_refs, refs = refs[: plan.members], refs[plan.members :]
    total_refs, refs = refs[: plan.groups], refs[plan.groups :]
    (state_ref, logs_ref), refs = refs[:2], refs[2:]
    rows = plan.chunk_rows
    if chunk > 0:
        group_logs_ref, refs = refs[0], refs[1:]
    far_parts = chunk * len(plan.far) if last else 0
    far_refs, refs = refs[:far_parts], refs[far_parts:]
    send_refs, refs = refs[: plan.members], refs[plan.members :]
    if chunk == 0:
        before_ref, group_logs_ref = refs[:2]
        for step, total_ref in enumerate(total_refs):
            group = lax.rem(plan.group() - step + plan.groups, plan.groups)
            group_logs_ref[group] = total_ref[rows:]
        before = jnp.zeros((LOG_ROWS, plan.size), F32)
        for group in range(plan.groups - 1):
            before += jnp.where(group < plan.group(), group_logs_ref[group], 0.0)
        for b in range(plan.members - 1):
            before += jnp.where(b < plan.member(), logs_ref[b], 0.0)
        before_ref[...] = before
    groups_ref, held_ref = refs[-2:]
    stage_groups(plan, total_refs, groups_ref)
    state = state_ref[plan.chunk_of(plan.member(), chunk)]
    for group in range(plan.groups - 1):
        after = own_decays(plan, group_logs_ref.at[group], chunk) * state + groups_ref[group]
        state = jnp.where(group < plan.group(), after, state)
    for way, part_ref in zip(plan.ways, part_refs):
        held_ref[plan.toward(way)] = part_ref[:rows]
    for b in range(plan.members):
        summary = held_ref[b]
        held_ref[b] = state
        state = own_decays(plan, logs_ref.at[b], chunk) * state + summary
    for i, (way, send_ref) in enumerate(zip(plan.ways, send_refs)):
        if way in plan.far and last:
            for c in range(chunk):
                send_ref[c * rows : (c + 1) * rows] = far_refs[c * len(plan.far) + i - 1][...]
            send_ref[chunk * rows :] = held_ref[plan.toward(way)]
        else:
            send_ref[...] = held_ref[plan.toward(way)]


def suffixes(plan, held_ref, logs_ref, grad):
    found = []
    for b in reversed(range(plan.members)):
        found.append(grad)
        grad = own_decays(plan, logs_ref.at[b]) * grad + held_ref[b]
    return found[::-1], grad


def prefixes(plan, held_ref, logs_ref, total, scale):
    found = []
    for b in range(plan.members):
        found.append(total)
        total = total + scale * held_ref[b]
        scale = scale * own_decays(plan, logs_ref.at[b])
    return found


def early_body(plan, *refs):
    part_refs, refs = refs[: plan.members], refs[plan.members :]
    (logs_ref, grad_ref), send_refs, held_ref = refs[:2], refs[3:-1], refs[-1]
    for k, part_ref in enumerate(part_refs):
        held_ref[plan.peer(k)] = part_ref[...]
    first = plan.group() == 0
    zero = jnp.zeros((plan.rows, plan.size), F32)
    before = prefixes(plan, held_ref, logs_ref, zero, zero + 1.0)
    after = suffixes(plan, held_ref, logs_ref, grad_ref[plan.rows_of(plan.member())])[0]
    for b in range(plan.members):
        held_ref[b] = jnp.where(first, before[b], after[b])
    for way, send_ref in zip(plan.early_ways, send_refs):
        send_ref[: plan.rows] = held_ref[plan.toward(way)]
        if send_ref.shape[0] > plan.rows:
            send_ref[plan.rows :] = logs_ref[0]


def group_grad_body(plan, *refs):
    part_refs, (logs_ref, _, total_ref, held_ref) = refs[: plan.members], refs[plan.members :]
    for k, part_ref in enumerate(part_refs):
        held_ref[plan.peer(k)] = part_ref[...]
    zero = jnp.zeros((plan.rows, plan.size), F32)
    total_ref[...] = suffixes(plan, held_ref, logs_ref, zero)[1]


def reverse_scan_body(plan, *refs):
    part_refs, refs = refs[: plan.members], refs[plan.members :]
    total_refs, refs = refs[: plan.groups], refs[plan.groups :]
    (logs_ref, group_logs_ref, grad_ref, _), refs = refs[:4], refs[4:]
    send_refs, (groups_ref, held_ref) = refs[:-2], refs[-2:]
    stage_groups(plan, total_refs, groups_ref)
    for k, part_ref in enumerate(part_refs):
        held_ref[plan.peer(k)] = part_ref[...]
    grad = grad_ref[plan.rows_of(plan.member())]
    leaving = grad
    for group in reversed(range(plan.groups)):
        leaving = jnp.where(group == plan.group(), grad, leaving)
        grad = own_decays(plan, group_logs_ref.at[group]) * grad + groups_ref[group]
    total = jnp.zeros((plan.rows, plan.size), F32)
    scale = total + 1.0
    for group in range(plan.groups - 1):
        earlier = group < plan.group()
        total = jnp.where(earlier, total + scale * groups_ref[group], total)
        decays = own_decays(plan, group_logs_ref.at[group])
        scale = jnp.where(earlier, scale * decays, scale)
    after = suffixes(plan, held_ref, logs_ref, leaving)[0]
    before = prefixes(plan, held_ref, logs_ref, total, scale)
    if plan.groups == 2:
        first = plan.group() == 0
        found = [[jnp.where(first, after[b], before[b]) for b in range(plan.members)]]
    else:
        found = [before, after]
    for i, values in enumerate(found):
        for b in range(plan.members):
            held_ref[b] = values[b]
        for k in range(plan.members):
            send_refs[i * plan.members + k][...] = held_ref[plan.peer(k)]


def decay_matrix(cum_ref, cum_col, causal, h):
    spread = cum_col[:, h : h + 1] - cum_ref[h : h + 1, :]
    return jnp.exp(jnp.where(causal, jnp.minimum(spread, 0.0), MASKED))


def intra_body(
    plan,
    query_ref,
    key_ref,
    value_ref,
    cum_ref,
    cum_col_ref,
    upstream_ref,
    gain_ref,
    *refs,
):
    weight_ref, intra_ref, gained_ref, query_decayed_ref = refs[-4:]
    causal = causal_mask(query_ref.shape[0])
    cum_col = cum_col_ref[...]
    growth = jnp.exp(cum_col)
    for h in range(plan.heads):
        cut = lanes(h, plan.size)
        query = query_ref[:, cut]
        scores = dot(query, key_ref[:, cut], CONTRACT_COLS)
        weights = (scores * decay_matrix(cum_ref, cum_col, causal, h)).astype(BF16)
        weight_ref[h] = weights
        intra_ref[:, cut] = dot(weights, value_ref[:, cut])
        gained_ref[:, cut] = gain_ref[:, cut] * upstream_ref[:, cut].astype(F32)
        query_decayed = query.astype(F32) * growth[:, h : h + 1]
        query_decayed_ref[h] = jnp.transpose(query_decayed).astype(BF16)


def attended_body(plan, *refs):
    count = len(plan.last_messages())
    state_refs, refs = refs[:count], refs[count:]
    intra_ref, query_ref, cum_col_ref, gained_ref = refs[:4]
    attended_ref, sums_ref, states_ref = refs[4:]
    size, length = plan.size, query_ref.shape[0]
    for (way, chunk), state_ref in zip(plan.last_messages(), state_refs):
        member = plan.toward(way)
        part = plan.rows_of(member) if chunk is None else plan.chunk_of(member, chunk)
        states_ref[part] = state_ref[...].astype(BF16)
    growth = jnp.exp(cum_col_ref[...])
    square = jnp.zeros((length, size), F32)
    inner = jnp.zeros((length, size), F32)
    for h in range(plan.heads):
        cut = lanes(h, size)
        carried = dot(query_ref[:, cut], states_ref[cut])
        attended = intra_ref[:, cut] + growth[:, h : h + 1] * carried
        attended_ref[:, cut] = attended
        square += attended * attended
        inner += gained_ref[:, cut] * attended
    ones = jnp.ones((8, 3 * size), BF16)
    is_square = lax.broadcasted_iota(jnp.int32, (8, length), 0) == 0
    sums_ref[...] = jnp.where(
        is_square,
        dot(ones, split(square), CONTRACT_COLS),
        dot(ones, split(inner), CONTRACT_COLS),
    )


def attn_grad_body(plan, parties, *refs):
    sums_refs, refs = refs[:parties], refs[parties:]
    attended_ref, query_decayed_ref, gained_ref, attn_grad_ref, held_ref = refs[:5]
    send_refs = refs[5:]
    size, length = plan.size, attended_ref.shape[0]
    feature_count = plan.heads * size * parties
    sums = sum(ref[...] for ref in sums_refs)
    inv_row = lax.rsqrt(sums[:1] / feature_count + EPSILON)
    coefficient_row = sums[1:2] * inv_row * inv_row * inv_row / feature_count
    is_inverse = lax.broadcasted_iota(jnp.int32, (8, length), 0) == 0
    columns = jnp.transpose(jnp.where(is_inverse, inv_row, coefficient_row))
    inv_rms = jnp.broadcast_to(columns[:, :1], (length, size))
    coefficient = jnp.broadcast_to(columns[:, 1:2], (length, size))
    for h in range(plan.heads):
        cut = lanes(h, size)
        attn_grad = gained_ref[:, cut] * inv_rms - attended_ref[:, cut] * coefficient
        attn_grad = attn_grad.astype(BF16)
        attn_grad_ref[:, cut] = attn_grad
        held_ref[cut] = dot(query_decayed_ref[h], attn_grad)
    for k, send_ref in enumerate(send_refs):
        send_ref[...] = held_ref[plan.rows_of(plan.peer(k))]


def score_grad_body(
    plan,
    attn_grad_ref,
    query_ref,
    key_ref,
    value_ref,
    states_ref,
    weight_ref,
    cum_ref,
    cum_col_ref,
    query_grad_ref,
    key_part_ref,
    value_part_ref,
    shrink_ref,
):
    length = query_ref.shape[0]
    causal = causal_mask(length)
    cum_col = cum_col_ref[...]
    growth = jnp.exp(cum_col)
    shrink = jnp.exp(cum_col[length - 1 : length, :] - cum_col)
    for h in range(plan.heads):
        cut = lanes(h, plan.size)
        attn_grad = attn_grad_ref[:, cut]
        scores = dot(attn_grad, value_ref[:, cut], CONTRACT_COLS)
        score_grad = (scores * decay_matrix(cum_ref, cum_col, causal, h)).astype(BF16)
        carried = dot(attn_grad, states_ref[cut], CONTRACT_COLS)
        query_grad = dot(score_grad, key_ref[:, cut]) + growth[:, h : h + 1] * carried
        query_grad_ref[:, cut] = query_grad.astype(BF16)
        key_part_ref[:, cut] = dot(score_grad, query_ref[:, cut], CONTRACT_ROWS)
        value_part_ref[:, cut] = dot(weight_ref[h], attn_grad, CONTRACT_ROWS)
        shrink_ref[h] = jnp.broadcast_to(shrink[:, h : h + 1], (length, plan.size))


def finish_body(plan, ways, *refs):
    early_refs, refs = refs[: len(ways)], refs[len(ways) :]
    late_refs, refs = refs[: len(ways)], refs[len(ways) :]
    key_part_ref, value_part_ref, key_ref, value_ref, shrink_ref = refs[:5]
    summary_ref, before_ref, logs_ref = refs[5:8]
    key_out, value_out, total_out, key_grad_ref, value_grad_ref, total_ref, sems = refs[-7:]
    size, rows = plan.size, plan.rows
    first = plan.group() == 0
    copies = []
    for i, way in enumerate(ways):
        owner = plan.toward(way)
        before, after = early_refs[i][:rows], late_refs[i][:rows]
        if plan.groups == 2:
            before, after = jnp.where(first, before, after), jnp.where(first, after, before)
        for j in range(plan.own):
            head = owner * plan.own + j
            part = pl.ds(pl.multiple_of(head * size, size), size)
            cut = slice(i * rows + j * size, i * rows + (j + 1) * size)
            grads = after[lanes(j, size)]
            log_before = before_ref[pl.ds(head, 1)]
            scale = jnp.exp(log_before)
            scale_next = jnp.exp(log_before + logs_ref[plan.member(), pl.ds(head, 1)])
            total_ref[cut] = (
                before[lanes(j, size)] + scale * summary_ref[part] + scale_next * grads
            )
            grads = grads.astype(BF16)
            key_state = dot(value_ref[:, part], grads, CONTRACT_COLS)
            key_grad_ref[:, cut] = (key_part_ref[:, part] + shrink_ref[head] * key_state).astype(BF16)
            value_state = dot(key_ref[:, part], grads)
            value_grad_ref[:, cut] = (value_part_ref[:, part] + shrink_ref[head] * value_state).astype(BF16)
        done, place = lanes(i, rows), plan.rows_of(owner)
        for source, target in [
            (total_ref.at[done], total_out.at[place]),
            (key_grad_ref.at[:, done], key_out.at[:, place]),
            (value_grad_ref.at[:, done], value_out.at[:, place]),
        ]:
            copies.append(pltpu.make_async_copy(source, target, sems.at[len(copies)]))
            copies[-1].start()
    for copy in copies:
        copy.wait()


def on_device(
    query_rows, key_rows, value_rows, log_decay, out_grad, norm_gain, state_in, state_out_grad
):
    heads, length = log_decay.shape
    size = state_in.shape[1]
    width = heads * size
    parties = lax.axis_size("head")
    plan = Plan(heads, size, lax.axis_size("seq"))
    bind = lambda body, *extra: functools.partial(body, plan, *extra)
    gain = norm_gain.reshape(1, width)
    piece = shaped((plan.rows, size))
    pieces = [piece] * plan.members
    chunk_piece = shaped((plan.chunk_rows, size))
    chunk_pieces = [chunk_piece] * plan.members
    logged = shaped((plan.chunk_rows + LOG_ROWS, size))
    block_logs = shaped((plan.members, LOG_ROWS, size))
    group_logs = shaped((plan.groups, LOG_ROWS, size))
    table = shaped((length, width))
    rounded = shaped((length, width), BF16)
    hold = pltpu.VMEM((plan.members, plan.rows, size), F32)
    hold_groups = pltpu.VMEM((plan.groups, plan.rows, size), F32)
    hold_chunk = pltpu.VMEM((plan.members, plan.chunk_rows, size), F32)
    hold_chunk_groups = pltpu.VMEM((plan.groups, plan.chunk_rows, size), F32)
    chunks = range(plan.chunks)
    state_rows = state_in.reshape(width, size)

    messages = plan.first_messages()
    *sends, cum_log, cum_col = call(
        bind(summary_body),
        [chunk_piece if chunk else logged for _, chunk in messages]
        + [shaped((heads, length)), shaped((length, heads))],
        [pltpu.with_memory_space_constraint(x, pltpu.HBM) for x in (key_rows, value_rows, log_decay)],
        [
            pltpu.VMEM((width, size), F32),
            pltpu.VMEM((length, width), BF16),
            pltpu.VMEM((length, width), BF16),
            pltpu.VMEM((heads, length), F32),
            pltpu.SemaphoreType.DMA((3,)),
        ],
        specs=[HBM] * 3,
    )
    received = {key: plan.swap(send, key[0]) for key, send in zip(messages, sends)}
    parts = [[received[way, c] for way in plan.ways] for c in chunks]
    totals = []
    for c in chunks:
        if c == 0:
            total, logs = call(
                bind(group_total_body, c), [logged, block_logs], parts[c], [hold_chunk]
            )
        else:
            (total,) = call(
                bind(group_total_body, c),
                [chunk_piece],
                [*parts[c], logs],
                [hold_chunk],
                flops=LONG,
            )
        totals.append([total] + plan.from_groups(total))
    states = {}
    far_parts = []
    for c in chunks:
        last = c == plan.chunks - 1
        operands = [*parts[c], *totals[c], state_rows, logs]
        outs = [piece if way in plan.far and last else chunk_piece for way in plan.ways]
        if c == 0:
            outs += [shaped((LOG_ROWS, size)), group_logs]
        else:
            operands += [all_logs]
        sends = call(
            bind(forward_scan_body, c),
            outs,
            operands + (far_parts if last else []),
            [hold_chunk_groups, hold_chunk],
        )
        if c == 0:
            before, all_logs = sends[plan.members :]
        for way, send in zip(plan.ways, sends):
            if way not in plan.far:
                states[way, c] = plan.swap(send, way)
            elif last:
                states[way, None] = plan.swap(send, way)
            else:
                far_parts.append(send)
    early = [states[way, 0] for way in plan.near] if plan.chunks > 1 else []
    weights, intra, gained, query_decayed = call(
        bind(intra_body),
        [
            shaped((heads, length, length), BF16),
            table,
            table,
            shaped((heads, size, length), BF16),
        ],
        [query_rows, key_rows, value_rows, cum_log, cum_col, out_grad, gain, *early],
        specs=[VMEM] * 7 + [ANY] * len(early),
        flops=LONG // 10,
    )
    attended, sums, states = call(
        bind(attended_body),
        [table, shaped((8, length)), shaped((width, size), BF16)],
        [*[states[key] for key in plan.last_messages()], intra, query_rows, cum_col, gained],
    )
    all_sums = [sums] + [
        lax.ppermute(sums, "head", [(i, (i + step) % parties) for i in range(parties)])
        for step in range(1, parties)
    ]
    attn_grad, summary, *sends = call(
        bind(attn_grad_body, parties),
        [rounded, shaped((width, size))] + pieces,
        [*all_sums, attended, query_decayed, gained],
    )
    parts = plan.swap_in_group(sends)
    query_grad, key_part, value_part, shrink = call(
        bind(score_grad_body),
        [rounded, table, table, shaped((heads, length, size))],
        [attn_grad, query_rows, key_rows, value_rows, states, weights, cum_log, cum_col],
        flops=10 * heads * length * length * size,
    )
    grad_rows = state_out_grad.reshape(width, size)
    two_sided = plan.groups == 2
    tie, swapped = key_part, []
    if two_sided:
        sends = call(
            bind(early_body),
            [piece, shaped((plan.rows + LOG_ROWS, size))] + pieces[2:],
            [*parts, logs, grad_rows, key_part],
            [hold],
            specs=[VMEM] * (plan.members + 2) + [ANY],
        )
        tie = sends[0]
        swapped = [dict(zip(plan.early_ways, plan.swap_in_group(sends, plan.early_ways)))]
    (total,) = call(
        bind(group_grad_body),
        [piece],
        [*parts, logs, tie],
        [hold],
        specs=[VMEM] * (plan.members + 1) + [ANY],
    )
    totals = [total] + plan.from_groups(total)
    sends = call(
        bind(reverse_scan_body),
        pieces * (1 if two_sided else 2),
        [*parts, *totals, logs, all_logs, grad_rows, swapped[0][plan.early_ways[1]] if two_sided else tie],
        [hold_groups, hold],
        specs=[VMEM] * (plan.members + plan.groups + 3) + [ANY],
    )
    for first in range(0, len(sends), plan.members):
        pieces_back = plan.swap_in_group(sends[first : first + plan.members])
        swapped.append(dict(zip(plan.ways, pieces_back)))
    outs = []
    for ways in ([0], plan.far + plan.near):
        if not ways:
            continue
        operands = [
            *[pieces_back[way] for pieces_back in swapped for way in ways],
            key_part,
            value_part,
            key_rows,
            value_rows,
            shrink,
            summary,
            before,
            logs,
        ]
        count = len(operands)
        outs = call(
            bind(finish_body, ways),
            [rounded, rounded, shaped((width, size))],
            [*operands, *outs],
            [
                pltpu.VMEM((length, len(ways) * plan.rows), BF16),
                pltpu.VMEM((length, len(ways) * plan.rows), BF16),
                pltpu.VMEM((len(ways) * plan.rows, size), F32),
                pltpu.SemaphoreType.DMA((3 * len(ways),)),
            ],
            specs=[VMEM] * count + [HBM] * len(outs),
            out_specs=[HBM] * 3,
            aliases={count + i: i for i in range(len(outs))},
        )
    key_grad, value_grad, state_in_grad = outs
    return (query_grad, key_grad, value_grad, state_in_grad.reshape(heads, size, size))


def solution(mesh):
    return jax.shard_map(
        on_device,
        mesh=mesh,
        in_specs=(
            P("seq", "head"),
            P("seq", "head"),
            P("seq", "head"),
            P("head", "seq"),
            P("seq", "head"),
            P("head"),
            P("head", None, None),
            P("head", None, None),
        ),
        out_specs=(P("seq", "head"), P("seq", "head"), P("seq", "head"), P("head", None, None)),
        check_vma=False,
    )
```

```python
import functools

import jax
import jax.numpy as jnp
from jax import lax
from jax.experimental import pallas as pl
from jax.experimental.pallas import tpu as pltpu
from jax.sharding import PartitionSpec as P

EPSILON = 1e-06
F32 = jnp.float32
BF16 = jnp.bfloat16
LOG_ROWS = 8
LONG = 10**10
MASKED = -1e30

CONTRACT_ROWS = (((0,), (0,)), ((), ()))
CONTRACT_COLS = (((1,), (1,)), ((), ()))
VMEM = pl.BlockSpec(memory_space=pltpu.VMEM)
HBM = pl.BlockSpec(memory_space=pltpu.HBM)
ANY = pl.BlockSpec(memory_space=pl.ANY)


def call(body, outs, operands, scratch=(), flops=0, specs=None, out_specs=None, aliases=None):
    return pl.pallas_call(
        body,
        out_shape=outs,
        in_specs=specs or [VMEM] * len(operands),
        out_specs=out_specs or [VMEM] * len(outs),
        scratch_shapes=list(scratch),
        input_output_aliases=aliases or {},
        compiler_params=pltpu.CompilerParams(vmem_limit_bytes=24 * 1024 * 1024),
        cost_estimate=pl.CostEstimate(flops=flops, bytes_accessed=0, transcendentals=0),
    )(*operands)


def shaped(shape, dtype=F32):
    return jax.ShapeDtypeStruct(shape, dtype)


def dot(a, b, dims=(((1,), (0,)), ((), ()))):
    return lax.dot_general(a, b, dims, preferred_element_type=F32)


def split(x):
    high = x.astype(BF16)
    rest = x - high.astype(F32)
    middle = rest.astype(BF16)
    low = (rest - middle.astype(F32)).astype(BF16)
    return jnp.concatenate([high, middle, low], axis=1)


def thrice(x):
    return jnp.concatenate([x, x, x], axis=1)


def lanes(h, size):
    return slice(h * size, (h + 1) * size)


def causal_mask(length):
    row = lax.broadcasted_iota(jnp.int32, (length, length), 0)
    col = lax.broadcasted_iota(jnp.int32, (length, length), 1)
    return row >= col


class Plan:
    def __init__(self, heads, size, blocks):
        self.heads, self.size, self.blocks = heads, size, blocks
        self.members = next(m for m in (4, 2, 1) if heads % m == 0 and blocks % m == 0)
        self.groups = blocks // self.members
        self.own = heads // self.members
        self.rows = self.own * size
        self.chunks = self.own
        self.chunk_rows = self.rows // self.chunks
        self.near = [way for way in range(self.members) if way.bit_count() == 1]
        self.far = [way for way in range(self.members) if way.bit_count() > 1]
        self.ways = [0] + self.far + self.near
        self.early_ways = [0] + self.near[::-1] + self.far
        self.late_ways = [0] + self.far + self.near[::-1]

    def member(self):
        return lax.rem(lax.axis_index("seq"), self.members)

    def group(self):
        return lax.div(lax.axis_index("seq"), self.members)

    def peer(self, k):
        return self.toward(self.ways[k])

    def toward(self, way):
        return lax.bitwise_xor(self.member(), way)

    def rows_of(self, member):
        return pl.ds(pl.multiple_of(member * self.rows, self.rows), self.rows)

    def chunk_of(self, member, chunk):
        start = member * self.rows + chunk * self.chunk_rows
        return pl.ds(pl.multiple_of(start, self.chunk_rows), self.chunk_rows)

    def swap(self, piece, way):
        span = self.members
        pairs = [(i, i // span * span + (i % span ^ way)) for i in range(self.blocks)]
        return lax.ppermute(piece, "seq", pairs) if way else piece

    def swap_in_group(self, pieces, order=None):
        return [self.swap(piece, way) for way, piece in zip(order or self.ways, pieces)]

    def first_messages(self):
        return [(way, c) for c in range(self.chunks) for way in self.ways]

    def last_messages(self):
        cuts = [(way, c) for c in range(self.chunks) for way in [0] + self.near]
        return cuts + [(way, None) for way in self.far]

    def from_groups(self, piece):
        return [
            lax.ppermute(
                piece,
                "seq",
                [(i, (i + step * self.members) % self.blocks) for i in range(self.blocks)],
            )
            for step in range(1, self.groups)
        ]


def own_decays(plan, log_tile_ref, chunk=None):
    count = plan.own if chunk is None else plan.own // plan.chunks
    first = plan.member() * plan.own + (0 if chunk is None else chunk * count)
    rows = [log_tile_ref[pl.ds(first + j, 1), :] for j in range(count)]
    return jnp.concatenate([jnp.broadcast_to(jnp.exp(row), (plan.size, plan.size)) for row in rows])


def summary_body(plan, key_hbm, value_hbm, decay_hbm, *refs):
    count = len(plan.first_messages())
    send_refs, refs = refs[:count], refs[count:]
    cum_ref, cum_col_ref, held_ref, key_ref, value_ref, decay_ref, sems = refs
    length, heads, size = key_ref.shape[0], plan.heads, plan.size
    copies = [
        pltpu.make_async_copy(source, target, sems.at[i])
        for i, (source, target) in enumerate(
            [(decay_hbm, decay_ref), (key_hbm, key_ref), (value_hbm, value_ref)]
        )
    ]
    for copy in copies:
        copy.start()
    causal = thrice(jnp.where(causal_mask(length), 1.0, 0.0).astype(BF16))
    copies[0].wait()
    decay = split(decay_ref[...])
    cum_col = dot(causal, decay, CONTRACT_COLS)
    cum_row = dot(decay, causal, CONTRACT_COLS)
    cum_ref[...] = cum_row
    cum_col_ref[...] = cum_col
    shrink = jnp.exp(cum_col[length - 1 : length, :] - cum_col)
    copies[1].wait()
    copies[2].wait()
    for h in range(heads):
        key_decayed = (key_ref[:, lanes(h, size)].astype(F32) * shrink[:, h : h + 1]).astype(BF16)
        held_ref[h * size : (h + 1) * size] = dot(
            key_decayed, value_ref[:, lanes(h, size)], CONTRACT_ROWS
        )
    log_tile = jnp.broadcast_to(cum_row[:, length - 1 : length], (heads, size))
    if heads < LOG_ROWS:
        log_tile = jnp.concatenate([log_tile, jnp.zeros((LOG_ROWS - heads, size), F32)])
    for (way, chunk), send_ref in zip(plan.first_messages(), send_refs):
        send_ref[: plan.chunk_rows] = held_ref[plan.chunk_of(plan.toward(way), chunk)]
        if chunk == 0:
            send_ref[plan.chunk_rows :] = log_tile


def group_total_body(plan, chunk, *refs):
    part_refs, refs = refs[: plan.members], refs[plan.members :]
    rows = plan.chunk_rows
    if chunk == 0:
        total_ref, logs_ref = refs[:2]
        for k, part_ref in enumerate(part_refs):
            logs_ref[plan.peer(k)] = part_ref[rows:]
        total_ref[rows:] = sum(logs_ref[b] for b in range(plan.members))
    else:
        logs_ref, total_ref = refs[:2]
    held_ref = refs[2]
    for way, part_ref in zip(plan.ways, part_refs):
        held_ref[plan.toward(way)] = part_ref[:rows]
    total = jnp.zeros((rows, plan.size), F32)
    for b in range(plan.members):
        total = own_decays(plan, logs_ref.at[b], chunk) * total + held_ref[b]
    total_ref[:rows] = total


def stage_groups(plan, total_refs, held_ref):
    rows = held_ref.shape[1]
    for step, total_ref in enumerate(total_refs):
        held_ref[lax.rem(plan.group() - step + plan.groups, plan.groups)] = total_ref[:rows]


def forward_scan_body(plan, chunk, *refs):
    last = chunk == plan.chunks - 1
    part_refs, refs = refs[: plan.members], refs[plan.members :]
    total_refs, refs = refs[: plan.groups], refs[plan.groups :]
    (state_ref, logs_ref), refs = refs[:2], refs[2:]
    rows = plan.chunk_rows
    if chunk > 0:
        group_logs_ref, refs = refs[0], refs[1:]
    far_parts = chunk * len(plan.far) if last else 0
    far_refs, refs = refs[:far_parts], refs[far_parts:]
    send_refs, refs = refs[: plan.members], refs[plan.members :]
    if chunk == 0:
        before_ref, group_logs_ref = refs[:2]
        for step, total_ref in enumerate(total_refs):
            group = lax.rem(plan.group() - step + plan.groups, plan.groups)
            group_logs_ref[group] = total_ref[rows:]
        before = jnp.zeros((LOG_ROWS, plan.size), F32)
        for group in range(plan.groups - 1):
            before += jnp.where(group < plan.group(), group_logs_ref[group], 0.0)
        for b in range(plan.members - 1):
            before += jnp.where(b < plan.member(), logs_ref[b], 0.0)
        before_ref[...] = before
    groups_ref, held_ref = refs[-2:]
    stage_groups(plan, total_refs, groups_ref)
    state = state_ref[plan.chunk_of(plan.member(), chunk)]
    for group in range(plan.groups - 1):
        after = own_decays(plan, group_logs_ref.at[group], chunk) * state + groups_ref[group]
        state = jnp.where(group < plan.group(), after, state)
    for way, part_ref in zip(plan.ways, part_refs):
        held_ref[plan.toward(way)] = part_ref[:rows]
    for b in range(plan.members):
        summary = held_ref[b]
        held_ref[b] = state
        state = own_decays(plan, logs_ref.at[b], chunk) * state + summary
    for i, (way, send_ref) in enumerate(zip(plan.ways, send_refs)):
        if way in plan.far and last:
            for c in range(chunk):
                send_ref[c * rows : (c + 1) * rows] = far_refs[c * len(plan.far) + i - 1][...]
            send_ref[chunk * rows :] = held_ref[plan.toward(way)]
        else:
            send_ref[...] = held_ref[plan.toward(way)]


def suffixes(plan, held_ref, logs_ref, grad):
    found = []
    for b in reversed(range(plan.members)):
        found.append(grad)
        grad = own_decays(plan, logs_ref.at[b]) * grad + held_ref[b]
    return found[::-1], grad


def prefixes(plan, held_ref, logs_ref, total, scale):
    found = []
    for b in range(plan.members):
        found.append(total)
        total = total + scale * held_ref[b]
        scale = scale * own_decays(plan, logs_ref.at[b])
    return found


def early_body(plan, *refs):
    part_refs, refs = refs[: plan.members], refs[plan.members :]
    (logs_ref, grad_ref), send_refs, held_ref = refs[:2], refs[3:-1], refs[-1]
    for k, part_ref in enumerate(part_refs):
        held_ref[plan.peer(k)] = part_ref[...]
    first = plan.group() == 0
    zero = jnp.zeros((plan.rows, plan.size), F32)
    before = prefixes(plan, held_ref, logs_ref, zero, zero + 1.0)
    after = suffixes(plan, held_ref, logs_ref, grad_ref[plan.rows_of(plan.member())])[0]
    for b in range(plan.members):
        held_ref[b] = jnp.where(first, before[b], after[b])
    for way, send_ref in zip(plan.early_ways, send_refs):
        send_ref[: plan.rows] = held_ref[plan.toward(way)]
        if send_ref.shape[0] > plan.rows:
            send_ref[plan.rows :] = logs_ref[0]


def group_grad_body(plan, *refs):
    part_refs, (logs_ref, _, total_ref, held_ref) = refs[: plan.members], refs[plan.members :]
    for k, part_ref in enumerate(part_refs):
        held_ref[plan.peer(k)] = part_ref[...]
    zero = jnp.zeros((plan.rows, plan.size), F32)
    total_ref[...] = suffixes(plan, held_ref, logs_ref, zero)[1]


def reverse_scan_body(plan, *refs):
    part_refs, refs = refs[: plan.members], refs[plan.members :]
    total_refs, refs = refs[: plan.groups], refs[plan.groups :]
    (logs_ref, group_logs_ref, grad_ref, _), refs = refs[:4], refs[4:]
    send_refs, (groups_ref, held_ref) = refs[:-2], refs[-2:]
    stage_groups(plan, total_refs, groups_ref)
    for k, part_ref in enumerate(part_refs):
        held_ref[plan.peer(k)] = part_ref[...]
    grad = grad_ref[plan.rows_of(plan.member())]
    leaving = grad
    for group in reversed(range(plan.groups)):
        leaving = jnp.where(group == plan.group(), grad, leaving)
        grad = own_decays(plan, group_logs_ref.at[group]) * grad + groups_ref[group]
    total = jnp.zeros((plan.rows, plan.size), F32)
    scale = total + 1.0
    for group in range(plan.groups - 1):
        earlier = group < plan.group()
        total = jnp.where(earlier, total + scale * groups_ref[group], total)
        decays = own_decays(plan, group_logs_ref.at[group])
        scale = jnp.where(earlier, scale * decays, scale)
    after = suffixes(plan, held_ref, logs_ref, leaving)[0]
    before = prefixes(plan, held_ref, logs_ref, total, scale)
    if plan.groups == 2:
        first = plan.group() == 0
        found = [[jnp.where(first, after[b], before[b]) for b in range(plan.members)]]
    else:
        found = [before, after]
    for i, values in enumerate(found):
        for b in range(plan.members):
            held_ref[b] = values[b]
        for k in range(plan.members):
            send_refs[i * plan.members + k][...] = held_ref[plan.toward(plan.late_ways[k])]


def decay_matrix(cum_ref, cum_col, causal, h):
    spread = cum_col[:, h : h + 1] - cum_ref[h : h + 1, :]
    return jnp.exp(jnp.where(causal, jnp.minimum(spread, 0.0), MASKED))


def intra_body(
    plan,
    query_ref,
    key_ref,
    value_ref,
    cum_ref,
    cum_col_ref,
    upstream_ref,
    gain_ref,
    *refs,
):
    weight_ref, intra_ref, gained_ref, query_decayed_ref = refs[-4:]
    causal = causal_mask(query_ref.shape[0])
    cum_col = cum_col_ref[...]
    growth = jnp.exp(cum_col)
    for h in range(plan.heads):
        cut = lanes(h, plan.size)
        query = query_ref[:, cut]
        scores = dot(query, key_ref[:, cut], CONTRACT_COLS)
        weights = (scores * decay_matrix(cum_ref, cum_col, causal, h)).astype(BF16)
        weight_ref[h] = weights
        intra_ref[:, cut] = dot(weights, value_ref[:, cut])
        gained_ref[:, cut] = gain_ref[:, cut] * upstream_ref[:, cut].astype(F32)
        query_decayed = query.astype(F32) * growth[:, h : h + 1]
        query_decayed_ref[h] = jnp.transpose(query_decayed).astype(BF16)


def attended_body(plan, *refs):
    count = len(plan.last_messages())
    state_refs, refs = refs[:count], refs[count:]
    intra_ref, query_ref, cum_col_ref, gained_ref = refs[:4]
    attended_ref, sums_ref, states_ref = refs[4:]
    size, length = plan.size, query_ref.shape[0]
    for (way, chunk), state_ref in zip(plan.last_messages(), state_refs):
        member = plan.toward(way)
        part = plan.rows_of(member) if chunk is None else plan.chunk_of(member, chunk)
        states_ref[part] = state_ref[...].astype(BF16)
    growth = jnp.exp(cum_col_ref[...])
    square = jnp.zeros((length, size), F32)
    inner = jnp.zeros((length, size), F32)
    for h in range(plan.heads):
        cut = lanes(h, size)
        carried = dot(query_ref[:, cut], states_ref[cut])
        attended = intra_ref[:, cut] + growth[:, h : h + 1] * carried
        attended_ref[:, cut] = attended
        square += attended * attended
        inner += gained_ref[:, cut] * attended
    ones = jnp.ones((8, 3 * size), BF16)
    is_square = lax.broadcasted_iota(jnp.int32, (8, length), 0) == 0
    sums_ref[...] = jnp.where(
        is_square,
        dot(ones, split(square), CONTRACT_COLS),
        dot(ones, split(inner), CONTRACT_COLS),
    )


def attn_grad_body(plan, parties, *refs):
    sums_refs, refs = refs[:parties], refs[parties:]
    attended_ref, query_decayed_ref, gained_ref, attn_grad_ref, held_ref = refs[:5]
    send_refs = refs[5:]
    size, length = plan.size, attended_ref.shape[0]
    feature_count = plan.heads * size * parties
    sums = sum(ref[...] for ref in sums_refs)
    inv_row = lax.rsqrt(sums[:1] / feature_count + EPSILON)
    coefficient_row = sums[1:2] * inv_row * inv_row * inv_row / feature_count
    is_inverse = lax.broadcasted_iota(jnp.int32, (8, length), 0) == 0
    columns = jnp.transpose(jnp.where(is_inverse, inv_row, coefficient_row))
    inv_rms = jnp.broadcast_to(columns[:, :1], (length, size))
    coefficient = jnp.broadcast_to(columns[:, 1:2], (length, size))
    for h in range(plan.heads):
        cut = lanes(h, size)
        attn_grad = gained_ref[:, cut] * inv_rms - attended_ref[:, cut] * coefficient
        attn_grad = attn_grad.astype(BF16)
        attn_grad_ref[:, cut] = attn_grad
        held_ref[cut] = dot(query_decayed_ref[h], attn_grad)
    for k, send_ref in enumerate(send_refs):
        send_ref[...] = held_ref[plan.rows_of(plan.peer(k))]


def score_grad_body(
    plan,
    attn_grad_ref,
    query_ref,
    key_ref,
    value_ref,
    states_ref,
    weight_ref,
    cum_ref,
    cum_col_ref,
    query_grad_ref,
    key_part_ref,
    value_part_ref,
    shrink_ref,
):
    length = query_ref.shape[0]
    causal = causal_mask(length)
    cum_col = cum_col_ref[...]
    growth = jnp.exp(cum_col)
    shrink = jnp.exp(cum_col[length - 1 : length, :] - cum_col)
    for h in range(plan.heads):
        cut = lanes(h, plan.size)
        attn_grad = attn_grad_ref[:, cut]
        scores = dot(attn_grad, value_ref[:, cut], CONTRACT_COLS)
        score_grad = (scores * decay_matrix(cum_ref, cum_col, causal, h)).astype(BF16)
        carried = dot(attn_grad, states_ref[cut], CONTRACT_COLS)
        query_grad = dot(score_grad, key_ref[:, cut]) + growth[:, h : h + 1] * carried
        query_grad_ref[:, cut] = query_grad.astype(BF16)
        key_part_ref[:, cut] = dot(score_grad, query_ref[:, cut], CONTRACT_ROWS)
        value_part_ref[:, cut] = dot(weight_ref[h], attn_grad, CONTRACT_ROWS)
        shrink_ref[h] = jnp.broadcast_to(shrink[:, h : h + 1], (length, plan.size))


def finish_body(plan, ways, *refs):
    count = len(ways)
    early_refs = dict(zip([way for way in plan.early_ways if way in ways], refs[:count]))
    late_refs = dict(zip(ways, refs[count : 2 * count]))
    refs = refs[2 * count :]
    key_part_ref, value_part_ref, key_ref, value_ref, shrink_ref = refs[:5]
    summary_ref, before_ref, logs_ref = refs[5:8]
    key_out, value_out, total_out, key_grad_ref, value_grad_ref, total_ref, sems = refs[-7:]
    size, rows = plan.size, plan.rows
    first = plan.group() == 0
    copies = []
    for i, way in enumerate(ways):
        owner = plan.toward(way)
        before, after = early_refs[way][:rows], late_refs[way][:rows]
        if plan.groups == 2:
            before, after = jnp.where(first, before, after), jnp.where(first, after, before)
        for j in range(plan.own):
            head = owner * plan.own + j
            part = pl.ds(pl.multiple_of(head * size, size), size)
            cut = slice(i * rows + j * size, i * rows + (j + 1) * size)
            grads = after[lanes(j, size)]
            log_before = before_ref[pl.ds(head, 1)]
            scale = jnp.exp(log_before)
            scale_next = jnp.exp(log_before + logs_ref[plan.member(), pl.ds(head, 1)])
            total_ref[cut] = (
                before[lanes(j, size)] + scale * summary_ref[part] + scale_next * grads
            )
            grads = grads.astype(BF16)
            key_state = dot(value_ref[:, part], grads, CONTRACT_COLS)
            key_grad_ref[:, cut] = (key_part_ref[:, part] + shrink_ref[head] * key_state).astype(BF16)
            value_state = dot(key_ref[:, part], grads)
            value_grad_ref[:, cut] = (value_part_ref[:, part] + shrink_ref[head] * value_state).astype(BF16)
        done, place = lanes(i, rows), plan.rows_of(owner)
        for source, target in [
            (total_ref.at[done], total_out.at[place]),
            (key_grad_ref.at[:, done], key_out.at[:, place]),
            (value_grad_ref.at[:, done], value_out.at[:, place]),
        ]:
            copies.append(pltpu.make_async_copy(source, target, sems.at[len(copies)]))
            copies[-1].start()
    for copy in copies:
        copy.wait()


def on_device(
    query_rows, key_rows, value_rows, log_decay, out_grad, norm_gain, state_in, state_out_grad
):
    heads, length = log_decay.shape
    size = state_in.shape[1]
    width = heads * size
    parties = lax.axis_size("head")
    plan = Plan(heads, size, lax.axis_size("seq"))
    bind = lambda body, *extra: functools.partial(body, plan, *extra)
    gain = norm_gain.reshape(1, width)
    piece = shaped((plan.rows, size))
    pieces = [piece] * plan.members
    chunk_piece = shaped((plan.chunk_rows, size))
    chunk_pieces = [chunk_piece] * plan.members
    logged = shaped((plan.chunk_rows + LOG_ROWS, size))
    block_logs = shaped((plan.members, LOG_ROWS, size))
    group_logs = shaped((plan.groups, LOG_ROWS, size))
    table = shaped((length, width))
    rounded = shaped((length, width), BF16)
    hold = pltpu.VMEM((plan.members, plan.rows, size), F32)
    hold_groups = pltpu.VMEM((plan.groups, plan.rows, size), F32)
    hold_chunk = pltpu.VMEM((plan.members, plan.chunk_rows, size), F32)
    hold_chunk_groups = pltpu.VMEM((plan.groups, plan.chunk_rows, size), F32)
    chunks = range(plan.chunks)
    state_rows = state_in.reshape(width, size)

    messages = plan.first_messages()
    *sends, cum_log, cum_col = call(
        bind(summary_body),
        [chunk_piece if chunk else logged for _, chunk in messages]
        + [shaped((heads, length)), shaped((length, heads))],
        [pltpu.with_memory_space_constraint(x, pltpu.HBM) for x in (key_rows, value_rows, log_decay)],
        [
            pltpu.VMEM((width, size), F32),
            pltpu.VMEM((length, width), BF16),
            pltpu.VMEM((length, width), BF16),
            pltpu.VMEM((heads, length), F32),
            pltpu.SemaphoreType.DMA((3,)),
        ],
        specs=[HBM] * 3,
    )
    received = {key: plan.swap(send, key[0]) for key, send in zip(messages, sends)}
    parts = [[received[way, c] for way in plan.ways] for c in chunks]
    totals = []
    for c in chunks:
        if c == 0:
            total, logs = call(
                bind(group_total_body, c), [logged, block_logs], parts[c], [hold_chunk]
            )
        else:
            (total,) = call(
                bind(group_total_body, c),
                [chunk_piece],
                [*parts[c], logs],
                [hold_chunk],
                flops=LONG,
            )
        totals.append([total] + plan.from_groups(total))
    states = {}
    far_parts = []
    for c in chunks:
        last = c == plan.chunks - 1
        operands = [*parts[c], *totals[c], state_rows, logs]
        outs = [piece if way in plan.far and last else chunk_piece for way in plan.ways]
        if c == 0:
            outs += [shaped((LOG_ROWS, size)), group_logs]
        else:
            operands += [all_logs]
        sends = call(
            bind(forward_scan_body, c),
            outs,
            operands + (far_parts if last else []),
            [hold_chunk_groups, hold_chunk],
        )
        if c == 0:
            before, all_logs = sends[plan.members :]
        for way, send in zip(plan.ways, sends):
            if way not in plan.far:
                states[way, c] = plan.swap(send, way)
            elif last:
                states[way, None] = plan.swap(send, way)
            else:
                far_parts.append(send)
    early = [states[way, 0] for way in plan.near] if plan.chunks > 1 else []
    weights, intra, gained, query_decayed = call(
        bind(intra_body),
        [
            shaped((heads, length, length), BF16),
            table,
            table,
            shaped((heads, size, length), BF16),
        ],
        [query_rows, key_rows, value_rows, cum_log, cum_col, out_grad, gain, *early],
        specs=[VMEM] * 7 + [ANY] * len(early),
        flops=LONG // 10,
    )
    attended, sums, states = call(
        bind(attended_body),
        [table, shaped((8, length)), shaped((width, size), BF16)],
        [*[states[key] for key in plan.last_messages()], intra, query_rows, cum_col, gained],
    )
    all_sums = [sums] + [
        lax.ppermute(sums, "head", [(i, (i + step) % parties) for i in range(parties)])
        for step in range(1, parties)
    ]
    attn_grad, summary, *sends = call(
        bind(attn_grad_body, parties),
        [rounded, shaped((width, size))] + pieces,
        [*all_sums, attended, query_decayed, gained],
    )
    parts = plan.swap_in_group(sends)
    query_grad, key_part, value_part, shrink = call(
        bind(score_grad_body),
        [rounded, table, table, shaped((heads, length, size))],
        [attn_grad, query_rows, key_rows, value_rows, states, weights, cum_log, cum_col],
        flops=10 * heads * length * length * size,
    )
    grad_rows = state_out_grad.reshape(width, size)
    two_sided = plan.groups == 2
    tie, swapped = key_part, []
    if two_sided:
        sends = call(
            bind(early_body),
            [piece, shaped((plan.rows + LOG_ROWS, size))] + pieces[2:],
            [*parts, logs, grad_rows, key_part],
            [hold],
            specs=[VMEM] * (plan.members + 2) + [ANY],
        )
        tie = sends[0]
        swapped = [dict(zip(plan.early_ways, plan.swap_in_group(sends, plan.early_ways)))]
    (total,) = call(
        bind(group_grad_body),
        [piece],
        [*parts, logs, tie],
        [hold],
        specs=[VMEM] * (plan.members + 1) + [ANY],
    )
    totals = [total] + plan.from_groups(total)
    sends = call(
        bind(reverse_scan_body),
        pieces * (1 if two_sided else 2),
        [*parts, *totals, logs, all_logs, grad_rows, swapped[0][plan.early_ways[1]] if two_sided else tie],
        [hold_groups, hold],
        specs=[VMEM] * (plan.members + plan.groups + 3) + [ANY],
    )
    for first in range(0, len(sends), plan.members):
        pieces_back = plan.swap_in_group(sends[first : first + plan.members], plan.late_ways)
        swapped.append(dict(zip(plan.late_ways, pieces_back)))
    outs = []
    for ways in ([0], plan.late_ways[1:]):
        if not ways:
            continue
        operands = [
            *[swapped[0][way] for way in plan.early_ways if way in ways],
            *[swapped[1][way] for way in ways],
            key_part,
            value_part,
            key_rows,
            value_rows,
            shrink,
            summary,
            before,
            logs,
        ]
        count = len(operands)
        outs = call(
            bind(finish_body, ways),
            [rounded, rounded, shaped((width, size))],
            [*operands, *outs],
            [
                pltpu.VMEM((length, len(ways) * plan.rows), BF16),
                pltpu.VMEM((length, len(ways) * plan.rows), BF16),
                pltpu.VMEM((len(ways) * plan.rows, size), F32),
                pltpu.SemaphoreType.DMA((3 * len(ways),)),
            ],
            specs=[VMEM] * count + [HBM] * len(outs),
            out_specs=[HBM] * 3,
            aliases={count + i: i for i in range(len(outs))},
        )
    key_grad, value_grad, state_in_grad = outs
    return (query_grad, key_grad, value_grad, state_in_grad.reshape(heads, size, size))


def solution(mesh):
    return jax.shard_map(
        on_device,
        mesh=mesh,
        in_specs=(
            P("seq", "head"),
            P("seq", "head"),
            P("seq", "head"),
            P("head", "seq"),
            P("seq", "head"),
            P("head"),
            P("head", None, None),
            P("head", None, None),
        ),
        out_specs=(P("seq", "head"), P("seq", "head"), P("seq", "head"), P("head", None, None)),
        check_vma=False,
    )
```

```python
import functools

import jax
import jax.numpy as jnp
from jax import lax
from jax.experimental import pallas as pl
from jax.experimental.pallas import tpu as pltpu
from jax.sharding import PartitionSpec as P

EPSILON = 1e-06
F32 = jnp.float32
BF16 = jnp.bfloat16
LOG_ROWS = 8
LONG = 10**10
MASKED = -1e30

CONTRACT_ROWS = (((0,), (0,)), ((), ()))
CONTRACT_COLS = (((1,), (1,)), ((), ()))
VMEM = pl.BlockSpec(memory_space=pltpu.VMEM)
HBM = pl.BlockSpec(memory_space=pltpu.HBM)
ANY = pl.BlockSpec(memory_space=pl.ANY)


def call(body, outs, operands, scratch=(), flops=0, specs=None, out_specs=None, aliases=None):
    return pl.pallas_call(
        body,
        out_shape=outs,
        in_specs=specs or [VMEM] * len(operands),
        out_specs=out_specs or [VMEM] * len(outs),
        scratch_shapes=list(scratch),
        input_output_aliases=aliases or {},
        compiler_params=pltpu.CompilerParams(vmem_limit_bytes=24 * 1024 * 1024),
        cost_estimate=pl.CostEstimate(flops=flops, bytes_accessed=0, transcendentals=0),
    )(*operands)


def shaped(shape, dtype=F32):
    return jax.ShapeDtypeStruct(shape, dtype)


def dot(a, b, dims=(((1,), (0,)), ((), ()))):
    return lax.dot_general(a, b, dims, preferred_element_type=F32)


def split(x):
    high = x.astype(BF16)
    rest = x - high.astype(F32)
    middle = rest.astype(BF16)
    low = (rest - middle.astype(F32)).astype(BF16)
    return jnp.concatenate([high, middle, low], axis=1)


def thrice(x):
    return jnp.concatenate([x, x, x], axis=1)


def lanes(h, size):
    return slice(h * size, (h + 1) * size)


def causal_mask(length):
    row = lax.broadcasted_iota(jnp.int32, (length, length), 0)
    col = lax.broadcasted_iota(jnp.int32, (length, length), 1)
    return row >= col


class Plan:
    def __init__(self, heads, size, blocks):
        self.heads, self.size, self.blocks = heads, size, blocks
        self.members = next(m for m in (4, 2, 1) if heads % m == 0 and blocks % m == 0)
        self.groups = blocks // self.members
        self.own = heads // self.members
        self.rows = self.own * size
        self.chunks = self.own
        self.chunk_rows = self.rows // self.chunks
        self.near = [way for way in range(self.members) if way.bit_count() == 1]
        self.far = [way for way in range(self.members) if way.bit_count() > 1]
        self.ways = [0] + self.far + self.near
        self.early_ways = [0] + self.near[::-1] + self.far
        self.late_ways = [0] + self.near[::-1] + self.far

    def member(self):
        return lax.rem(lax.axis_index("seq"), self.members)

    def group(self):
        return lax.div(lax.axis_index("seq"), self.members)

    def peer(self, k):
        return self.toward(self.ways[k])

    def toward(self, way):
        return lax.bitwise_xor(self.member(), way)

    def rows_of(self, member):
        return pl.ds(pl.multiple_of(member * self.rows, self.rows), self.rows)

    def chunk_of(self, member, chunk):
        start = member * self.rows + chunk * self.chunk_rows
        return pl.ds(pl.multiple_of(start, self.chunk_rows), self.chunk_rows)

    def swap(self, piece, way):
        span = self.members
        pairs = [(i, i // span * span + (i % span ^ way)) for i in range(self.blocks)]
        return lax.ppermute(piece, "seq", pairs) if way else piece

    def swap_in_group(self, pieces, order=None):
        return [self.swap(piece, way) for way, piece in zip(order or self.ways, pieces)]

    def first_messages(self):
        return [(way, c) for c in range(self.chunks) for way in self.ways]

    def last_messages(self):
        cuts = [(way, c) for c in range(self.chunks) for way in [0] + self.near]
        return cuts + [(way, None) for way in self.far]

    def from_groups(self, piece):
        return [
            lax.ppermute(
                piece,
                "seq",
                [(i, (i + step * self.members) % self.blocks) for i in range(self.blocks)],
            )
            for step in range(1, self.groups)
        ]


def own_decays(plan, log_tile_ref, chunk=None):
    count = plan.own if chunk is None else plan.own // plan.chunks
    first = plan.member() * plan.own + (0 if chunk is None else chunk * count)
    rows = [log_tile_ref[pl.ds(first + j, 1), :] for j in range(count)]
    return jnp.concatenate([jnp.broadcast_to(jnp.exp(row), (plan.size, plan.size)) for row in rows])


def summary_body(plan, key_hbm, value_hbm, decay_hbm, *refs):
    count = len(plan.first_messages())
    send_refs, refs = refs[:count], refs[count:]
    cum_ref, cum_col_ref, held_ref, key_ref, value_ref, decay_ref, sems = refs
    length, heads, size = key_ref.shape[0], plan.heads, plan.size
    copies = [
        pltpu.make_async_copy(source, target, sems.at[i])
        for i, (source, target) in enumerate(
            [(decay_hbm, decay_ref), (key_hbm, key_ref), (value_hbm, value_ref)]
        )
    ]
    for copy in copies:
        copy.start()
    causal = thrice(jnp.where(causal_mask(length), 1.0, 0.0).astype(BF16))
    copies[0].wait()
    decay = split(decay_ref[...])
    cum_col = dot(causal, decay, CONTRACT_COLS)
    cum_row = dot(decay, causal, CONTRACT_COLS)
    cum_ref[...] = cum_row
    cum_col_ref[...] = cum_col
    shrink = jnp.exp(cum_col[length - 1 : length, :] - cum_col)
    copies[1].wait()
    copies[2].wait()
    for h in range(heads):
        key_decayed = (key_ref[:, lanes(h, size)].astype(F32) * shrink[:, h : h + 1]).astype(BF16)
        held_ref[h * size : (h + 1) * size] = dot(
            key_decayed, value_ref[:, lanes(h, size)], CONTRACT_ROWS
        )
    log_tile = jnp.broadcast_to(cum_row[:, length - 1 : length], (heads, size))
    if heads < LOG_ROWS:
        log_tile = jnp.concatenate([log_tile, jnp.zeros((LOG_ROWS - heads, size), F32)])
    for (way, chunk), send_ref in zip(plan.first_messages(), send_refs):
        send_ref[: plan.chunk_rows] = held_ref[plan.chunk_of(plan.toward(way), chunk)]
        if chunk == 0:
            send_ref[plan.chunk_rows :] = log_tile


def group_total_body(plan, chunk, *refs):
    part_refs, refs = refs[: plan.members], refs[plan.members :]
    rows = plan.chunk_rows
    if chunk == 0:
        total_ref, logs_ref = refs[:2]
        for k, part_ref in enumerate(part_refs):
            logs_ref[plan.peer(k)] = part_ref[rows:]
        total_ref[rows:] = sum(logs_ref[b] for b in range(plan.members))
    else:
        logs_ref, total_ref = refs[:2]
    held_ref = refs[2]
    for way, part_ref in zip(plan.ways, part_refs):
        held_ref[plan.toward(way)] = part_ref[:rows]
    total = jnp.zeros((rows, plan.size), F32)
    for b in range(plan.members):
        total = own_decays(plan, logs_ref.at[b], chunk) * total + held_ref[b]
    total_ref[:rows] = total


def stage_groups(plan, total_refs, held_ref):
    rows = held_ref.shape[1]
    for step, total_ref in enumerate(total_refs):
        held_ref[lax.rem(plan.group() - step + plan.groups, plan.groups)] = total_ref[:rows]


def forward_scan_body(plan, chunk, *refs):
    last = chunk == plan.chunks - 1
    part_refs, refs = refs[: plan.members], refs[plan.members :]
    total_refs, refs = refs[: plan.groups], refs[plan.groups :]
    (state_ref, logs_ref), refs = refs[:2], refs[2:]
    rows = plan.chunk_rows
    if chunk > 0:
        group_logs_ref, refs = refs[0], refs[1:]
    far_parts = chunk * len(plan.far) if last else 0
    far_refs, refs = refs[:far_parts], refs[far_parts:]
    send_refs, refs = refs[: plan.members], refs[plan.members :]
    if chunk == 0:
        before_ref, group_logs_ref = refs[:2]
        for step, total_ref in enumerate(total_refs):
            group = lax.rem(plan.group() - step + plan.groups, plan.groups)
            group_logs_ref[group] = total_ref[rows:]
        before = jnp.zeros((LOG_ROWS, plan.size), F32)
        for group in range(plan.groups - 1):
            before += jnp.where(group < plan.group(), group_logs_ref[group], 0.0)
        for b in range(plan.members - 1):
            before += jnp.where(b < plan.member(), logs_ref[b], 0.0)
        before_ref[...] = before
    groups_ref, held_ref = refs[-2:]
    stage_groups(plan, total_refs, groups_ref)
    state = state_ref[plan.chunk_of(plan.member(), chunk)]
    for group in range(plan.groups - 1):
        after = own_decays(plan, group_logs_ref.at[group], chunk) * state + groups_ref[group]
        state = jnp.where(group < plan.group(), after, state)
    for way, part_ref in zip(plan.ways, part_refs):
        held_ref[plan.toward(way)] = part_ref[:rows]
    for b in range(plan.members):
        summary = held_ref[b]
        held_ref[b] = state
        state = own_decays(plan, logs_ref.at[b], chunk) * state + summary
    for i, (way, send_ref) in enumerate(zip(plan.ways, send_refs)):
        if way in plan.far and last:
            for c in range(chunk):
                send_ref[c * rows : (c + 1) * rows] = far_refs[c * len(plan.far) + i - 1][...]
            send_ref[chunk * rows :] = held_ref[plan.toward(way)]
        else:
            send_ref[...] = held_ref[plan.toward(way)]


def suffixes(plan, held_ref, logs_ref, grad):
    found = []
    for b in reversed(range(plan.members)):
        found.append(grad)
        grad = own_decays(plan, logs_ref.at[b]) * grad + held_ref[b]
    return found[::-1], grad


def prefixes(plan, held_ref, logs_ref, total, scale):
    found = []
    for b in range(plan.members):
        found.append(total)
        total = total + scale * held_ref[b]
        scale = scale * own_decays(plan, logs_ref.at[b])
    return found


def early_body(plan, *refs):
    part_refs, refs = refs[: plan.members], refs[plan.members :]
    (logs_ref, grad_ref), send_refs, held_ref = refs[:2], refs[3:-1], refs[-1]
    for k, part_ref in enumerate(part_refs):
        held_ref[plan.peer(k)] = part_ref[...]
    first = plan.group() == 0
    zero = jnp.zeros((plan.rows, plan.size), F32)
    before = prefixes(plan, held_ref, logs_ref, zero, zero + 1.0)
    after = suffixes(plan, held_ref, logs_ref, grad_ref[plan.rows_of(plan.member())])[0]
    for b in range(plan.members):
        held_ref[b] = jnp.where(first, before[b], after[b])
    for way, send_ref in zip(plan.early_ways, send_refs):
        send_ref[: plan.rows] = held_ref[plan.toward(way)]
        if send_ref.shape[0] > plan.rows:
            send_ref[plan.rows :] = logs_ref[0]


def group_grad_body(plan, *refs):
    part_refs, (logs_ref, _, total_ref, held_ref) = refs[: plan.members], refs[plan.members :]
    for k, part_ref in enumerate(part_refs):
        held_ref[plan.peer(k)] = part_ref[...]
    zero = jnp.zeros((plan.rows, plan.size), F32)
    total_ref[...] = suffixes(plan, held_ref, logs_ref, zero)[1]


def reverse_scan_body(plan, *refs):
    part_refs, refs = refs[: plan.members], refs[plan.members :]
    total_refs, refs = refs[: plan.groups], refs[plan.groups :]
    (logs_ref, group_logs_ref, grad_ref, _), refs = refs[:4], refs[4:]
    send_refs, (groups_ref, held_ref) = refs[:-2], refs[-2:]
    stage_groups(plan, total_refs, groups_ref)
    for k, part_ref in enumerate(part_refs):
        held_ref[plan.peer(k)] = part_ref[...]
    grad = grad_ref[plan.rows_of(plan.member())]
    leaving = grad
    for group in reversed(range(plan.groups)):
        leaving = jnp.where(group == plan.group(), grad, leaving)
        grad = own_decays(plan, group_logs_ref.at[group]) * grad + groups_ref[group]
    total = jnp.zeros((plan.rows, plan.size), F32)
    scale = total + 1.0
    for group in range(plan.groups - 1):
        earlier = group < plan.group()
        total = jnp.where(earlier, total + scale * groups_ref[group], total)
        decays = own_decays(plan, group_logs_ref.at[group])
        scale = jnp.where(earlier, scale * decays, scale)
    after = suffixes(plan, held_ref, logs_ref, leaving)[0]
    before = prefixes(plan, held_ref, logs_ref, total, scale)
    if plan.groups == 2:
        first = plan.group() == 0
        found = [[jnp.where(first, after[b], before[b]) for b in range(plan.members)]]
    else:
        found = [before, after]
    for i, values in enumerate(found):
        for b in range(plan.members):
            held_ref[b] = values[b]
        for k in range(plan.members):
            send_refs[i * plan.members + k][...] = held_ref[plan.toward(plan.late_ways[k])]


def decay_matrix(cum_ref, cum_col, causal, h):
    spread = cum_col[:, h : h + 1] - cum_ref[h : h + 1, :]
    return jnp.exp(jnp.where(causal, jnp.minimum(spread, 0.0), MASKED))


def intra_body(
    plan,
    query_ref,
    key_ref,
    value_ref,
    cum_ref,
    cum_col_ref,
    upstream_ref,
    gain_ref,
    *refs,
):
    weight_ref, intra_ref, gained_ref, query_decayed_ref = refs[-4:]
    causal = causal_mask(query_ref.shape[0])
    cum_col = cum_col_ref[...]
    growth = jnp.exp(cum_col)
    for h in range(plan.heads):
        cut = lanes(h, plan.size)
        query = query_ref[:, cut]
        scores = dot(query, key_ref[:, cut], CONTRACT_COLS)
        weights = (scores * decay_matrix(cum_ref, cum_col, causal, h)).astype(BF16)
        weight_ref[h] = weights
        intra_ref[:, cut] = dot(weights, value_ref[:, cut])
        gained_ref[:, cut] = gain_ref[:, cut] * upstream_ref[:, cut].astype(F32)
        query_decayed = query.astype(F32) * growth[:, h : h + 1]
        query_decayed_ref[h] = jnp.transpose(query_decayed).astype(BF16)


def attended_body(plan, *refs):
    count = len(plan.last_messages())
    state_refs, refs = refs[:count], refs[count:]
    intra_ref, query_ref, cum_col_ref, gained_ref = refs[:4]
    attended_ref, sums_ref, states_ref = refs[4:]
    size, length = plan.size, query_ref.shape[0]
    for (way, chunk), state_ref in zip(plan.last_messages(), state_refs):
        member = plan.toward(way)
        part = plan.rows_of(member) if chunk is None else plan.chunk_of(member, chunk)
        states_ref[part] = state_ref[...].astype(BF16)
    growth = jnp.exp(cum_col_ref[...])
    square = jnp.zeros((length, size), F32)
    inner = jnp.zeros((length, size), F32)
    for h in range(plan.heads):
        cut = lanes(h, size)
        carried = dot(query_ref[:, cut], states_ref[cut])
        attended = intra_ref[:, cut] + growth[:, h : h + 1] * carried
        attended_ref[:, cut] = attended
        square += attended * attended
        inner += gained_ref[:, cut] * attended
    ones = jnp.ones((8, 3 * size), BF16)
    is_square = lax.broadcasted_iota(jnp.int32, (8, length), 0) == 0
    sums_ref[...] = jnp.where(
        is_square,
        dot(ones, split(square), CONTRACT_COLS),
        dot(ones, split(inner), CONTRACT_COLS),
    )


def attn_grad_body(plan, parties, *refs):
    sums_refs, refs = refs[:parties], refs[parties:]
    attended_ref, query_decayed_ref, gained_ref, attn_grad_ref, held_ref = refs[:5]
    send_refs = refs[5:]
    size, length = plan.size, attended_ref.shape[0]
    feature_count = plan.heads * size * parties
    sums = sum(ref[...] for ref in sums_refs)
    inv_row = lax.rsqrt(sums[:1] / feature_count + EPSILON)
    coefficient_row = sums[1:2] * inv_row * inv_row * inv_row / feature_count
    is_inverse = lax.broadcasted_iota(jnp.int32, (8, length), 0) == 0
    columns = jnp.transpose(jnp.where(is_inverse, inv_row, coefficient_row))
    inv_rms = jnp.broadcast_to(columns[:, :1], (length, size))
    coefficient = jnp.broadcast_to(columns[:, 1:2], (length, size))
    for h in range(plan.heads):
        cut = lanes(h, size)
        attn_grad = gained_ref[:, cut] * inv_rms - attended_ref[:, cut] * coefficient
        attn_grad = attn_grad.astype(BF16)
        attn_grad_ref[:, cut] = attn_grad
        held_ref[cut] = dot(query_decayed_ref[h], attn_grad)
    for k, send_ref in enumerate(send_refs):
        send_ref[...] = held_ref[plan.rows_of(plan.peer(k))]


def score_grad_body(
    plan,
    attn_grad_ref,
    query_ref,
    key_ref,
    value_ref,
    states_ref,
    weight_ref,
    cum_ref,
    cum_col_ref,
    query_grad_ref,
    key_part_ref,
    value_part_ref,
    shrink_ref,
):
    length = query_ref.shape[0]
    causal = causal_mask(length)
    cum_col = cum_col_ref[...]
    growth = jnp.exp(cum_col)
    shrink = jnp.exp(cum_col[length - 1 : length, :] - cum_col)
    for h in range(plan.heads):
        cut = lanes(h, plan.size)
        attn_grad = attn_grad_ref[:, cut]
        scores = dot(attn_grad, value_ref[:, cut], CONTRACT_COLS)
        score_grad = (scores * decay_matrix(cum_ref, cum_col, causal, h)).astype(BF16)
        carried = dot(attn_grad, states_ref[cut], CONTRACT_COLS)
        query_grad = dot(score_grad, key_ref[:, cut]) + growth[:, h : h + 1] * carried
        query_grad_ref[:, cut] = query_grad.astype(BF16)
        key_part_ref[:, cut] = dot(score_grad, query_ref[:, cut], CONTRACT_ROWS)
        value_part_ref[:, cut] = dot(weight_ref[h], attn_grad, CONTRACT_ROWS)
        shrink_ref[h] = jnp.broadcast_to(shrink[:, h : h + 1], (length, plan.size))


def finish_body(plan, ways, *refs):
    count = len(ways)
    early_refs = dict(zip([way for way in plan.early_ways if way in ways], refs[:count]))
    late_refs = dict(zip(ways, refs[count : 2 * count]))
    refs = refs[2 * count :]
    key_part_ref, value_part_ref, key_ref, value_ref, shrink_ref = refs[:5]
    summary_ref, before_ref, logs_ref = refs[5:8]
    key_out, value_out, total_out, key_grad_ref, value_grad_ref, total_ref, sems = refs[-7:]
    size, rows = plan.size, plan.rows
    first = plan.group() == 0
    copies = []
    for i, way in enumerate(ways):
        owner = plan.toward(way)
        before, after = early_refs[way][:rows], late_refs[way][:rows]
        if plan.groups == 2:
            before, after = jnp.where(first, before, after), jnp.where(first, after, before)
        for j in range(plan.own):
            head = owner * plan.own + j
            part = pl.ds(pl.multiple_of(head * size, size), size)
            cut = slice(i * rows + j * size, i * rows + (j + 1) * size)
            grads = after[lanes(j, size)]
            log_before = before_ref[pl.ds(head, 1)]
            scale = jnp.exp(log_before)
            scale_next = jnp.exp(log_before + logs_ref[plan.member(), pl.ds(head, 1)])
            total_ref[cut] = (
                before[lanes(j, size)] + scale * summary_ref[part] + scale_next * grads
            )
            grads = grads.astype(BF16)
            key_state = dot(value_ref[:, part], grads, CONTRACT_COLS)
            key_grad_ref[:, cut] = (key_part_ref[:, part] + shrink_ref[head] * key_state).astype(BF16)
            value_state = dot(key_ref[:, part], grads)
            value_grad_ref[:, cut] = (value_part_ref[:, part] + shrink_ref[head] * value_state).astype(BF16)
        done, place = lanes(i, rows), plan.rows_of(owner)
        for source, target in [
            (total_ref.at[done], total_out.at[place]),
            (key_grad_ref.at[:, done], key_out.at[:, place]),
            (value_grad_ref.at[:, done], value_out.at[:, place]),
        ]:
            copies.append(pltpu.make_async_copy(source, target, sems.at[len(copies)]))
            copies[-1].start()
    for copy in copies:
        copy.wait()


def on_device(
    query_rows, key_rows, value_rows, log_decay, out_grad, norm_gain, state_in, state_out_grad
):
    heads, length = log_decay.shape
    size = state_in.shape[1]
    width = heads * size
    parties = lax.axis_size("head")
    plan = Plan(heads, size, lax.axis_size("seq"))
    bind = lambda body, *extra: functools.partial(body, plan, *extra)
    gain = norm_gain.reshape(1, width)
    piece = shaped((plan.rows, size))
    pieces = [piece] * plan.members
    chunk_piece = shaped((plan.chunk_rows, size))
    chunk_pieces = [chunk_piece] * plan.members
    logged = shaped((plan.chunk_rows + LOG_ROWS, size))
    block_logs = shaped((plan.members, LOG_ROWS, size))
    group_logs = shaped((plan.groups, LOG_ROWS, size))
    table = shaped((length, width))
    rounded = shaped((length, width), BF16)
    hold = pltpu.VMEM((plan.members, plan.rows, size), F32)
    hold_groups = pltpu.VMEM((plan.groups, plan.rows, size), F32)
    hold_chunk = pltpu.VMEM((plan.members, plan.chunk_rows, size), F32)
    hold_chunk_groups = pltpu.VMEM((plan.groups, plan.chunk_rows, size), F32)
    chunks = range(plan.chunks)
    state_rows = state_in.reshape(width, size)

    messages = plan.first_messages()
    *sends, cum_log, cum_col = call(
        bind(summary_body),
        [chunk_piece if chunk else logged for _, chunk in messages]
        + [shaped((heads, length)), shaped((length, heads))],
        [pltpu.with_memory_space_constraint(x, pltpu.HBM) for x in (key_rows, value_rows, log_decay)],
        [
            pltpu.VMEM((width, size), F32),
            pltpu.VMEM((length, width), BF16),
            pltpu.VMEM((length, width), BF16),
            pltpu.VMEM((heads, length), F32),
            pltpu.SemaphoreType.DMA((3,)),
        ],
        specs=[HBM] * 3,
    )
    received = {key: plan.swap(send, key[0]) for key, send in zip(messages, sends)}
    parts = [[received[way, c] for way in plan.ways] for c in chunks]
    totals = []
    for c in chunks:
        if c == 0:
            total, logs = call(
                bind(group_total_body, c), [logged, block_logs], parts[c], [hold_chunk]
            )
        else:
            (total,) = call(
                bind(group_total_body, c),
                [chunk_piece],
                [*parts[c], logs],
                [hold_chunk],
                flops=LONG,
            )
        totals.append([total] + plan.from_groups(total))
    states = {}
    far_parts = []
    for c in chunks:
        last = c == plan.chunks - 1
        operands = [*parts[c], *totals[c], state_rows, logs]
        outs = [piece if way in plan.far and last else chunk_piece for way in plan.ways]
        if c == 0:
            outs += [shaped((LOG_ROWS, size)), group_logs]
        else:
            operands += [all_logs]
        sends = call(
            bind(forward_scan_body, c),
            outs,
            operands + (far_parts if last else []),
            [hold_chunk_groups, hold_chunk],
        )
        if c == 0:
            before, all_logs = sends[plan.members :]
        for way, send in zip(plan.ways, sends):
            if way not in plan.far:
                states[way, c] = plan.swap(send, way)
            elif last:
                states[way, None] = plan.swap(send, way)
            else:
                far_parts.append(send)
    early = [states[way, 0] for way in plan.near] if plan.chunks > 1 else []
    weights, intra, gained, query_decayed = call(
        bind(intra_body),
        [
            shaped((heads, length, length), BF16),
            table,
            table,
            shaped((heads, size, length), BF16),
        ],
        [query_rows, key_rows, value_rows, cum_log, cum_col, out_grad, gain, *early],
        specs=[VMEM] * 7 + [ANY] * len(early),
        flops=LONG // 10,
    )
    attended, sums, states = call(
        bind(attended_body),
        [table, shaped((8, length)), shaped((width, size), BF16)],
        [*[states[key] for key in plan.last_messages()], intra, query_rows, cum_col, gained],
    )
    all_sums = [sums] + [
        lax.ppermute(sums, "head", [(i, (i + step) % parties) for i in range(parties)])
        for step in reversed(range(1, parties))
    ]
    attn_grad, summary, *sends = call(
        bind(attn_grad_body, parties),
        [rounded, shaped((width, size))] + pieces,
        [*all_sums, attended, query_decayed, gained],
    )
    parts = plan.swap_in_group(sends)
    query_grad, key_part, value_part, shrink = call(
        bind(score_grad_body),
        [rounded, table, table, shaped((heads, length, size))],
        [attn_grad, query_rows, key_rows, value_rows, states, weights, cum_log, cum_col],
        flops=10 * heads * length * length * size,
    )
    grad_rows = state_out_grad.reshape(width, size)
    two_sided = plan.groups == 2
    tie, swapped = key_part, []
    if two_sided:
        sends = call(
            bind(early_body),
            [piece, shaped((plan.rows + LOG_ROWS, size))] + pieces[2:],
            [*parts, logs, grad_rows, key_part],
            [hold],
            specs=[VMEM] * (plan.members + 2) + [ANY],
        )
        tie = sends[0]
        swapped = [dict(zip(plan.early_ways, plan.swap_in_group(sends, plan.early_ways)))]
    (total,) = call(
        bind(group_grad_body),
        [piece],
        [*parts, logs, tie],
        [hold],
        specs=[VMEM] * (plan.members + 1) + [ANY],
    )
    totals = [total] + plan.from_groups(total)
    sends = call(
        bind(reverse_scan_body),
        pieces * (1 if two_sided else 2),
        [*parts, *totals, logs, all_logs, grad_rows, swapped[0][plan.early_ways[1]] if two_sided else tie],
        [hold_groups, hold],
        specs=[VMEM] * (plan.members + plan.groups + 3) + [ANY],
    )
    for first in range(0, len(sends), plan.members):
        pieces_back = plan.swap_in_group(sends[first : first + plan.members], plan.late_ways)
        swapped.append(dict(zip(plan.late_ways, pieces_back)))
    outs = []
    for ways in ([0], plan.late_ways[1:]):
        if not ways:
            continue
        operands = [
            *[swapped[0][way] for way in plan.early_ways if way in ways],
            *[swapped[1][way] for way in ways],
            key_part,
            value_part,
            key_rows,
            value_rows,
            shrink,
            summary,
            before,
            logs,
        ]
        count = len(operands)
        outs = call(
            bind(finish_body, ways),
            [rounded, rounded, shaped((width, size))],
            [*operands, *outs],
            [
                pltpu.VMEM((length, len(ways) * plan.rows), BF16),
                pltpu.VMEM((length, len(ways) * plan.rows), BF16),
                pltpu.VMEM((len(ways) * plan.rows, size), F32),
                pltpu.SemaphoreType.DMA((3 * len(ways),)),
            ],
            specs=[VMEM] * count + [HBM] * len(outs),
            out_specs=[HBM] * 3,
            aliases={count + i: i for i in range(len(outs))},
        )
    key_grad, value_grad, state_in_grad = outs
    return (query_grad, key_grad, value_grad, state_in_grad.reshape(heads, size, size))


def solution(mesh):
    return jax.shard_map(
        on_device,
        mesh=mesh,
        in_specs=(
            P("seq", "head"),
            P("seq", "head"),
            P("seq", "head"),
            P("head", "seq"),
            P("seq", "head"),
            P("head"),
            P("head", None, None),
            P("head", None, None),
        ),
        out_specs=(P("seq", "head"), P("seq", "head"), P("seq", "head"), P("head", None, None)),
        check_vma=False,
    )
```

```python
import functools

import jax
import jax.numpy as jnp
from jax import lax
from jax.experimental import pallas as pl
from jax.experimental.pallas import tpu as pltpu
from jax.sharding import PartitionSpec as P

EPSILON = 1e-06
F32 = jnp.float32
BF16 = jnp.bfloat16
LOG_ROWS = 8
LONG = 10**10
MASKED = -1e30

CONTRACT_ROWS = (((0,), (0,)), ((), ()))
CONTRACT_COLS = (((1,), (1,)), ((), ()))
VMEM = pl.BlockSpec(memory_space=pltpu.VMEM)
HBM = pl.BlockSpec(memory_space=pltpu.HBM)
ANY = pl.BlockSpec(memory_space=pl.ANY)


def call(body, outs, operands, scratch=(), flops=0, specs=None, out_specs=None, aliases=None):
    return pl.pallas_call(
        body,
        out_shape=outs,
        in_specs=specs or [VMEM] * len(operands),
        out_specs=out_specs or [VMEM] * len(outs),
        scratch_shapes=list(scratch),
        input_output_aliases=aliases or {},
        compiler_params=pltpu.CompilerParams(vmem_limit_bytes=24 * 1024 * 1024),
        cost_estimate=pl.CostEstimate(flops=flops, bytes_accessed=0, transcendentals=0),
    )(*operands)


def shaped(shape, dtype=F32):
    return jax.ShapeDtypeStruct(shape, dtype)


def dot(a, b, dims=(((1,), (0,)), ((), ()))):
    return lax.dot_general(a, b, dims, preferred_element_type=F32)


def split(x):
    high = x.astype(BF16)
    rest = x - high.astype(F32)
    middle = rest.astype(BF16)
    low = (rest - middle.astype(F32)).astype(BF16)
    return jnp.concatenate([high, middle, low], axis=1)


def thrice(x):
    return jnp.concatenate([x, x, x], axis=1)


def lanes(h, size):
    return slice(h * size, (h + 1) * size)


def causal_mask(length):
    row = lax.broadcasted_iota(jnp.int32, (length, length), 0)
    col = lax.broadcasted_iota(jnp.int32, (length, length), 1)
    return row >= col


class Plan:
    def __init__(self, heads, size, blocks):
        self.heads, self.size, self.blocks = heads, size, blocks
        self.members = next(m for m in (4, 2, 1) if heads % m == 0 and blocks % m == 0)
        self.groups = blocks // self.members
        self.own = heads // self.members
        self.rows = self.own * size
        self.chunks = self.own
        self.chunk_rows = self.rows // self.chunks
        self.near = [way for way in range(self.members) if way.bit_count() == 1]
        self.far = [way for way in range(self.members) if way.bit_count() > 1]
        self.ways = [0] + self.far + self.near
        self.early_ways = [0] + self.near[::-1] + self.far
        self.late_ways = [0] + self.near[::-1] + self.far

    def member(self):
        return lax.rem(lax.axis_index("seq"), self.members)

    def group(self):
        return lax.div(lax.axis_index("seq"), self.members)

    def peer(self, k):
        return self.toward(self.ways[k])

    def toward(self, way):
        return lax.bitwise_xor(self.member(), way)

    def rows_of(self, member):
        return pl.ds(pl.multiple_of(member * self.rows, self.rows), self.rows)

    def chunk_of(self, member, chunk):
        start = member * self.rows + chunk * self.chunk_rows
        return pl.ds(pl.multiple_of(start, self.chunk_rows), self.chunk_rows)

    def swap(self, piece, way):
        span = self.members
        pairs = [(i, i // span * span + (i % span ^ way)) for i in range(self.blocks)]
        return lax.ppermute(piece, "seq", pairs) if way else piece

    def swap_in_group(self, pieces, order=None):
        return [self.swap(piece, way) for way, piece in zip(order or self.ways, pieces)]

    def first_messages(self):
        return [(way, c) for c in range(self.chunks) for way in self.ways]

    def last_messages(self):
        cuts = [(way, c) for c in range(self.chunks) for way in [0] + self.near]
        return cuts + [(way, None) for way in self.far]

    def from_groups(self, piece):
        return [
            lax.ppermute(
                piece,
                "seq",
                [(i, (i + step * self.members) % self.blocks) for i in range(self.blocks)],
            )
            for step in range(1, self.groups)
        ]


def own_decays(plan, log_tile_ref, chunk=None):
    count = plan.own if chunk is None else plan.own // plan.chunks
    first = plan.member() * plan.own + (0 if chunk is None else chunk * count)
    rows = [log_tile_ref[pl.ds(first + j, 1), :] for j in range(count)]
    return jnp.concatenate([jnp.broadcast_to(jnp.exp(row), (plan.size, plan.size)) for row in rows])


def summary_body(plan, key_hbm, value_hbm, decay_hbm, *refs):
    count = len(plan.first_messages())
    send_refs, refs = refs[:count], refs[count:]
    cum_ref, cum_col_ref, held_ref, key_ref, value_ref, decay_ref, sems = refs
    length, heads, size = key_ref.shape[0], plan.heads, plan.size
    copies = [
        pltpu.make_async_copy(source, target, sems.at[i])
        for i, (source, target) in enumerate(
            [(decay_hbm, decay_ref), (key_hbm, key_ref), (value_hbm, value_ref)]
        )
    ]
    for copy in copies:
        copy.start()
    causal = thrice(jnp.where(causal_mask(length), 1.0, 0.0).astype(BF16))
    copies[0].wait()
    decay = split(decay_ref[...])
    cum_col = dot(causal, decay, CONTRACT_COLS)
    cum_row = dot(decay, causal, CONTRACT_COLS)
    cum_ref[...] = cum_row
    cum_col_ref[...] = cum_col
    shrink = jnp.exp(cum_col[length - 1 : length, :] - cum_col)
    copies[1].wait()
    copies[2].wait()
    for h in range(heads):
        key_decayed = (key_ref[:, lanes(h, size)].astype(F32) * shrink[:, h : h + 1]).astype(BF16)
        held_ref[h * size : (h + 1) * size] = dot(
            key_decayed, value_ref[:, lanes(h, size)], CONTRACT_ROWS
        )
    log_tile = jnp.broadcast_to(cum_row[:, length - 1 : length], (heads, size))
    if heads < LOG_ROWS:
        log_tile = jnp.concatenate([log_tile, jnp.zeros((LOG_ROWS - heads, size), F32)])
    for (way, chunk), send_ref in zip(plan.first_messages(), send_refs):
        send_ref[: plan.chunk_rows] = held_ref[plan.chunk_of(plan.toward(way), chunk)]
        if chunk == 0:
            send_ref[plan.chunk_rows :] = log_tile


def group_total_body(plan, chunk, *refs):
    part_refs, refs = refs[: plan.members], refs[plan.members :]
    rows = plan.chunk_rows
    if chunk == 0:
        total_ref, logs_ref = refs[:2]
        for k, part_ref in enumerate(part_refs):
            logs_ref[plan.peer(k)] = part_ref[rows:]
        total_ref[rows:] = sum(logs_ref[b] for b in range(plan.members))
    else:
        logs_ref, total_ref = refs[:2]
    held_ref = refs[2]
    for way, part_ref in zip(plan.ways, part_refs):
        held_ref[plan.toward(way)] = part_ref[:rows]
    total = jnp.zeros((rows, plan.size), F32)
    for b in range(plan.members):
        total = own_decays(plan, logs_ref.at[b], chunk) * total + held_ref[b]
    total_ref[:rows] = total


def stage_groups(plan, total_refs, held_ref):
    rows = held_ref.shape[1]
    for step, total_ref in enumerate(total_refs):
        held_ref[lax.rem(plan.group() - step + plan.groups, plan.groups)] = total_ref[:rows]


def forward_scan_body(plan, chunk, *refs):
    last = chunk == plan.chunks - 1
    part_refs, refs = refs[: plan.members], refs[plan.members :]
    total_refs, refs = refs[: plan.groups], refs[plan.groups :]
    (state_ref, logs_ref), refs = refs[:2], refs[2:]
    rows = plan.chunk_rows
    if chunk > 0:
        group_logs_ref, refs = refs[0], refs[1:]
    far_parts = chunk * len(plan.far) if last else 0
    far_refs, refs = refs[:far_parts], refs[far_parts:]
    send_refs, refs = refs[: plan.members], refs[plan.members :]
    if chunk == 0:
        before_ref, group_logs_ref = refs[:2]
        for step, total_ref in enumerate(total_refs):
            group = lax.rem(plan.group() - step + plan.groups, plan.groups)
            group_logs_ref[group] = total_ref[rows:]
        before = jnp.zeros((LOG_ROWS, plan.size), F32)
        for group in range(plan.groups - 1):
            before += jnp.where(group < plan.group(), group_logs_ref[group], 0.0)
        for b in range(plan.members - 1):
            before += jnp.where(b < plan.member(), logs_ref[b], 0.0)
        before_ref[...] = before
    groups_ref, held_ref = refs[-2:]
    stage_groups(plan, total_refs, groups_ref)
    state = state_ref[plan.chunk_of(plan.member(), chunk)]
    for group in range(plan.groups - 1):
        after = own_decays(plan, group_logs_ref.at[group], chunk) * state + groups_ref[group]
        state = jnp.where(group < plan.group(), after, state)
    for way, part_ref in zip(plan.ways, part_refs):
        held_ref[plan.toward(way)] = part_ref[:rows]
    for b in range(plan.members):
        summary = held_ref[b]
        held_ref[b] = state
        state = own_decays(plan, logs_ref.at[b], chunk) * state + summary
    for i, (way, send_ref) in enumerate(zip(plan.ways, send_refs)):
        if way in plan.far and last:
            for c in range(chunk):
                send_ref[c * rows : (c + 1) * rows] = far_refs[c * len(plan.far) + i - 1][...]
            send_ref[chunk * rows :] = held_ref[plan.toward(way)]
        else:
            send_ref[...] = held_ref[plan.toward(way)]


def suffixes(plan, held_ref, logs_ref, grad):
    found = []
    for b in reversed(range(plan.members)):
        found.append(grad)
        grad = own_decays(plan, logs_ref.at[b]) * grad + held_ref[b]
    return found[::-1], grad


def prefixes(plan, held_ref, logs_ref, total, scale):
    found = []
    for b in range(plan.members):
        found.append(total)
        total = total + scale * held_ref[b]
        scale = scale * own_decays(plan, logs_ref.at[b])
    return found


def early_body(plan, *refs):
    part_refs, refs = refs[: plan.members], refs[plan.members :]
    (logs_ref, grad_ref), send_refs, held_ref = refs[:2], refs[3:-1], refs[-1]
    for k, part_ref in enumerate(part_refs):
        held_ref[plan.peer(k)] = part_ref[...]
    first = plan.group() == 0
    zero = jnp.zeros((plan.rows, plan.size), F32)
    before = prefixes(plan, held_ref, logs_ref, zero, zero + 1.0)
    after = suffixes(plan, held_ref, logs_ref, grad_ref[plan.rows_of(plan.member())])[0]
    for b in range(plan.members):
        held_ref[b] = jnp.where(first, before[b], after[b])
    for way, send_ref in zip(plan.early_ways, send_refs):
        send_ref[: plan.rows] = held_ref[plan.toward(way)]
        if send_ref.shape[0] > plan.rows:
            send_ref[plan.rows :] = logs_ref[0]


def group_grad_body(plan, *refs):
    part_refs, (logs_ref, _, total_ref, held_ref) = refs[: plan.members], refs[plan.members :]
    for k, part_ref in enumerate(part_refs):
        held_ref[plan.peer(k)] = part_ref[...]
    zero = jnp.zeros((plan.rows, plan.size), F32)
    total_ref[...] = suffixes(plan, held_ref, logs_ref, zero)[1]


def reverse_scan_body(plan, *refs):
    part_refs, refs = refs[: plan.members], refs[plan.members :]
    total_refs, refs = refs[: plan.groups], refs[plan.groups :]
    (logs_ref, group_logs_ref, grad_ref, _), refs = refs[:4], refs[4:]
    send_refs, (groups_ref, held_ref) = refs[:-2], refs[-2:]
    stage_groups(plan, total_refs, groups_ref)
    for k, part_ref in enumerate(part_refs):
        held_ref[plan.peer(k)] = part_ref[...]
    grad = grad_ref[plan.rows_of(plan.member())]
    leaving = grad
    for group in reversed(range(plan.groups)):
        leaving = jnp.where(group == plan.group(), grad, leaving)
        grad = own_decays(plan, group_logs_ref.at[group]) * grad + groups_ref[group]
    total = jnp.zeros((plan.rows, plan.size), F32)
    scale = total + 1.0
    for group in range(plan.groups - 1):
        earlier = group < plan.group()
        total = jnp.where(earlier, total + scale * groups_ref[group], total)
        decays = own_decays(plan, group_logs_ref.at[group])
        scale = jnp.where(earlier, scale * decays, scale)
    after = suffixes(plan, held_ref, logs_ref, leaving)[0]
    before = prefixes(plan, held_ref, logs_ref, total, scale)
    if plan.groups == 2:
        first = plan.group() == 0
        found = [[jnp.where(first, after[b], before[b]) for b in range(plan.members)]]
    else:
        found = [before, after]
    for i, values in enumerate(found):
        for b in range(plan.members):
            held_ref[b] = values[b]
        for k in range(plan.members):
            send_refs[i * plan.members + k][...] = held_ref[plan.toward(plan.late_ways[k])]


def decay_matrix(cum_ref, cum_col, causal, h):
    spread = cum_col[:, h : h + 1] - cum_ref[h : h + 1, :]
    return jnp.exp(jnp.where(causal, jnp.minimum(spread, 0.0), MASKED))


def intra_body(
    plan,
    query_ref,
    key_ref,
    value_ref,
    cum_ref,
    cum_col_ref,
    upstream_ref,
    gain_ref,
    *refs,
):
    weight_ref, intra_ref, gained_ref, query_decayed_ref = refs[-4:]
    causal = causal_mask(query_ref.shape[0])
    cum_col = cum_col_ref[...]
    growth = jnp.exp(cum_col)
    for h in range(plan.heads):
        cut = lanes(h, plan.size)
        query = query_ref[:, cut]
        scores = dot(query, key_ref[:, cut], CONTRACT_COLS)
        weights = (scores * decay_matrix(cum_ref, cum_col, causal, h)).astype(BF16)
        weight_ref[h] = weights
        intra_ref[:, cut] = dot(weights, value_ref[:, cut])
        gained_ref[:, cut] = gain_ref[:, cut] * upstream_ref[:, cut].astype(F32)
        query_decayed = query.astype(F32) * growth[:, h : h + 1]
        query_decayed_ref[h] = jnp.transpose(query_decayed).astype(BF16)


def attended_body(plan, *refs):
    count = len(plan.last_messages())
    state_refs, refs = refs[:count], refs[count:]
    intra_ref, query_ref, cum_col_ref, gained_ref = refs[:4]
    attended_ref, sums_ref, states_ref = refs[4:]
    size, length = plan.size, query_ref.shape[0]
    for (way, chunk), state_ref in zip(plan.last_messages(), state_refs):
        member = plan.toward(way)
        part = plan.rows_of(member) if chunk is None else plan.chunk_of(member, chunk)
        states_ref[part] = state_ref[...].astype(BF16)
    growth = jnp.exp(cum_col_ref[...])
    square = jnp.zeros((length, size), F32)
    inner = jnp.zeros((length, size), F32)
    for h in range(plan.heads):
        cut = lanes(h, size)
        carried = dot(query_ref[:, cut], states_ref[cut])
        attended = intra_ref[:, cut] + growth[:, h : h + 1] * carried
        attended_ref[:, cut] = attended
        square += attended * attended
        inner += gained_ref[:, cut] * attended
    ones = jnp.ones((8, 3 * size), BF16)
    is_square = lax.broadcasted_iota(jnp.int32, (8, length), 0) == 0
    sums_ref[...] = jnp.where(
        is_square,
        dot(ones, split(square), CONTRACT_COLS),
        dot(ones, split(inner), CONTRACT_COLS),
    )


def attn_grad_body(plan, parties, *refs):
    sums_refs, refs = refs[:parties], refs[parties:]
    attended_ref, query_decayed_ref, gained_ref, attn_grad_ref, held_ref = refs[:5]
    send_refs = refs[5:]
    size, length = plan.size, attended_ref.shape[0]
    feature_count = plan.heads * size * parties
    sums = sum(ref[...] for ref in sums_refs)
    inv_row = lax.rsqrt(sums[:1] / feature_count + EPSILON)
    coefficient_row = sums[1:2] * inv_row * inv_row * inv_row / feature_count
    is_inverse = lax.broadcasted_iota(jnp.int32, (8, length), 0) == 0
    columns = jnp.transpose(jnp.where(is_inverse, inv_row, coefficient_row))
    inv_rms = jnp.broadcast_to(columns[:, :1], (length, size))
    coefficient = jnp.broadcast_to(columns[:, 1:2], (length, size))
    for h in range(plan.heads):
        cut = lanes(h, size)
        attn_grad = gained_ref[:, cut] * inv_rms - attended_ref[:, cut] * coefficient
        attn_grad = attn_grad.astype(BF16)
        attn_grad_ref[:, cut] = attn_grad
        held_ref[cut] = dot(query_decayed_ref[h], attn_grad)
    for k, send_ref in enumerate(send_refs):
        send_ref[...] = held_ref[plan.rows_of(plan.peer(k))]


def score_grad_body(
    plan,
    attn_grad_ref,
    query_ref,
    key_ref,
    value_ref,
    states_ref,
    weight_ref,
    cum_ref,
    cum_col_ref,
    query_grad_ref,
    key_part_ref,
    value_part_ref,
    shrink_ref,
):
    length = query_ref.shape[0]
    causal = causal_mask(length)
    cum_col = cum_col_ref[...]
    growth = jnp.exp(cum_col)
    shrink = jnp.exp(cum_col[length - 1 : length, :] - cum_col)
    for h in range(plan.heads):
        cut = lanes(h, plan.size)
        attn_grad = attn_grad_ref[:, cut]
        scores = dot(attn_grad, value_ref[:, cut], CONTRACT_COLS)
        score_grad = (scores * decay_matrix(cum_ref, cum_col, causal, h)).astype(BF16)
        carried = dot(attn_grad, states_ref[cut], CONTRACT_COLS)
        query_grad = dot(score_grad, key_ref[:, cut]) + growth[:, h : h + 1] * carried
        query_grad_ref[:, cut] = query_grad.astype(BF16)
        key_part_ref[:, cut] = dot(score_grad, query_ref[:, cut], CONTRACT_ROWS)
        value_part_ref[:, cut] = dot(weight_ref[h], attn_grad, CONTRACT_ROWS)
        shrink_ref[h] = jnp.broadcast_to(shrink[:, h : h + 1], (length, plan.size))


def finish_body(plan, ways, *refs):
    count = len(ways)
    early_refs = dict(zip([way for way in plan.early_ways if way in ways], refs[:count]))
    late_refs = dict(zip(ways, refs[count : 2 * count]))
    refs = refs[2 * count :]
    key_part_ref, value_part_ref, key_ref, value_ref, shrink_ref = refs[:5]
    summary_ref, before_ref, logs_ref = refs[5:8]
    key_out, value_out, total_out, key_grad_ref, value_grad_ref, total_ref, sems = refs[-7:]
    size, rows = plan.size, plan.rows
    first = plan.group() == 0
    copies = []
    for i, way in enumerate(ways):
        owner = plan.toward(way)
        before, after = early_refs[way][:rows], late_refs[way][:rows]
        if plan.groups == 2:
            before, after = jnp.where(first, before, after), jnp.where(first, after, before)
        for j in range(plan.own):
            head = owner * plan.own + j
            part = pl.ds(pl.multiple_of(head * size, size), size)
            cut = slice(i * rows + j * size, i * rows + (j + 1) * size)
            grads = after[lanes(j, size)]
            log_before = before_ref[pl.ds(head, 1)]
            scale = jnp.exp(log_before)
            scale_next = jnp.exp(log_before + logs_ref[plan.member(), pl.ds(head, 1)])
            total_ref[cut] = (
                before[lanes(j, size)] + scale * summary_ref[part] + scale_next * grads
            )
            grads = grads.astype(BF16)
            key_state = dot(value_ref[:, part], grads, CONTRACT_COLS)
            key_grad_ref[:, cut] = (key_part_ref[:, part] + shrink_ref[head] * key_state).astype(BF16)
            value_state = dot(key_ref[:, part], grads)
            value_grad_ref[:, cut] = (value_part_ref[:, part] + shrink_ref[head] * value_state).astype(BF16)
        done, place = lanes(i, rows), plan.rows_of(owner)
        for source, target in [
            (total_ref.at[done], total_out.at[place]),
            (key_grad_ref.at[:, done], key_out.at[:, place]),
            (value_grad_ref.at[:, done], value_out.at[:, place]),
        ]:
            copies.append(pltpu.make_async_copy(source, target, sems.at[len(copies)]))
            copies[-1].start()
    for copy in copies:
        copy.wait()


def on_device(
    query_rows, key_rows, value_rows, log_decay, out_grad, norm_gain, state_in, state_out_grad
):
    heads, length = log_decay.shape
    size = state_in.shape[1]
    width = heads * size
    parties = lax.axis_size("head")
    plan = Plan(heads, size, lax.axis_size("seq"))
    bind = lambda body, *extra: functools.partial(body, plan, *extra)
    gain = norm_gain.reshape(1, width)
    piece = shaped((plan.rows, size))
    pieces = [piece] * plan.members
    chunk_piece = shaped((plan.chunk_rows, size))
    chunk_pieces = [chunk_piece] * plan.members
    logged = shaped((plan.chunk_rows + LOG_ROWS, size))
    block_logs = shaped((plan.members, LOG_ROWS, size))
    group_logs = shaped((plan.groups, LOG_ROWS, size))
    table = shaped((length, width))
    rounded = shaped((length, width), BF16)
    hold = pltpu.VMEM((plan.members, plan.rows, size), F32)
    hold_groups = pltpu.VMEM((plan.groups, plan.rows, size), F32)
    hold_chunk = pltpu.VMEM((plan.members, plan.chunk_rows, size), F32)
    hold_chunk_groups = pltpu.VMEM((plan.groups, plan.chunk_rows, size), F32)
    chunks = range(plan.chunks)
    state_rows = state_in.reshape(width, size)

    messages = plan.first_messages()
    *sends, cum_log, cum_col = call(
        bind(summary_body),
        [chunk_piece if chunk else logged for _, chunk in messages]
        + [shaped((heads, length)), shaped((length, heads))],
        [pltpu.with_memory_space_constraint(x, pltpu.HBM) for x in (key_rows, value_rows, log_decay)],
        [
            pltpu.VMEM((width, size), F32),
            pltpu.VMEM((length, width), BF16),
            pltpu.VMEM((length, width), BF16),
            pltpu.VMEM((heads, length), F32),
            pltpu.SemaphoreType.DMA((3,)),
        ],
        specs=[HBM] * 3,
    )
    received = {key: plan.swap(send, key[0]) for key, send in zip(messages, sends)}
    parts = [[received[way, c] for way in plan.ways] for c in chunks]
    totals = []
    for c in chunks:
        if c == 0:
            total, logs = call(
                bind(group_total_body, c), [logged, block_logs], parts[c], [hold_chunk]
            )
        else:
            (total,) = call(
                bind(group_total_body, c),
                [chunk_piece],
                [*parts[c], logs],
                [hold_chunk],
                flops=LONG,
            )
        totals.append([total] + plan.from_groups(total))
    states = {}
    far_parts = []
    for c in chunks:
        last = c == plan.chunks - 1
        operands = [*parts[c], *totals[c], state_rows, logs]
        outs = [piece if way in plan.far and last else chunk_piece for way in plan.ways]
        if c == 0:
            outs += [shaped((LOG_ROWS, size)), group_logs]
        else:
            operands += [all_logs]
        sends = call(
            bind(forward_scan_body, c),
            outs,
            operands + (far_parts if last else []),
            [hold_chunk_groups, hold_chunk],
        )
        if c == 0:
            before, all_logs = sends[plan.members :]
        for way, send in zip(plan.ways, sends):
            if way not in plan.far:
                states[way, c] = plan.swap(send, way)
            elif last:
                states[way, None] = plan.swap(send, way)
            else:
                far_parts.append(send)
    early = [states[way, 0] for way in plan.near] if plan.chunks > 1 else []
    weights, intra, gained, query_decayed = call(
        bind(intra_body),
        [
            shaped((heads, length, length), BF16),
            table,
            table,
            shaped((heads, size, length), BF16),
        ],
        [query_rows, key_rows, value_rows, cum_log, cum_col, out_grad, gain, *early],
        specs=[VMEM] * 7 + [ANY] * len(early),
        flops=LONG // 10,
    )
    attended, sums, states = call(
        bind(attended_body),
        [table, shaped((8, length)), shaped((width, size), BF16)],
        [*[states[key] for key in plan.last_messages()], intra, query_rows, cum_col, gained],
    )
    all_sums = [sums] + [
        lax.ppermute(sums, "head", [(i, (i + step) % parties) for i in range(parties)])
        for step in range(1, parties)
    ]
    attn_grad, summary, *sends = call(
        bind(attn_grad_body, parties),
        [rounded, shaped((width, size))] + pieces,
        [*all_sums, attended, query_decayed, gained],
    )
    parts = plan.swap_in_group(sends)
    query_grad, key_part, value_part, shrink = call(
        bind(score_grad_body),
        [rounded, table, table, shaped((heads, length, size))],
        [attn_grad, query_rows, key_rows, value_rows, states, weights, cum_log, cum_col],
        flops=10 * heads * length * length * size,
    )
    grad_rows = state_out_grad.reshape(width, size)
    two_sided = plan.groups == 2
    tie, swapped = key_part, []
    if two_sided:
        sends = call(
            bind(early_body),
            [piece, shaped((plan.rows + LOG_ROWS, size))] + pieces[2:],
            [*parts, logs, grad_rows, key_part],
            [hold],
            specs=[VMEM] * (plan.members + 2) + [ANY],
        )
        tie = sends[0]
        swapped = [dict(zip(plan.early_ways, plan.swap_in_group(sends, plan.early_ways)))]
    (total,) = call(
        bind(group_grad_body),
        [piece],
        [*parts, logs, tie],
        [hold],
        specs=[VMEM] * (plan.members + 1) + [ANY],
    )
    totals = [total] + plan.from_groups(total)
    sends = call(
        bind(reverse_scan_body),
        pieces * (1 if two_sided else 2),
        [*parts, *totals, logs, all_logs, grad_rows, swapped[0][plan.early_ways[1]] if two_sided else tie],
        [hold_groups, hold],
        specs=[VMEM] * (plan.members + plan.groups + 3) + [ANY],
    )
    for first in range(0, len(sends), plan.members):
        pieces_back = plan.swap_in_group(sends[first : first + plan.members], plan.late_ways)
        swapped.append(dict(zip(plan.late_ways, pieces_back)))
    outs = []
    for ways in ([0], plan.late_ways[1:]):
        if not ways:
            continue
        operands = [
            *[swapped[0][way] for way in plan.early_ways if way in ways],
            *[swapped[1][way] for way in ways],
            key_part,
            value_part,
            key_rows,
            value_rows,
            shrink,
            summary,
            before,
            logs,
        ]
        count = len(operands)
        outs = call(
            bind(finish_body, ways),
            [rounded, rounded, shaped((width, size))],
            [*operands, *outs],
            [
                pltpu.VMEM((length, len(ways) * plan.rows), BF16),
                pltpu.VMEM((length, len(ways) * plan.rows), BF16),
                pltpu.VMEM((len(ways) * plan.rows, size), F32),
                pltpu.SemaphoreType.DMA((3 * len(ways),)),
            ],
            specs=[VMEM] * count + [HBM] * len(outs),
            out_specs=[HBM] * 3,
            aliases={count + i: i for i in range(len(outs))},
        )
    key_grad, value_grad, state_in_grad = outs
    return (query_grad, key_grad, value_grad, state_in_grad.reshape(heads, size, size))


def solution(mesh):
    return jax.shard_map(
        on_device,
        mesh=mesh,
        in_specs=(
            P("seq", "head"),
            P("seq", "head"),
            P("seq", "head"),
            P("head", "seq"),
            P("seq", "head"),
            P("head"),
            P("head", None, None),
            P("head", None, None),
        ),
        out_specs=(P("seq", "head"), P("seq", "head"), P("seq", "head"), P("head", None, None)),
        check_vma=False,
    )
```

```python
import functools

import jax
import jax.numpy as jnp
from jax import lax
from jax.experimental import pallas as pl
from jax.experimental.pallas import tpu as pltpu
from jax.sharding import PartitionSpec as P

EPSILON = 1e-06
F32 = jnp.float32
BF16 = jnp.bfloat16
LOG_ROWS = 8
LONG = 10**10
MASKED = -1e30

CONTRACT_ROWS = (((0,), (0,)), ((), ()))
CONTRACT_COLS = (((1,), (1,)), ((), ()))
VMEM = pl.BlockSpec(memory_space=pltpu.VMEM)
HBM = pl.BlockSpec(memory_space=pltpu.HBM)
ANY = pl.BlockSpec(memory_space=pl.ANY)


def call(body, outs, operands, scratch=(), flops=0, specs=None, out_specs=None, aliases=None):
    return pl.pallas_call(
        body,
        out_shape=outs,
        in_specs=specs or [VMEM] * len(operands),
        out_specs=out_specs or [VMEM] * len(outs),
        scratch_shapes=list(scratch),
        input_output_aliases=aliases or {},
        compiler_params=pltpu.CompilerParams(vmem_limit_bytes=24 * 1024 * 1024),
        cost_estimate=pl.CostEstimate(flops=flops, bytes_accessed=0, transcendentals=0),
    )(*operands)


def shaped(shape, dtype=F32):
    return jax.ShapeDtypeStruct(shape, dtype)


def dot(a, b, dims=(((1,), (0,)), ((), ()))):
    return lax.dot_general(a, b, dims, preferred_element_type=F32)


def split(x):
    high = x.astype(BF16)
    rest = x - high.astype(F32)
    middle = rest.astype(BF16)
    low = (rest - middle.astype(F32)).astype(BF16)
    return jnp.concatenate([high, middle, low], axis=1)


def thrice(x):
    return jnp.concatenate([x, x, x], axis=1)


def lanes(h, size):
    return slice(h * size, (h + 1) * size)


def causal_mask(length):
    row = lax.broadcasted_iota(jnp.int32, (length, length), 0)
    col = lax.broadcasted_iota(jnp.int32, (length, length), 1)
    return row >= col


class Plan:
    def __init__(self, heads, size, blocks):
        self.heads, self.size, self.blocks = heads, size, blocks
        self.members = next(m for m in (4, 2, 1) if heads % m == 0 and blocks % m == 0)
        self.groups = blocks // self.members
        self.own = heads // self.members
        self.rows = self.own * size
        self.chunks = self.own
        self.chunk_rows = self.rows // self.chunks
        self.near = [way for way in range(self.members) if way.bit_count() == 1]
        self.far = [way for way in range(self.members) if way.bit_count() > 1]
        self.ways = [0] + self.far + self.near
        self.early_ways = [0] + self.near + self.far
        self.late_ways = [0] + self.far + self.near[::-1]

    def member(self):
        return lax.rem(lax.axis_index("seq"), self.members)

    def group(self):
        return lax.div(lax.axis_index("seq"), self.members)

    def peer(self, k):
        return self.toward(self.ways[k])

    def toward(self, way):
        return lax.bitwise_xor(self.member(), way)

    def rows_of(self, member):
        return pl.ds(pl.multiple_of(member * self.rows, self.rows), self.rows)

    def chunk_of(self, member, chunk):
        start = member * self.rows + chunk * self.chunk_rows
        return pl.ds(pl.multiple_of(start, self.chunk_rows), self.chunk_rows)

    def swap(self, piece, way):
        span = self.members
        pairs = [(i, i // span * span + (i % span ^ way)) for i in range(self.blocks)]
        return lax.ppermute(piece, "seq", pairs) if way else piece

    def swap_in_group(self, pieces, order=None):
        return [self.swap(piece, way) for way, piece in zip(order or self.ways, pieces)]

    def first_messages(self):
        return [(way, c) for c in range(self.chunks) for way in self.ways]

    def last_messages(self):
        cuts = [(way, c) for c in range(self.chunks) for way in [0] + self.near]
        return cuts + [(way, None) for way in self.far]

    def from_groups(self, piece):
        return [
            lax.ppermute(
                piece,
                "seq",
                [(i, (i + step * self.members) % self.blocks) for i in range(self.blocks)],
            )
            for step in range(1, self.groups)
        ]


def own_decays(plan, log_tile_ref, chunk=None):
    count = plan.own if chunk is None else plan.own // plan.chunks
    first = plan.member() * plan.own + (0 if chunk is None else chunk * count)
    rows = [log_tile_ref[pl.ds(first + j, 1), :] for j in range(count)]
    return jnp.concatenate([jnp.broadcast_to(jnp.exp(row), (plan.size, plan.size)) for row in rows])


def summary_body(plan, key_hbm, value_hbm, decay_hbm, *refs):
    count = len(plan.first_messages())
    send_refs, refs = refs[:count], refs[count:]
    cum_ref, cum_col_ref, held_ref, key_ref, value_ref, decay_ref, sems = refs
    length, heads, size = key_ref.shape[0], plan.heads, plan.size
    copies = [
        pltpu.make_async_copy(source, target, sems.at[i])
        for i, (source, target) in enumerate(
            [(decay_hbm, decay_ref), (key_hbm, key_ref), (value_hbm, value_ref)]
        )
    ]
    for copy in copies:
        copy.start()
    causal = thrice(jnp.where(causal_mask(length), 1.0, 0.0).astype(BF16))
    copies[0].wait()
    decay = split(decay_ref[...])
    cum_col = dot(causal, decay, CONTRACT_COLS)
    cum_row = dot(decay, causal, CONTRACT_COLS)
    cum_ref[...] = cum_row
    cum_col_ref[...] = cum_col
    shrink = jnp.exp(cum_col[length - 1 : length, :] - cum_col)
    copies[1].wait()
    copies[2].wait()
    for h in range(heads):
        key_decayed = (key_ref[:, lanes(h, size)].astype(F32) * shrink[:, h : h + 1]).astype(BF16)
        held_ref[h * size : (h + 1) * size] = dot(
            key_decayed, value_ref[:, lanes(h, size)], CONTRACT_ROWS
        )
    log_tile = jnp.broadcast_to(cum_row[:, length - 1 : length], (heads, size))
    if heads < LOG_ROWS:
        log_tile = jnp.concatenate([log_tile, jnp.zeros((LOG_ROWS - heads, size), F32)])
    for (way, chunk), send_ref in zip(plan.first_messages(), send_refs):
        send_ref[: plan.chunk_rows] = held_ref[plan.chunk_of(plan.toward(way), chunk)]
        if chunk == 0:
            send_ref[plan.chunk_rows :] = log_tile


def group_total_body(plan, chunk, *refs):
    part_refs, refs = refs[: plan.members], refs[plan.members :]
    rows = plan.chunk_rows
    if chunk == 0:
        total_ref, logs_ref = refs[:2]
        for k, part_ref in enumerate(part_refs):
            logs_ref[plan.peer(k)] = part_ref[rows:]
        total_ref[rows:] = sum(logs_ref[b] for b in range(plan.members))
    else:
        logs_ref, total_ref = refs[:2]
    held_ref = refs[2]
    for way, part_ref in zip(plan.ways, part_refs):
        held_ref[plan.toward(way)] = part_ref[:rows]
    total = jnp.zeros((rows, plan.size), F32)
    for b in range(plan.members):
        total = own_decays(plan, logs_ref.at[b], chunk) * total + held_ref[b]
    total_ref[:rows] = total


def stage_groups(plan, total_refs, held_ref):
    rows = held_ref.shape[1]
    for step, total_ref in enumerate(total_refs):
        held_ref[lax.rem(plan.group() - step + plan.groups, plan.groups)] = total_ref[:rows]


def forward_scan_body(plan, chunk, *refs):
    last = chunk == plan.chunks - 1
    part_refs, refs = refs[: plan.members], refs[plan.members :]
    total_refs, refs = refs[: plan.groups], refs[plan.groups :]
    (state_ref, logs_ref), refs = refs[:2], refs[2:]
    rows = plan.chunk_rows
    if chunk > 0:
        group_logs_ref, refs = refs[0], refs[1:]
    far_parts = chunk * len(plan.far) if last else 0
    far_refs, refs = refs[:far_parts], refs[far_parts:]
    send_refs, refs = refs[: plan.members], refs[plan.members :]
    if chunk == 0:
        before_ref, group_logs_ref = refs[:2]
        for step, total_ref in enumerate(total_refs):
            group = lax.rem(plan.group() - step + plan.groups, plan.groups)
            group_logs_ref[group] = total_ref[rows:]
        before = jnp.zeros((LOG_ROWS, plan.size), F32)
        for group in range(plan.groups - 1):
            before += jnp.where(group < plan.group(), group_logs_ref[group], 0.0)
        for b in range(plan.members - 1):
            before += jnp.where(b < plan.member(), logs_ref[b], 0.0)
        before_ref[...] = before
    groups_ref, held_ref = refs[-2:]
    stage_groups(plan, total_refs, groups_ref)
    state = state_ref[plan.chunk_of(plan.member(), chunk)]
    for group in range(plan.groups - 1):
        after = own_decays(plan, group_logs_ref.at[group], chunk) * state + groups_ref[group]
        state = jnp.where(group < plan.group(), after, state)
    for way, part_ref in zip(plan.ways, part_refs):
        held_ref[plan.toward(way)] = part_ref[:rows]
    for b in range(plan.members):
        summary = held_ref[b]
        held_ref[b] = state
        state = own_decays(plan, logs_ref.at[b], chunk) * state + summary
    for i, (way, send_ref) in enumerate(zip(plan.ways, send_refs)):
        if way in plan.far and last:
            for c in range(chunk):
                send_ref[c * rows : (c + 1) * rows] = far_refs[c * len(plan.far) + i - 1][...]
            send_ref[chunk * rows :] = held_ref[plan.toward(way)]
        else:
            send_ref[...] = held_ref[plan.toward(way)]


def suffixes(plan, held_ref, logs_ref, grad):
    found = []
    for b in reversed(range(plan.members)):
        found.append(grad)
        grad = own_decays(plan, logs_ref.at[b]) * grad + held_ref[b]
    return found[::-1], grad


def prefixes(plan, held_ref, logs_ref, total, scale):
    found = []
    for b in range(plan.members):
        found.append(total)
        total = total + scale * held_ref[b]
        scale = scale * own_decays(plan, logs_ref.at[b])
    return found


def early_body(plan, *refs):
    part_refs, refs = refs[: plan.members], refs[plan.members :]
    (logs_ref, grad_ref), send_refs, held_ref = refs[:2], refs[3:-1], refs[-1]
    for k, part_ref in enumerate(part_refs):
        held_ref[plan.peer(k)] = part_ref[...]
    first = plan.group() == 0
    zero = jnp.zeros((plan.rows, plan.size), F32)
    before = prefixes(plan, held_ref, logs_ref, zero, zero + 1.0)
    after = suffixes(plan, held_ref, logs_ref, grad_ref[plan.rows_of(plan.member())])[0]
    for b in range(plan.members):
        held_ref[b] = jnp.where(first, before[b], after[b])
    for way, send_ref in zip(plan.early_ways, send_refs):
        send_ref[: plan.rows] = held_ref[plan.toward(way)]
        if send_ref.shape[0] > plan.rows:
            send_ref[plan.rows :] = logs_ref[0]


def group_grad_body(plan, *refs):
    part_refs, (logs_ref, _, total_ref, held_ref) = refs[: plan.members], refs[plan.members :]
    for k, part_ref in enumerate(part_refs):
        held_ref[plan.peer(k)] = part_ref[...]
    zero = jnp.zeros((plan.rows, plan.size), F32)
    total_ref[...] = suffixes(plan, held_ref, logs_ref, zero)[1]


def reverse_scan_body(plan, *refs):
    part_refs, refs = refs[: plan.members], refs[plan.members :]
    total_refs, refs = refs[: plan.groups], refs[plan.groups :]
    (logs_ref, group_logs_ref, grad_ref, _), refs = refs[:4], refs[4:]
    send_refs, (groups_ref, held_ref) = refs[:-2], refs[-2:]
    stage_groups(plan, total_refs, groups_ref)
    for k, part_ref in enumerate(part_refs):
        held_ref[plan.peer(k)] = part_ref[...]
    grad = grad_ref[plan.rows_of(plan.member())]
    leaving = grad
    for group in reversed(range(plan.groups)):
        leaving = jnp.where(group == plan.group(), grad, leaving)
        grad = own_decays(plan, group_logs_ref.at[group]) * grad + groups_ref[group]
    total = jnp.zeros((plan.rows, plan.size), F32)
    scale = total + 1.0
    for group in range(plan.groups - 1):
        earlier = group < plan.group()
        total = jnp.where(earlier, total + scale * groups_ref[group], total)
        decays = own_decays(plan, group_logs_ref.at[group])
        scale = jnp.where(earlier, scale * decays, scale)
    after = suffixes(plan, held_ref, logs_ref, leaving)[0]
    before = prefixes(plan, held_ref, logs_ref, total, scale)
    if plan.groups == 2:
        first = plan.group() == 0
        found = [[jnp.where(first, after[b], before[b]) for b in range(plan.members)]]
    else:
        found = [before, after]
    for i, values in enumerate(found):
        for b in range(plan.members):
            held_ref[b] = values[b]
        for k in range(plan.members):
            send_refs[i * plan.members + k][...] = held_ref[plan.toward(plan.late_ways[k])]


def decay_matrix(cum_ref, cum_col, causal, h):
    spread = cum_col[:, h : h + 1] - cum_ref[h : h + 1, :]
    return jnp.exp(jnp.where(causal, jnp.minimum(spread, 0.0), MASKED))


def intra_body(
    plan,
    query_ref,
    key_ref,
    value_ref,
    cum_ref,
    cum_col_ref,
    upstream_ref,
    gain_ref,
    *refs,
):
    weight_ref, intra_ref, gained_ref, query_decayed_ref = refs[-4:]
    causal = causal_mask(query_ref.shape[0])
    cum_col = cum_col_ref[...]
    growth = jnp.exp(cum_col)
    for h in range(plan.heads):
        cut = lanes(h, plan.size)
        query = query_ref[:, cut]
        scores = dot(query, key_ref[:, cut], CONTRACT_COLS)
        weights = (scores * decay_matrix(cum_ref, cum_col, causal, h)).astype(BF16)
        weight_ref[h] = weights
        intra_ref[:, cut] = dot(weights, value_ref[:, cut])
        gained_ref[:, cut] = gain_ref[:, cut] * upstream_ref[:, cut].astype(F32)
        query_decayed = query.astype(F32) * growth[:, h : h + 1]
        query_decayed_ref[h] = jnp.transpose(query_decayed).astype(BF16)


def attended_body(plan, *refs):
    count = len(plan.last_messages())
    state_refs, refs = refs[:count], refs[count:]
    intra_ref, query_ref, cum_col_ref, gained_ref = refs[:4]
    attended_ref, sums_ref, states_ref = refs[4:]
    size, length = plan.size, query_ref.shape[0]
    for (way, chunk), state_ref in zip(plan.last_messages(), state_refs):
        member = plan.toward(way)
        part = plan.rows_of(member) if chunk is None else plan.chunk_of(member, chunk)
        states_ref[part] = state_ref[...].astype(BF16)
    growth = jnp.exp(cum_col_ref[...])
    square = jnp.zeros((length, size), F32)
    inner = jnp.zeros((length, size), F32)
    for h in range(plan.heads):
        cut = lanes(h, size)
        carried = dot(query_ref[:, cut], states_ref[cut])
        attended = intra_ref[:, cut] + growth[:, h : h + 1] * carried
        attended_ref[:, cut] = attended
        square += attended * attended
        inner += gained_ref[:, cut] * attended
    ones = jnp.ones((8, 3 * size), BF16)
    is_square = lax.broadcasted_iota(jnp.int32, (8, length), 0) == 0
    sums_ref[...] = jnp.where(
        is_square,
        dot(ones, split(square), CONTRACT_COLS),
        dot(ones, split(inner), CONTRACT_COLS),
    )


def attn_grad_body(plan, parties, *refs):
    sums_refs, refs = refs[:parties], refs[parties:]
    attended_ref, query_decayed_ref, gained_ref, attn_grad_ref, held_ref = refs[:5]
    send_refs = refs[5:]
    size, length = plan.size, attended_ref.shape[0]
    feature_count = plan.heads * size * parties
    sums = sum(ref[...] for ref in sums_refs)
    inv_row = lax.rsqrt(sums[:1] / feature_count + EPSILON)
    coefficient_row = sums[1:2] * inv_row * inv_row * inv_row / feature_count
    is_inverse = lax.broadcasted_iota(jnp.int32, (8, length), 0) == 0
    columns = jnp.transpose(jnp.where(is_inverse, inv_row, coefficient_row))
    inv_rms = jnp.broadcast_to(columns[:, :1], (length, size))
    coefficient = jnp.broadcast_to(columns[:, 1:2], (length, size))
    for h in range(plan.heads):
        cut = lanes(h, size)
        attn_grad = gained_ref[:, cut] * inv_rms - attended_ref[:, cut] * coefficient
        attn_grad = attn_grad.astype(BF16)
        attn_grad_ref[:, cut] = attn_grad
        held_ref[cut] = dot(query_decayed_ref[h], attn_grad)
    for k, send_ref in enumerate(send_refs):
        send_ref[...] = held_ref[plan.rows_of(plan.peer(k))]


def score_grad_body(
    plan,
    attn_grad_ref,
    query_ref,
    key_ref,
    value_ref,
    states_ref,
    weight_ref,
    cum_ref,
    cum_col_ref,
    query_grad_ref,
    key_part_ref,
    value_part_ref,
    shrink_ref,
):
    length = query_ref.shape[0]
    causal = causal_mask(length)
    cum_col = cum_col_ref[...]
    growth = jnp.exp(cum_col)
    shrink = jnp.exp(cum_col[length - 1 : length, :] - cum_col)
    for h in range(plan.heads):
        cut = lanes(h, plan.size)
        attn_grad = attn_grad_ref[:, cut]
        scores = dot(attn_grad, value_ref[:, cut], CONTRACT_COLS)
        score_grad = (scores * decay_matrix(cum_ref, cum_col, causal, h)).astype(BF16)
        carried = dot(attn_grad, states_ref[cut], CONTRACT_COLS)
        query_grad = dot(score_grad, key_ref[:, cut]) + growth[:, h : h + 1] * carried
        query_grad_ref[:, cut] = query_grad.astype(BF16)
        key_part_ref[:, cut] = dot(score_grad, query_ref[:, cut], CONTRACT_ROWS)
        value_part_ref[:, cut] = dot(weight_ref[h], attn_grad, CONTRACT_ROWS)
        shrink_ref[h] = jnp.broadcast_to(shrink[:, h : h + 1], (length, plan.size))


def finish_body(plan, ways, *refs):
    count = len(ways)
    early_refs = dict(zip([way for way in plan.early_ways if way in ways], refs[:count]))
    late_refs = dict(zip(ways, refs[count : 2 * count]))
    refs = refs[2 * count :]
    key_part_ref, value_part_ref, key_ref, value_ref, shrink_ref = refs[:5]
    summary_ref, before_ref, logs_ref = refs[5:8]
    key_out, value_out, total_out, key_grad_ref, value_grad_ref, total_ref, sems = refs[-7:]
    size, rows = plan.size, plan.rows
    first = plan.group() == 0
    copies = []
    for i, way in enumerate(ways):
        owner = plan.toward(way)
        before, after = early_refs[way][:rows], late_refs[way][:rows]
        if plan.groups == 2:
            before, after = jnp.where(first, before, after), jnp.where(first, after, before)
        for j in range(plan.own):
            head = owner * plan.own + j
            part = pl.ds(pl.multiple_of(head * size, size), size)
            cut = slice(i * rows + j * size, i * rows + (j + 1) * size)
            grads = after[lanes(j, size)]
            log_before = before_ref[pl.ds(head, 1)]
            scale = jnp.exp(log_before)
            scale_next = jnp.exp(log_before + logs_ref[plan.member(), pl.ds(head, 1)])
            total_ref[cut] = (
                before[lanes(j, size)] + scale * summary_ref[part] + scale_next * grads
            )
            grads = grads.astype(BF16)
            key_state = dot(value_ref[:, part], grads, CONTRACT_COLS)
            key_grad_ref[:, cut] = (key_part_ref[:, part] + shrink_ref[head] * key_state).astype(BF16)
            value_state = dot(key_ref[:, part], grads)
            value_grad_ref[:, cut] = (value_part_ref[:, part] + shrink_ref[head] * value_state).astype(BF16)
        done, place = lanes(i, rows), plan.rows_of(owner)
        for source, target in [
            (total_ref.at[done], total_out.at[place]),
            (key_grad_ref.at[:, done], key_out.at[:, place]),
            (value_grad_ref.at[:, done], value_out.at[:, place]),
        ]:
            copies.append(pltpu.make_async_copy(source, target, sems.at[len(copies)]))
            copies[-1].start()
    for copy in copies:
        copy.wait()


def on_device(
    query_rows, key_rows, value_rows, log_decay, out_grad, norm_gain, state_in, state_out_grad
):
    heads, length = log_decay.shape
    size = state_in.shape[1]
    width = heads * size
    parties = lax.axis_size("head")
    plan = Plan(heads, size, lax.axis_size("seq"))
    bind = lambda body, *extra: functools.partial(body, plan, *extra)
    gain = norm_gain.reshape(1, width)
    piece = shaped((plan.rows, size))
    pieces = [piece] * plan.members
    chunk_piece = shaped((plan.chunk_rows, size))
    chunk_pieces = [chunk_piece] * plan.members
    logged = shaped((plan.chunk_rows + LOG_ROWS, size))
    block_logs = shaped((plan.members, LOG_ROWS, size))
    group_logs = shaped((plan.groups, LOG_ROWS, size))
    table = shaped((length, width))
    rounded = shaped((length, width), BF16)
    hold = pltpu.VMEM((plan.members, plan.rows, size), F32)
    hold_groups = pltpu.VMEM((plan.groups, plan.rows, size), F32)
    hold_chunk = pltpu.VMEM((plan.members, plan.chunk_rows, size), F32)
    hold_chunk_groups = pltpu.VMEM((plan.groups, plan.chunk_rows, size), F32)
    chunks = range(plan.chunks)
    state_rows = state_in.reshape(width, size)

    messages = plan.first_messages()
    *sends, cum_log, cum_col = call(
        bind(summary_body),
        [chunk_piece if chunk else logged for _, chunk in messages]
        + [shaped((heads, length)), shaped((length, heads))],
        [pltpu.with_memory_space_constraint(x, pltpu.HBM) for x in (key_rows, value_rows, log_decay)],
        [
            pltpu.VMEM((width, size), F32),
            pltpu.VMEM((length, width), BF16),
            pltpu.VMEM((length, width), BF16),
            pltpu.VMEM((heads, length), F32),
            pltpu.SemaphoreType.DMA((3,)),
        ],
        specs=[HBM] * 3,
    )
    received = {key: plan.swap(send, key[0]) for key, send in zip(messages, sends)}
    parts = [[received[way, c] for way in plan.ways] for c in chunks]
    totals = []
    for c in chunks:
        if c == 0:
            total, logs = call(
                bind(group_total_body, c), [logged, block_logs], parts[c], [hold_chunk]
            )
        else:
            (total,) = call(
                bind(group_total_body, c),
                [chunk_piece],
                [*parts[c], logs],
                [hold_chunk],
                flops=LONG,
            )
        totals.append([total] + plan.from_groups(total))
    states = {}
    far_parts = []
    for c in chunks:
        last = c == plan.chunks - 1
        operands = [*parts[c], *totals[c], state_rows, logs]
        outs = [piece if way in plan.far and last else chunk_piece for way in plan.ways]
        if c == 0:
            outs += [shaped((LOG_ROWS, size)), group_logs]
        else:
            operands += [all_logs]
        sends = call(
            bind(forward_scan_body, c),
            outs,
            operands + (far_parts if last else []),
            [hold_chunk_groups, hold_chunk],
        )
        if c == 0:
            before, all_logs = sends[plan.members :]
        for way, send in zip(plan.ways, sends):
            if way not in plan.far:
                states[way, c] = plan.swap(send, way)
            elif last:
                states[way, None] = plan.swap(send, way)
            else:
                far_parts.append(send)
    early = [states[way, 0] for way in plan.near] if plan.chunks > 1 else []
    weights, intra, gained, query_decayed = call(
        bind(intra_body),
        [
            shaped((heads, length, length), BF16),
            table,
            table,
            shaped((heads, size, length), BF16),
        ],
        [query_rows, key_rows, value_rows, cum_log, cum_col, out_grad, gain, *early],
        specs=[VMEM] * 7 + [ANY] * len(early),
        flops=LONG // 10,
    )
    attended, sums, states = call(
        bind(attended_body),
        [table, shaped((8, length)), shaped((width, size), BF16)],
        [*[states[key] for key in plan.last_messages()], intra, query_rows, cum_col, gained],
    )
    all_sums = [sums] + [
        lax.ppermute(sums, "head", [(i, (i + step) % parties) for i in range(parties)])
        for step in range(1, parties)
    ]
    attn_grad, summary, *sends = call(
        bind(attn_grad_body, parties),
        [rounded, shaped((width, size))] + pieces,
        [*all_sums, attended, query_decayed, gained],
    )
    parts = plan.swap_in_group(sends)
    query_grad, key_part, value_part, shrink = call(
        bind(score_grad_body),
        [rounded, table, table, shaped((heads, length, size))],
        [attn_grad, query_rows, key_rows, value_rows, states, weights, cum_log, cum_col],
        flops=10 * heads * length * length * size,
    )
    grad_rows = state_out_grad.reshape(width, size)
    two_sided = plan.groups == 2
    tie, swapped = key_part, []
    if two_sided:
        sends = call(
            bind(early_body),
            [piece, shaped((plan.rows + LOG_ROWS, size))] + pieces[2:],
            [*parts, logs, grad_rows, key_part],
            [hold],
            specs=[VMEM] * (plan.members + 2) + [ANY],
        )
        tie = sends[0]
        swapped = [dict(zip(plan.early_ways, plan.swap_in_group(sends, plan.early_ways)))]
    (total,) = call(
        bind(group_grad_body),
        [piece],
        [*parts, logs, tie],
        [hold],
        specs=[VMEM] * (plan.members + 1) + [ANY],
    )
    totals = [total] + plan.from_groups(total)
    sends = call(
        bind(reverse_scan_body),
        pieces * (1 if two_sided else 2),
        [*parts, *totals, logs, all_logs, grad_rows, swapped[0][plan.early_ways[1]] if two_sided else tie],
        [hold_groups, hold],
        specs=[VMEM] * (plan.members + plan.groups + 3) + [ANY],
    )
    for first in range(0, len(sends), plan.members):
        pieces_back = plan.swap_in_group(sends[first : first + plan.members], plan.late_ways)
        swapped.append(dict(zip(plan.late_ways, pieces_back)))
    outs = []
    for ways in ([0], plan.late_ways[1:]):
        if not ways:
            continue
        operands = [
            *[swapped[0][way] for way in plan.early_ways if way in ways],
            *[swapped[1][way] for way in ways],
            key_part,
            value_part,
            key_rows,
            value_rows,
            shrink,
            summary,
            before,
            logs,
        ]
        count = len(operands)
        outs = call(
            bind(finish_body, ways),
            [rounded, rounded, shaped((width, size))],
            [*operands, *outs],
            [
                pltpu.VMEM((length, len(ways) * plan.rows), BF16),
                pltpu.VMEM((length, len(ways) * plan.rows), BF16),
                pltpu.VMEM((len(ways) * plan.rows, size), F32),
                pltpu.SemaphoreType.DMA((3 * len(ways),)),
            ],
            specs=[VMEM] * count + [HBM] * len(outs),
            out_specs=[HBM] * 3,
            aliases={count + i: i for i in range(len(outs))},
        )
    key_grad, value_grad, state_in_grad = outs
    return (query_grad, key_grad, value_grad, state_in_grad.reshape(heads, size, size))


def solution(mesh):
    return jax.shard_map(
        on_device,
        mesh=mesh,
        in_specs=(
            P("seq", "head"),
            P("seq", "head"),
            P("seq", "head"),
            P("head", "seq"),
            P("seq", "head"),
            P("head"),
            P("head", None, None),
            P("head", None, None),
        ),
        out_specs=(P("seq", "head"), P("seq", "head"), P("seq", "head"), P("head", None, None)),
        check_vma=False,
    )
```

```python
import functools

import jax
import jax.numpy as jnp
from jax import lax
from jax.experimental import pallas as pl
from jax.experimental.pallas import tpu as pltpu
from jax.sharding import PartitionSpec as P

EPSILON = 1e-06
F32 = jnp.float32
BF16 = jnp.bfloat16
LOG_ROWS = 8
LONG = 10**10
MASKED = -1e30

CONTRACT_ROWS = (((0,), (0,)), ((), ()))
CONTRACT_COLS = (((1,), (1,)), ((), ()))
VMEM = pl.BlockSpec(memory_space=pltpu.VMEM)
HBM = pl.BlockSpec(memory_space=pltpu.HBM)
ANY = pl.BlockSpec(memory_space=pl.ANY)


def call(body, outs, operands, scratch=(), flops=0, specs=None, out_specs=None, aliases=None):
    return pl.pallas_call(
        body,
        out_shape=outs,
        in_specs=specs or [VMEM] * len(operands),
        out_specs=out_specs or [VMEM] * len(outs),
        scratch_shapes=list(scratch),
        input_output_aliases=aliases or {},
        compiler_params=pltpu.CompilerParams(vmem_limit_bytes=24 * 1024 * 1024),
        cost_estimate=pl.CostEstimate(flops=flops, bytes_accessed=0, transcendentals=0),
    )(*operands)


def shaped(shape, dtype=F32):
    return jax.ShapeDtypeStruct(shape, dtype)


def dot(a, b, dims=(((1,), (0,)), ((), ()))):
    return lax.dot_general(a, b, dims, preferred_element_type=F32)


def split(x):
    high = x.astype(BF16)
    rest = x - high.astype(F32)
    middle = rest.astype(BF16)
    low = (rest - middle.astype(F32)).astype(BF16)
    return jnp.concatenate([high, middle, low], axis=1)


def thrice(x):
    return jnp.concatenate([x, x, x], axis=1)


def lanes(h, size):
    return slice(h * size, (h + 1) * size)


def causal_mask(length):
    row = lax.broadcasted_iota(jnp.int32, (length, length), 0)
    col = lax.broadcasted_iota(jnp.int32, (length, length), 1)
    return row >= col


class Plan:
    def __init__(self, heads, size, blocks):
        self.heads, self.size, self.blocks = heads, size, blocks
        self.members = next(m for m in (4, 2, 1) if heads % m == 0 and blocks % m == 0)
        self.groups = blocks // self.members
        self.own = heads // self.members
        self.rows = self.own * size
        self.chunks = self.own
        self.chunk_rows = self.rows // self.chunks
        self.near = [way for way in range(self.members) if way.bit_count() == 1]
        self.far = [way for way in range(self.members) if way.bit_count() > 1]
        self.ways = [0] + self.far + self.near
        self.early_ways = [0] + self.near[1:] + self.far + self.near[:1]
        self.late_ways = [0] + self.far + self.near[::-1]

    def member(self):
        return lax.rem(lax.axis_index("seq"), self.members)

    def group(self):
        return lax.div(lax.axis_index("seq"), self.members)

    def peer(self, k):
        return self.toward(self.ways[k])

    def toward(self, way):
        return lax.bitwise_xor(self.member(), way)

    def rows_of(self, member):
        return pl.ds(pl.multiple_of(member * self.rows, self.rows), self.rows)

    def chunk_of(self, member, chunk):
        start = member * self.rows + chunk * self.chunk_rows
        return pl.ds(pl.multiple_of(start, self.chunk_rows), self.chunk_rows)

    def swap(self, piece, way):
        span = self.members
        pairs = [(i, i // span * span + (i % span ^ way)) for i in range(self.blocks)]
        return lax.ppermute(piece, "seq", pairs) if way else piece

    def swap_in_group(self, pieces, order=None):
        return [self.swap(piece, way) for way, piece in zip(order or self.ways, pieces)]

    def first_messages(self):
        return [(way, c) for c in range(self.chunks) for way in self.ways]

    def last_messages(self):
        cuts = [(way, c) for c in range(self.chunks) for way in [0] + self.near]
        return cuts + [(way, None) for way in self.far]

    def from_groups(self, piece):
        return [
            lax.ppermute(
                piece,
                "seq",
                [(i, (i + step * self.members) % self.blocks) for i in range(self.blocks)],
            )
            for step in range(1, self.groups)
        ]


def own_decays(plan, log_tile_ref, chunk=None):
    count = plan.own if chunk is None else plan.own // plan.chunks
    first = plan.member() * plan.own + (0 if chunk is None else chunk * count)
    rows = [log_tile_ref[pl.ds(first + j, 1), :] for j in range(count)]
    return jnp.concatenate([jnp.broadcast_to(jnp.exp(row), (plan.size, plan.size)) for row in rows])


def summary_body(plan, key_hbm, value_hbm, decay_hbm, *refs):
    count = len(plan.first_messages())
    send_refs, refs = refs[:count], refs[count:]
    cum_ref, cum_col_ref, held_ref, key_ref, value_ref, decay_ref, sems = refs
    length, heads, size = key_ref.shape[0], plan.heads, plan.size
    copies = [
        pltpu.make_async_copy(source, target, sems.at[i])
        for i, (source, target) in enumerate(
            [(decay_hbm, decay_ref), (key_hbm, key_ref), (value_hbm, value_ref)]
        )
    ]
    for copy in copies:
        copy.start()
    causal = thrice(jnp.where(causal_mask(length), 1.0, 0.0).astype(BF16))
    copies[0].wait()
    decay = split(decay_ref[...])
    cum_col = dot(causal, decay, CONTRACT_COLS)
    cum_row = dot(decay, causal, CONTRACT_COLS)
    cum_ref[...] = cum_row
    cum_col_ref[...] = cum_col
    shrink = jnp.exp(cum_col[length - 1 : length, :] - cum_col)
    copies[1].wait()
    copies[2].wait()
    for h in range(heads):
        key_decayed = (key_ref[:, lanes(h, size)].astype(F32) * shrink[:, h : h + 1]).astype(BF16)
        held_ref[h * size : (h + 1) * size] = dot(
            key_decayed, value_ref[:, lanes(h, size)], CONTRACT_ROWS
        )
    log_tile = jnp.broadcast_to(cum_row[:, length - 1 : length], (heads, size))
    if heads < LOG_ROWS:
        log_tile = jnp.concatenate([log_tile, jnp.zeros((LOG_ROWS - heads, size), F32)])
    for (way, chunk), send_ref in zip(plan.first_messages(), send_refs):
        send_ref[: plan.chunk_rows] = held_ref[plan.chunk_of(plan.toward(way), chunk)]
        if chunk == 0:
            send_ref[plan.chunk_rows :] = log_tile


def group_total_body(plan, chunk, *refs):
    part_refs, refs = refs[: plan.members], refs[plan.members :]
    rows = plan.chunk_rows
    if chunk == 0:
        total_ref, logs_ref = refs[:2]
        for k, part_ref in enumerate(part_refs):
            logs_ref[plan.peer(k)] = part_ref[rows:]
        total_ref[rows:] = sum(logs_ref[b] for b in range(plan.members))
    else:
        logs_ref, total_ref = refs[:2]
    held_ref = refs[2]
    for way, part_ref in zip(plan.ways, part_refs):
        held_ref[plan.toward(way)] = part_ref[:rows]
    total = jnp.zeros((rows, plan.size), F32)
    for b in range(plan.members):
        total = own_decays(plan, logs_ref.at[b], chunk) * total + held_ref[b]
    total_ref[:rows] = total


def stage_groups(plan, total_refs, held_ref):
    rows = held_ref.shape[1]
    for step, total_ref in enumerate(total_refs):
        held_ref[lax.rem(plan.group() - step + plan.groups, plan.groups)] = total_ref[:rows]


def forward_scan_body(plan, chunk, *refs):
    last = chunk == plan.chunks - 1
    part_refs, refs = refs[: plan.members], refs[plan.members :]
    total_refs, refs = refs[: plan.groups], refs[plan.groups :]
    (state_ref, logs_ref), refs = refs[:2], refs[2:]
    rows = plan.chunk_rows
    if chunk > 0:
        group_logs_ref, refs = refs[0], refs[1:]
    far_parts = chunk * len(plan.far) if last else 0
    far_refs, refs = refs[:far_parts], refs[far_parts:]
    send_refs, refs = refs[: plan.members], refs[plan.members :]
    if chunk == 0:
        before_ref, group_logs_ref = refs[:2]
        for step, total_ref in enumerate(total_refs):
            group = lax.rem(plan.group() - step + plan.groups, plan.groups)
            group_logs_ref[group] = total_ref[rows:]
        before = jnp.zeros((LOG_ROWS, plan.size), F32)
        for group in range(plan.groups - 1):
            before += jnp.where(group < plan.group(), group_logs_ref[group], 0.0)
        for b in range(plan.members - 1):
            before += jnp.where(b < plan.member(), logs_ref[b], 0.0)
        before_ref[...] = before
    groups_ref, held_ref = refs[-2:]
    stage_groups(plan, total_refs, groups_ref)
    state = state_ref[plan.chunk_of(plan.member(), chunk)]
    for group in range(plan.groups - 1):
        after = own_decays(plan, group_logs_ref.at[group], chunk) * state + groups_ref[group]
        state = jnp.where(group < plan.group(), after, state)
    for way, part_ref in zip(plan.ways, part_refs):
        held_ref[plan.toward(way)] = part_ref[:rows]
    for b in range(plan.members):
        summary = held_ref[b]
        held_ref[b] = state
        state = own_decays(plan, logs_ref.at[b], chunk) * state + summary
    for i, (way, send_ref) in enumerate(zip(plan.ways, send_refs)):
        if way in plan.far and last:
            for c in range(chunk):
                send_ref[c * rows : (c + 1) * rows] = far_refs[c * len(plan.far) + i - 1][...]
            send_ref[chunk * rows :] = held_ref[plan.toward(way)]
        else:
            send_ref[...] = held_ref[plan.toward(way)]


def suffixes(plan, held_ref, logs_ref, grad):
    found = []
    for b in reversed(range(plan.members)):
        found.append(grad)
        grad = own_decays(plan, logs_ref.at[b]) * grad + held_ref[b]
    return found[::-1], grad


def prefixes(plan, held_ref, logs_ref, total, scale):
    found = []
    for b in range(plan.members):
        found.append(total)
        total = total + scale * held_ref[b]
        scale = scale * own_decays(plan, logs_ref.at[b])
    return found


def early_body(plan, *refs):
    part_refs, refs = refs[: plan.members], refs[plan.members :]
    (logs_ref, grad_ref), send_refs, held_ref = refs[:2], refs[3:-1], refs[-1]
    for k, part_ref in enumerate(part_refs):
        held_ref[plan.peer(k)] = part_ref[...]
    first = plan.group() == 0
    zero = jnp.zeros((plan.rows, plan.size), F32)
    before = prefixes(plan, held_ref, logs_ref, zero, zero + 1.0)
    after = suffixes(plan, held_ref, logs_ref, grad_ref[plan.rows_of(plan.member())])[0]
    for b in range(plan.members):
        held_ref[b] = jnp.where(first, before[b], after[b])
    for way, send_ref in zip(plan.early_ways, send_refs):
        send_ref[: plan.rows] = held_ref[plan.toward(way)]
        if send_ref.shape[0] > plan.rows:
            send_ref[plan.rows :] = logs_ref[0]


def group_grad_body(plan, *refs):
    part_refs, (logs_ref, _, total_ref, held_ref) = refs[: plan.members], refs[plan.members :]
    for k, part_ref in enumerate(part_refs):
        held_ref[plan.peer(k)] = part_ref[...]
    zero = jnp.zeros((plan.rows, plan.size), F32)
    total_ref[...] = suffixes(plan, held_ref, logs_ref, zero)[1]


def reverse_scan_body(plan, *refs):
    part_refs, refs = refs[: plan.members], refs[plan.members :]
    total_refs, refs = refs[: plan.groups], refs[plan.groups :]
    (logs_ref, group_logs_ref, grad_ref, _), refs = refs[:4], refs[4:]
    send_refs, (groups_ref, held_ref) = refs[:-2], refs[-2:]
    stage_groups(plan, total_refs, groups_ref)
    for k, part_ref in enumerate(part_refs):
        held_ref[plan.peer(k)] = part_ref[...]
    grad = grad_ref[plan.rows_of(plan.member())]
    leaving = grad
    for group in reversed(range(plan.groups)):
        leaving = jnp.where(group == plan.group(), grad, leaving)
        grad = own_decays(plan, group_logs_ref.at[group]) * grad + groups_ref[group]
    total = jnp.zeros((plan.rows, plan.size), F32)
    scale = total + 1.0
    for group in range(plan.groups - 1):
        earlier = group < plan.group()
        total = jnp.where(earlier, total + scale * groups_ref[group], total)
        decays = own_decays(plan, group_logs_ref.at[group])
        scale = jnp.where(earlier, scale * decays, scale)
    after = suffixes(plan, held_ref, logs_ref, leaving)[0]
    before = prefixes(plan, held_ref, logs_ref, total, scale)
    if plan.groups == 2:
        first = plan.group() == 0
        found = [[jnp.where(first, after[b], before[b]) for b in range(plan.members)]]
    else:
        found = [before, after]
    for i, values in enumerate(found):
        for b in range(plan.members):
            held_ref[b] = values[b]
        for k in range(plan.members):
            send_refs[i * plan.members + k][...] = held_ref[plan.toward(plan.late_ways[k])]


def decay_matrix(cum_ref, cum_col, causal, h):
    spread = cum_col[:, h : h + 1] - cum_ref[h : h + 1, :]
    return jnp.exp(jnp.where(causal, jnp.minimum(spread, 0.0), MASKED))


def intra_body(
    plan,
    query_ref,
    key_ref,
    value_ref,
    cum_ref,
    cum_col_ref,
    upstream_ref,
    gain_ref,
    *refs,
):
    weight_ref, intra_ref, gained_ref, query_decayed_ref = refs[-4:]
    causal = causal_mask(query_ref.shape[0])
    cum_col = cum_col_ref[...]
    growth = jnp.exp(cum_col)
    for h in range(plan.heads):
        cut = lanes(h, plan.size)
        query = query_ref[:, cut]
        scores = dot(query, key_ref[:, cut], CONTRACT_COLS)
        weights = (scores * decay_matrix(cum_ref, cum_col, causal, h)).astype(BF16)
        weight_ref[h] = weights
        intra_ref[:, cut] = dot(weights, value_ref[:, cut])
        gained_ref[:, cut] = gain_ref[:, cut] * upstream_ref[:, cut].astype(F32)
        query_decayed = query.astype(F32) * growth[:, h : h + 1]
        query_decayed_ref[h] = jnp.transpose(query_decayed).astype(BF16)


def attended_body(plan, *refs):
    count = len(plan.last_messages())
    state_refs, refs = refs[:count], refs[count:]
    intra_ref, query_ref, cum_col_ref, gained_ref = refs[:4]
    attended_ref, sums_ref, states_ref = refs[4:]
    size, length = plan.size, query_ref.shape[0]
    for (way, chunk), state_ref in zip(plan.last_messages(), state_refs):
        member = plan.toward(way)
        part = plan.rows_of(member) if chunk is None else plan.chunk_of(member, chunk)
        states_ref[part] = state_ref[...].astype(BF16)
    growth = jnp.exp(cum_col_ref[...])
    square = jnp.zeros((length, size), F32)
    inner = jnp.zeros((length, size), F32)
    for h in range(plan.heads):
        cut = lanes(h, size)
        carried = dot(query_ref[:, cut], states_ref[cut])
        attended = intra_ref[:, cut] + growth[:, h : h + 1] * carried
        attended_ref[:, cut] = attended
        square += attended * attended
        inner += gained_ref[:, cut] * attended
    ones = jnp.ones((8, 3 * size), BF16)
    is_square = lax.broadcasted_iota(jnp.int32, (8, length), 0) == 0
    sums_ref[...] = jnp.where(
        is_square,
        dot(ones, split(square), CONTRACT_COLS),
        dot(ones, split(inner), CONTRACT_COLS),
    )


def attn_grad_body(plan, parties, *refs):
    sums_refs, refs = refs[:parties], refs[parties:]
    attended_ref, query_decayed_ref, gained_ref, attn_grad_ref, held_ref = refs[:5]
    send_refs = refs[5:]
    size, length = plan.size, attended_ref.shape[0]
    feature_count = plan.heads * size * parties
    sums = sum(ref[...] for ref in sums_refs)
    inv_row = lax.rsqrt(sums[:1] / feature_count + EPSILON)
    coefficient_row = sums[1:2] * inv_row * inv_row * inv_row / feature_count
    is_inverse = lax.broadcasted_iota(jnp.int32, (8, length), 0) == 0
    columns = jnp.transpose(jnp.where(is_inverse, inv_row, coefficient_row))
    inv_rms = jnp.broadcast_to(columns[:, :1], (length, size))
    coefficient = jnp.broadcast_to(columns[:, 1:2], (length, size))
    for h in range(plan.heads):
        cut = lanes(h, size)
        attn_grad = gained_ref[:, cut] * inv_rms - attended_ref[:, cut] * coefficient
        attn_grad = attn_grad.astype(BF16)
        attn_grad_ref[:, cut] = attn_grad
        held_ref[cut] = dot(query_decayed_ref[h], attn_grad)
    for k, send_ref in enumerate(send_refs):
        send_ref[...] = held_ref[plan.rows_of(plan.peer(k))]


def score_grad_body(
    plan,
    attn_grad_ref,
    query_ref,
    key_ref,
    value_ref,
    states_ref,
    weight_ref,
    cum_ref,
    cum_col_ref,
    query_grad_ref,
    key_part_ref,
    value_part_ref,
    shrink_ref,
):
    length = query_ref.shape[0]
    causal = causal_mask(length)
    cum_col = cum_col_ref[...]
    growth = jnp.exp(cum_col)
    shrink = jnp.exp(cum_col[length - 1 : length, :] - cum_col)
    for h in range(plan.heads):
        cut = lanes(h, plan.size)
        attn_grad = attn_grad_ref[:, cut]
        scores = dot(attn_grad, value_ref[:, cut], CONTRACT_COLS)
        score_grad = (scores * decay_matrix(cum_ref, cum_col, causal, h)).astype(BF16)
        carried = dot(attn_grad, states_ref[cut], CONTRACT_COLS)
        query_grad = dot(score_grad, key_ref[:, cut]) + growth[:, h : h + 1] * carried
        query_grad_ref[:, cut] = query_grad.astype(BF16)
        key_part_ref[:, cut] = dot(score_grad, query_ref[:, cut], CONTRACT_ROWS)
        value_part_ref[:, cut] = dot(weight_ref[h], attn_grad, CONTRACT_ROWS)
        shrink_ref[h] = jnp.broadcast_to(shrink[:, h : h + 1], (length, plan.size))


def finish_body(plan, ways, *refs):
    count = len(ways)
    early_refs = dict(zip([way for way in plan.early_ways if way in ways], refs[:count]))
    late_refs = dict(zip(ways, refs[count : 2 * count]))
    refs = refs[2 * count :]
    key_part_ref, value_part_ref, key_ref, value_ref, shrink_ref = refs[:5]
    summary_ref, before_ref, logs_ref = refs[5:8]
    key_out, value_out, total_out, key_grad_ref, value_grad_ref, total_ref, sems = refs[-7:]
    size, rows = plan.size, plan.rows
    first = plan.group() == 0
    copies = []
    for i, way in enumerate(ways):
        owner = plan.toward(way)
        before, after = early_refs[way][:rows], late_refs[way][:rows]
        if plan.groups == 2:
            before, after = jnp.where(first, before, after), jnp.where(first, after, before)
        for j in range(plan.own):
            head = owner * plan.own + j
            part = pl.ds(pl.multiple_of(head * size, size), size)
            cut = slice(i * rows + j * size, i * rows + (j + 1) * size)
            grads = after[lanes(j, size)]
            log_before = before_ref[pl.ds(head, 1)]
            scale = jnp.exp(log_before)
            scale_next = jnp.exp(log_before + logs_ref[plan.member(), pl.ds(head, 1)])
            total_ref[cut] = (
                before[lanes(j, size)] + scale * summary_ref[part] + scale_next * grads
            )
            grads = grads.astype(BF16)
            key_state = dot(value_ref[:, part], grads, CONTRACT_COLS)
            key_grad_ref[:, cut] = (key_part_ref[:, part] + shrink_ref[head] * key_state).astype(BF16)
            value_state = dot(key_ref[:, part], grads)
            value_grad_ref[:, cut] = (value_part_ref[:, part] + shrink_ref[head] * value_state).astype(BF16)
        done, place = lanes(i, rows), plan.rows_of(owner)
        for source, target in [
            (total_ref.at[done], total_out.at[place]),
            (key_grad_ref.at[:, done], key_out.at[:, place]),
            (value_grad_ref.at[:, done], value_out.at[:, place]),
        ]:
            copies.append(pltpu.make_async_copy(source, target, sems.at[len(copies)]))
            copies[-1].start()
    for copy in copies:
        copy.wait()


def on_device(
    query_rows, key_rows, value_rows, log_decay, out_grad, norm_gain, state_in, state_out_grad
):
    heads, length = log_decay.shape
    size = state_in.shape[1]
    width = heads * size
    parties = lax.axis_size("head")
    plan = Plan(heads, size, lax.axis_size("seq"))
    bind = lambda body, *extra: functools.partial(body, plan, *extra)
    gain = norm_gain.reshape(1, width)
    piece = shaped((plan.rows, size))
    pieces = [piece] * plan.members
    chunk_piece = shaped((plan.chunk_rows, size))
    chunk_pieces = [chunk_piece] * plan.members
    logged = shaped((plan.chunk_rows + LOG_ROWS, size))
    block_logs = shaped((plan.members, LOG_ROWS, size))
    group_logs = shaped((plan.groups, LOG_ROWS, size))
    table = shaped((length, width))
    rounded = shaped((length, width), BF16)
    hold = pltpu.VMEM((plan.members, plan.rows, size), F32)
    hold_groups = pltpu.VMEM((plan.groups, plan.rows, size), F32)
    hold_chunk = pltpu.VMEM((plan.members, plan.chunk_rows, size), F32)
    hold_chunk_groups = pltpu.VMEM((plan.groups, plan.chunk_rows, size), F32)
    chunks = range(plan.chunks)
    state_rows = state_in.reshape(width, size)

    messages = plan.first_messages()
    *sends, cum_log, cum_col = call(
        bind(summary_body),
        [chunk_piece if chunk else logged for _, chunk in messages]
        + [shaped((heads, length)), shaped((length, heads))],
        [pltpu.with_memory_space_constraint(x, pltpu.HBM) for x in (key_rows, value_rows, log_decay)],
        [
            pltpu.VMEM((width, size), F32),
            pltpu.VMEM((length, width), BF16),
            pltpu.VMEM((length, width), BF16),
            pltpu.VMEM((heads, length), F32),
            pltpu.SemaphoreType.DMA((3,)),
        ],
        specs=[HBM] * 3,
    )
    received = {key: plan.swap(send, key[0]) for key, send in zip(messages, sends)}
    parts = [[received[way, c] for way in plan.ways] for c in chunks]
    totals = []
    for c in chunks:
        if c == 0:
            total, logs = call(
                bind(group_total_body, c), [logged, block_logs], parts[c], [hold_chunk]
            )
        else:
            (total,) = call(
                bind(group_total_body, c),
                [chunk_piece],
                [*parts[c], logs],
                [hold_chunk],
                flops=LONG,
            )
        totals.append([total] + plan.from_groups(total))
    states = {}
    far_parts = []
    for c in chunks:
        last = c == plan.chunks - 1
        operands = [*parts[c], *totals[c], state_rows, logs]
        outs = [piece if way in plan.far and last else chunk_piece for way in plan.ways]
        if c == 0:
            outs += [shaped((LOG_ROWS, size)), group_logs]
        else:
            operands += [all_logs]
        sends = call(
            bind(forward_scan_body, c),
            outs,
            operands + (far_parts if last else []),
            [hold_chunk_groups, hold_chunk],
        )
        if c == 0:
            before, all_logs = sends[plan.members :]
        for way, send in zip(plan.ways, sends):
            if way not in plan.far:
                states[way, c] = plan.swap(send, way)
            elif last:
                states[way, None] = plan.swap(send, way)
            else:
                far_parts.append(send)
    early = [states[way, 0] for way in plan.near] if plan.chunks > 1 else []
    weights, intra, gained, query_decayed = call(
        bind(intra_body),
        [
            shaped((heads, length, length), BF16),
            table,
            table,
            shaped((heads, size, length), BF16),
        ],
        [query_rows, key_rows, value_rows, cum_log, cum_col, out_grad, gain, *early],
        specs=[VMEM] * 7 + [ANY] * len(early),
        flops=LONG // 10,
    )
    attended, sums, states = call(
        bind(attended_body),
        [table, shaped((8, length)), shaped((width, size), BF16)],
        [*[states[key] for key in plan.last_messages()], intra, query_rows, cum_col, gained],
    )
    all_sums = [sums] + [
        lax.ppermute(sums, "head", [(i, (i + step) % parties) for i in range(parties)])
        for step in range(1, parties)
    ]
    attn_grad, summary, *sends = call(
        bind(attn_grad_body, parties),
        [rounded, shaped((width, size))] + pieces,
        [*all_sums, attended, query_decayed, gained],
    )
    parts = plan.swap_in_group(sends)
    query_grad, key_part, value_part, shrink = call(
        bind(score_grad_body),
        [rounded, table, table, shaped((heads, length, size))],
        [attn_grad, query_rows, key_rows, value_rows, states, weights, cum_log, cum_col],
        flops=10 * heads * length * length * size,
    )
    grad_rows = state_out_grad.reshape(width, size)
    two_sided = plan.groups == 2
    tie, swapped = key_part, []
    if two_sided:
        sends = call(
            bind(early_body),
            [piece, shaped((plan.rows + LOG_ROWS, size))] + pieces[2:],
            [*parts, logs, grad_rows, key_part],
            [hold],
            specs=[VMEM] * (plan.members + 2) + [ANY],
        )
        tie = sends[0]
        swapped = [dict(zip(plan.early_ways, plan.swap_in_group(sends, plan.early_ways)))]
    (total,) = call(
        bind(group_grad_body),
        [piece],
        [*parts, logs, tie],
        [hold],
        specs=[VMEM] * (plan.members + 1) + [ANY],
    )
    totals = [total] + plan.from_groups(total)
    sends = call(
        bind(reverse_scan_body),
        pieces * (1 if two_sided else 2),
        [*parts, *totals, logs, all_logs, grad_rows, swapped[0][plan.early_ways[1]] if two_sided else tie],
        [hold_groups, hold],
        specs=[VMEM] * (plan.members + plan.groups + 3) + [ANY],
    )
    for first in range(0, len(sends), plan.members):
        pieces_back = plan.swap_in_group(sends[first : first + plan.members], plan.late_ways)
        swapped.append(dict(zip(plan.late_ways, pieces_back)))
    outs = []
    for ways in ([0], plan.late_ways[1:]):
        if not ways:
            continue
        operands = [
            *[swapped[0][way] for way in plan.early_ways if way in ways],
            *[swapped[1][way] for way in ways],
            key_part,
            value_part,
            key_rows,
            value_rows,
            shrink,
            summary,
            before,
            logs,
        ]
        count = len(operands)
        outs = call(
            bind(finish_body, ways),
            [rounded, rounded, shaped((width, size))],
            [*operands, *outs],
            [
                pltpu.VMEM((length, len(ways) * plan.rows), BF16),
                pltpu.VMEM((length, len(ways) * plan.rows), BF16),
                pltpu.VMEM((len(ways) * plan.rows, size), F32),
                pltpu.SemaphoreType.DMA((3 * len(ways),)),
            ],
            specs=[VMEM] * count + [HBM] * len(outs),
            out_specs=[HBM] * 3,
            aliases={count + i: i for i in range(len(outs))},
        )
    key_grad, value_grad, state_in_grad = outs
    return (query_grad, key_grad, value_grad, state_in_grad.reshape(heads, size, size))


def solution(mesh):
    return jax.shard_map(
        on_device,
        mesh=mesh,
        in_specs=(
            P("seq", "head"),
            P("seq", "head"),
            P("seq", "head"),
            P("head", "seq"),
            P("seq", "head"),
            P("head"),
            P("head", None, None),
            P("head", None, None),
        ),
        out_specs=(P("seq", "head"), P("seq", "head"), P("seq", "head"), P("head", None, None)),
        check_vma=False,
    )
```

```python
import functools

import jax
import jax.numpy as jnp
from jax import lax
from jax.experimental import pallas as pl
from jax.experimental.pallas import tpu as pltpu
from jax.sharding import PartitionSpec as P

EPSILON = 1e-06
F32 = jnp.float32
BF16 = jnp.bfloat16
LOG_ROWS = 8
LONG = 10**10
MASKED = -1e30

CONTRACT_ROWS = (((0,), (0,)), ((), ()))
CONTRACT_COLS = (((1,), (1,)), ((), ()))
VMEM = pl.BlockSpec(memory_space=pltpu.VMEM)
HBM = pl.BlockSpec(memory_space=pltpu.HBM)
ANY = pl.BlockSpec(memory_space=pl.ANY)


def call(body, outs, operands, scratch=(), flops=0, specs=None, out_specs=None, aliases=None):
    return pl.pallas_call(
        body,
        out_shape=outs,
        in_specs=specs or [VMEM] * len(operands),
        out_specs=out_specs or [VMEM] * len(outs),
        scratch_shapes=list(scratch),
        input_output_aliases=aliases or {},
        compiler_params=pltpu.CompilerParams(vmem_limit_bytes=24 * 1024 * 1024),
        cost_estimate=pl.CostEstimate(flops=flops, bytes_accessed=0, transcendentals=0),
    )(*operands)


def shaped(shape, dtype=F32):
    return jax.ShapeDtypeStruct(shape, dtype)


def dot(a, b, dims=(((1,), (0,)), ((), ()))):
    return lax.dot_general(a, b, dims, preferred_element_type=F32)


def split(x):
    high = x.astype(BF16)
    rest = x - high.astype(F32)
    middle = rest.astype(BF16)
    low = (rest - middle.astype(F32)).astype(BF16)
    return jnp.concatenate([high, middle, low], axis=1)


def thrice(x):
    return jnp.concatenate([x, x, x], axis=1)


def lanes(h, size):
    return slice(h * size, (h + 1) * size)


def causal_mask(length):
    row = lax.broadcasted_iota(jnp.int32, (length, length), 0)
    col = lax.broadcasted_iota(jnp.int32, (length, length), 1)
    return row >= col


class Plan:
    def __init__(self, heads, size, blocks):
        self.heads, self.size, self.blocks = heads, size, blocks
        self.members = next(m for m in (4, 2, 1) if heads % m == 0 and blocks % m == 0)
        self.groups = blocks // self.members
        self.own = heads // self.members
        self.rows = self.own * size
        self.chunks = self.own
        self.chunk_rows = self.rows // self.chunks
        self.near = [way for way in range(self.members) if way.bit_count() == 1]
        self.far = [way for way in range(self.members) if way.bit_count() > 1]
        self.ways = [0] + self.far + self.near
        self.early_ways = [0] + self.near[::-1] + self.far
        self.late_ways = [0] + self.far + self.near[::-1]

    def member(self):
        return lax.rem(lax.axis_index("seq"), self.members)

    def group(self):
        return lax.div(lax.axis_index("seq"), self.members)

    def peer(self, k):
        return self.toward(self.ways[k])

    def toward(self, way):
        return lax.bitwise_xor(self.member(), way)

    def rows_of(self, member):
        return pl.ds(pl.multiple_of(member * self.rows, self.rows), self.rows)

    def chunk_of(self, member, chunk):
        start = member * self.rows + chunk * self.chunk_rows
        return pl.ds(pl.multiple_of(start, self.chunk_rows), self.chunk_rows)

    def swap(self, piece, way):
        span = self.members
        pairs = [(i, i // span * span + (i % span ^ way)) for i in range(self.blocks)]
        return lax.ppermute(piece, "seq", pairs) if way else piece

    def swap_in_group(self, pieces, order=None):
        return [self.swap(piece, way) for way, piece in zip(order or self.ways, pieces)]

    def first_messages(self):
        return [(way, c) for c in range(self.chunks) for way in self.ways]

    def last_messages(self):
        cuts = [(way, c) for c in range(self.chunks) for way in [0] + self.near[:: -1 if c else 1]]
        return cuts + [(way, None) for way in self.far]

    def from_groups(self, piece):
        return [
            lax.ppermute(
                piece,
                "seq",
                [(i, (i + step * self.members) % self.blocks) for i in range(self.blocks)],
            )
            for step in range(1, self.groups)
        ]


def own_decays(plan, log_tile_ref, chunk=None):
    count = plan.own if chunk is None else plan.own // plan.chunks
    first = plan.member() * plan.own + (0 if chunk is None else chunk * count)
    rows = [log_tile_ref[pl.ds(first + j, 1), :] for j in range(count)]
    return jnp.concatenate([jnp.broadcast_to(jnp.exp(row), (plan.size, plan.size)) for row in rows])


def summary_body(plan, key_hbm, value_hbm, decay_hbm, *refs):
    count = len(plan.first_messages())
    send_refs, refs = refs[:count], refs[count:]
    cum_ref, cum_col_ref, held_ref, key_ref, value_ref, decay_ref, sems = refs
    length, heads, size = key_ref.shape[0], plan.heads, plan.size
    copies = [
        pltpu.make_async_copy(source, target, sems.at[i])
        for i, (source, target) in enumerate(
            [(decay_hbm, decay_ref), (key_hbm, key_ref), (value_hbm, value_ref)]
        )
    ]
    for copy in copies:
        copy.start()
    causal = thrice(jnp.where(causal_mask(length), 1.0, 0.0).astype(BF16))
    copies[0].wait()
    decay = split(decay_ref[...])
    cum_col = dot(causal, decay, CONTRACT_COLS)
    cum_row = dot(decay, causal, CONTRACT_COLS)
    cum_ref[...] = cum_row
    cum_col_ref[...] = cum_col
    shrink = jnp.exp(cum_col[length - 1 : length, :] - cum_col)
    copies[1].wait()
    copies[2].wait()
    for h in range(heads):
        key_decayed = (key_ref[:, lanes(h, size)].astype(F32) * shrink[:, h : h + 1]).astype(BF16)
        held_ref[h * size : (h + 1) * size] = dot(
            key_decayed, value_ref[:, lanes(h, size)], CONTRACT_ROWS
        )
    log_tile = jnp.broadcast_to(cum_row[:, length - 1 : length], (heads, size))
    if heads < LOG_ROWS:
        log_tile = jnp.concatenate([log_tile, jnp.zeros((LOG_ROWS - heads, size), F32)])
    for (way, chunk), send_ref in zip(plan.first_messages(), send_refs):
        send_ref[: plan.chunk_rows] = held_ref[plan.chunk_of(plan.toward(way), chunk)]
        if chunk == 0:
            send_ref[plan.chunk_rows :] = log_tile


def group_total_body(plan, chunk, *refs):
    part_refs, refs = refs[: plan.members], refs[plan.members :]
    rows = plan.chunk_rows
    if chunk == 0:
        total_ref, logs_ref = refs[:2]
        for k, part_ref in enumerate(part_refs):
            logs_ref[plan.peer(k)] = part_ref[rows:]
        total_ref[rows:] = sum(logs_ref[b] for b in range(plan.members))
    else:
        logs_ref, total_ref = refs[:2]
    held_ref = refs[2]
    for way, part_ref in zip(plan.ways, part_refs):
        held_ref[plan.toward(way)] = part_ref[:rows]
    total = jnp.zeros((rows, plan.size), F32)
    for b in range(plan.members):
        total = own_decays(plan, logs_ref.at[b], chunk) * total + held_ref[b]
    total_ref[:rows] = total


def stage_groups(plan, total_refs, held_ref):
    rows = held_ref.shape[1]
    for step, total_ref in enumerate(total_refs):
        held_ref[lax.rem(plan.group() - step + plan.groups, plan.groups)] = total_ref[:rows]


def forward_scan_body(plan, chunk, *refs):
    last = chunk == plan.chunks - 1
    part_refs, refs = refs[: plan.members], refs[plan.members :]
    total_refs, refs = refs[: plan.groups], refs[plan.groups :]
    (state_ref, logs_ref), refs = refs[:2], refs[2:]
    rows = plan.chunk_rows
    if chunk > 0:
        group_logs_ref, refs = refs[0], refs[1:]
    far_parts = chunk * len(plan.far) if last else 0
    far_refs, refs = refs[:far_parts], refs[far_parts:]
    send_refs, refs = refs[: plan.members], refs[plan.members :]
    if chunk == 0:
        before_ref, group_logs_ref = refs[:2]
        for step, total_ref in enumerate(total_refs):
            group = lax.rem(plan.group() - step + plan.groups, plan.groups)
            group_logs_ref[group] = total_ref[rows:]
        before = jnp.zeros((LOG_ROWS, plan.size), F32)
        for group in range(plan.groups - 1):
            before += jnp.where(group < plan.group(), group_logs_ref[group], 0.0)
        for b in range(plan.members - 1):
            before += jnp.where(b < plan.member(), logs_ref[b], 0.0)
        before_ref[...] = before
    groups_ref, held_ref = refs[-2:]
    stage_groups(plan, total_refs, groups_ref)
    state = state_ref[plan.chunk_of(plan.member(), chunk)]
    for group in range(plan.groups - 1):
        after = own_decays(plan, group_logs_ref.at[group], chunk) * state + groups_ref[group]
        state = jnp.where(group < plan.group(), after, state)
    for way, part_ref in zip(plan.ways, part_refs):
        held_ref[plan.toward(way)] = part_ref[:rows]
    for b in range(plan.members):
        summary = held_ref[b]
        held_ref[b] = state
        state = own_decays(plan, logs_ref.at[b], chunk) * state + summary
    for i, (way, send_ref) in enumerate(zip(plan.ways, send_refs)):
        if way in plan.far and last:
            for c in range(chunk):
                send_ref[c * rows : (c + 1) * rows] = far_refs[c * len(plan.far) + i - 1][...]
            send_ref[chunk * rows :] = held_ref[plan.toward(way)]
        else:
            send_ref[...] = held_ref[plan.toward(way)]


def suffixes(plan, held_ref, logs_ref, grad):
    found = []
    for b in reversed(range(plan.members)):
        found.append(grad)
        grad = own_decays(plan, logs_ref.at[b]) * grad + held_ref[b]
    return found[::-1], grad


def prefixes(plan, held_ref, logs_ref, total, scale):
    found = []
    for b in range(plan.members):
        found.append(total)
        total = total + scale * held_ref[b]
        scale = scale * own_decays(plan, logs_ref.at[b])
    return found


def early_body(plan, *refs):
    part_refs, refs = refs[: plan.members], refs[plan.members :]
    (logs_ref, grad_ref), send_refs, held_ref = refs[:2], refs[3:-1], refs[-1]
    for k, part_ref in enumerate(part_refs):
        held_ref[plan.peer(k)] = part_ref[...]
    first = plan.group() == 0
    zero = jnp.zeros((plan.rows, plan.size), F32)
    before = prefixes(plan, held_ref, logs_ref, zero, zero + 1.0)
    after = suffixes(plan, held_ref, logs_ref, grad_ref[plan.rows_of(plan.member())])[0]
    for b in range(plan.members):
        held_ref[b] = jnp.where(first, before[b], after[b])
    for way, send_ref in zip(plan.early_ways, send_refs):
        send_ref[: plan.rows] = held_ref[plan.toward(way)]
        if send_ref.shape[0] > plan.rows:
            send_ref[plan.rows :] = logs_ref[0]


def group_grad_body(plan, *refs):
    part_refs, (logs_ref, _, total_ref, held_ref) = refs[: plan.members], refs[plan.members :]
    for k, part_ref in enumerate(part_refs):
        held_ref[plan.peer(k)] = part_ref[...]
    zero = jnp.zeros((plan.rows, plan.size), F32)
    total_ref[...] = suffixes(plan, held_ref, logs_ref, zero)[1]


def reverse_scan_body(plan, *refs):
    part_refs, refs = refs[: plan.members], refs[plan.members :]
    total_refs, refs = refs[: plan.groups], refs[plan.groups :]
    (logs_ref, group_logs_ref, grad_ref, _), refs = refs[:4], refs[4:]
    send_refs, (groups_ref, held_ref) = refs[:-2], refs[-2:]
    stage_groups(plan, total_refs, groups_ref)
    for k, part_ref in enumerate(part_refs):
        held_ref[plan.peer(k)] = part_ref[...]
    grad = grad_ref[plan.rows_of(plan.member())]
    leaving = grad
    for group in reversed(range(plan.groups)):
        leaving = jnp.where(group == plan.group(), grad, leaving)
        grad = own_decays(plan, group_logs_ref.at[group]) * grad + groups_ref[group]
    total = jnp.zeros((plan.rows, plan.size), F32)
    scale = total + 1.0
    for group in range(plan.groups - 1):
        earlier = group < plan.group()
        total = jnp.where(earlier, total + scale * groups_ref[group], total)
        decays = own_decays(plan, group_logs_ref.at[group])
        scale = jnp.where(earlier, scale * decays, scale)
    after = suffixes(plan, held_ref, logs_ref, leaving)[0]
    before = prefixes(plan, held_ref, logs_ref, total, scale)
    if plan.groups == 2:
        first = plan.group() == 0
        found = [[jnp.where(first, after[b], before[b]) for b in range(plan.members)]]
    else:
        found = [before, after]
    for i, values in enumerate(found):
        for b in range(plan.members):
            held_ref[b] = values[b]
        for k in range(plan.members):
            send_refs[i * plan.members + k][...] = held_ref[plan.toward(plan.late_ways[k])]


def decay_matrix(cum_ref, cum_col, causal, h):
    spread = cum_col[:, h : h + 1] - cum_ref[h : h + 1, :]
    return jnp.exp(jnp.where(causal, jnp.minimum(spread, 0.0), MASKED))


def intra_body(
    plan,
    query_ref,
    key_ref,
    value_ref,
    cum_ref,
    cum_col_ref,
    upstream_ref,
    gain_ref,
    *refs,
):
    weight_ref, intra_ref, gained_ref, query_decayed_ref = refs[-4:]
    causal = causal_mask(query_ref.shape[0])
    cum_col = cum_col_ref[...]
    growth = jnp.exp(cum_col)
    for h in range(plan.heads):
        cut = lanes(h, plan.size)
        query = query_ref[:, cut]
        scores = dot(query, key_ref[:, cut], CONTRACT_COLS)
        weights = (scores * decay_matrix(cum_ref, cum_col, causal, h)).astype(BF16)
        weight_ref[h] = weights
        intra_ref[:, cut] = dot(weights, value_ref[:, cut])
        gained_ref[:, cut] = gain_ref[:, cut] * upstream_ref[:, cut].astype(F32)
        query_decayed = query.astype(F32) * growth[:, h : h + 1]
        query_decayed_ref[h] = jnp.transpose(query_decayed).astype(BF16)


def attended_body(plan, *refs):
    count = len(plan.last_messages())
    state_refs, refs = refs[:count], refs[count:]
    intra_ref, query_ref, cum_col_ref, gained_ref = refs[:4]
    attended_ref, sums_ref, states_ref = refs[4:]
    size, length = plan.size, query_ref.shape[0]
    for (way, chunk), state_ref in zip(plan.last_messages(), state_refs):
        member = plan.toward(way)
        part = plan.rows_of(member) if chunk is None else plan.chunk_of(member, chunk)
        states_ref[part] = state_ref[...].astype(BF16)
    growth = jnp.exp(cum_col_ref[...])
    square = jnp.zeros((length, size), F32)
    inner = jnp.zeros((length, size), F32)
    for h in range(plan.heads):
        cut = lanes(h, size)
        carried = dot(query_ref[:, cut], states_ref[cut])
        attended = intra_ref[:, cut] + growth[:, h : h + 1] * carried
        attended_ref[:, cut] = attended
        square += attended * attended
        inner += gained_ref[:, cut] * attended
    ones = jnp.ones((8, 3 * size), BF16)
    is_square = lax.broadcasted_iota(jnp.int32, (8, length), 0) == 0
    sums_ref[...] = jnp.where(
        is_square,
        dot(ones, split(square), CONTRACT_COLS),
        dot(ones, split(inner), CONTRACT_COLS),
    )


def attn_grad_body(plan, parties, *refs):
    sums_refs, refs = refs[:parties], refs[parties:]
    attended_ref, query_decayed_ref, gained_ref, attn_grad_ref, held_ref = refs[:5]
    send_refs = refs[5:]
    size, length = plan.size, attended_ref.shape[0]
    feature_count = plan.heads * size * parties
    sums = sum(ref[...] for ref in sums_refs)
    inv_row = lax.rsqrt(sums[:1] / feature_count + EPSILON)
    coefficient_row = sums[1:2] * inv_row * inv_row * inv_row / feature_count
    is_inverse = lax.broadcasted_iota(jnp.int32, (8, length), 0) == 0
    columns = jnp.transpose(jnp.where(is_inverse, inv_row, coefficient_row))
    inv_rms = jnp.broadcast_to(columns[:, :1], (length, size))
    coefficient = jnp.broadcast_to(columns[:, 1:2], (length, size))
    for h in range(plan.heads):
        cut = lanes(h, size)
        attn_grad = gained_ref[:, cut] * inv_rms - attended_ref[:, cut] * coefficient
        attn_grad = attn_grad.astype(BF16)
        attn_grad_ref[:, cut] = attn_grad
        held_ref[cut] = dot(query_decayed_ref[h], attn_grad)
    for k, send_ref in enumerate(send_refs):
        send_ref[...] = held_ref[plan.rows_of(plan.peer(k))]


def score_grad_body(
    plan,
    attn_grad_ref,
    query_ref,
    key_ref,
    value_ref,
    states_ref,
    weight_ref,
    cum_ref,
    cum_col_ref,
    query_grad_ref,
    key_part_ref,
    value_part_ref,
    shrink_ref,
):
    length = query_ref.shape[0]
    causal = causal_mask(length)
    cum_col = cum_col_ref[...]
    growth = jnp.exp(cum_col)
    shrink = jnp.exp(cum_col[length - 1 : length, :] - cum_col)
    for h in range(plan.heads):
        cut = lanes(h, plan.size)
        attn_grad = attn_grad_ref[:, cut]
        scores = dot(attn_grad, value_ref[:, cut], CONTRACT_COLS)
        score_grad = (scores * decay_matrix(cum_ref, cum_col, causal, h)).astype(BF16)
        carried = dot(attn_grad, states_ref[cut], CONTRACT_COLS)
        query_grad = dot(score_grad, key_ref[:, cut]) + growth[:, h : h + 1] * carried
        query_grad_ref[:, cut] = query_grad.astype(BF16)
        key_part_ref[:, cut] = dot(score_grad, query_ref[:, cut], CONTRACT_ROWS)
        value_part_ref[:, cut] = dot(weight_ref[h], attn_grad, CONTRACT_ROWS)
        shrink_ref[h] = jnp.broadcast_to(shrink[:, h : h + 1], (length, plan.size))


def finish_body(plan, ways, *refs):
    count = len(ways)
    early_refs = dict(zip([way for way in plan.early_ways if way in ways], refs[:count]))
    late_refs = dict(zip(ways, refs[count : 2 * count]))
    refs = refs[2 * count :]
    key_part_ref, value_part_ref, key_ref, value_ref, shrink_ref = refs[:5]
    summary_ref, before_ref, logs_ref = refs[5:8]
    key_out, value_out, total_out, key_grad_ref, value_grad_ref, total_ref, sems = refs[-7:]
    size, rows = plan.size, plan.rows
    first = plan.group() == 0
    copies = []
    for i, way in enumerate(ways):
        owner = plan.toward(way)
        before, after = early_refs[way][:rows], late_refs[way][:rows]
        if plan.groups == 2:
            before, after = jnp.where(first, before, after), jnp.where(first, after, before)
        for j in range(plan.own):
            head = owner * plan.own + j
            part = pl.ds(pl.multiple_of(head * size, size), size)
            cut = slice(i * rows + j * size, i * rows + (j + 1) * size)
            grads = after[lanes(j, size)]
            log_before = before_ref[pl.ds(head, 1)]
            scale = jnp.exp(log_before)
            scale_next = jnp.exp(log_before + logs_ref[plan.member(), pl.ds(head, 1)])
            total_ref[cut] = (
                before[lanes(j, size)] + scale * summary_ref[part] + scale_next * grads
            )
            grads = grads.astype(BF16)
            key_state = dot(value_ref[:, part], grads, CONTRACT_COLS)
            key_grad_ref[:, cut] = (key_part_ref[:, part] + shrink_ref[head] * key_state).astype(BF16)
            value_state = dot(key_ref[:, part], grads)
            value_grad_ref[:, cut] = (value_part_ref[:, part] + shrink_ref[head] * value_state).astype(BF16)
        done, place = lanes(i, rows), plan.rows_of(owner)
        for source, target in [
            (total_ref.at[done], total_out.at[place]),
            (key_grad_ref.at[:, done], key_out.at[:, place]),
            (value_grad_ref.at[:, done], value_out.at[:, place]),
        ]:
            copies.append(pltpu.make_async_copy(source, target, sems.at[len(copies)]))
            copies[-1].start()
    for copy in copies:
        copy.wait()


def on_device(
    query_rows, key_rows, value_rows, log_decay, out_grad, norm_gain, state_in, state_out_grad
):
    heads, length = log_decay.shape
    size = state_in.shape[1]
    width = heads * size
    parties = lax.axis_size("head")
    plan = Plan(heads, size, lax.axis_size("seq"))
    bind = lambda body, *extra: functools.partial(body, plan, *extra)
    gain = norm_gain.reshape(1, width)
    piece = shaped((plan.rows, size))
    pieces = [piece] * plan.members
    chunk_piece = shaped((plan.chunk_rows, size))
    chunk_pieces = [chunk_piece] * plan.members
    logged = shaped((plan.chunk_rows + LOG_ROWS, size))
    block_logs = shaped((plan.members, LOG_ROWS, size))
    group_logs = shaped((plan.groups, LOG_ROWS, size))
    table = shaped((length, width))
    rounded = shaped((length, width), BF16)
    hold = pltpu.VMEM((plan.members, plan.rows, size), F32)
    hold_groups = pltpu.VMEM((plan.groups, plan.rows, size), F32)
    hold_chunk = pltpu.VMEM((plan.members, plan.chunk_rows, size), F32)
    hold_chunk_groups = pltpu.VMEM((plan.groups, plan.chunk_rows, size), F32)
    chunks = range(plan.chunks)
    state_rows = state_in.reshape(width, size)

    messages = plan.first_messages()
    *sends, cum_log, cum_col = call(
        bind(summary_body),
        [chunk_piece if chunk else logged for _, chunk in messages]
        + [shaped((heads, length)), shaped((length, heads))],
        [pltpu.with_memory_space_constraint(x, pltpu.HBM) for x in (key_rows, value_rows, log_decay)],
        [
            pltpu.VMEM((width, size), F32),
            pltpu.VMEM((length, width), BF16),
            pltpu.VMEM((length, width), BF16),
            pltpu.VMEM((heads, length), F32),
            pltpu.SemaphoreType.DMA((3,)),
        ],
        specs=[HBM] * 3,
    )
    received = {key: plan.swap(send, key[0]) for key, send in zip(messages, sends)}
    parts = [[received[way, c] for way in plan.ways] for c in chunks]
    totals = []
    for c in chunks:
        if c == 0:
            total, logs = call(
                bind(group_total_body, c), [logged, block_logs], parts[c], [hold_chunk]
            )
        else:
            (total,) = call(
                bind(group_total_body, c),
                [chunk_piece],
                [*parts[c], logs],
                [hold_chunk],
                flops=LONG,
            )
        totals.append([total] + plan.from_groups(total))
    states = {}
    far_parts = []
    for c in chunks:
        last = c == plan.chunks - 1
        operands = [*parts[c], *totals[c], state_rows, logs]
        outs = [piece if way in plan.far and last else chunk_piece for way in plan.ways]
        if c == 0:
            outs += [shaped((LOG_ROWS, size)), group_logs]
        else:
            operands += [all_logs]
        sends = call(
            bind(forward_scan_body, c),
            outs,
            operands + (far_parts if last else []),
            [hold_chunk_groups, hold_chunk],
        )
        if c == 0:
            before, all_logs = sends[plan.members :]
        for way, send in zip(plan.ways, sends):
            if way not in plan.far:
                states[way, c] = plan.swap(send, way)
            elif last:
                states[way, None] = plan.swap(send, way)
            else:
                far_parts.append(send)
    early = [states[way, 0] for way in plan.near] if plan.chunks > 1 else []
    weights, intra, gained, query_decayed = call(
        bind(intra_body),
        [
            shaped((heads, length, length), BF16),
            table,
            table,
            shaped((heads, size, length), BF16),
        ],
        [query_rows, key_rows, value_rows, cum_log, cum_col, out_grad, gain, *early],
        specs=[VMEM] * 7 + [ANY] * len(early),
        flops=LONG // 10,
    )
    attended, sums, states = call(
        bind(attended_body),
        [table, shaped((8, length)), shaped((width, size), BF16)],
        [*[states[key] for key in plan.last_messages()], intra, query_rows, cum_col, gained],
    )
    all_sums = [sums] + [
        lax.ppermute(sums, "head", [(i, (i + step) % parties) for i in range(parties)])
        for step in range(1, parties)
    ]
    attn_grad, summary, *sends = call(
        bind(attn_grad_body, parties),
        [rounded, shaped((width, size))] + pieces,
        [*all_sums, attended, query_decayed, gained],
    )
    parts = plan.swap_in_group(sends)
    query_grad, key_part, value_part, shrink = call(
        bind(score_grad_body),
        [rounded, table, table, shaped((heads, length, size))],
        [attn_grad, query_rows, key_rows, value_rows, states, weights, cum_log, cum_col],
        flops=10 * heads * length * length * size,
    )
    grad_rows = state_out_grad.reshape(width, size)
    two_sided = plan.groups == 2
    tie, swapped = key_part, []
    if two_sided:
        sends = call(
            bind(early_body),
            [piece, shaped((plan.rows + LOG_ROWS, size))] + pieces[2:],
            [*parts, logs, grad_rows, key_part],
            [hold],
            specs=[VMEM] * (plan.members + 2) + [ANY],
        )
        tie = sends[0]
        swapped = [dict(zip(plan.early_ways, plan.swap_in_group(sends, plan.early_ways)))]
    (total,) = call(
        bind(group_grad_body),
        [piece],
        [*parts, logs, tie],
        [hold],
        specs=[VMEM] * (plan.members + 1) + [ANY],
    )
    totals = [total] + plan.from_groups(total)
    sends = call(
        bind(reverse_scan_body),
        pieces * (1 if two_sided else 2),
        [*parts, *totals, logs, all_logs, grad_rows, swapped[0][plan.early_ways[1]] if two_sided else tie],
        [hold_groups, hold],
        specs=[VMEM] * (plan.members + plan.groups + 3) + [ANY],
    )
    for first in range(0, len(sends), plan.members):
        pieces_back = plan.swap_in_group(sends[first : first + plan.members], plan.late_ways)
        swapped.append(dict(zip(plan.late_ways, pieces_back)))
    outs = []
    for ways in ([0], plan.late_ways[1:]):
        if not ways:
            continue
        operands = [
            *[swapped[0][way] for way in plan.early_ways if way in ways],
            *[swapped[1][way] for way in ways],
            key_part,
            value_part,
            key_rows,
            value_rows,
            shrink,
            summary,
            before,
            logs,
        ]
        count = len(operands)
        outs = call(
            bind(finish_body, ways),
            [rounded, rounded, shaped((width, size))],
            [*operands, *outs],
            [
                pltpu.VMEM((length, len(ways) * plan.rows), BF16),
                pltpu.VMEM((length, len(ways) * plan.rows), BF16),
                pltpu.VMEM((len(ways) * plan.rows, size), F32),
                pltpu.SemaphoreType.DMA((3 * len(ways),)),
            ],
            specs=[VMEM] * count + [HBM] * len(outs),
            out_specs=[HBM] * 3,
            aliases={count + i: i for i in range(len(outs))},
        )
    key_grad, value_grad, state_in_grad = outs
    return (query_grad, key_grad, value_grad, state_in_grad.reshape(heads, size, size))


def solution(mesh):
    return jax.shard_map(
        on_device,
        mesh=mesh,
        in_specs=(
            P("seq", "head"),
            P("seq", "head"),
            P("seq", "head"),
            P("head", "seq"),
            P("seq", "head"),
            P("head"),
            P("head", None, None),
            P("head", None, None),
        ),
        out_specs=(P("seq", "head"), P("seq", "head"), P("seq", "head"), P("head", None, None)),
        check_vma=False,
    )
```
